32 devices in a mesh: frame: 8 (over y, x, core), batch: 4 (over z).
Axes of the slice: x: 2, y: 2, z: 4, core: 2. Of those that a mesh axis runs over, the one named last changes fastest.
Arguments:
- tokens: bfloat16 [16, 1024, 1024], P('batch', 'frame'), may hold values from -6 to 6
- out_cotangent: bfloat16 [16, 1024, 1024], P('batch', 'frame'), may hold values from -6 to 6
- buckets: int32 [16], P('batch'), may hold values from 0 to 1
- noise_levels: int32 [16, 4], P('batch'), may hold values from 0 to 999
- owned_block: int32 [32], replicated, may hold values from 0 to 31, as said below
- master: float32 [32, 589824], P(('frame', 'batch'))
- first_moment: float32 [32, 589824], P(('frame', 'batch'))
- second_moment: float32 [32, 589824], P(('frame', 'batch')), as said below
Outputs:
- activations: bfloat16 [16, 1024, 1024], P('batch', 'frame')
- input_grad: bfloat16 [16, 1024, 1024], P('batch', 'frame')
- new_master: float32 [32, 589824], P(('frame', 'batch'))
- new_first: float32 [32, 589824], P(('frame', 'batch'))
- new_second: float32 [32, 589824], P(('frame', 'batch'))
The draws below stay inside these ranges and needn't reach their ends.
Inputs may be any that keep to these rules, and one draw needn't show every extreme that they name: `owned_block`: a permutation: every block of the flattened weights has exactly one owner. `second_moment`: positive.
All inputs are finite; a program needn't handle non-finite values.
Results may differ from the reference program's by a relative error of at most 0.012.
Values may be sent and summed in bfloat16 or wider, within the bound.
A program may use at most 448 MiB of HBM per device.

```python
import math
import jax
import jax.numpy as jnp
from jax import lax

D = 1024
H = 16
HD = 64
FF = 4096
FRAME_LO = 256
STEP = 10
SEQ = 1024
BATCHES = 16
FRAMES = 4
PARAMS = 18874368
BLK = 589824


def owner_order(key):
    return jax.random.permutation(jax.random.fold_in(key, 71), PARAMS // BLK).astype(jnp.int32)


def entry_region(key):
    owners = owner_order(key)
    offsets = owners[:, None] * BLK + jnp.arange(BLK, dtype=jnp.int32)[None, :]
    bounds = [6 * D * D, 9 * D * D, 10 * D * D, 10 * D * D + D * FF]
    region = jnp.zeros(offsets.shape, jnp.int32)
    for boundary in bounds:
        region = region + (offsets >= boundary).astype(jnp.int32)
    return region


def region_pick(region, choices_list):
    picked = jnp.full(region.shape, choices_list[0], jnp.float32)
    for region_id in range(1, 5):
        picked = jnp.where(region == region_id, choices_list[region_id], picked)
    return picked


def weight_scales():
    return [D ** (-0.5), D ** (-0.5), 4.0 * D ** (-0.5), D ** (-0.5), FF ** (-0.5)]


def grad_scales():
    root_tokens = math.sqrt(BATCHES * SEQ)
    return [0.2 * root_tokens, 0.05 * root_tokens, 0.05 * root_tokens, 0.15 * root_tokens, 0.3 * root_tokens]


def draw_owned_block(key, part):
    return owner_order(key)


def draw_master(key, part):
    region = entry_region(key)
    key = jax.random.fold_in(key, 1)
    spread = region_pick(region, weight_scales())
    values = jax.random.truncated_normal(key, -3.0, 3.0, region.shape, jnp.float32)
    return values * spread


def draw_first_moment(key, part):
    region = entry_region(key)
    key = jax.random.fold_in(key, 2)
    spread = region_pick(region, grad_scales())
    values = jax.random.truncated_normal(key, -3.0, 3.0, region.shape, jnp.float32)
    return values * spread


def draw_second_moment(key, part):
    region = entry_region(key)
    key = jax.random.fold_in(key, 3)
    spread = region_pick(region, grad_scales())
    factor = jnp.exp(jax.random.uniform(key, region.shape, jnp.float32, 0.0, math.log(4.0)))
    return factor * spread * spread


def place_ends(array, rng, low, top_value):
    longest = array.shape.index(max(array.shape))
    spots = []
    for shift in (0, 1):
        where = [jax.random.randint(jax.random.fold_in(rng, axis), (), 0, length) for axis, length in enumerate(array.shape)]
        where[longest] = (where[longest] + shift) % array.shape[longest]
        spots.append(tuple(where))
    return array.at[spots[0]].set(low).at[spots[1]].set(top_value)


def block_scale(rng, shape, pieces, low, top_value):
    def one(dim, parts):
        steps = jax.random.uniform(jax.random.fold_in(jax.random.fold_in(rng, 6), dim), (parts,), jnp.float32, low / len(pieces), top_value / len(pieces))
        return jnp.repeat(jnp.exp(steps), shape[dim] // parts).reshape((-1,) + (1,) * (len(shape) - dim - 1))

    gain = one(*pieces[0])
    for cut in pieces[1:]:
        gain = gain * one(*cut)
    return gain


def bell_draw(stream_key, dims, deviation, bound, shards=(), kind=jnp.bfloat16):
    entries = jax.random.normal(stream_key, dims, jnp.float32) * deviation
    if len(shards) > 0:
        entries = block_scale(stream_key, dims, shards, -0.22, 0.18) * entries
    return jnp.clip(entries, min=-bound, max=bound).astype(kind)


def setup_inputs(seed: int = 0) -> dict:
    key_list = jax.random.split(jax.random.key(seed), 9)
    return {
        "tokens": bell_draw(key_list[0], (BATCHES, SEQ, D), 1.0, 6.0, ((0, 4), (1, 8))),
        "out_cotangent": bell_draw(key_list[1], (BATCHES, SEQ, D), 1.0, 6.0, ((0, 4), (1, 8))),
        "buckets": place_ends(jax.random.randint(key_list[2], (BATCHES,), 0, 2), jax.random.fold_in(key_list[2], 1), 0, 1).astype(jnp.int32),
        "noise_levels": place_ends(jax.random.randint(key_list[3], (BATCHES, FRAMES), 0, 1000), jax.random.fold_in(key_list[3], 1), 0, 999).astype(jnp.int32),
        "owned_block": draw_owned_block(jax.random.fold_in(key_list[8], 71), 0),
        "master": draw_master(jax.random.fold_in(key_list[8], 71), 0),
        "first_moment": draw_first_moment(jax.random.fold_in(key_list[8], 71), 0),
        "second_moment": draw_second_moment(jax.random.fold_in(key_list[8], 71), 0),
    }


@jax.custom_vjp
def low(v):
    return lax.optimization_barrier(v.astype(jnp.bfloat16)).astype(jnp.float32)

@jax.custom_vjp
def low_back(v):
    return v

def low_keep(v):
    return (low(v), None)

def low_pass(kept, grad):
    return (grad,)

def back_keep(v):
    return (v, None)

def back_low(kept, grad):
    return (low(grad),)
low.defvjp(low_keep, low_pass)
low_back.defvjp(back_keep, back_low)
HIGHEST = lax.Precision.HIGHEST
NEG_FILL = -1e+30
BETA_ONE = 0.5
BETA_TWO = 0.5
LEARN_RATE = 0.05
WEIGHT_DECAY = 0.1
ADAM_EPS = 1e-08

def layer_norm(values):
    centre = values - lax.optimization_barrier(jnp.mean(values, axis=-1, keepdims=True))
    return centre * lax.rsqrt(lax.optimization_barrier(jnp.mean(centre * centre, axis=-1, keepdims=True)) + 1e-06)

def noise_embedding(levels, feature_width):
    half_width = feature_width // 2
    frequencies = jnp.exp(-math.log(10000.0) * jnp.arange(half_width, dtype=jnp.float32) / half_width)
    angles = levels.astype(jnp.float32)[:, None] * frequencies[None, :]
    return jnp.concatenate([jnp.cos(angles), jnp.sin(angles)], axis=1)

def split_flat(flat_values, model_width, hidden_width):
    matrix_shapes = ((model_width, 6 * model_width), (model_width, 3 * model_width), (model_width, model_width), (model_width, hidden_width), (hidden_width, model_width))
    matrices = []
    offset_now = 0
    for matrix_shape in matrix_shapes:
        entry_count = matrix_shape[0] * matrix_shape[1]
        matrices.append(flat_values[offset_now:offset_now + entry_count].reshape(matrix_shape))
        offset_now = offset_now + entry_count
    return matrices

def attend_rows(query_rows, end_rows, key_all, value_all):
    scores = low_back(jnp.einsum('qhd,khd->hqk', query_rows, key_all, precision=HIGHEST))
    key_index = jnp.arange(key_all.shape[0], dtype=jnp.int32)
    visible = key_index[None, None, :] < end_rows[None, :, None]
    scores = jnp.where(visible, scores, NEG_FILL)
    row_peak = lax.optimization_barrier(jnp.max(scores, axis=-1, keepdims=True))
    weights = jnp.exp(scores - row_peak)
    probability = weights / lax.optimization_barrier(jnp.sum(weights, axis=-1, keepdims=True))
    return jnp.einsum('hqk,khd->qhd', low(probability), value_all, precision=HIGHEST)

def block_forward(inputs, w_ada, w_qkv, w_out, w_in, w_down, silu_cond, frame_of, frame_end):
    seq_len, model_width = inputs.shape
    modulation = jnp.dot(silu_cond, w_ada, precision=HIGHEST)
    token_mod = jnp.take(modulation, frame_of, axis=0)
    shift_one, scale_one, gate_one, shift_two, scale_two, gate_two = jnp.split(token_mod, 6, axis=1)
    h_one = low(layer_norm(inputs) * (1.0 + scale_one) + shift_one)
    projected = jnp.dot(h_one, w_qkv, precision=HIGHEST)
    queries = low(low_back(projected[:, :model_width] * HD ** (-0.5)))
    key_part = low(low_back(projected[:, model_width:2 * model_width]))
    value_part = low(low_back(projected[:, 2 * model_width:]))
    q_heads = queries.reshape(seq_len, H, HD)
    k_heads = key_part.reshape(seq_len, H, HD)
    v_heads = value_part.reshape(seq_len, H, HD)
    row_block = math.gcd(seq_len, 512)
    block_count = seq_len // row_block

    def attend_one(block_args):
        return attend_rows(block_args[0], block_args[1], k_heads, v_heads)
    attended = lax.map(jax.checkpoint(attend_one), (q_heads.reshape(block_count, row_block, H, HD), frame_end.reshape(block_count, row_block)))
    attended = low(low_back(attended.reshape(seq_len, model_width)))
    attn_out = low_back(jnp.dot(attended, w_out, precision=HIGHEST))
    middle = inputs + gate_one * attn_out
    h_two = low(layer_norm(middle) * (1.0 + scale_two) + shift_two)
    pre_act = low_back(jnp.dot(h_two, w_in, precision=HIGHEST))
    activated = low(jax.nn.gelu(pre_act, approximate=True))
    mlp_out = low_back(jnp.dot(activated, w_down, precision=HIGHEST))
    return middle + gate_two * mlp_out

def reference(tokens, out_cotangent, buckets, noise_levels, owned_block, master, first_moment, second_moment):
    block_size = master.shape[1]
    inverse_order = jnp.argsort(owned_block)
    weight_flat = low(jnp.take(master, inverse_order, axis=0).reshape(-1))
    matrices = split_flat(weight_flat, D, FF)
    positions = jnp.arange(SEQ, dtype=jnp.int32)

    def one_sequence(totals, sequence_item):
        inputs, cotangent, bucket, levels = sequence_item
        frame_len = FRAME_LO * (1 + 3 * bucket)
        frame_of = positions // frame_len
        frame_end = (frame_of + 1) * frame_len
        silu_cond = low(jax.nn.silu(noise_embedding(levels, D)))

        def forward(x_values, w_ada, w_qkv, w_out, w_in, w_down):
            return block_forward(x_values, w_ada, w_qkv, w_out, w_in, w_down, silu_cond, frame_of, frame_end)
        result, pull_back = jax.vjp(forward, inputs.astype(jnp.float32), *matrices)
        gradients = pull_back(cotangent.astype(jnp.float32))
        totals = tuple((running_total + new_grad for running_total, new_grad in zip(totals, gradients[1:])))
        return (totals, (result.astype(jnp.bfloat16), gradients[0].astype(jnp.bfloat16)))
    start_totals = tuple((jnp.zeros_like(matrix) for matrix in matrices))
    totals, (outputs, input_grads) = lax.scan(one_sequence, start_totals, (tokens, out_cotangent, buckets, noise_levels))
    grad_flat = jnp.concatenate([running_total.reshape(-1) for running_total in totals])
    grad_rows = jnp.take(grad_flat.reshape(-1, block_size), owned_block, axis=0)
    new_first = BETA_ONE * first_moment + (1.0 - BETA_ONE) * grad_rows
    new_second = BETA_TWO * second_moment + (1.0 - BETA_TWO) * grad_rows * grad_rows
    fix_one = 1.0 - BETA_ONE ** STEP
    fix_two = 1.0 - BETA_TWO ** STEP
    update = new_first / fix_one / (jnp.sqrt(new_second / fix_two) + ADAM_EPS)
    new_master = master - LEARN_RATE * (update + WEIGHT_DECAY * master)
    return (outputs, input_grads, new_master, new_first, new_second)
```

```python
from functools import partial
import math

import jax
import jax.numpy as jnp
import numpy as np
from jax import lax
from jax.experimental import pallas as pl
from jax.experimental.pallas import tpu as pltpu
from jax.sharding import PartitionSpec as P

H = 16
HD = 64
FF = 4096
FRAME_LO = 256
STEP = 10

HIGHEST = lax.Precision.HIGHEST
NEG_FILL = -1e30
BETA_ONE = 0.5
BETA_TWO = 0.5
LEARN_RATE = 0.05
WEIGHT_DECAY = 0.1
ADAM_EPS = 1e-08
MESH = pl.DeviceIdType.MESH
F32 = jnp.float32
BF16 = jnp.bfloat16
ANY = pl.BlockSpec(memory_space=pl.ANY)
VMEM_LIMIT = 60 * 1024 * 1024

ROWS = 576
GROUP = 144
FIRST = 10
KINDS = (("qkv", 1024, 3), ("out", 1024, 1), ("in", 1024, 4), ("down", 4096, 1))
SPANS = {"qkv": (96, 864), "out": (864, 1120), "in": (1120, 2144), "down": (2144, 3168)}
HELD = 3168


def pieces(kind, z):
    if kind == "qkv":
        found = [(96 + 16 * j, 16, 16 * z, j) for j in range(3)]
        for k in range(5):
            found += [(144 + 144 * k + 48 * j, 48, 64 + 192 * k + 48 * z, j) for j in range(3)]
        return found
    if kind == "out":
        return [(864, 144, 144 * z, 0), (1008, 112, 576 + 112 * z, 0)]
    if kind == "in":
        return [(1120, 1024, 0, z)]
    found = [(2144, 16, 16 * z, 0)]
    return found + [(2160 + 144 * k, 144, 64 + 576 * k + 144 * z, 0) for k in range(7)]


def block_rows(block):
    t = np.arange(GROUP)
    groups = []
    for z in range(4):
        if block == 10:
            i = t - 96
            rows = np.where(t < 96, 96 * z + t, 384 + 3 * (16 * z + i % 16) + i // 16)
        elif 11 <= block <= 15:
            rows = 3 * (48 * z + t % 48) + t // 48
        elif block == 17:
            rows = np.where(t < 112, 112 * z + t, 448 + 4 * (t - 112) + z)
        elif 18 <= block <= 23:
            rows = 4 * t + z
        elif block == 24:
            rows = np.where(t < 128, 4 * t + z, 512 + 16 * z + t - 128)
        else:
            rows = GROUP * z + t
        groups.append(rows)
    return np.concatenate(groups)


def ada_rows(z):
    t = jnp.arange(GROUP, dtype=jnp.int32)
    rows = [96 * b + 24 * z + t // 6 for b in range(10)]
    rows.append(jnp.where(t < 96, 960 + 16 * z + t // 6, -1))
    return jnp.concatenate(rows), jnp.tile(t % 6, 11)


def frame_index():
    return lax.axis_index("frame"), lax.axis_index("batch")


def strip_of(f):
    return 4 * (f % 2) + f // 2


def greet(devices):
    barrier = pltpu.get_barrier_semaphore()
    for device in devices:
        pl.semaphore_signal(barrier, inc=1, device_id=device, device_id_type=MESH)
    pl.semaphore_wait(barrier, len(devices))


def greet_all(total, batch):
    f, z = frame_index()
    me = f * batch + z
    barrier = pltpu.get_barrier_semaphore()

    def hail(k, carry):
        other = (me + k) % total
        pl.semaphore_signal(barrier, inc=1, device_id=(other // batch, other % batch), device_id_type=MESH)
        return carry

    lax.fori_loop(1, total, hail, 0)
    pl.semaphore_wait(barrier, total - 1)


def remote(src, dst, send, recv, device):
    copy = pltpu.make_async_remote_copy(
        src_ref=src, dst_ref=dst, send_sem=send, recv_sem=recv, device_id=device, device_id_type=MESH
    )
    copy.start()
    return copy


def local(src, dst, sem):
    copy = pltpu.make_async_copy(src, dst, sem)
    copy.start()
    return copy


def video_kernel(videos, per, arrays, *refs):
    ins, outs = refs[:arrays], refs[arrays : 2 * arrays]
    send, recv, own = refs[2 * arrays :]
    f, z = frame_index()
    mine, g = f // per, f % per
    others = [((mine + k) % videos, k) for k in range(1, videos)]
    greet([(v * per + g, z) for v, k in others])
    copies = []
    for a in range(arrays):
        for v, k in others:
            copies.append(
                remote(ins[a].at[v], outs[a].at[mine], send.at[a, k], recv.at[a, k], (v * per + g, z))
            )
        copies.append(local(ins[a].at[mine], outs[a].at[mine], own.at[a]))
    for copy in copies:
        copy.wait()


def swap_videos(arrays, videos, per, ident):
    count = len(arrays)
    return pl.pallas_call(
        partial(video_kernel, videos, per, count),
        out_shape=[jax.ShapeDtypeStruct(a.shape, a.dtype) for a in arrays],
        in_specs=[ANY] * count,
        out_specs=[ANY] * count,
        scratch_shapes=[
            pltpu.SemaphoreType.DMA((count, videos)),
            pltpu.SemaphoreType.DMA((count, videos)),
            pltpu.SemaphoreType.DMA((count,)),
        ],
        compiler_params=pltpu.CompilerParams(collective_id=ident, has_side_effects=True),
        name="swap_videos",
    )(*arrays)


def scatter_kernel(total, batch, blk, levels, tok, cot, cut, all_levels, tok_out, cot_out, send, recv, vsend, vrecv, lsend, lrecv, own):
    f, z = frame_index()
    me = f * batch + z
    greet_all(total, batch)
    mine, g = f // 2, f % 2

    def group(k, start):
        other = (me + k) % total
        of, oz = other // batch, other % batch
        copy = pltpu.make_async_remote_copy(
            src_ref=blk.at[pl.ds(pl.multiple_of(GROUP * oz, 16), GROUP), pl.ds(pl.multiple_of(128 * strip_of(of), 128), 128)],
            dst_ref=cut.at[me],
            send_sem=send.at[k],
            recv_sem=recv.at[k],
            device_id=(of, oz),
            device_id_type=MESH,
        )
        if start:
            copy.start()
        else:
            copy.wait()

    copies = []
    for k in range(1, batch):
        copies.append(remote(levels, all_levels.at[z], lsend.at[k], lrecv.at[k], (f, (z + k) % batch)))
    copies.append(local(levels, all_levels.at[z], own.at[0]))
    lax.fori_loop(1, total, lambda k, c: (group(k, True), c)[1], 0)
    copies.append(
        local(
            blk.at[pl.ds(pl.multiple_of(GROUP * z, 16), GROUP), pl.ds(pl.multiple_of(128 * strip_of(f), 128), 128)],
            cut.at[me],
            own.at[1],
        )
    )
    for a, (src, dst) in enumerate(((tok, tok_out), (cot, cot_out))):
        for k in range(1, 4):
            v = (mine + k) % 4
            copies.append(remote(src.at[v], dst.at[mine], vsend.at[a, k], vrecv.at[a, k], (v * 2 + g, z)))
        copies.append(local(src.at[mine], dst.at[mine], own.at[2 + a]))
    for copy in copies:
        copy.wait()
    lax.fori_loop(1, total, lambda k, c: (group(k, False), c)[1], 0)


def scatter_blocks(blk, levels, tok, cot, total, batch):
    return pl.pallas_call(
        partial(scatter_kernel, total, batch),
        out_shape=[
            jax.ShapeDtypeStruct((total, GROUP, 128), BF16),
            jax.ShapeDtypeStruct((batch,) + levels.shape, levels.dtype),
            jax.ShapeDtypeStruct(tok.shape, tok.dtype),
            jax.ShapeDtypeStruct(cot.shape, cot.dtype),
        ],
        in_specs=[ANY] * 4,
        out_specs=[ANY] * 4,
        scratch_shapes=[
            pltpu.SemaphoreType.DMA((total,)),
            pltpu.SemaphoreType.DMA((total,)),
            pltpu.SemaphoreType.DMA((2, 4)),
            pltpu.SemaphoreType.DMA((2, 4)),
            pltpu.SemaphoreType.DMA((batch,)),
            pltpu.SemaphoreType.DMA((batch,)),
            pltpu.SemaphoreType.DMA((4,)),
        ],
        compiler_params=pltpu.CompilerParams(collective_id=0, has_side_effects=True),
        name="scatter_blocks",
    )(blk, levels, tok, cot)


def collect_kernel(total, batch, cut, act, grad, blk, act_out, grad_out, send, recv, vsend, vrecv, own):
    f, z = frame_index()
    me = f * batch + z
    greet_all(total, batch)
    mine, g = f // 2, f % 2

    def spot(of, oz):
        return blk.at[pl.ds(pl.multiple_of(GROUP * oz, 16), GROUP), pl.ds(pl.multiple_of(128 * strip_of(of), 128), 128)]

    def group(k, start):
        other = (me + k) % total
        copy = pltpu.make_async_remote_copy(
            src_ref=cut.at[other],
            dst_ref=spot(f, z),
            send_sem=send.at[k],
            recv_sem=recv.at[k],
            device_id=(other // batch, other % batch),
            device_id_type=MESH,
        )
        if start:
            copy.start()
        else:
            copy.wait()

    lax.fori_loop(1, total, lambda k, c: (group(k, True), c)[1], 0)
    copies = [local(cut.at[me], spot(f, z), own.at[0])]
    for a, (src, dst) in enumerate(((act, act_out), (grad, grad_out))):
        for k in range(1, 4):
            v = (mine + k) % 4
            copies.append(remote(src.at[v], dst.at[mine], vsend.at[a, k], vrecv.at[a, k], (v * 2 + g, z)))
        copies.append(local(src.at[mine], dst.at[mine], own.at[1 + a]))
    for copy in copies:
        copy.wait()
    lax.fori_loop(1, total, lambda k, c: (group(k, False), c)[1], 0)


def collect_blocks(cut, act, grad, total, batch):
    return pl.pallas_call(
        partial(collect_kernel, total, batch),
        out_shape=[
            jax.ShapeDtypeStruct((ROWS, 1024), BF16),
            jax.ShapeDtypeStruct(act.shape, act.dtype),
            jax.ShapeDtypeStruct(grad.shape, grad.dtype),
        ],
        in_specs=[ANY] * 3,
        out_specs=[ANY] * 3,
        scratch_shapes=[
            pltpu.SemaphoreType.DMA((total,)),
            pltpu.SemaphoreType.DMA((total,)),
            pltpu.SemaphoreType.DMA((2, 4)),
            pltpu.SemaphoreType.DMA((2, 4)),
            pltpu.SemaphoreType.DMA((3,)),
        ],
        compiler_params=pltpu.CompilerParams(collective_id=3, has_side_effects=True),
        name="collect_blocks",
    )(cut, act, grad)


def plane():
    f, z = frame_index()
    y, x, c = f // 4, (f // 2) % 2, f % 2
    at_x = (4 * y + 2 * (1 - x) + c, z)
    at_y = (4 * (1 - y) + 2 * x + c, z)
    at_c = (4 * y + 2 * x + 1 - c, z)
    return y, x, c, z, at_x, at_y, at_c


def lanes(first, count):
    return pl.ds(pl.multiple_of(first, 128), count)


def gather_kernel(total, batch, held, mod, *refs):
    mats = dict(zip([kind for kind, _, _ in KINDS], refs[:4]))
    mod_out, zsend, zrecv, psend, precv, msend, mrecv, own = refs[4:]
    y, x, c, z, at_x, at_y, at_c = plane()
    f = 4 * y + 2 * x + c
    me = f * batch + z
    strip = 4 * c + 2 * y + x
    greet_all(total, batch)

    def mod_group(k, start):
        other = (me + k) % total
        of, oz = other // batch, other % batch
        copy = pltpu.make_async_remote_copy(
            src_ref=mod.at[4 * oz + of // 2],
            dst_ref=mod_out.at[z, :, lanes(128 * strip, 128)],
            send_sem=msend.at[k],
            recv_sem=mrecv.at[k],
            device_id=(of, oz),
            device_id_type=MESH,
        )
        if start:
            copy.start()
        else:
            copy.wait()

    sends = []
    for m, (kind, _, _) in enumerate(KINDS):
        for k in range(1, batch):
            for row, count, to, j in pieces(kind, z):
                src = held.at[pl.ds(row, count)]
                dst = mats[kind].at[pl.ds(pl.multiple_of(to, 16), count), lanes(1024 * j + 128 * strip, 128)]
                remote(src, dst, zsend.at[m, k], zrecv.at[m, k], (f, (z + k) % batch))
        for row, count, to, j in pieces(kind, z):
            local(
                held.at[pl.ds(row, count)],
                mats[kind].at[pl.ds(pl.multiple_of(to, 16), count), lanes(1024 * j + 128 * strip, 128)],
                own.at[m],
            )
        if m == 0:
            lax.fori_loop(1, total, lambda k, cc: (mod_group(k, True), cc)[1], 0)
    mod_own = local(mod.at[4 * z + f // 2], mod_out.at[z, :, lanes(128 * strip, 128)], own.at[4])

    def whole(m):
        lo, hi = SPANS[KINDS[m][0]]
        return held.at[pl.ds(lo, hi - lo)]

    def z_wait(m):
        for k in range(1, batch):
            pltpu.make_async_copy(whole(m), whole(m), zrecv.at[m, k]).wait()
        pltpu.make_async_copy(whole(m), whole(m), own.at[m]).wait()

    slots = {}
    counter = [0]

    def push(key, mat, row, count, col, width, device):
        s = counter[0]
        counter[0] += 1
        ref = mat.at[pl.ds(row, count), lanes(col, width)]
        slots.setdefault(key, []).append(remote(ref, ref, psend.at[s], precv.at[s], device))

    def first(m):
        kind, depth, blocks = KINDS[m]
        half = depth // 2
        for j in range(blocks):
            push((m, 1), mats[kind], 0, half, 1024 * j + 128 * strip, 128, at_x)
            push((m, 1), mats[kind], half, half, 1024 * j + 128 * strip, 128, at_y)

    def second(m):
        kind, depth, blocks = KINDS[m]
        half = depth // 2
        for copy in slots[(m, 1)]:
            copy.wait_recv()
        for j in range(blocks):
            push((m, 2), mats[kind], 0, half, 1024 * j + 512 * c + 256 * y, 256, at_y)
            for yy in range(2):
                push((m, 2), mats[kind], half, half, 1024 * j + 512 * c + 256 * yy + 128 * x, 128, at_x)

    def third(m):
        kind, depth, blocks = KINDS[m]
        for copy in slots[(m, 2)]:
            copy.wait_recv()
        for j in range(blocks):
            push((m, 3), mats[kind], 0, depth, 1024 * j + 512 * c, 512, at_c)

    z_wait(0)
    first(0)
    z_wait(1)
    first(1)
    second(0)
    z_wait(2)
    first(2)
    second(1)
    third(0)
    z_wait(3)
    first(3)
    second(2)
    third(1)
    second(3)
    third(2)
    third(3)
    for m in range(4):
        for copy in slots[(m, 3)]:
            copy.wait_recv()
    for copies in slots.values():
        for copy in copies:
            copy.wait_send()
    for m in range(4):
        for k in range(1, batch):
            pltpu.make_async_copy(whole(m), whole(m), zsend.at[m, k]).wait()
    mod_own.wait()
    lax.fori_loop(1, total, lambda k, cc: (mod_group(k, False), cc)[1], 0)


def gather_matrices(held, mod, total, batch):
    return pl.pallas_call(
        partial(gather_kernel, total, batch),
        out_shape=[jax.ShapeDtypeStruct((depth, 1024 * blocks), BF16) for _, depth, blocks in KINDS]
        + [jax.ShapeDtypeStruct((batch, mod.shape[1], 1024), F32)],
        in_specs=[ANY] * 2,
        out_specs=[ANY] * 5,
        scratch_shapes=[
            pltpu.SemaphoreType.DMA((4, batch)),
            pltpu.SemaphoreType.DMA((4, batch)),
            pltpu.SemaphoreType.DMA((54,)),
            pltpu.SemaphoreType.DMA((54,)),
            pltpu.SemaphoreType.DMA((total,)),
            pltpu.SemaphoreType.DMA((total,)),
            pltpu.SemaphoreType.DMA((5,)),
        ],
        compiler_params=pltpu.CompilerParams(collective_id=1, has_side_effects=True),
        name="gather_matrices",
    )(held, mod)


def add_rows(dst, dst_col, src, src_col, width, first, count):
    step = 128

    def body(i, carry):
        rows = pl.ds(pl.multiple_of(first + i * step, 16), step)
        dst[rows, lanes(dst_col, width)] = dst[rows, lanes(dst_col, width)] + src[rows, lanes(src_col, width)]
        return carry

    lax.fori_loop(0, count // step, body, 0)


ORDER = (3, 2, 1, 0)


def reduce_kernel(total, batch, *refs):
    grads, dmod, out, dmod_out = refs[:4], refs[4], refs[5], refs[6]
    own, got, half_sum, strip_sum = refs[7:11], refs[11:15], refs[15:19], refs[19:23]
    zgot, psend, precv, lsem, zsend, zrecv, msend, mrecv, mown = refs[23:]
    y, x, c, z, at_x, at_y, at_c = plane()
    f = 4 * y + 2 * x + c
    me = f * batch + z
    greet_all(total, batch)

    def mod_group(k, start):
        other = (me + k) % total
        of, oz = other // batch, other % batch
        copy = pltpu.make_async_remote_copy(
            src_ref=dmod.at[:, lanes(128 * strip_of(of), 128)],
            dst_ref=dmod_out.at[me],
            send_sem=msend.at[k],
            recv_sem=mrecv.at[k],
            device_id=(of, oz),
            device_id_type=MESH,
        )
        if start:
            copy.start()
        else:
            copy.wait()

    slots = {}
    counter = [0]

    def push(key, src, dst, device):
        s = counter[0]
        counter[0] += 1
        slots.setdefault(key, []).append(remote(src, dst, psend.at[s], precv.at[s], device))

    def arrive(key):
        for copy in slots[key]:
            copy.wait_recv()

    def zero(m):
        kind, depth, blocks = KINDS[m]
        for j in range(blocks):
            push((m, 0), grads[m].at[:, lanes(1024 * j + 512 * (1 - c), 512)], got[m].at[:, lanes(512 * j, 512)], at_c)
        loads[m] = [
            local(grads[m].at[:, lanes(1024 * j + 512 * c, 512)], own[m].at[:, lanes(512 * j, 512)], lsem.at[m, j])
            for j in range(blocks)
        ]

    def first(m):
        kind, depth, blocks = KINDS[m]
        half = depth // 2
        for copy in loads[m]:
            copy.wait()
        arrive((m, 0))
        add_rows(own[m], 0, got[m], 0, 512 * blocks, 0, depth)
        for j in range(blocks):
            for yy in range(2):
                push(
                    (m, 1),
                    own[m].at[pl.ds(0, half), lanes(512 * j + 256 * yy + 128 * (1 - x), 128)],
                    half_sum[m].at[pl.ds(0, half), lanes(256 * j + 128 * yy, 128)],
                    at_x,
                )
            push(
                (m, 1),
                own[m].at[pl.ds(half, half), lanes(512 * j + 256 * (1 - y), 256)],
                half_sum[m].at[pl.ds(half, half), lanes(256 * j, 256)],
                at_y,
            )

    def second(m):
        kind, depth, blocks = KINDS[m]
        half = depth // 2
        arrive((m, 1))
        for j in range(blocks):
            for yy in range(2):
                add_rows(half_sum[m], 256 * j + 128 * yy, own[m], 512 * j + 256 * yy + 128 * x, 128, 0, half)
            add_rows(half_sum[m], 256 * j, own[m], 512 * j + 256 * y, 256, half, half)
        for j in range(blocks):
            push(
                (m, 2),
                half_sum[m].at[pl.ds(0, half), lanes(256 * j + 128 * (1 - y), 128)],
                strip_sum[m].at[pl.ds(0, half), lanes(128 * j, 128)],
                at_y,
            )
            push(
                (m, 2),
                half_sum[m].at[pl.ds(half, half), lanes(256 * j + 128 * (1 - x), 128)],
                strip_sum[m].at[pl.ds(half, half), lanes(128 * j, 128)],
                at_x,
            )

    def third(m):
        kind, depth, blocks = KINDS[m]
        half = depth // 2
        arrive((m, 2))
        for j in range(blocks):
            add_rows(strip_sum[m], 128 * j, half_sum[m], 256 * j + 128 * y, 128, 0, half)
            add_rows(strip_sum[m], 128 * j, half_sum[m], 256 * j + 128 * x, 128, half, half)
        for k in range(1, batch):
            to = (z + k) % batch
            for row, count, at, j in pieces(kind, to):
                remote(
                    strip_sum[m].at[pl.ds(pl.multiple_of(at, 16), count), lanes(128 * j, 128)],
                    zgot.at[k - 1, pl.ds(row, count)],
                    zsend.at[m, k],
                    zrecv.at[m, k],
                    (f, to),
                )

    def whole(m, k):
        lo, hi = SPANS[KINDS[m][0]]
        return zgot.at[k - 1, pl.ds(lo, hi - lo)]

    def last(m):
        kind, depth, blocks = KINDS[m]
        for k in range(1, batch):
            pltpu.make_async_copy(whole(m, k), whole(m, k), zrecv.at[m, k]).wait()
        for row, count, at, j in pieces(kind, z):
            step = 128 if count == 1024 else count

            def body(i, carry, row=row, at=at, j=j, step=step):
                rows = pl.ds(pl.multiple_of(row + i * step, 16), step)
                mine = strip_sum[m][pl.ds(pl.multiple_of(at + i * step, 16), step), lanes(128 * j, 128)]
                total_sum = mine.astype(F32)
                for k in range(batch - 1):
                    total_sum = total_sum + zgot[k, rows, :].astype(F32)
                out[rows, :] = total_sum.astype(BF16)
                return carry

            lax.fori_loop(0, count // step, body, 0)

    loads = {}
    a, b, cc, d = ORDER
    zero(a)
    zero(b)
    zero(cc)
    zero(d)
    lax.fori_loop(1, total, lambda k, u: (mod_group(k, True), u)[1], 0)
    mod_own = local(dmod.at[:, lanes(128 * strip_of(f), 128)], dmod_out.at[me], mown)
    out[pl.ds(0, 96), :] = jnp.zeros((96, 128), BF16)
    first(a)
    first(b)
    second(a)
    first(cc)
    second(b)
    third(a)
    first(d)
    second(cc)
    third(b)
    second(d)
    last(a)
    third(cc)
    last(b)
    third(d)
    last(cc)
    last(d)
    for copies in slots.values():
        for copy in copies:
            copy.wait_send()
    for m in range(4):
        for k in range(1, batch):
            pltpu.make_async_copy(whole(m, k), whole(m, k), zsend.at[m, k]).wait()
    mod_own.wait()
    lax.fori_loop(1, total, lambda k, u: (mod_group(k, False), u)[1], 0)


def reduce_matrices(grads, dmod, total, batch):
    def bufs(width):
        return [pltpu.VMEM((depth, blocks * width), BF16) for _, depth, blocks in KINDS]

    return pl.pallas_call(
        partial(reduce_kernel, total, batch),
        out_shape=[
            jax.ShapeDtypeStruct((HELD, 128), BF16),
            jax.ShapeDtypeStruct((total, dmod.shape[0], 128), F32),
        ],
        in_specs=[ANY] * 5,
        out_specs=[pl.BlockSpec(memory_space=pltpu.VMEM), ANY],
        scratch_shapes=bufs(512)
        + bufs(512)
        + bufs(256)
        + bufs(128)
        + [
            pltpu.VMEM((batch - 1, HELD, 128), BF16),
            pltpu.SemaphoreType.DMA((54,)),
            pltpu.SemaphoreType.DMA((54,)),
            pltpu.SemaphoreType.DMA((4, 4)),
            pltpu.SemaphoreType.DMA((4, batch)),
            pltpu.SemaphoreType.DMA((4, batch)),
            pltpu.SemaphoreType.DMA((total,)),
            pltpu.SemaphoreType.DMA((total,)),
            pltpu.SemaphoreType.DMA,
        ],
        compiler_params=pltpu.CompilerParams(
            collective_id=2, has_side_effects=True, vmem_limit_bytes=VMEM_LIMIT
        ),
        name="reduce_matrices",
    )(*grads, dmod)


def pick_kernel(index, src, dst):
    def body(i, carry):
        dst[i] = src[index[i]]
        return carry

    lax.fori_loop(0, dst.shape[0], body, 0)


def pick_blocks(index, src):
    whole = pl.BlockSpec(memory_space=pltpu.VMEM)
    return pl.pallas_call(
        pick_kernel,
        out_shape=jax.ShapeDtypeStruct((index.shape[0],) + src.shape[1:], src.dtype),
        in_specs=[pl.BlockSpec(memory_space=pltpu.SMEM), whole],
        out_specs=whole,
        name="pick_blocks",
    )(index, src)


def key_positions(rows, piece, per):
    i = lax.broadcasted_iota(jnp.int32, (rows, 1), 0)
    local_rows = rows // per
    return ((i % local_rows) // piece * per + i // local_rows) * piece + i % piece


def scores_t(k, q, ends, piece, per):
    s = lax.dot_general(k, q, (((1,), (1,)), ((), ())), preferred_element_type=F32)
    pos = key_positions(k.shape[0], piece, per)
    cols = []
    for t in range(q.shape[0] // piece):
        part = s[:, t * piece : (t + 1) * piece]
        cols.append(jnp.where(pos < ends[t], part, NEG_FILL))
    return jnp.concatenate(cols, axis=1)


def attend_kernel(piece, per, ends, q, k, v, o):
    outs = []
    for a in range(2):
        cut = slice(64 * a, 64 * a + 64)
        s = scores_t(k[:, cut], q[:, cut], ends, piece, per)
        peak = jnp.max(s, axis=0, keepdims=True)
        e = jnp.exp(s - peak)
        p = (e * (1.0 / jnp.sum(e, axis=0, keepdims=True))).astype(BF16)
        outs.append(lax.dot_general(p, v[:, cut], (((0,), (0,)), ((), ())), preferred_element_type=F32))
    o[...] = jnp.concatenate(outs, axis=1).astype(BF16)


def attend(ends, q, kv, piece, per):
    rows, width = q.shape
    keys = kv.shape[0]
    pairs = width // 128
    return pl.pallas_call(
        partial(attend_kernel, piece, per),
        grid_spec=pltpu.PrefetchScalarGridSpec(
            num_scalar_prefetch=1,
            grid=(pairs,),
            in_specs=[
                pl.BlockSpec((rows, 128), lambda h, e: (0, h)),
                pl.BlockSpec((keys, 128), lambda h, e: (0, h)),
                pl.BlockSpec((keys, 128), lambda h, e: (0, h + pairs)),
            ],
            out_specs=pl.BlockSpec((rows, 128), lambda h, e: (0, h)),
        ),
        out_shape=jax.ShapeDtypeStruct((rows, width), BF16),
        compiler_params=pltpu.CompilerParams(vmem_limit_bytes=VMEM_LIMIT),
        cost_estimate=pl.CostEstimate(
            flops=4 * rows * keys * width, bytes_accessed=4 * (rows + keys) * width, transcendentals=rows * keys * H
        ),
        name="attend",
    )(ends, q, kv, kv)


def attend_back_kernel(piece, per, ends, q, k, v, do, dq, dk, dv):
    dqs, dks, dvs = [], [], []
    for a in range(2):
        cut = slice(64 * a, 64 * a + 64)
        qa, ka, va, da = q[:, cut], k[:, cut], v[:, cut], do[:, cut]
        s = scores_t(ka, qa, ends, piece, per)
        peak = jnp.max(s, axis=0, keepdims=True)
        e = jnp.exp(s - peak)
        p = e * (1.0 / jnp.sum(e, axis=0, keepdims=True))
        dvs.append(jnp.dot(p.astype(BF16), da, preferred_element_type=F32))
        dp = lax.dot_general(va, da, (((1,), (1,)), ((), ())), preferred_element_type=F32)
        pdp = p * dp
        row = jnp.sum(pdp, axis=0, keepdims=True)
        ds = (pdp - p * row).astype(BF16)
        dks.append(jnp.dot(ds, qa, preferred_element_type=F32))
        dqs.append(lax.dot_general(ds, ka, (((0,), (0,)), ((), ())), preferred_element_type=F32))
    dq[...] = jnp.concatenate(dqs, axis=1).astype(BF16)
    dk[...] = jnp.concatenate(dks, axis=1).astype(BF16)
    dv[...] = jnp.concatenate(dvs, axis=1).astype(BF16)


def attend_back(ends, q, kv, do, piece, per):
    rows, width = q.shape
    keys = kv.shape[0]
    pairs = width // 128
    mine = pl.BlockSpec((rows, 128), lambda h, e: (0, h))
    allk = pl.BlockSpec((keys, 128), lambda h, e: (0, h))
    return pl.pallas_call(
        partial(attend_back_kernel, piece, per),
        grid_spec=pltpu.PrefetchScalarGridSpec(
            num_scalar_prefetch=1,
            grid=(pairs,),
            in_specs=[mine, allk, pl.BlockSpec((keys, 128), lambda h, e: (0, h + pairs)), mine],
            out_specs=[mine, allk, allk],
        ),
        out_shape=[
            jax.ShapeDtypeStruct((rows, width), BF16),
            jax.ShapeDtypeStruct((keys, width), BF16),
            jax.ShapeDtypeStruct((keys, width), BF16),
        ],
        compiler_params=pltpu.CompilerParams(vmem_limit_bytes=VMEM_LIMIT),
        cost_estimate=pl.CostEstimate(
            flops=10 * rows * keys * width, bytes_accessed=6 * (rows + keys) * width, transcendentals=rows * keys * H
        ),
        name="attend_back",
    )(ends, q, kv, kv, do)


def layer_stats(values):
    centre = values - jnp.mean(values, axis=-1, keepdims=True)
    inv_std = lax.rsqrt(jnp.mean(centre * centre, axis=-1, keepdims=True) + 1e-06)
    return (centre * inv_std, inv_std)


def norm_back(upstream, normed, inv_std):
    mean_grad = jnp.mean(upstream, axis=-1, keepdims=True)
    mean_cross = jnp.mean(upstream * normed, axis=-1, keepdims=True)
    return inv_std * (upstream - mean_grad - normed * mean_cross)


def noise_embedding(levels, feature_width):
    half_width = feature_width // 2
    frequencies = jnp.exp(
        -math.log(10000.0) * jnp.arange(half_width, dtype=jnp.float32) / half_width
    )
    angles = levels.astype(jnp.float32)[:, None] * frequencies[None, :]
    return jnp.concatenate([jnp.cos(angles), jnp.sin(angles)], axis=1)


def silu_embedding(levels, width):
    return jax.nn.silu(noise_embedding(levels, width)).astype(BF16)


def split_flat(flat_values, model_width, hidden_width):
    matrix_shapes = (
        (model_width, 6 * model_width),
        (model_width, 3 * model_width),
        (model_width, model_width),
        (model_width, hidden_width),
        (hidden_width, model_width),
    )
    matrices = []
    offset_now = 0
    for matrix_shape in matrix_shapes:
        entry_count = matrix_shape[0] * matrix_shape[1]
        matrices.append(flat_values[offset_now : offset_now + entry_count].reshape(matrix_shape))
        offset_now = offset_now + entry_count
    return matrices


def shards(
    frame_size,
    batch_size,
    tokens,
    out_cotangent,
    buckets,
    noise_levels,
    owned_block,
    master,
    first_moment,
    second_moment,
):
    micro_count, piece, width = tokens.shape
    block_size = master.shape[1]
    frame_count = noise_levels.shape[1]
    total = frame_size * batch_size
    videos = micro_count
    per = frame_size // videos
    rows = videos * piece
    keys = rows * per
    q_scale = HD ** (-0.5)
    f, z = frame_index()
    me = f * batch_size + z
    mine, g = f // per, f % per
    direct = frame_size == 8 and batch_size == 4 and block_size == ROWS * 1024 and videos == 4 and frame_count == 4

    if direct:
        inverse = jnp.argsort(owned_block).astype(jnp.int32)
        table = jnp.asarray(np.stack([block_rows(b) for b in range(total)]).astype(np.int32))
        own_rows = lax.dynamic_index_in_dim(table, owned_block[me], 0, keepdims=False)
        swap = (own_rows[:, None] == jnp.arange(ROWS, dtype=jnp.int32)[None, :]).astype(BF16)
        cut_block = jnp.dot(swap, master.reshape(ROWS, 1024).astype(BF16), preferred_element_type=F32).astype(BF16)
        levels = jnp.zeros((8, 128), jnp.int32).at[:4, :4].set(noise_levels)
        cut, all_levels, tok, cot = scatter_blocks(cut_block, levels, tokens, out_cotangent, total, batch_size)
        ordered = pick_blocks(inverse, cut)
        held = ordered[FIRST:].reshape(HELD, 128)
        cond = silu_embedding(all_levels[:, :4, :4].reshape(64), width)
        ada_row, ada_col = ada_rows(z)
        spread = (ada_row[None, :] == jnp.arange(width, dtype=jnp.int32)[:, None]).astype(BF16)
        cond_rows = jnp.dot(cond, spread, preferred_element_type=F32).astype(BF16)
        six = (ada_col[None, :] == jnp.arange(6, dtype=jnp.int32)[:, None]).astype(BF16)
        cond_all = (cond_rows.reshape(16, 1, 4, -1) * six[None, :, None, :]).reshape(384, -1)
        mod_part = jnp.dot(
            cond_all, ordered[: FIRST + 1].reshape(-1, 128), preferred_element_type=F32
        ).reshape(16, 24, 128)
        w_qkv, w_out, w_in, w_down, mod_parts = gather_matrices(held, mod_part, total, batch_size)
        modulation = jnp.sum(mod_parts, axis=0).reshape(6, 4, width).transpose(1, 0, 2)
    else:
        tok, cot = swap_videos([tokens, out_cotangent], videos, per, 0)
        gathered = lax.all_gather(master.astype(BF16), ("frame", "batch"), axis=0, tiled=True)
        placed = jnp.take(gathered, jnp.argsort(owned_block), axis=0).reshape(-1)
        w_ada, w_qkv, w_out, w_in, w_down = split_flat(placed, width, FF)
        cond = silu_embedding(lax.dynamic_index_in_dim(noise_levels, mine, 0, keepdims=False), width)
        modulation = jnp.dot(cond, w_ada, preferred_element_type=F32).reshape(frame_count, 6, width)

    frame_len = FRAME_LO * (1 + 3 * buckets[mine])
    piece_at = (jnp.arange(videos, dtype=jnp.int32) * per + g) * piece
    piece_frame = piece_at // frame_len
    ends = (piece_frame + 1) * frame_len
    selector = (piece_frame[:, None] == jnp.arange(frame_count, dtype=jnp.int32)[None, :]).astype(F32)
    piece_mod = jnp.einsum("pf,fjd->jpd", selector, modulation, precision=HIGHEST)
    shift_one, scale_one, gate_one, shift_two, scale_two, gate_two = [piece_mod[j][:, None, :] for j in range(6)]

    def flat(a):
        return a.reshape(rows, a.shape[-1])

    def cube(a):
        return a.reshape(videos, piece, a.shape[-1])

    x_float = tok.astype(F32)
    normed_one, inv_one = layer_stats(x_float)
    h_one = flat((normed_one * (1.0 + scale_one) + shift_one).astype(BF16))
    projected = jnp.dot(h_one, w_qkv, preferred_element_type=F32)
    queries = (projected[:, :width] * q_scale).astype(BF16)
    kv_own = projected[:, width:].astype(BF16)

    def partners(k):
        return [(i, i // per * per + (i + k) % per) for i in range(frame_size)]

    kv_all = jnp.zeros((per, rows, 2 * width), BF16)
    kv_all = lax.dynamic_update_index_in_dim(kv_all, kv_own, g, 0)
    for k in range(1, per):
        kv_all = lax.dynamic_update_index_in_dim(
            kv_all, lax.ppermute(kv_own, "frame", partners(k)), (g + per - k) % per, 0
        )
    kv_all = kv_all.reshape(keys, 2 * width)
    attended = attend(ends, queries, kv_all, piece, per)
    attn_out = jnp.dot(attended, w_out, preferred_element_type=F32)
    middle = x_float + gate_one * cube(attn_out)
    normed_two, inv_two = layer_stats(middle)
    h_two = flat((normed_two * (1.0 + scale_two) + shift_two).astype(BF16))
    pre_act = jnp.dot(h_two, w_in, preferred_element_type=F32)
    activated, gelu_back = jax.vjp(partial(jax.nn.gelu, approximate=True), pre_act)
    act_low = activated.astype(BF16)
    mlp_out = jnp.dot(act_low, w_down, preferred_element_type=F32)
    block_output = (middle + gate_two * cube(mlp_out)).astype(BF16)

    grad_out = cot.astype(F32)
    d_mlp = flat((gate_two * grad_out).astype(BF16))
    g_down = jnp.dot(act_low.T, d_mlp, preferred_element_type=F32).astype(BF16)
    d_act = jnp.dot(d_mlp, w_down.T, preferred_element_type=F32)
    d_pre = gelu_back(d_act)[0].astype(BF16)
    g_in = jnp.dot(h_two.T, d_pre, preferred_element_type=F32).astype(BF16)
    d_htwo = cube(jnp.dot(d_pre, w_in.T, preferred_element_type=F32))
    d_gate_two = jnp.sum(grad_out * cube(mlp_out), axis=1)
    d_scale_two = jnp.sum(d_htwo * normed_two, axis=1)
    d_shift_two = jnp.sum(d_htwo, axis=1)
    d_middle = grad_out + norm_back(d_htwo * (1.0 + scale_two), normed_two, inv_two)
    d_attn = flat((gate_one * d_middle).astype(BF16))
    d_gate_one = jnp.sum(d_middle * cube(attn_out), axis=1)
    g_out = jnp.dot(attended.T, d_attn, preferred_element_type=F32).astype(BF16)
    d_attended = jnp.dot(d_attn, w_out.T, preferred_element_type=F32).astype(BF16)
    dq, dk, dv = attend_back(ends, queries, kv_all, d_attended, piece, per)
    dkv = jnp.concatenate([dk, dv], axis=1).reshape(per, rows, 2 * width)
    dkv_own = lax.dynamic_index_in_dim(dkv, g, 0, keepdims=False).astype(F32)
    for k in range(1, per):
        sent = lax.dynamic_index_in_dim(dkv, (g + k) % per, 0, keepdims=False)
        dkv_own = dkv_own + lax.ppermute(sent, "frame", partners(k)).astype(F32)
    d_proj = jnp.concatenate([dq * jnp.asarray(q_scale, BF16), dkv_own.astype(BF16)], axis=1)
    g_qkv = jnp.dot(h_one.T, d_proj, preferred_element_type=F32).astype(BF16)
    d_hone = cube(jnp.dot(d_proj, w_qkv.T, preferred_element_type=F32))
    d_scale_one = jnp.sum(d_hone * normed_one, axis=1)
    d_shift_one = jnp.sum(d_hone, axis=1)
    d_input = d_middle + norm_back(d_hone * (1.0 + scale_one), normed_one, inv_one)
    input_grad = d_input.astype(BF16)
    piece_dmod = jnp.stack([d_shift_one, d_scale_one, d_gate_one, d_shift_two, d_scale_two, d_gate_two])
    frame_dmod = jnp.einsum("pf,jpd->jfd", selector, piece_dmod, precision=HIGHEST)

    if direct:
        held_grad, dmod_parts = reduce_matrices(
            [g_qkv, g_out, g_in, g_down], frame_dmod.reshape(24, width), total, batch_size
        )
        dmod_all = jnp.sum(dmod_parts.reshape(4, 2, 4, 24, 128), axis=1).transpose(1, 0, 2, 3).reshape(384, 128)
        ada_grad = lax.dot_general(
            cond_all.astype(F32), dmod_all, (((0,), (0,)), ((), ())), precision=HIGHEST
        ).astype(BF16)
        edge = jnp.concatenate([ada_grad[FIRST * GROUP : FIRST * GROUP + 96], held_grad[96:GROUP]], axis=0)
        ordered_grad = jnp.concatenate([ada_grad[: FIRST * GROUP], edge, held_grad[GROUP:]], axis=0)
        cut_grad = pick_blocks(owned_block, ordered_grad.reshape(total, GROUP, 128))
        grad_block, outputs, input_grads = collect_blocks(cut_grad, block_output, input_grad, total, batch_size)
        shard_total = lax.dot_general(
            swap, grad_block, (((0,), (0,)), ((), ())), preferred_element_type=F32
        ).reshape(1, block_size)
    else:
        outputs, input_grads = swap_videos([block_output, input_grad], videos, per, 1)
        g_ada = lax.dot_general(
            cond.astype(F32),
            frame_dmod.transpose(1, 0, 2).reshape(frame_count, 6 * width),
            (((0,), (0,)), ((), ())),
            precision=HIGHEST,
        )
        flat_grads = jnp.concatenate(
            [piece_grad.astype(F32).reshape(-1) for piece_grad in (g_ada, g_qkv, g_out, g_in, g_down)]
        )
        arranged = jnp.take(flat_grads.reshape(-1, block_size), owned_block, axis=0).reshape(-1)
        shard_total = lax.psum_scatter(
            arranged, ("frame", "batch"), scatter_dimension=0, tiled=True
        ).reshape(1, block_size)
    new_first = BETA_ONE * first_moment + (1.0 - BETA_ONE) * shard_total
    new_second = BETA_TWO * second_moment + (1.0 - BETA_TWO) * shard_total * shard_total
    fix_one = 1.0 - BETA_ONE**STEP
    fix_two = 1.0 - BETA_TWO**STEP
    update = new_first / fix_one / (jnp.sqrt(new_second / fix_two) + ADAM_EPS)
    new_master = master - LEARN_RATE * (update + WEIGHT_DECAY * master)
    return (outputs, input_grads, new_master, new_first, new_second)


def solution(mesh):
    placed = (
        P("batch", "frame", None),
        P("batch", "frame", None),
        P("batch"),
        P("batch", None),
        P(),
        P(("frame", "batch"), None),
        P(("frame", "batch"), None),
        P(("frame", "batch"), None),
    )
    return jax.shard_map(
        partial(shards, mesh.shape["frame"], mesh.shape["batch"]),
        mesh=mesh,
        in_specs=placed,
        out_specs=(
            P("batch", "frame", None),
            P("batch", "frame", None),
            P(("frame", "batch"), None),
            P(("frame", "batch"), None),
            P(("frame", "batch"), None),
        ),
        check_vma=False,
    )
```

```python
from functools import partial
import math

import jax
import jax.numpy as jnp
import numpy as np
from jax import lax
from jax.experimental import pallas as pl
from jax.experimental.pallas import tpu as pltpu
from jax.sharding import PartitionSpec as P

H = 16
HD = 64
FF = 4096
FRAME_LO = 256
STEP = 10

HIGHEST = lax.Precision.HIGHEST
NEG_FILL = -1e30
BETA_ONE = 0.5
BETA_TWO = 0.5
LEARN_RATE = 0.05
WEIGHT_DECAY = 0.1
ADAM_EPS = 1e-08
MESH = pl.DeviceIdType.MESH
F32 = jnp.float32
BF16 = jnp.bfloat16
ANY = pl.BlockSpec(memory_space=pl.ANY)
VMEM_LIMIT = 60 * 1024 * 1024

ROWS = 576
GROUP = 144
FIRST = 10
KINDS = (("qkv", 1024, 3), ("out", 1024, 1), ("in", 1024, 4), ("down", 4096, 1))
SPANS = {"qkv": (96, 864), "out": (864, 1120), "in": (1120, 2144), "down": (2144, 3168)}
HELD = 3168


def pieces(kind, z):
    if kind == "qkv":
        found = [(96 + 16 * j, 16, 16 * z, j) for j in range(3)]
        for k in range(5):
            found += [(144 + 144 * k + 48 * j, 48, 64 + 192 * k + 48 * z, j) for j in range(3)]
        return found
    if kind == "out":
        return [(864, 144, 144 * z, 0), (1008, 112, 576 + 112 * z, 0)]
    if kind == "in":
        return [(1120, 1024, 0, z)]
    found = [(2144, 16, 16 * z, 0)]
    return found + [(2160 + 144 * k, 144, 64 + 576 * k + 144 * z, 0) for k in range(7)]


def block_rows(block):
    t = np.arange(GROUP)
    groups = []
    for z in range(4):
        if block == 10:
            i = t - 96
            rows = np.where(t < 96, 96 * z + t, 384 + 3 * (16 * z + i % 16) + i // 16)
        elif 11 <= block <= 15:
            rows = 3 * (48 * z + t % 48) + t // 48
        elif block == 17:
            rows = np.where(t < 112, 112 * z + t, 448 + 4 * (t - 112) + z)
        elif 18 <= block <= 23:
            rows = 4 * t + z
        elif block == 24:
            rows = np.where(t < 128, 4 * t + z, 512 + 16 * z + t - 128)
        else:
            rows = GROUP * z + t
        groups.append(rows)
    return np.concatenate(groups)


def ada_rows(z):
    t = jnp.arange(GROUP, dtype=jnp.int32)
    rows = [96 * b + 24 * z + t // 6 for b in range(10)]
    rows.append(jnp.where(t < 96, 960 + 16 * z + t // 6, -1))
    return jnp.concatenate(rows), jnp.tile(t % 6, 11)


def frame_index():
    return lax.axis_index("frame"), lax.axis_index("batch")


def strip_of(f):
    return 4 * (f % 2) + f // 2


def greet(devices):
    barrier = pltpu.get_barrier_semaphore()
    for device in devices:
        pl.semaphore_signal(barrier, inc=1, device_id=device, device_id_type=MESH)
    pl.semaphore_wait(barrier, len(devices))


def greet_all(total, batch):
    f, z = frame_index()
    me = f * batch + z
    barrier = pltpu.get_barrier_semaphore()

    def hail(k, carry):
        other = (me + k) % total
        pl.semaphore_signal(barrier, inc=1, device_id=(other // batch, other % batch), device_id_type=MESH)
        return carry

    lax.fori_loop(1, total, hail, 0)
    pl.semaphore_wait(barrier, total - 1)


def remote(src, dst, send, recv, device):
    copy = pltpu.make_async_remote_copy(
        src_ref=src, dst_ref=dst, send_sem=send, recv_sem=recv, device_id=device, device_id_type=MESH
    )
    copy.start()
    return copy


def local(src, dst, sem):
    copy = pltpu.make_async_copy(src, dst, sem)
    copy.start()
    return copy


def video_kernel(videos, per, arrays, *refs):
    ins, outs = refs[:arrays], refs[arrays : 2 * arrays]
    send, recv, own = refs[2 * arrays :]
    f, z = frame_index()
    mine, g = f // per, f % per
    others = [((mine + k) % videos, k) for k in range(1, videos)]
    greet([(v * per + g, z) for v, k in others])
    copies = []
    for a in range(arrays):
        for v, k in others:
            copies.append(
                remote(ins[a].at[v], outs[a].at[mine], send.at[a, k], recv.at[a, k], (v * per + g, z))
            )
        copies.append(local(ins[a].at[mine], outs[a].at[mine], own.at[a]))
    for copy in copies:
        copy.wait()


def swap_videos(arrays, videos, per, ident):
    count = len(arrays)
    return pl.pallas_call(
        partial(video_kernel, videos, per, count),
        out_shape=[jax.ShapeDtypeStruct(a.shape, a.dtype) for a in arrays],
        in_specs=[ANY] * count,
        out_specs=[ANY] * count,
        scratch_shapes=[
            pltpu.SemaphoreType.DMA((count, videos)),
            pltpu.SemaphoreType.DMA((count, videos)),
            pltpu.SemaphoreType.DMA((count,)),
        ],
        compiler_params=pltpu.CompilerParams(collective_id=ident, has_side_effects=True),
        name="swap_videos",
    )(*arrays)


def scatter_kernel(total, batch, blk, levels, tok, cot, cut, all_levels, tok_out, cot_out, send, recv, vsend, vrecv, lsend, lrecv, own):
    f, z = frame_index()
    me = f * batch + z
    greet_all(total, batch)
    mine, g = f // 2, f % 2

    def group(k, start):
        other = (me + k) % total
        of, oz = other // batch, other % batch
        copy = pltpu.make_async_remote_copy(
            src_ref=blk.at[pl.ds(pl.multiple_of(GROUP * oz, 16), GROUP), pl.ds(pl.multiple_of(128 * strip_of(of), 128), 128)],
            dst_ref=cut.at[me],
            send_sem=send.at[k],
            recv_sem=recv.at[k],
            device_id=(of, oz),
            device_id_type=MESH,
        )
        if start:
            copy.start()
        else:
            copy.wait()

    copies = []
    for k in range(1, batch):
        copies.append(remote(levels, all_levels.at[z], lsend.at[k], lrecv.at[k], (f, (z + k) % batch)))
    copies.append(local(levels, all_levels.at[z], own.at[0]))
    lax.fori_loop(1, total, lambda k, c: (group(k, True), c)[1], 0)
    copies.append(
        local(
            blk.at[pl.ds(pl.multiple_of(GROUP * z, 16), GROUP), pl.ds(pl.multiple_of(128 * strip_of(f), 128), 128)],
            cut.at[me],
            own.at[1],
        )
    )
    for a, (src, dst) in enumerate(((tok, tok_out), (cot, cot_out))):
        for k in range(1, 4):
            v = (mine + k) % 4
            copies.append(remote(src.at[v], dst.at[mine], vsend.at[a, k], vrecv.at[a, k], (v * 2 + g, z)))
        copies.append(local(src.at[mine], dst.at[mine], own.at[2 + a]))
    for copy in copies:
        copy.wait()
    lax.fori_loop(1, total, lambda k, c: (group(k, False), c)[1], 0)


def scatter_blocks(blk, levels, tok, cot, total, batch):
    return pl.pallas_call(
        partial(scatter_kernel, total, batch),
        out_shape=[
            jax.ShapeDtypeStruct((total, GROUP, 128), BF16),
            jax.ShapeDtypeStruct((batch,) + levels.shape, levels.dtype),
            jax.ShapeDtypeStruct(tok.shape, tok.dtype),
            jax.ShapeDtypeStruct(cot.shape, cot.dtype),
        ],
        in_specs=[ANY] * 4,
        out_specs=[ANY] * 4,
        scratch_shapes=[
            pltpu.SemaphoreType.DMA((total,)),
            pltpu.SemaphoreType.DMA((total,)),
            pltpu.SemaphoreType.DMA((2, 4)),
            pltpu.SemaphoreType.DMA((2, 4)),
            pltpu.SemaphoreType.DMA((batch,)),
            pltpu.SemaphoreType.DMA((batch,)),
            pltpu.SemaphoreType.DMA((4,)),
        ],
        compiler_params=pltpu.CompilerParams(collective_id=0, has_side_effects=True),
        name="scatter_blocks",
    )(blk, levels, tok, cot)


def collect_kernel(total, batch, cut, act, grad, blk, act_out, grad_out, send, recv, vsend, vrecv, own):
    f, z = frame_index()
    me = f * batch + z
    greet_all(total, batch)
    mine, g = f // 2, f % 2

    def spot(of, oz):
        return blk.at[pl.ds(pl.multiple_of(GROUP * oz, 16), GROUP), pl.ds(pl.multiple_of(128 * strip_of(of), 128), 128)]

    def group(k, start):
        other = (me + k) % total
        copy = pltpu.make_async_remote_copy(
            src_ref=cut.at[other],
            dst_ref=spot(f, z),
            send_sem=send.at[k],
            recv_sem=recv.at[k],
            device_id=(other // batch, other % batch),
            device_id_type=MESH,
        )
        if start:
            copy.start()
        else:
            copy.wait()

    lax.fori_loop(1, total, lambda k, c: (group(k, True), c)[1], 0)
    copies = [local(cut.at[me], spot(f, z), own.at[0])]
    for a, (src, dst) in enumerate(((act, act_out), (grad, grad_out))):
        for k in range(1, 4):
            v = (mine + k) % 4
            copies.append(remote(src.at[v], dst.at[mine], vsend.at[a, k], vrecv.at[a, k], (v * 2 + g, z)))
        copies.append(local(src.at[mine], dst.at[mine], own.at[1 + a]))
    for copy in copies:
        copy.wait()
    lax.fori_loop(1, total, lambda k, c: (group(k, False), c)[1], 0)


def collect_blocks(cut, act, grad, total, batch):
    return pl.pallas_call(
        partial(collect_kernel, total, batch),
        out_shape=[
            jax.ShapeDtypeStruct((ROWS, 1024), BF16),
            jax.ShapeDtypeStruct(act.shape, act.dtype),
            jax.ShapeDtypeStruct(grad.shape, grad.dtype),
        ],
        in_specs=[ANY] * 3,
        out_specs=[ANY] * 3,
        scratch_shapes=[
            pltpu.SemaphoreType.DMA((total,)),
            pltpu.SemaphoreType.DMA((total,)),
            pltpu.SemaphoreType.DMA((2, 4)),
            pltpu.SemaphoreType.DMA((2, 4)),
            pltpu.SemaphoreType.DMA((3,)),
        ],
        compiler_params=pltpu.CompilerParams(collective_id=3, has_side_effects=True),
        name="collect_blocks",
    )(cut, act, grad)


def plane():
    f, z = frame_index()
    y, x, c = f // 4, (f // 2) % 2, f % 2
    at_x = (4 * y + 2 * (1 - x) + c, z)
    at_y = (4 * (1 - y) + 2 * x + c, z)
    at_c = (4 * y + 2 * x + 1 - c, z)
    return y, x, c, z, at_x, at_y, at_c


def lanes(first, count):
    return pl.ds(pl.multiple_of(first, 128), count)


UNITS = (
    [("qkv", 0, 1024, 1024 * j) for j in range(3)]
    + [("out", 0, 1024, 0)]
    + [("in", 0, 1024, 1024 * j) for j in range(4)]
    + [("down", 0, 1216, 0), ("down", 1216, 1152, 0), ("down", 2368, 1152, 0), ("down", 3520, 576, 0)]
)
DOWN_READY = (1152, 2304, 3456, 4096)
DEALS = (
    [("qkv", j, 0, 1024) for j in range(3)]
    + [("out", 0, 0, 1024), ("in", None, 0, 1024)]
    + [("down", 0, first, count) for first, count in ((0, 1216), (1216, 1152), (2368, 1152), (3520, 576))]
)
DEAL_OF = (0, 1, 2, 3, 4, 4, 4, 4, 5, 6, 7, 8)
DEAL_ROWS = (256, 256, 256, 256, 1024, 304, 288, 288, 144)


def deal_pieces(d, z):
    kind, j, first, count = DEALS[d]
    last = first + count
    found = []
    for row, rows, to, col in pieces(kind, z):
        base = pieces(kind, 0)[len(found)][2] if kind == "down" else None
        found.append((row, rows, to, col, base))
    if kind == "down":
        return [p[:4] for p in found if first <= p[4] < last]
    if kind == "qkv":
        return [p[:4] for p in found if p[3] == j]
    return [p[:4] for p in found]


GELU_A = math.sqrt(2.0 / math.pi)
GELU_B = 0.044715


def row_loop(count, step, body):
    def one(i, carry):
        body(pl.multiple_of(i * step, step))
        return carry

    lax.fori_loop(0, count // step, one, 0)


def norm_rows(values):
    centre = values - jnp.mean(values, axis=-1, keepdims=True)
    inv_std = lax.rsqrt(jnp.mean(centre * centre, axis=-1, keepdims=True) + 1e-06)
    return centre * inv_std, inv_std


def forward_kernel(total, batch, piece, per, sel, ends, tok, held, mod, *refs):
    hbm, vm, sems = refs[:17], refs[17:33], refs[33:]
    wq_o, wo_o, wi_o, wd_o, h1_o, q_o, kv_o, att_o, a_o, x1_o, h2_o, gp_o, u_o, m_o, y_o, pm_o, mod_in = hbm
    wq, wo, wi, wd, h1, q, kv, att, a, x1, h2, gp, u, m, pm, mod_v = vm
    zsend, zrecv, psend, precv, msend, mrecv, own, wsem, osem, kvsend, kvrecv = sems
    mats = {"qkv": wq, "out": wo, "in": wi, "down": wd}
    mats_o = {"qkv": wq_o, "out": wo_o, "in": wi_o, "down": wd_o}
    y, x, c, z, at_x, at_y, at_c = plane()
    f = 4 * y + 2 * x + c
    me = f * batch + z
    strip = 4 * c + 2 * y + x
    greet_all(total, batch)

    def mod_group(k, start):
        other = (me + k) % total
        of, oz = other // batch, other % batch
        copy = pltpu.make_async_remote_copy(
            src_ref=mod.at[4 * oz + of // 2],
            dst_ref=mod_v.at[z, :, lanes(128 * strip, 128)],
            send_sem=msend.at[k],
            recv_sem=mrecv.at[k],
            device_id=(of, oz),
            device_id_type=MESH,
        )
        if start:
            copy.start()
        else:
            copy.wait()

    def spot(kind, to, count, j):
        return mats[kind].at[pl.ds(pl.multiple_of(to, 16), count), lanes(1024 * j + 128 * strip, 128)]

    for d, (kind, _, _, _) in enumerate(DEALS):
        for k in range(1, batch):
            for row, count, to, j in deal_pieces(d, z):
                remote(
                    held.at[pl.ds(row, count)], spot(kind, to, count, j), zsend.at[d, k], zrecv.at[d, k],
                    (f, (z + k) % batch),
                )
        for row, count, to, j in deal_pieces(d, z):
            local(held.at[pl.ds(row, count)], spot(kind, to, count, j), own.at[d])
        if d == 0:
            lax.fori_loop(1, total, lambda k, t: (mod_group(k, True), t)[1], 0)
            mod_own = local(mod.at[4 * z + f // 2], mod_v.at[z, :, lanes(128 * strip, 128)], own.at[len(DEALS)])

    def whole(d):
        return held.at[pl.ds(0, DEAL_ROWS[d])]

    dealt = set()

    def deal_wait(d):
        if d in dealt:
            return
        dealt.add(d)
        for k in range(1, batch):
            pltpu.make_async_copy(whole(d), whole(d), zrecv.at[d, k]).wait()
        pltpu.make_async_copy(whole(d), whole(d), own.at[d]).wait()

    slots = {}
    counter = [0]

    def push(key, mat, row, count, col, width, device):
        s = counter[0]
        counter[0] += 1
        ref = mat.at[pl.ds(row, count), lanes(col, width)]
        slots.setdefault(key, []).append(remote(ref, ref, psend.at[s], precv.at[s], device))

    def stage_a(n):
        kind, row, rows, col = UNITS[n]
        half = rows // 2
        deal_wait(DEAL_OF[n])
        push((n, 1), mats[kind], row, half, col + 128 * strip, 128, at_x)
        push((n, 1), mats[kind], row + half, half, col + 128 * strip, 128, at_y)

    def stage_b(n):
        kind, row, rows, col = UNITS[n]
        half = rows // 2
        for copy in slots[(n, 1)]:
            copy.wait_recv()
        push((n, 2), mats[kind], row, half, col + 512 * c + 256 * y, 256, at_y)
        for yy in range(2):
            push((n, 2), mats[kind], row + half, half, col + 512 * c + 256 * yy + 128 * x, 128, at_x)

    def stage_c(n):
        kind, row, rows, col = UNITS[n]
        for copy in slots[(n, 2)]:
            copy.wait_recv()
        push((n, 3), mats[kind], row, rows, col + 512 * c, 512, at_c)

    saves = []

    def ready(n):
        kind, row, rows, col = UNITS[n]
        for copy in slots[(n, 3)]:
            copy.wait_recv()
        ref = (pl.ds(row, rows), pl.ds(col, 1024))
        saves.append(local(mats[kind].at[ref], mats_o[kind].at[ref], wsem.at[n]))

    pumped = [0]
    last_unit = len(UNITS)

    def pump():
        s = pumped[0]
        pumped[0] += 1
        if 0 <= s - 2 < last_unit:
            stage_b(s - 2)
        if s < last_unit:
            stage_a(s)
        if 0 <= s - 3 < last_unit:
            stage_c(s - 3)

    def pump_to(s):
        while pumped[0] <= s:
            pump()

    def save(src, dst, n):
        saves.append(local(src, dst, osem.at[n]))

    pump_to(0)
    lax.fori_loop(1, total, lambda k, t: (mod_group(k, False), t)[1], 0)
    mod_own.wait()
    for j in range(6):
        for p in range(4):
            value = jnp.zeros((1, 1024), F32)
            for fr in range(4):
                row = mod_v[0, pl.ds(4 * j + fr, 1), :]
                for s in range(1, batch):
                    row = row + mod_v[s, pl.ds(4 * j + fr, 1), :]
                value = value + sel[p, fr] * row
            pm[pl.ds(4 * j + p, 1), :] = value
    save(pm, pm_o, 0)

    def mod_row(j, p):
        return pm[pl.ds(4 * j + p, 1), :]

    step = 32
    for p in range(4):
        shift, scale = mod_row(0, p), mod_row(1, p)

        def one(i, p=p, shift=shift, scale=scale):
            rows = pl.ds(pl.multiple_of(p * piece + i, step), step)
            normed, _ = norm_rows(tok[rows, :].astype(F32))
            h1[rows, :] = (normed * (1.0 + scale) + shift).astype(BF16)

        row_loop(piece, step, one)
    save(h1, h1_o, 1)

    pump_to(4)
    for j in range(3):
        pump_to(3 + j)
        ready(j)

        def cols(n, j=j):
            value = jnp.dot(h1[...], wq[:, lanes(1024 * j + n, 512)], preferred_element_type=F32)
            if j == 0:
                q[:, lanes(n, 512)] = (value * HD ** (-0.5)).astype(BF16)
            else:
                kv[c, :, lanes(1024 * (j - 1) + n, 512)] = value.astype(BF16)

        row_loop(1024, 512, cols)
    save(q, q_o, 2)
    kv_copy = remote(kv.at[c], kv.at[c], kvsend, kvrecv, at_c)
    pump_to(6)
    kv_copy.wait_recv()
    save(kv, kv_o, 3)

    keys = 2 * 4 * piece
    end_of = [ends[t] for t in range(4)]

    def heads(h):
        outs = []
        for e in range(2):
            def part(ref_cols):
                return lanes(ref_cols, 128)

            k_pair = kv[:, :, part(128 * h)].reshape(keys, 128)
            v_pair = kv[:, :, part(1024 + 128 * h)].reshape(keys, 128)
            q_pair = q[:, part(128 * h)]
            cut = slice(64 * e, 64 * e + 64)
            s = scores_t(k_pair[:, cut], q_pair[:, cut], end_of, piece, per)
            peak = jnp.max(s, axis=0, keepdims=True)
            w = jnp.exp(s - peak)
            prob = (w * (1.0 / jnp.sum(w, axis=0, keepdims=True))).astype(BF16)
            outs.append(
                lax.dot_general(prob, v_pair[:, cut], (((0,), (0,)), ((), ())), preferred_element_type=F32)
            )
        att[:, lanes(128 * h, 128)] = jnp.concatenate(outs, axis=1).astype(BF16)

    for n in range(4):
        lax.fori_loop(2 * n, 2 * n + 2, lambda h, t: (heads(h), t)[1], 0)
        pump_to(7 + n)
    save(att, att_o, 4)

    ready(3)

    def out_cols(n):
        a[:, lanes(n, 512)] = jnp.dot(att[...], wo[:, lanes(n, 512)], preferred_element_type=F32)

    row_loop(1024, 512, out_cols)
    save(a, a_o, 5)
    for p in range(4):
        gate, shift, scale = mod_row(2, p), mod_row(3, p), mod_row(4, p)

        def two(i, p=p, gate=gate, shift=shift, scale=scale):
            rows = pl.ds(pl.multiple_of(p * piece + i, step), step)
            middle = tok[rows, :].astype(F32) + gate * a[rows, :]
            x1[rows, :] = middle
            normed, _ = norm_rows(middle)
            h2[rows, :] = (normed * (1.0 + scale) + shift).astype(BF16)

        row_loop(piece, step, two)
    save(x1, x1_o, 6)
    save(h2, h2_o, 7)

    for j in range(4):
        pump_to(11 + j)
        ready(4 + j)

        def in_cols(n, j=j):
            col = 1024 * j + n
            pre = jnp.dot(h2[...], wi[:, lanes(col, 256)], preferred_element_type=F32)
            square = pre * pre
            t = jnp.tanh(GELU_A * (pre + GELU_B * (square * pre)))
            lift = 0.5 * (1.0 + t)
            u[:, lanes(col, 256)] = (pre * lift).astype(BF16)
            slope = lift + (0.5 * GELU_A) * pre * (1.0 - t * t) * (1.0 + 3.0 * GELU_B * square)
            gp[:, lanes(col, 256)] = slope.astype(BF16)

        row_loop(1024, 256, in_cols)
    save(u, u_o, 8)
    save(gp, gp_o, 9)
    before = 0
    for n in range(4):
        ready(8 + n)
        depth = DOWN_READY[n] - before

        def down_cols(col, n=n, before=before, depth=depth):
            part = jnp.dot(
                u[:, pl.ds(before, depth)], wd[pl.ds(before, depth), lanes(col, 512)], preferred_element_type=F32
            )
            if n == 0:
                m[:, lanes(col, 512)] = part
            else:
                m[:, lanes(col, 512)] = m[:, lanes(col, 512)] + part

        row_loop(1024, 512, down_cols)
        before = DOWN_READY[n]
    save(m, m_o, 10)
    for p in range(4):
        gate = mod_row(5, p)

        def three(i, p=p, gate=gate):
            rows = pl.ds(pl.multiple_of(p * piece + i, step), step)
            h1[rows, :] = (x1[rows, :] + gate * m[rows, :]).astype(BF16)

        if p == 0:
            saves[1].wait()
        row_loop(piece, step, three)
    saves_h1 = saves[1]
    save(h1, y_o, 11)
    for copy in saves:
        if copy is not saves_h1:
            copy.wait()
    kv_copy.wait_send()
    for copies in slots.values():
        for copy in copies:
            copy.wait_send()
    for d in range(len(DEALS)):
        for k in range(1, batch):
            pltpu.make_async_copy(whole(d), whole(d), zsend.at[d, k]).wait()


def forward(sel, ends, tok, held, mod, total, batch, piece, per):
    def out(*shape, dtype=BF16):
        return jax.ShapeDtypeStruct(shape, dtype)

    outs = [out(depth, 1024 * blocks) for _, depth, blocks in KINDS] + [
        out(512, 1024),
        out(512, 1024),
        out(2, 512, 2048),
        out(512, 1024),
        out(512, 1024, dtype=F32),
        out(512, 1024, dtype=F32),
        out(512, 1024),
        out(512, 4096),
        out(512, 4096),
        out(512, 1024, dtype=F32),
        out(512, 1024),
        out(24, 1024, dtype=F32),
    ]
    bufs = [pltpu.VMEM(o.shape, o.dtype) for o in outs[:14]] + [
        pltpu.VMEM((24, 1024), F32),
        pltpu.VMEM((batch, 24, 1024), F32),
    ]
    smem = pl.BlockSpec(memory_space=pltpu.SMEM)
    dma = pltpu.SemaphoreType.DMA
    return pl.pallas_call(
        partial(forward_kernel_entry, total, batch, piece, per),
        out_shape=outs,
        in_specs=[smem, smem, pl.BlockSpec(memory_space=pltpu.VMEM), ANY, ANY],
        out_specs=[ANY] * len(outs),
        scratch_shapes=bufs
        + [
            dma((len(DEALS), batch)),
            dma((len(DEALS), batch)),
            dma((6 * len(UNITS),)),
            dma((6 * len(UNITS),)),
            dma((total,)),
            dma((total,)),
            dma((len(DEALS) + 1,)),
            dma((len(UNITS),)),
            dma((12,)),
            dma,
            dma,
        ],
        compiler_params=pltpu.CompilerParams(
            collective_id=1, has_side_effects=True, vmem_limit_bytes=VMEM_LIMIT
        ),
        name="forward",
    )(sel, ends, tok, held, mod)


def forward_kernel_entry(total, batch, piece, per, sel, ends, tok, held, mod, *refs):
    forward_kernel(total, batch, piece, per, sel, ends, tok, held, mod, *refs[:16], None, *refs[16:])


def add_rows(dst, dst_col, src, src_col, width, first, count):
    step = 128

    def body(i, carry):
        rows = pl.ds(pl.multiple_of(first + i * step, 16), step)
        dst[rows, lanes(dst_col, width)] = dst[rows, lanes(dst_col, width)] + src[rows, lanes(src_col, width)]
        return carry

    lax.fori_loop(0, count // step, body, 0)


ORDER = (3, 2, 1, 0)


def reduce_kernel(total, batch, *refs):
    grads, dmod, out, dmod_out = refs[:4], refs[4], refs[5], refs[6]
    own, got, half_sum, strip_sum = refs[7:11], refs[11:15], refs[15:19], refs[19:23]
    zgot, psend, precv, lsem, zsend, zrecv, msend, mrecv, mown = refs[23:]
    y, x, c, z, at_x, at_y, at_c = plane()
    f = 4 * y + 2 * x + c
    me = f * batch + z
    greet_all(total, batch)

    def mod_group(k, start):
        other = (me + k) % total
        of, oz = other // batch, other % batch
        copy = pltpu.make_async_remote_copy(
            src_ref=dmod.at[:, lanes(128 * strip_of(of), 128)],
            dst_ref=dmod_out.at[me],
            send_sem=msend.at[k],
            recv_sem=mrecv.at[k],
            device_id=(of, oz),
            device_id_type=MESH,
        )
        if start:
            copy.start()
        else:
            copy.wait()

    slots = {}
    counter = [0]

    def push(key, src, dst, device):
        s = counter[0]
        counter[0] += 1
        slots.setdefault(key, []).append(remote(src, dst, psend.at[s], precv.at[s], device))

    def arrive(key):
        for copy in slots[key]:
            copy.wait_recv()

    def zero(m):
        kind, depth, blocks = KINDS[m]
        for j in range(blocks):
            push((m, 0), grads[m].at[:, lanes(1024 * j + 512 * (1 - c), 512)], got[m].at[:, lanes(512 * j, 512)], at_c)
        loads[m] = [
            local(grads[m].at[:, lanes(1024 * j + 512 * c, 512)], own[m].at[:, lanes(512 * j, 512)], lsem.at[m, j])
            for j in range(blocks)
        ]

    def first(m):
        kind, depth, blocks = KINDS[m]
        half = depth // 2
        for copy in loads[m]:
            copy.wait()
        arrive((m, 0))
        add_rows(own[m], 0, got[m], 0, 512 * blocks, 0, depth)
        for j in range(blocks):
            for yy in range(2):
                push(
                    (m, 1),
                    own[m].at[pl.ds(0, half), lanes(512 * j + 256 * yy + 128 * (1 - x), 128)],
                    half_sum[m].at[pl.ds(0, half), lanes(256 * j + 128 * yy, 128)],
                    at_x,
                )
            push(
                (m, 1),
                own[m].at[pl.ds(half, half), lanes(512 * j + 256 * (1 - y), 256)],
                half_sum[m].at[pl.ds(half, half), lanes(256 * j, 256)],
                at_y,
            )

    def second(m):
        kind, depth, blocks = KINDS[m]
        half = depth // 2
        arrive((m, 1))
        for j in range(blocks):
            for yy in range(2):
                add_rows(half_sum[m], 256 * j + 128 * yy, own[m], 512 * j + 256 * yy + 128 * x, 128, 0, half)
            add_rows(half_sum[m], 256 * j, own[m], 512 * j + 256 * y, 256, half, half)
        for j in range(blocks):
            push(
                (m, 2),
                half_sum[m].at[pl.ds(0, half), lanes(256 * j + 128 * (1 - y), 128)],
                strip_sum[m].at[pl.ds(0, half), lanes(128 * j, 128)],
                at_y,
            )
            push(
                (m, 2),
                half_sum[m].at[pl.ds(half, half), lanes(256 * j + 128 * (1 - x), 128)],
                strip_sum[m].at[pl.ds(half, half), lanes(128 * j, 128)],
                at_x,
            )

    def third(m):
        kind, depth, blocks = KINDS[m]
        half = depth // 2
        arrive((m, 2))
        for j in range(blocks):
            add_rows(strip_sum[m], 128 * j, half_sum[m], 256 * j + 128 * y, 128, 0, half)
            add_rows(strip_sum[m], 128 * j, half_sum[m], 256 * j + 128 * x, 128, half, half)
        for k in range(1, batch):
            to = (z + k) % batch
            for row, count, at, j in pieces(kind, to):
                remote(
                    strip_sum[m].at[pl.ds(pl.multiple_of(at, 16), count), lanes(128 * j, 128)],
                    zgot.at[k - 1, pl.ds(row, count)],
                    zsend.at[m, k],
                    zrecv.at[m, k],
                    (f, to),
                )

    def whole(m, k):
        lo, hi = SPANS[KINDS[m][0]]
        return zgot.at[k - 1, pl.ds(lo, hi - lo)]

    def last(m):
        kind, depth, blocks = KINDS[m]
        for k in range(1, batch):
            pltpu.make_async_copy(whole(m, k), whole(m, k), zrecv.at[m, k]).wait()
        for row, count, at, j in pieces(kind, z):
            step = 128 if count == 1024 else count

            def body(i, carry, row=row, at=at, j=j, step=step):
                rows = pl.ds(pl.multiple_of(row + i * step, 16), step)
                mine = strip_sum[m][pl.ds(pl.multiple_of(at + i * step, 16), step), lanes(128 * j, 128)]
                total_sum = mine.astype(F32)
                for k in range(batch - 1):
                    total_sum = total_sum + zgot[k, rows, :].astype(F32)
                out[rows, :] = total_sum.astype(BF16)
                return carry

            lax.fori_loop(0, count // step, body, 0)

    loads = {}
    a, b, cc, d = ORDER
    zero(a)
    zero(b)
    zero(cc)
    zero(d)
    lax.fori_loop(1, total, lambda k, u: (mod_group(k, True), u)[1], 0)
    mod_own = local(dmod.at[:, lanes(128 * strip_of(f), 128)], dmod_out.at[me], mown)
    out[pl.ds(0, 96), :] = jnp.zeros((96, 128), BF16)
    first(a)
    first(b)
    second(a)
    first(cc)
    second(b)
    third(a)
    first(d)
    second(cc)
    third(b)
    second(d)
    last(a)
    third(cc)
    last(b)
    third(d)
    last(cc)
    last(d)
    for copies in slots.values():
        for copy in copies:
            copy.wait_send()
    for m in range(4):
        for k in range(1, batch):
            pltpu.make_async_copy(whole(m, k), whole(m, k), zsend.at[m, k]).wait()
    mod_own.wait()
    lax.fori_loop(1, total, lambda k, u: (mod_group(k, False), u)[1], 0)


def reduce_matrices(grads, dmod, total, batch):
    def bufs(width):
        return [pltpu.VMEM((depth, blocks * width), BF16) for _, depth, blocks in KINDS]

    return pl.pallas_call(
        partial(reduce_kernel, total, batch),
        out_shape=[
            jax.ShapeDtypeStruct((HELD, 128), BF16),
            jax.ShapeDtypeStruct((total, dmod.shape[0], 128), F32),
        ],
        in_specs=[ANY] * 5,
        out_specs=[pl.BlockSpec(memory_space=pltpu.VMEM), ANY],
        scratch_shapes=bufs(512)
        + bufs(512)
        + bufs(256)
        + bufs(128)
        + [
            pltpu.VMEM((batch - 1, HELD, 128), BF16),
            pltpu.SemaphoreType.DMA((54,)),
            pltpu.SemaphoreType.DMA((54,)),
            pltpu.SemaphoreType.DMA((4, 4)),
            pltpu.SemaphoreType.DMA((4, batch)),
            pltpu.SemaphoreType.DMA((4, batch)),
            pltpu.SemaphoreType.DMA((total,)),
            pltpu.SemaphoreType.DMA((total,)),
            pltpu.SemaphoreType.DMA,
        ],
        compiler_params=pltpu.CompilerParams(
            collective_id=2, has_side_effects=True, vmem_limit_bytes=VMEM_LIMIT
        ),
        name="reduce_matrices",
    )(*grads, dmod)


def pick_kernel(index, src, dst):
    def body(i, carry):
        dst[i] = src[index[i]]
        return carry

    lax.fori_loop(0, dst.shape[0], body, 0)


def pick_blocks(index, src):
    whole = pl.BlockSpec(memory_space=pltpu.VMEM)
    return pl.pallas_call(
        pick_kernel,
        out_shape=jax.ShapeDtypeStruct((index.shape[0],) + src.shape[1:], src.dtype),
        in_specs=[pl.BlockSpec(memory_space=pltpu.SMEM), whole],
        out_specs=whole,
        name="pick_blocks",
    )(index, src)


def cut_kernel(rows, master, out):
    swap = (rows[...] == lax.broadcasted_iota(jnp.int32, (ROWS, ROWS), 1)).astype(BF16)
    for s in range(8):
        strip = master[pl.ds(s, ROWS, stride=8), :].astype(BF16)
        out[:, 128 * s : 128 * s + 128] = jnp.dot(swap, strip, preferred_element_type=F32).astype(BF16)


def cut_owned(rows, master):
    whole = pl.BlockSpec(memory_space=pltpu.VMEM)
    return pl.pallas_call(
        cut_kernel,
        out_shape=jax.ShapeDtypeStruct((ROWS, 1024), BF16),
        in_specs=[whole, whole],
        out_specs=whole,
        compiler_params=pltpu.CompilerParams(vmem_limit_bytes=VMEM_LIMIT),
        name="cut_owned",
    )(rows, master)


def adam(grad, master, first, second):
    new_first = BETA_ONE * first + (1.0 - BETA_ONE) * grad
    new_second = BETA_TWO * second + (1.0 - BETA_TWO) * grad * grad
    fix_one = 1.0 - BETA_ONE**STEP
    fix_two = 1.0 - BETA_TWO**STEP
    update = new_first / fix_one / (jnp.sqrt(new_second / fix_two) + ADAM_EPS)
    return master - LEARN_RATE * (update + WEIGHT_DECAY * master), new_first, new_second


def update_kernel(rows, grad, master, first, second, new_master, new_first, new_second):
    base = pl.program_id(0) * GROUP
    swap = (rows[...] == base + lax.broadcasted_iota(jnp.int32, (GROUP, ROWS), 0)).astype(BF16)
    for s in range(8):
        at = pl.ds(s, GROUP, stride=8)
        value = jnp.dot(swap, grad[:, 128 * s : 128 * s + 128], preferred_element_type=F32)
        new_master[at, :], new_first[at, :], new_second[at, :] = adam(
            value, master[at, :], first[at, :], second[at, :]
        )


def update_owned(rows, grad, master, first, second):
    part = pl.BlockSpec((8 * GROUP, 128), lambda i: (i, 0))
    return pl.pallas_call(
        update_kernel,
        grid=(ROWS // GROUP,),
        out_shape=[jax.ShapeDtypeStruct(master.shape, F32)] * 3,
        in_specs=[
            pl.BlockSpec((1, ROWS), lambda i: (0, 0)),
            pl.BlockSpec((ROWS, 1024), lambda i: (0, 0)),
            part,
            part,
            part,
        ],
        out_specs=[part] * 3,
        compiler_params=pltpu.CompilerParams(vmem_limit_bytes=VMEM_LIMIT),
        name="update_owned",
    )(rows, grad, master, first, second)


def key_positions(rows, piece, per):
    i = lax.broadcasted_iota(jnp.int32, (rows, 1), 0)
    local_rows = rows // per
    return ((i % local_rows) // piece * per + i // local_rows) * piece + i % piece


def scores_t(k, q, ends, piece, per):
    s = lax.dot_general(k, q, (((1,), (1,)), ((), ())), preferred_element_type=F32)
    pos = key_positions(k.shape[0], piece, per)
    cols = []
    for t in range(q.shape[0] // piece):
        part = s[:, t * piece : (t + 1) * piece]
        cols.append(jnp.where(pos < ends[t], part, NEG_FILL))
    return jnp.concatenate(cols, axis=1)


def attend_kernel(piece, per, ends, q, k, v, o):
    outs = []
    for a in range(2):
        cut = slice(64 * a, 64 * a + 64)
        s = scores_t(k[:, cut], q[:, cut], ends, piece, per)
        peak = jnp.max(s, axis=0, keepdims=True)
        e = jnp.exp(s - peak)
        p = (e * (1.0 / jnp.sum(e, axis=0, keepdims=True))).astype(BF16)
        outs.append(lax.dot_general(p, v[:, cut], (((0,), (0,)), ((), ())), preferred_element_type=F32))
    o[...] = jnp.concatenate(outs, axis=1).astype(BF16)


def attend(ends, q, kv, piece, per):
    rows, width = q.shape
    keys = kv.shape[0]
    pairs = width // 128
    return pl.pallas_call(
        partial(attend_kernel, piece, per),
        grid_spec=pltpu.PrefetchScalarGridSpec(
            num_scalar_prefetch=1,
            grid=(pairs,),
            in_specs=[
                pl.BlockSpec((rows, 128), lambda h, e: (0, h)),
                pl.BlockSpec((keys, 128), lambda h, e: (0, h)),
                pl.BlockSpec((keys, 128), lambda h, e: (0, h + pairs)),
            ],
            out_specs=pl.BlockSpec((rows, 128), lambda h, e: (0, h)),
        ),
        out_shape=jax.ShapeDtypeStruct((rows, width), BF16),
        compiler_params=pltpu.CompilerParams(vmem_limit_bytes=VMEM_LIMIT),
        cost_estimate=pl.CostEstimate(
            flops=4 * rows * keys * width, bytes_accessed=4 * (rows + keys) * width, transcendentals=rows * keys * H
        ),
        name="attend",
    )(ends, q, kv, kv)


def attend_back_kernel(piece, per, ends, q, k, v, do, dq, dk, dv):
    dqs, dks, dvs = [], [], []
    for a in range(2):
        cut = slice(64 * a, 64 * a + 64)
        qa, ka, va, da = q[:, cut], k[:, cut], v[:, cut], do[:, cut]
        s = scores_t(ka, qa, ends, piece, per)
        peak = jnp.max(s, axis=0, keepdims=True)
        e = jnp.exp(s - peak)
        p = e * (1.0 / jnp.sum(e, axis=0, keepdims=True))
        dvs.append(jnp.dot(p.astype(BF16), da, preferred_element_type=F32))
        dp = lax.dot_general(va, da, (((1,), (1,)), ((), ())), preferred_element_type=F32)
        pdp = p * dp
        row = jnp.sum(pdp, axis=0, keepdims=True)
        ds = (pdp - p * row).astype(BF16)
        dks.append(jnp.dot(ds, qa, preferred_element_type=F32))
        dqs.append(lax.dot_general(ds, ka, (((0,), (0,)), ((), ())), preferred_element_type=F32))
    dq[...] = jnp.concatenate(dqs, axis=1).astype(BF16)
    dk[...] = jnp.concatenate(dks, axis=1).astype(BF16)
    dv[...] = jnp.concatenate(dvs, axis=1).astype(BF16)


def attend_back(ends, q, kv, do, piece, per):
    rows, width = q.shape
    keys = kv.shape[0]
    pairs = width // 128
    mine = pl.BlockSpec((rows, 128), lambda h, e: (0, h))
    allk = pl.BlockSpec((keys, 128), lambda h, e: (0, h))
    return pl.pallas_call(
        partial(attend_back_kernel, piece, per),
        grid_spec=pltpu.PrefetchScalarGridSpec(
            num_scalar_prefetch=1,
            grid=(pairs,),
            in_specs=[mine, allk, pl.BlockSpec((keys, 128), lambda h, e: (0, h + pairs)), mine],
            out_specs=[mine, allk, allk],
        ),
        out_shape=[
            jax.ShapeDtypeStruct((rows, width), BF16),
            jax.ShapeDtypeStruct((keys, width), BF16),
            jax.ShapeDtypeStruct((keys, width), BF16),
        ],
        compiler_params=pltpu.CompilerParams(vmem_limit_bytes=VMEM_LIMIT),
        cost_estimate=pl.CostEstimate(
            flops=10 * rows * keys * width, bytes_accessed=6 * (rows + keys) * width, transcendentals=rows * keys * H
        ),
        name="attend_back",
    )(ends, q, kv, kv, do)


def layer_stats(values):
    centre = values - jnp.mean(values, axis=-1, keepdims=True)
    inv_std = lax.rsqrt(jnp.mean(centre * centre, axis=-1, keepdims=True) + 1e-06)
    return (centre * inv_std, inv_std)


def norm_back(upstream, normed, inv_std):
    mean_grad = jnp.mean(upstream, axis=-1, keepdims=True)
    mean_cross = jnp.mean(upstream * normed, axis=-1, keepdims=True)
    return inv_std * (upstream - mean_grad - normed * mean_cross)


def noise_embedding(levels, feature_width):
    half_width = feature_width // 2
    frequencies = jnp.exp(
        -math.log(10000.0) * jnp.arange(half_width, dtype=jnp.float32) / half_width
    )
    angles = levels.astype(jnp.float32)[:, None] * frequencies[None, :]
    return jnp.concatenate([jnp.cos(angles), jnp.sin(angles)], axis=1)


def silu_embedding(levels, width):
    return jax.nn.silu(noise_embedding(levels, width)).astype(BF16)


def split_flat(flat_values, model_width, hidden_width):
    matrix_shapes = (
        (model_width, 6 * model_width),
        (model_width, 3 * model_width),
        (model_width, model_width),
        (model_width, hidden_width),
        (hidden_width, model_width),
    )
    matrices = []
    offset_now = 0
    for matrix_shape in matrix_shapes:
        entry_count = matrix_shape[0] * matrix_shape[1]
        matrices.append(flat_values[offset_now : offset_now + entry_count].reshape(matrix_shape))
        offset_now = offset_now + entry_count
    return matrices


def shards(
    frame_size,
    batch_size,
    tokens,
    out_cotangent,
    buckets,
    noise_levels,
    owned_block,
    master,
    first_moment,
    second_moment,
):
    micro_count, piece, width = tokens.shape
    block_size = master.shape[1]
    frame_count = noise_levels.shape[1]
    total = frame_size * batch_size
    videos = micro_count
    per = frame_size // videos
    rows = videos * piece
    keys = rows * per
    q_scale = HD ** (-0.5)
    f, z = frame_index()
    me = f * batch_size + z
    mine, g = f // per, f % per
    direct = frame_size == 8 and batch_size == 4 and block_size == ROWS * 1024 and videos == 4 and frame_count == 4

    if direct:
        inverse = jnp.argsort(owned_block).astype(jnp.int32)
        table = jnp.asarray(np.stack([block_rows(b) for b in range(total)]).astype(np.int32))
        own_rows = lax.dynamic_index_in_dim(table, owned_block[me], 0, keepdims=False)
        cut_block = cut_owned(own_rows[:, None], master.reshape(-1, 128))
        levels = jnp.zeros((8, 128), jnp.int32).at[:4, :4].set(noise_levels)
        cut, all_levels, tok, cot = scatter_blocks(cut_block, levels, tokens, out_cotangent, total, batch_size)
        ordered = pick_blocks(inverse, cut)
        held = ordered[FIRST:].reshape(HELD, 128)
        cond = silu_embedding(all_levels[:, :4, :4].reshape(64), width)
        ada_row, ada_col = ada_rows(z)
        spread = (ada_row[None, :] == jnp.arange(width, dtype=jnp.int32)[:, None]).astype(BF16)
        cond_rows = jnp.dot(cond, spread, preferred_element_type=F32).astype(BF16)
        six = (ada_col[None, :] == jnp.arange(6, dtype=jnp.int32)[:, None]).astype(BF16)
        cond_all = (cond_rows.reshape(16, 1, 4, -1) * six[None, :, None, :]).reshape(384, -1)
        mod_part = jnp.dot(
            cond_all, ordered[: FIRST + 1].reshape(-1, 128), preferred_element_type=F32
        ).reshape(16, 24, 128)
    else:
        tok, cot = swap_videos([tokens, out_cotangent], videos, per, 0)
        gathered = lax.all_gather(master.astype(BF16), ("frame", "batch"), axis=0, tiled=True)
        placed = jnp.take(gathered, jnp.argsort(owned_block), axis=0).reshape(-1)
        w_ada, w_qkv, w_out, w_in, w_down = split_flat(placed, width, FF)
        cond = silu_embedding(lax.dynamic_index_in_dim(noise_levels, mine, 0, keepdims=False), width)
        modulation = jnp.dot(cond, w_ada, preferred_element_type=F32).reshape(frame_count, 6, width)

    frame_len = FRAME_LO * (1 + 3 * buckets[mine])
    piece_at = (jnp.arange(videos, dtype=jnp.int32) * per + g) * piece
    piece_frame = piece_at // frame_len
    ends = (piece_frame + 1) * frame_len
    selector = (piece_frame[:, None] == jnp.arange(frame_count, dtype=jnp.int32)[None, :]).astype(F32)

    def flat(a):
        return a.reshape(rows, a.shape[-1])

    def cube(a):
        return a.reshape(videos, piece, a.shape[-1])

    def partners(k):
        return [(i, i // per * per + (i + k) % per) for i in range(frame_size)]

    def split_mod(piece_mod):
        return [piece_mod[j][:, None, :] for j in range(6)]

    x_float = tok.astype(F32)
    normed_one, inv_one = layer_stats(x_float)
    if direct:
        (
            w_qkv, w_out, w_in, w_down, h_one, queries, kv_all, attended,
            attn_out, middle, h_two, slope, act_low, mlp_out, block_output, piece_mod,
        ) = forward(selector, ends, tok.reshape(rows, width), held, mod_part, total, batch_size, piece, per)
        kv_all = kv_all.reshape(keys, 2 * width)
        middle = cube(middle)
        block_output = cube(block_output)
        normed_two, inv_two = layer_stats(middle)
        shift_one, scale_one, gate_one, shift_two, scale_two, gate_two = split_mod(
            piece_mod.reshape(6, videos, width)
        )
    else:
        piece_mod = jnp.einsum("pf,fjd->jpd", selector, modulation, precision=HIGHEST)
        shift_one, scale_one, gate_one, shift_two, scale_two, gate_two = split_mod(piece_mod)

        h_one = flat((normed_one * (1.0 + scale_one) + shift_one).astype(BF16))
        projected = jnp.dot(h_one, w_qkv, preferred_element_type=F32)
        queries = (projected[:, :width] * q_scale).astype(BF16)
        kv_own = projected[:, width:].astype(BF16)

        kv_all = jnp.zeros((per, rows, 2 * width), BF16)
        kv_all = lax.dynamic_update_index_in_dim(kv_all, kv_own, g, 0)
        for k in range(1, per):
            kv_all = lax.dynamic_update_index_in_dim(
                kv_all, lax.ppermute(kv_own, "frame", partners(k)), (g + per - k) % per, 0
            )
        kv_all = kv_all.reshape(keys, 2 * width)
        attended = attend(ends, queries, kv_all, piece, per)
        attn_out = jnp.dot(attended, w_out, preferred_element_type=F32)
        middle = x_float + gate_one * cube(attn_out)
        normed_two, inv_two = layer_stats(middle)
        h_two = flat((normed_two * (1.0 + scale_two) + shift_two).astype(BF16))
        pre_act = jnp.dot(h_two, w_in, preferred_element_type=F32)
        activated, gelu_back = jax.vjp(partial(jax.nn.gelu, approximate=True), pre_act)
        act_low = activated.astype(BF16)
        slope = gelu_back(jnp.ones_like(pre_act))[0]
        mlp_out = jnp.dot(act_low, w_down, preferred_element_type=F32)
        block_output = (middle + gate_two * cube(mlp_out)).astype(BF16)

    grad_out = cot.astype(F32)
    d_mlp = flat((gate_two * grad_out).astype(BF16))
    g_down = jnp.dot(act_low.T, d_mlp, preferred_element_type=F32).astype(BF16)
    d_act = jnp.dot(d_mlp, w_down.T, preferred_element_type=F32)
    d_pre = (d_act * slope.astype(F32)).astype(BF16)
    g_in = jnp.dot(h_two.T, d_pre, preferred_element_type=F32).astype(BF16)
    d_htwo = cube(jnp.dot(d_pre, w_in.T, preferred_element_type=F32))
    d_gate_two = jnp.sum(grad_out * cube(mlp_out), axis=1)
    d_scale_two = jnp.sum(d_htwo * normed_two, axis=1)
    d_shift_two = jnp.sum(d_htwo, axis=1)
    d_middle = grad_out + norm_back(d_htwo * (1.0 + scale_two), normed_two, inv_two)
    d_attn = flat((gate_one * d_middle).astype(BF16))
    d_gate_one = jnp.sum(d_middle * cube(attn_out), axis=1)
    g_out = jnp.dot(attended.T, d_attn, preferred_element_type=F32).astype(BF16)
    d_attended = jnp.dot(d_attn, w_out.T, preferred_element_type=F32).astype(BF16)
    dq, dk, dv = attend_back(ends, queries, kv_all, d_attended, piece, per)
    dkv = jnp.concatenate([dk, dv], axis=1).reshape(per, rows, 2 * width)
    dkv_own = lax.dynamic_index_in_dim(dkv, g, 0, keepdims=False).astype(F32)
    for k in range(1, per):
        sent = lax.dynamic_index_in_dim(dkv, (g + k) % per, 0, keepdims=False)
        dkv_own = dkv_own + lax.ppermute(sent, "frame", partners(k)).astype(F32)
    d_proj = jnp.concatenate([dq * jnp.asarray(q_scale, BF16), dkv_own.astype(BF16)], axis=1)
    g_qkv = jnp.dot(h_one.T, d_proj, preferred_element_type=F32).astype(BF16)
    d_hone = cube(jnp.dot(d_proj, w_qkv.T, preferred_element_type=F32))
    d_scale_one = jnp.sum(d_hone * normed_one, axis=1)
    d_shift_one = jnp.sum(d_hone, axis=1)
    d_input = d_middle + norm_back(d_hone * (1.0 + scale_one), normed_one, inv_one)
    input_grad = d_input.astype(BF16)
    piece_dmod = jnp.stack([d_shift_one, d_scale_one, d_gate_one, d_shift_two, d_scale_two, d_gate_two])
    frame_dmod = jnp.einsum("pf,jpd->jfd", selector, piece_dmod, precision=HIGHEST)

    if direct:
        held_grad, dmod_parts = reduce_matrices(
            [g_qkv, g_out, g_in, g_down], frame_dmod.reshape(24, width), total, batch_size
        )
        dmod_all = jnp.sum(dmod_parts.reshape(4, 2, 4, 24, 128), axis=1).transpose(1, 0, 2, 3).reshape(384, 128)
        ada_grad = lax.dot_general(
            cond_all.astype(F32), dmod_all, (((0,), (0,)), ((), ())), precision=HIGHEST
        ).astype(BF16)
        edge = jnp.concatenate([ada_grad[FIRST * GROUP : FIRST * GROUP + 96], held_grad[96:GROUP]], axis=0)
        ordered_grad = jnp.concatenate([ada_grad[: FIRST * GROUP], edge, held_grad[GROUP:]], axis=0)
        cut_grad = pick_blocks(owned_block, ordered_grad.reshape(total, GROUP, 128))
        grad_block, outputs, input_grads = collect_blocks(cut_grad, block_output, input_grad, total, batch_size)
        updated = update_owned(
            own_rows[None, :],
            grad_block,
            master.reshape(-1, 128),
            first_moment.reshape(-1, 128),
            second_moment.reshape(-1, 128),
        )
        new_master, new_first, new_second = [a.reshape(1, block_size) for a in updated]
    else:
        outputs, input_grads = swap_videos([block_output, input_grad], videos, per, 1)
        g_ada = lax.dot_general(
            cond.astype(F32),
            frame_dmod.transpose(1, 0, 2).reshape(frame_count, 6 * width),
            (((0,), (0,)), ((), ())),
            precision=HIGHEST,
        )
        flat_grads = jnp.concatenate(
            [piece_grad.astype(F32).reshape(-1) for piece_grad in (g_ada, g_qkv, g_out, g_in, g_down)]
        )
        arranged = jnp.take(flat_grads.reshape(-1, block_size), owned_block, axis=0).reshape(-1)
        shard_total = lax.psum_scatter(
            arranged, ("frame", "batch"), scatter_dimension=0, tiled=True
        ).reshape(1, block_size)
        new_master, new_first, new_second = adam(shard_total, master, first_moment, second_moment)
    return (outputs, input_grads, new_master, new_first, new_second)


def solution(mesh):
    placed = (
        P("batch", "frame", None),
        P("batch", "frame", None),
        P("batch"),
        P("batch", None),
        P(),
        P(("frame", "batch"), None),
        P(("frame", "batch"), None),
        P(("frame", "batch"), None),
    )
    return jax.shard_map(
        partial(shards, mesh.shape["frame"], mesh.shape["batch"]),
        mesh=mesh,
        in_specs=placed,
        out_specs=(
            P("batch", "frame", None),
            P("batch", "frame", None),
            P(("frame", "batch"), None),
            P(("frame", "batch"), None),
            P(("frame", "batch"), None),
        ),
        check_vma=False,
    )
```

```python
from functools import partial
import math

import jax
import jax.numpy as jnp
import numpy as np
from jax import lax
from jax.experimental import pallas as pl
from jax.experimental.pallas import tpu as pltpu
from jax.sharding import PartitionSpec as P

H = 16
HD = 64
FF = 4096
FRAME_LO = 256
STEP = 10

HIGHEST = lax.Precision.HIGHEST
NEG_FILL = -1e30
BETA_ONE = 0.5
BETA_TWO = 0.5
LEARN_RATE = 0.05
WEIGHT_DECAY = 0.1
ADAM_EPS = 1e-08
MESH = pl.DeviceIdType.MESH
F32 = jnp.float32
BF16 = jnp.bfloat16
ANY = pl.BlockSpec(memory_space=pl.ANY)
VMEM_LIMIT = 60 * 1024 * 1024

ROWS = 576
GROUP = 144
FIRST = 10
KINDS = (("qkv", 1024, 3), ("out", 1024, 1), ("in", 1024, 4), ("down", 4096, 1))
SPANS = {"qkv": (96, 864), "out": (864, 1120), "in": (1120, 2144), "down": (2144, 3168)}
HELD = 3168


def pieces(kind, z):
    if kind == "qkv":
        found = [(96 + 16 * j, 16, 16 * z, j) for j in range(3)]
        for k in range(5):
            found += [(144 + 144 * k + 48 * j, 48, 64 + 192 * k + 48 * z, j) for j in range(3)]
        return found
    if kind == "out":
        return [(864, 144, 144 * z, 0), (1008, 112, 576 + 112 * z, 0)]
    if kind == "in":
        return [(1120, 1024, 0, z)]
    found = [(2144, 16, 16 * z, 0)]
    return found + [(2160 + 144 * k, 144, 64 + 576 * k + 144 * z, 0) for k in range(7)]


def block_rows(block):
    t = np.arange(GROUP)
    groups = []
    for z in range(4):
        if block == 10:
            i = t - 96
            rows = np.where(t < 96, 96 * z + t, 384 + 3 * (16 * z + i % 16) + i // 16)
        elif 11 <= block <= 15:
            rows = 3 * (48 * z + t % 48) + t // 48
        elif block == 17:
            rows = np.where(t < 112, 112 * z + t, 448 + 4 * (t - 112) + z)
        elif 18 <= block <= 23:
            rows = 4 * t + z
        elif block == 24:
            rows = np.where(t < 128, 4 * t + z, 512 + 16 * z + t - 128)
        else:
            rows = GROUP * z + t
        groups.append(rows)
    return np.concatenate(groups)


def ada_rows(z):
    t = jnp.arange(GROUP, dtype=jnp.int32)
    rows = [96 * b + 24 * z + t // 6 for b in range(10)]
    rows.append(jnp.where(t < 96, 960 + 16 * z + t // 6, -1))
    return jnp.concatenate(rows), jnp.tile(t % 6, 11)


def frame_index():
    return lax.axis_index("frame"), lax.axis_index("batch")


def strip_of(f):
    return 4 * (f % 2) + f // 2


def greet(devices):
    barrier = pltpu.get_barrier_semaphore()
    for device in devices:
        pl.semaphore_signal(barrier, inc=1, device_id=device, device_id_type=MESH)
    pl.semaphore_wait(barrier, len(devices))


def greet_all(total, batch):
    f, z = frame_index()
    me = f * batch + z
    barrier = pltpu.get_barrier_semaphore()

    def hail(k, carry):
        other = (me + k) % total
        pl.semaphore_signal(barrier, inc=1, device_id=(other // batch, other % batch), device_id_type=MESH)
        return carry

    lax.fori_loop(1, total, hail, 0)
    pl.semaphore_wait(barrier, total - 1)


def remote(src, dst, send, recv, device):
    copy = pltpu.make_async_remote_copy(
        src_ref=src, dst_ref=dst, send_sem=send, recv_sem=recv, device_id=device, device_id_type=MESH
    )
    copy.start()
    return copy


def local(src, dst, sem):
    copy = pltpu.make_async_copy(src, dst, sem)
    copy.start()
    return copy


def video_kernel(videos, per, arrays, *refs):
    ins, outs = refs[:arrays], refs[arrays : 2 * arrays]
    send, recv, own = refs[2 * arrays :]
    f, z = frame_index()
    mine, g = f // per, f % per
    others = [((mine + k) % videos, k) for k in range(1, videos)]
    greet([(v * per + g, z) for v, k in others])
    copies = []
    for a in range(arrays):
        for v, k in others:
            copies.append(
                remote(ins[a].at[v], outs[a].at[mine], send.at[a, k], recv.at[a, k], (v * per + g, z))
            )
        copies.append(local(ins[a].at[mine], outs[a].at[mine], own.at[a]))
    for copy in copies:
        copy.wait()


def swap_videos(arrays, videos, per, ident):
    count = len(arrays)
    return pl.pallas_call(
        partial(video_kernel, videos, per, count),
        out_shape=[jax.ShapeDtypeStruct(a.shape, a.dtype) for a in arrays],
        in_specs=[ANY] * count,
        out_specs=[ANY] * count,
        scratch_shapes=[
            pltpu.SemaphoreType.DMA((count, videos)),
            pltpu.SemaphoreType.DMA((count, videos)),
            pltpu.SemaphoreType.DMA((count,)),
        ],
        compiler_params=pltpu.CompilerParams(collective_id=ident, has_side_effects=True),
        name="swap_videos",
    )(*arrays)


def scatter_kernel(total, batch, blk, levels, tok, cot, cut, all_levels, tok_out, cot_out, send, recv, vsend, vrecv, lsend, lrecv, own):
    f, z = frame_index()
    me = f * batch + z
    greet_all(total, batch)
    mine, g = f // 2, f % 2

    def group(k, start):
        other = (me + k) % total
        of, oz = other // batch, other % batch
        copy = pltpu.make_async_remote_copy(
            src_ref=blk.at[pl.ds(pl.multiple_of(GROUP * oz, 16), GROUP), pl.ds(pl.multiple_of(128 * strip_of(of), 128), 128)],
            dst_ref=cut.at[me],
            send_sem=send.at[k],
            recv_sem=recv.at[k],
            device_id=(of, oz),
            device_id_type=MESH,
        )
        if start:
            copy.start()
        else:
            copy.wait()

    copies = []
    for k in range(1, batch):
        copies.append(remote(levels, all_levels.at[z], lsend.at[k], lrecv.at[k], (f, (z + k) % batch)))
    copies.append(local(levels, all_levels.at[z], own.at[0]))
    lax.fori_loop(1, total, lambda k, c: (group(k, True), c)[1], 0)
    copies.append(
        local(
            blk.at[pl.ds(pl.multiple_of(GROUP * z, 16), GROUP), pl.ds(pl.multiple_of(128 * strip_of(f), 128), 128)],
            cut.at[me],
            own.at[1],
        )
    )
    for a, (src, dst) in enumerate(((tok, tok_out), (cot, cot_out))):
        for k in range(1, 4):
            v = (mine + k) % 4
            copies.append(remote(src.at[v], dst.at[mine], vsend.at[a, k], vrecv.at[a, k], (v * 2 + g, z)))
        copies.append(local(src.at[mine], dst.at[mine], own.at[2 + a]))
    for copy in copies:
        copy.wait()
    lax.fori_loop(1, total, lambda k, c: (group(k, False), c)[1], 0)


def scatter_blocks(blk, levels, tok, cot, total, batch):
    return pl.pallas_call(
        partial(scatter_kernel, total, batch),
        out_shape=[
            jax.ShapeDtypeStruct((total, GROUP, 128), BF16),
            jax.ShapeDtypeStruct((batch,) + levels.shape, levels.dtype),
            jax.ShapeDtypeStruct(tok.shape, tok.dtype),
            jax.ShapeDtypeStruct(cot.shape, cot.dtype),
        ],
        in_specs=[ANY] * 4,
        out_specs=[ANY] * 4,
        scratch_shapes=[
            pltpu.SemaphoreType.DMA((total,)),
            pltpu.SemaphoreType.DMA((total,)),
            pltpu.SemaphoreType.DMA((2, 4)),
            pltpu.SemaphoreType.DMA((2, 4)),
            pltpu.SemaphoreType.DMA((batch,)),
            pltpu.SemaphoreType.DMA((batch,)),
            pltpu.SemaphoreType.DMA((4,)),
        ],
        compiler_params=pltpu.CompilerParams(collective_id=0, has_side_effects=True),
        name="scatter_blocks",
    )(blk, levels, tok, cot)


def collect_kernel(total, batch, cut, grad, blk, grad_out, send, recv, vsend, vrecv, own):
    f, z = frame_index()
    me = f * batch + z
    greet_all(total, batch)
    mine, g = f // 2, f % 2

    def spot(of, oz):
        return blk.at[pl.ds(pl.multiple_of(GROUP * oz, 16), GROUP), pl.ds(pl.multiple_of(128 * strip_of(of), 128), 128)]

    def group(k, start):
        other = (me + k) % total
        copy = pltpu.make_async_remote_copy(
            src_ref=cut.at[other],
            dst_ref=spot(f, z),
            send_sem=send.at[k],
            recv_sem=recv.at[k],
            device_id=(other // batch, other % batch),
            device_id_type=MESH,
        )
        if start:
            copy.start()
        else:
            copy.wait()

    lax.fori_loop(1, total, lambda k, c: (group(k, True), c)[1], 0)
    copies = [local(cut.at[me], spot(f, z), own.at[0])]
    for a, (src, dst) in enumerate(((grad, grad_out),)):
        for k in range(1, 4):
            v = (mine + k) % 4
            copies.append(remote(src.at[v], dst.at[mine], vsend.at[a, k], vrecv.at[a, k], (v * 2 + g, z)))
        copies.append(local(src.at[mine], dst.at[mine], own.at[1 + a]))
    for copy in copies:
        copy.wait()
    lax.fori_loop(1, total, lambda k, c: (group(k, False), c)[1], 0)


def collect_blocks(cut, grad, total, batch):
    return pl.pallas_call(
        partial(collect_kernel, total, batch),
        out_shape=[
            jax.ShapeDtypeStruct((ROWS, 1024), BF16),
            jax.ShapeDtypeStruct(grad.shape, grad.dtype),
        ],
        in_specs=[ANY] * 2,
        out_specs=[ANY] * 2,
        scratch_shapes=[
            pltpu.SemaphoreType.DMA((total,)),
            pltpu.SemaphoreType.DMA((total,)),
            pltpu.SemaphoreType.DMA((2, 4)),
            pltpu.SemaphoreType.DMA((2, 4)),
            pltpu.SemaphoreType.DMA((3,)),
        ],
        compiler_params=pltpu.CompilerParams(collective_id=3, has_side_effects=True),
        name="collect_blocks",
    )(cut, grad)


def plane():
    f, z = frame_index()
    y, x, c = f // 4, (f // 2) % 2, f % 2
    at_x = (4 * y + 2 * (1 - x) + c, z)
    at_y = (4 * (1 - y) + 2 * x + c, z)
    at_c = (4 * y + 2 * x + 1 - c, z)
    return y, x, c, z, at_x, at_y, at_c


def lanes(first, count):
    return pl.ds(pl.multiple_of(first, 128), count)


UNITS = (
    [("qkv", 0, 1024, 1024 * j) for j in range(3)]
    + [("out", 0, 1024, 0)]
    + [("in", 0, 1024, 1024 * j) for j in range(4)]
    + [("down", 1024 * n, 1024, 0) for n in range(4)]
)
DEALS = (
    [("qkv", j, 0, 1024) for j in range(3)]
    + [("out", 0, 0, 1024), ("in", None, 0, 1024)]
    + [("down", 0, first, count) for first, count in ((0, 1216), (1216, 1152), (2368, 1152), (3520, 576))]
)
DEAL_OF = (0, 1, 2, 3, 4, 4, 4, 4, 5, 6, 7, 8)
DEAL_ROWS = (256, 256, 256, 256, 1024, 304, 288, 288, 144)


def deal_pieces(d, z):
    kind, j, first, count = DEALS[d]
    last = first + count
    found = []
    for row, rows, to, col in pieces(kind, z):
        base = pieces(kind, 0)[len(found)][2] if kind == "down" else None
        found.append((row, rows, to, col, base))
    if kind == "down":
        return [p[:4] for p in found if first <= p[4] < last]
    if kind == "qkv":
        return [p[:4] for p in found if p[3] == j]
    return [p[:4] for p in found]


GELU_A = math.sqrt(2.0 / math.pi)
GELU_B = 0.044715


def row_loop(count, step, body):
    def one(i, carry):
        body(pl.multiple_of(i * step, step))
        return carry

    lax.fori_loop(0, count // step, one, 0)


def norm_rows(values):
    centre = values - jnp.mean(values, axis=-1, keepdims=True)
    inv_std = lax.rsqrt(jnp.mean(centre * centre, axis=-1, keepdims=True) + 1e-06)
    return centre * inv_std, inv_std


def lane_half(e):
    return lax.broadcasted_iota(jnp.int32, (1, 128), 1) // 64 == e


def choose(mask, one, other):
    return jnp.where(mask, one.astype(F32), other.astype(F32)).astype(BF16)


def three_parts(value):
    high = value.astype(BF16).astype(F32)
    rest = value - high
    middle = rest.astype(BF16).astype(F32)
    return high, middle, rest - middle


def in_lanes(parts, first):
    lane = lax.broadcasted_iota(jnp.int32, (1, 128), 1) % 64
    total = 0.0
    for n, part in enumerate(parts):
        total = total + jnp.where(lane == first + n, part, 0.0)
    return total


def query_mask(ends, piece):
    lane = lax.broadcasted_iota(jnp.int32, (piece, 128), 1) % 64
    found = []
    for t in range(4):
        hidden = (lane < 4) & (lane * FRAME_LO >= ends[t])
        found.append(jnp.where(hidden, NEG_FILL, 0.0))
    return jnp.concatenate(found, axis=0)


def key_mask(keys, piece, per):
    lane = lax.broadcasted_iota(jnp.int32, (keys, 128), 1) % 64
    quarter = key_positions(keys, piece, per) // FRAME_LO
    return jnp.where((lane == quarter) | ((lane >= 4) & (lane < 7)), 1.0, 0.0)


def dot_nt(a, b):
    return lax.dot_general(a, b, (((1,), (1,)), ((), ())), preferred_element_type=F32)


def dot_tn(a, b):
    return lax.dot_general(a, b, (((0,), (0,)), ((), ())), preferred_element_type=F32)


def dot_nn(a, b):
    return jnp.dot(a, b, preferred_element_type=F32)


def fold_rows(values):
    return values[:8] + values[8:]


def forward_kernel(total, batch, piece, per, sel, ends, tok, cot, held, mod, *refs):
    hbm, vm, sems = refs[:17], refs[17:36], refs[36:]
    wq_o, wo_o, wi_o, wd_o, h1_o, q_o, qb_o, kv_o, att_o, a_o, x1_o, h2_o, gp_o, u_o, y_o, pm_o, dg_o = hbm
    wq, wo, wi, wd, h1, q, qb, kv, att, a, x1, h2, gp, u, acc, pm, mod_v, dg, kmask = vm
    zsend, zrecv, psend, precv, msend, mrecv, own, wsem, osem, kvsend, kvrecv = sems
    mats = {"qkv": wq, "out": wo, "in": wi, "down": wd}
    mats_o = {"qkv": wq_o, "out": wo_o, "in": wi_o, "down": wd_o}
    y, x, c, z, at_x, at_y, at_c = plane()
    f = 4 * y + 2 * x + c
    me = f * batch + z
    strip = 4 * c + 2 * y + x
    greet_all(total, batch)

    def mod_group(k, start):
        other = (me + k) % total
        of, oz = other // batch, other % batch
        copy = pltpu.make_async_remote_copy(
            src_ref=mod.at[4 * oz + of // 2],
            dst_ref=mod_v.at[z, :, lanes(128 * strip, 128)],
            send_sem=msend.at[k],
            recv_sem=mrecv.at[k],
            device_id=(of, oz),
            device_id_type=MESH,
        )
        if start:
            copy.start()
        else:
            copy.wait()

    def spot(kind, to, count, j):
        return mats[kind].at[pl.ds(pl.multiple_of(to, 16), count), lanes(1024 * j + 128 * strip, 128)]

    for d, (kind, _, _, _) in enumerate(DEALS):
        for k in range(1, batch):
            for row, count, to, j in deal_pieces(d, z):
                remote(
                    held.at[pl.ds(row, count)], spot(kind, to, count, j), zsend.at[d, k], zrecv.at[d, k],
                    (f, (z + k) % batch),
                )
        for row, count, to, j in deal_pieces(d, z):
            local(held.at[pl.ds(row, count)], spot(kind, to, count, j), own.at[d])
        if d == 0:
            lax.fori_loop(1, total, lambda k, t: (mod_group(k, True), t)[1], 0)
            mod_own = local(mod.at[4 * z + f // 2], mod_v.at[z, :, lanes(128 * strip, 128)], own.at[len(DEALS)])

    def whole(d):
        return held.at[pl.ds(0, DEAL_ROWS[d])]

    dealt = set()

    def deal_wait(d):
        if d in dealt:
            return
        dealt.add(d)
        for k in range(1, batch):
            pltpu.make_async_copy(whole(d), whole(d), zrecv.at[d, k]).wait()
        pltpu.make_async_copy(whole(d), whole(d), own.at[d]).wait()

    slots = {}
    counter = [0]

    def push(key, mat, row, count, col, width, device):
        s = counter[0]
        counter[0] += 1
        ref = mat.at[pl.ds(row, count), lanes(col, width)]
        slots.setdefault(key, []).append(remote(ref, ref, psend.at[s], precv.at[s], device))

    def stage_a(n):
        kind, row, rows, col = UNITS[n]
        half = rows // 2
        deal_wait(DEAL_OF[n])
        push((n, 1), mats[kind], row, half, col + 128 * strip, 128, at_x)
        push((n, 1), mats[kind], row + half, half, col + 128 * strip, 128, at_y)

    def stage_b(n):
        kind, row, rows, col = UNITS[n]
        half = rows // 2
        for copy in slots[(n, 1)]:
            copy.wait_recv()
        push((n, 2), mats[kind], row, half, col + 512 * c + 256 * y, 256, at_y)
        for yy in range(2):
            push((n, 2), mats[kind], row + half, half, col + 512 * c + 256 * yy + 128 * x, 128, at_x)

    def stage_c(n):
        kind, row, rows, col = UNITS[n]
        for copy in slots[(n, 2)]:
            copy.wait_recv()
        push((n, 3), mats[kind], row, rows, col + 512 * c, 512, at_c)

    saves = []

    def ready(n):
        kind, row, rows, col = UNITS[n]
        for copy in slots[(n, 3)]:
            copy.wait_recv()
        ref = (pl.ds(row, rows), pl.ds(col, 1024))
        saves.append(local(mats[kind].at[ref], mats_o[kind].at[ref], wsem.at[n]))

    pumped = [0]
    last_unit = len(UNITS)

    def pump():
        s = pumped[0]
        pumped[0] += 1
        if 0 <= s - 2 < last_unit:
            stage_b(s - 2)
        if s < last_unit:
            stage_a(s)
        if 0 <= s - 3 < last_unit:
            stage_c(s - 3)

    def pump_to(s):
        while pumped[0] <= s:
            pump()

    def save(src, dst, n):
        saves.append(local(src, dst, osem.at[n]))

    pump_to(0)
    lax.fori_loop(1, total, lambda k, t: (mod_group(k, False), t)[1], 0)
    mod_own.wait()
    for j in range(6):
        for p in range(4):
            value = jnp.zeros((1, 1024), F32)
            for fr in range(4):
                row = mod_v[0, pl.ds(4 * j + fr, 1), :]
                for s in range(1, batch):
                    row = row + mod_v[s, pl.ds(4 * j + fr, 1), :]
                value = value + sel[p, fr] * row
            pm[pl.ds(4 * j + p, 1), :] = value
    save(pm, pm_o, 0)

    def mod_row(j, p):
        return pm[pl.ds(4 * j + p, 1), :]

    step = 32
    for p in range(4):
        shift, scale = mod_row(0, p), mod_row(1, p)

        def one(i, p=p, shift=shift, scale=scale):
            rows = pl.ds(pl.multiple_of(p * piece + i, step), step)
            normed, _ = norm_rows(tok[rows, :].astype(F32))
            h1[rows, :] = (normed * (1.0 + scale) + shift).astype(BF16)

        row_loop(piece, step, one)
    save(h1, h1_o, 1)
    saves_h1 = saves[-1]

    pump_to(4)
    for j in range(3):
        pump_to(3 + j)
        ready(j)

        def cols(n, j=j):
            value = jnp.dot(h1[...], wq[:, lanes(1024 * j + n, 512)], preferred_element_type=F32)
            if j == 0:
                q[:, lanes(n, 512)] = (value * HD ** (-0.5)).astype(BF16)
            else:
                kv[c, :, lanes(1024 * (j - 1) + n, 512)] = value.astype(BF16)

        row_loop(1024, 512, cols)
    save(q, q_o, 2)
    kv_copy = remote(kv.at[c], kv.at[c], kvsend, kvrecv, at_c)
    pump_to(6)
    kv_copy.wait_recv()
    save(kv, kv_o, 3)

    keys = 2 * 4 * piece
    qb_mask = query_mask([ends[t] for t in range(4)], piece)
    acc[:, 0:128] = qb_mask
    kmask[...] = key_mask(keys, piece, per).astype(BF16)

    def heads(h):
        pair = lanes(128 * h, 128)
        k_pair = kv[:, :, pair].reshape(keys, 128)
        v_pair = kv[:, :, lanes(1024 + 128 * h, 128)].reshape(keys, 128)
        q_pair = q[:, pair]
        outs, parts = [], []
        for e in range(2):
            mine = lane_half(e)
            s = dot_nt(choose(mine, q_pair, acc[:, 0:128]), choose(mine, k_pair, kmask[...]))
            peak = jnp.max(s, axis=1, keepdims=True)
            w = jnp.exp(s - peak).astype(BF16)
            o = dot_nn(w, choose(mine, v_pair, jnp.ones_like(v_pair)))
            outs.append(o / pltpu.roll(o, 64, 1))
            parts.append(-(peak + jnp.log(jnp.where(mine, 1.0, o))))
        att[:, pair] = choose(lane_half(0), outs[0], outs[1])
        level = jnp.where(lane_half(1), parts[0], parts[1])
        qb[:, pair] = (acc[:, 0:128] + in_lanes(three_parts(level), 4)).astype(BF16)

    for n in range(4):
        lax.fori_loop(2 * n, 2 * n + 2, lambda h, t: (heads(h), t)[1], 0)
        pump_to(7 + n)
    save(att, att_o, 4)
    save(qb, qb_o, 12)

    ready(3)

    def out_cols(n):
        value = dot_nn(att[...], wo[:, lanes(n, 512)])
        acc[:, lanes(n, 512)] = value
        a[:, lanes(n, 512)] = value.astype(BF16)

    row_loop(1024, 512, out_cols)
    save(a, a_o, 5)
    for p in range(4):
        gate, shift, scale = mod_row(2, p), mod_row(3, p), mod_row(4, p)

        def two(i, p=p, gate=gate, shift=shift, scale=scale):
            rows = pl.ds(pl.multiple_of(p * piece + i, step), step)
            middle = tok[rows, :].astype(F32) + gate * acc[rows, :]
            x1[rows, :] = middle
            normed, _ = norm_rows(middle)
            h2[rows, :] = (normed * (1.0 + scale) + shift).astype(BF16)

        row_loop(piece, step, two)
    save(x1, x1_o, 6)
    save(h2, h2_o, 7)

    for j in range(4):
        pump_to(11 + j)
        ready(4 + j)

        def in_cols(n, j=j):
            col = 1024 * j + n
            pre = jnp.dot(h2[...], wi[:, lanes(col, 512)], preferred_element_type=F32)
            square = pre * pre
            t = jnp.tanh(GELU_A * (pre + GELU_B * (square * pre)))
            lift = 0.5 * (1.0 + t)
            u[:, lanes(col, 512)] = (pre * lift).astype(BF16)
            slope = lift + (0.5 * GELU_A) * pre * (1.0 - t * t) * (1.0 + 3.0 * GELU_B * square)
            gp[:, lanes(col, 512)] = slope.astype(BF16)

        row_loop(1024, 512, in_cols)
    save(u, u_o, 8)
    save(gp, gp_o, 9)
    for n in range(4):
        ready(8 + n)

        def down_cols(col, n=n):
            part = dot_nn(u[:, 1024 * n : 1024 * n + 1024], wd[1024 * n : 1024 * n + 1024, lanes(col, 512)])
            if n == 0:
                acc[:, lanes(col, 512)] = part
            else:
                acc[:, lanes(col, 512)] = acc[:, lanes(col, 512)] + part

        row_loop(1024, 512, down_cols)
    saves_h1.wait()
    for p in range(4):
        gate = mod_row(5, p)

        def three(i, total_grad, p=p, gate=gate):
            rows = pl.ds(pl.multiple_of(p * piece + i * 16, 16), 16)
            value = acc[rows, :]
            h1[rows, :] = (x1[rows, :] + gate * value).astype(BF16)
            return total_grad + fold_rows(cot[rows, :].astype(F32) * value)

        part = lax.fori_loop(0, piece // 16, three, jnp.zeros((8, 1024), F32))
        dg[pl.ds(p, 1), :] = jnp.sum(part, axis=0, keepdims=True)
    dg[pl.ds(4, 4), :] = jnp.zeros((4, 1024), F32)
    save(dg, dg_o, 10)
    save(h1, y_o, 11)
    for copy in saves:
        if copy is not saves_h1:
            copy.wait()
    kv_copy.wait_send()
    for copies in slots.values():
        for copy in copies:
            copy.wait_send()
    for d in range(len(DEALS)):
        for k in range(1, batch):
            pltpu.make_async_copy(whole(d), whole(d), zsend.at[d, k]).wait()


def forward(sel, ends, tok, cot, held, mod, total, batch, piece, per):
    def out(*shape, dtype=BF16):
        return jax.ShapeDtypeStruct(shape, dtype)

    outs = [out(depth, 1024 * blocks) for _, depth, blocks in KINDS] + [
        out(512, 1024),
        out(512, 1024),
        out(512, 1024),
        out(2, 512, 2048),
        out(512, 1024),
        out(512, 1024),
        out(512, 1024, dtype=F32),
        out(512, 1024),
        out(512, 4096),
        out(512, 4096),
        out(512, 1024),
        out(24, 1024, dtype=F32),
        out(8, 1024, dtype=F32),
    ]
    bufs = [pltpu.VMEM(o.shape, o.dtype) for o in outs[:14]] + [
        pltpu.VMEM((512, 1024), F32),
        pltpu.VMEM((24, 1024), F32),
        pltpu.VMEM((batch, 24, 1024), F32),
        pltpu.VMEM((8, 1024), F32),
        pltpu.VMEM((1024, 128), BF16),
    ]
    smem = pl.BlockSpec(memory_space=pltpu.SMEM)
    dma = pltpu.SemaphoreType.DMA
    return pl.pallas_call(
        partial(forward_kernel, total, batch, piece, per),
        out_shape=outs,
        in_specs=[smem, smem] + [pl.BlockSpec(memory_space=pltpu.VMEM)] * 2 + [ANY, ANY],
        out_specs=[ANY] * len(outs),
        scratch_shapes=bufs
        + [
            dma((len(DEALS), batch)),
            dma((len(DEALS), batch)),
            dma((6 * len(UNITS),)),
            dma((6 * len(UNITS),)),
            dma((total,)),
            dma((total,)),
            dma((len(DEALS) + 1,)),
            dma((len(UNITS),)),
            dma((13,)),
            dma,
            dma,
        ],
        compiler_params=pltpu.CompilerParams(
            collective_id=1, has_side_effects=True, vmem_limit_bytes=VMEM_LIMIT
        ),
        name="forward",
    )(sel, ends, tok, cot, held, mod)


LEAVES = (
    [(3, 1024 * n, 0) for n in range(4)] + [(2, 0, j) for j in range(4)] + [(1, 0, 0)] + [(0, 0, j) for j in range(3)]
)
DEALS_AFTER = ((), (5,), (6,), (7, 8), (), (), (), (), (3,), (0,), (1,), (2,))


def backward_kernel(total, batch, piece, per, sel, pm, dg, *refs):
    wq, wo, wi, wd, h1_i, q_i, qb_i, kv_i, att_i, a_i, x1_i, h2_i, gp_i, u_i, y_i, tok_i, cot_i = refs[:17]
    out, dmod_out, grad_o, act_o = refs[17:21]
    big1, big2, big3, wa, wb, f1, f2, s1, s2, s3, s4, kv_got, dmv, dmf, kmask, ring = refs[21:37]
    got, half_sum, strip_sum, zgot = refs[37:41], refs[41:45], refs[45:49], refs[49]
    psend, precv, zsend, zrecv, msend, mrecv, vsend, vrecv, xsend, xrecv, lsem, asem, bsem = refs[50:]
    y, x, c, z, at_x, at_y, at_c = plane()
    f = 4 * y + 2 * x + c
    me = f * batch + z

    def load(src, dst, n):
        return local(src, dst, lsem.at[n])

    cot_l = load(cot_i, s3, 0)
    u_l = [load(u_i.at[:, pl.ds(1024 * n, 1024)], big1.at[:, pl.ds(1024 * n, 1024)], 1 + n) for n in range(4)]
    h2_l = load(h2_i, s2, 5)
    gp_l = load(gp_i, big2, 6)
    x1_l = load(x1_i, f2, 7)
    a_l = load(a_i, s4, 8)
    down_tiles = [wd.at[pl.ds(512 * t, 512)] for t in range(8)] + [wo.at[pl.ds(512 * t, 512)] for t in range(2)]
    in_tiles = [wi.at[:, pl.ds(512 * t, 512)] for t in range(8)] + [wq.at[:, pl.ds(512 * t, 512)] for t in range(6)]
    fetched = {}

    def fetch(tiles, buf, sem, t):
        if t < len(tiles):
            fetched[id(tiles), t] = local(tiles[t], buf.at[t % 2], sem.at[t % 2])

    for t in range(2):
        fetch(down_tiles, wb, bsem, t)
        fetch(in_tiles, wa, asem, t)

    def tile(tiles, buf, t):
        fetched[id(tiles), t].wait()
        return buf[t % 2]

    greet_all(total, batch)
    mine, g = f // per, f % per
    videos = []
    for k in range(1, 4):
        v = (mine + k) % 4
        videos.append(remote(y_i.at[v], act_o.at[mine], vsend.at[k], vrecv.at[k], (v * per + g, z)))
    videos.append(local(y_i.at[mine], act_o.at[mine], lsem.at[9]))

    slots = {}
    counter = [0]

    def push(key, src, dst, device):
        s = counter[0]
        counter[0] += 1
        slots.setdefault(key, []).append(remote(src, dst, psend.at[s], precv.at[s], device))

    def arrive(key):
        for copy in slots[key]:
            copy.wait_recv()

    def emit(n, left, right):
        m, row, j = LEAVES[n]
        for w in range(2):
            ring[n % 2, :, 512 * w : 512 * w + 512] = dot_tn(left, right[:, 512 * w : 512 * w + 512]).astype(BF16)
        push(
            (n, 0),
            ring.at[n % 2, :, lanes(512 * (1 - c), 512)],
            got[m].at[pl.ds(row, 1024), pl.ds(512 * j, 512)],
            at_c,
        )

    def add_block(dst, dst_row, dst_col, src, src_row, src_col, width, count):
        def body(i, carry):
            to = pl.ds(pl.multiple_of(dst_row + i * 128, 128), 128)
            at = pl.ds(pl.multiple_of(src_row + i * 128, 128), 128)
            dst[to, lanes(dst_col, width)] = dst[to, lanes(dst_col, width)] + src[at, lanes(src_col, width)]
            return carry

        lax.fori_loop(0, count // 128, body, 0)

    def step1(n):
        m, row, j = LEAVES[n]
        arrive((n, 0))
        add_block(got[m], row, 512 * j, ring.at[n % 2], 0, 512 * c, 512, 1024)
        for copy in slots[(n, 0)]:
            copy.wait_send()
        for yy in range(2):
            push(
                (n, 1),
                got[m].at[pl.ds(row, 512), lanes(512 * j + 256 * yy + 128 * (1 - x), 128)],
                half_sum[m].at[pl.ds(row, 512), lanes(256 * j + 128 * yy, 128)],
                at_x,
            )
        push(
            (n, 1),
            got[m].at[pl.ds(row + 512, 512), lanes(512 * j + 256 * (1 - y), 256)],
            half_sum[m].at[pl.ds(row + 512, 512), lanes(256 * j, 256)],
            at_y,
        )

    def step2(n):
        m, row, j = LEAVES[n]
        arrive((n, 1))
        for yy in range(2):
            add_block(half_sum[m], row, 256 * j + 128 * yy, got[m], row, 512 * j + 256 * yy + 128 * x, 128, 512)
        add_block(half_sum[m], row + 512, 256 * j, got[m], row + 512, 512 * j + 256 * y, 256, 512)
        push(
            (n, 2),
            half_sum[m].at[pl.ds(row, 512), lanes(256 * j + 128 * (1 - y), 128)],
            strip_sum[m].at[pl.ds(row, 512), lanes(128 * j, 128)],
            at_y,
        )
        push(
            (n, 2),
            half_sum[m].at[pl.ds(row + 512, 512), lanes(256 * j + 128 * (1 - x), 128)],
            strip_sum[m].at[pl.ds(row + 512, 512), lanes(128 * j, 128)],
            at_x,
        )

    def step3(n):
        m, row, j = LEAVES[n]
        arrive((n, 2))
        add_block(strip_sum[m], row, 128 * j, half_sum[m], row, 256 * j + 128 * y, 128, 512)
        add_block(strip_sum[m], row + 512, 128 * j, half_sum[m], row + 512, 256 * j + 128 * x, 128, 512)
        if m == 2:

            @pl.when(z != j)
            def _():
                k = (j - z + batch) % batch
                remote(
                    strip_sum[m].at[:, pl.ds(128 * j, 128)],
                    zgot.at[k - 1, pl.ds(1120, 1024)],
                    zsend.at[4, k],
                    zrecv.at[4, k],
                    (f, j),
                )

        for d in DEALS_AFTER[n]:
            for k in range(1, batch):
                to = (z + k) % batch
                for held_row, count, at, col in deal_pieces(d, to):
                    remote(
                        strip_sum[m].at[pl.ds(pl.multiple_of(at, 16), count), lanes(128 * col, 128)],
                        zgot.at[k - 1, pl.ds(held_row, count)],
                        zsend.at[d, k],
                        zrecv.at[d, k],
                        (f, to),
                    )

    def whole(d, k):
        return zgot.at[k - 1, pl.ds(0, DEAL_ROWS[d])]

    def last(d):
        m = [kind for kind, _, _ in KINDS].index(DEALS[d][0])
        for k in range(1, batch):
            pltpu.make_async_copy(whole(d, k), whole(d, k), zrecv.at[d, k]).wait()
        for row, count, at, j in deal_pieces(d, z):
            step = 128 if count == 1024 else count

            def body(i, carry, row=row, at=at, j=j, step=step):
                rows = pl.ds(pl.multiple_of(row + i * step, 16), step)
                value = strip_sum[m][pl.ds(pl.multiple_of(at + i * step, 16), step), lanes(128 * j, 128)]
                value = value.astype(F32)
                for k in range(batch - 1):
                    value = value + zgot[k, rows, :].astype(F32)
                out[rows, :] = value.astype(BF16)
                return carry

            lax.fori_loop(0, count // step, body, 0)

    def mod_row(j, p):
        return pm[pl.ds(4 * j + p, 1), :]

    def by_rows(p, body, sums):
        def one(i, carry):
            return body(pl.ds(pl.multiple_of(p * piece + i * 16, 16), 16), *carry)

        start = tuple(jnp.zeros((8, 1024), F32) for _ in range(sums))
        return [jnp.sum(s, axis=0, keepdims=True) for s in lax.fori_loop(0, piece // 16, one, start)]

    cot_l.wait()
    for p in range(4):
        gate = mod_row(5, p)

        def d_mlp(rows, gate=gate):
            s1[rows, :] = (gate * s3[rows, :].astype(F32)).astype(BF16)
            return ()

        by_rows(p, d_mlp, 0)
        dmv[pl.ds(20 + p, 1), :] = dg[pl.ds(p, 1), :]
    for n in range(4):
        u_l[n].wait()
        emit(n, big1[:, 1024 * n : 1024 * n + 1024], s1)
        if n >= 1:
            step1(n - 1)
    kv_l = [load(kv_i.at[d], big1.at[:, pl.ds(2048 * d, 2048)], 10 + d) for d in range(2)]
    gp_l.wait()
    for t in range(8):
        cols = slice(512 * t, 512 * t + 512)
        d_act = dot_nt(s1[...], tile(down_tiles, wb, t))
        big3[:, cols] = (d_act * big2[:, cols].astype(F32)).astype(BF16)
        fetch(down_tiles, wb, bsem, t + 2)
        if t == 0:
            step1(3)
        if t == 5:
            step2(0)
    h2_l.wait()
    for j in range(4):
        emit(4 + j, s2[...], big3.at[:, 1024 * j : 1024 * j + 1024])
        if j >= 1:
            step1(3 + j)
        if j == 1:
            step2(1)
    att_l = load(att_i, s2, 5)
    for t in range(8):
        part = dot_nt(big3[:, 512 * t : 512 * t + 512], tile(in_tiles, wa, t))
        f1[...] = part if t == 0 else f1[...] + part
        fetch(in_tiles, wa, asem, t + 2)
        if t == 0:
            step1(7)
        if t == 4:
            step2(2)
    qb_l = load(qb_i, big3.at[:, pl.ds(3072, 1024)], 6)
    step2(3)

    x1_l.wait()
    a_l.wait()
    for p in range(4):
        gate, scale = mod_row(2, p), mod_row(4, p)

        def back_two(rows, d_scale, d_shift, d_gate, gate=gate, scale=scale):
            normed, inv_std = norm_rows(f2[rows, :])
            d_h = f1[rows, :]
            d_mid = s3[rows, :].astype(F32) + norm_back(d_h * (1.0 + scale), normed, inv_std)
            f2[rows, :] = d_mid
            s1[rows, :] = (gate * d_mid).astype(BF16)
            return (
                d_scale + fold_rows(d_h * normed),
                d_shift + fold_rows(d_h),
                d_gate + fold_rows(d_mid * s4[rows, :].astype(F32)),
            )

        d_scale, d_shift, d_gate = by_rows(p, back_two, 3)
        dmv[pl.ds(16 + p, 1), :] = d_scale
        dmv[pl.ds(12 + p, 1), :] = d_shift
        dmv[pl.ds(8 + p, 1), :] = d_gate
    q_l = load(q_i, s4, 8)
    step3(0)

    att_l.wait()
    emit(8, s2[...], s1)
    for t in range(2):
        s3[:, 512 * t : 512 * t + 512] = dot_nt(s1[...], tile(down_tiles, wb, 8 + t)).astype(BF16)
    h1_l = load(h1_i, wb.at[0], 7)
    tok_l = load(tok_i, wb.at[1], 12)
    step1(8)
    step3(1)

    keys = 2 * 4 * piece
    kmask[...] = key_mask(keys, piece, per).astype(BF16)
    for copy in kv_l:
        copy.wait()
    qb_l.wait()
    q_l.wait()

    def heads(h):
        pair = lanes(128 * h, 128)
        k_pair = jnp.concatenate([big1[:, lanes(2048 * d + 128 * h, 128)] for d in range(2)], axis=0)
        v_pair = jnp.concatenate([big1[:, lanes(2048 * d + 1024 + 128 * h, 128)] for d in range(2)], axis=0)
        dks, dvs, dqs = [], [], []
        first = lane_half(0)
        ones = in_lanes([1.0, 1.0, 1.0], 0)
        for e in range(2):
            mask = lane_half(e)
            k_e = choose(mask, k_pair, kmask[...])
            v_e = choose(mask, v_pair, ones)
            dk = dv = 0.0
            dq = []
            for w in range(2):
                rows = slice(256 * w, 256 * w + 256)
                q_w, d_w, o_w = s4[rows, pair], s3[rows, pair], s2[rows, pair]
                q_e = choose(mask, q_w, big3[rows, lanes(3072 + 128 * h, 128)])
                dot_rows = jnp.sum(
                    jnp.where(mask, d_w.astype(F32) * o_w.astype(F32), 0.0), axis=1, keepdims=True
                )
                d_e = choose(mask, d_w, in_lanes(three_parts(-dot_rows), 0))
                prob = jnp.exp(dot_nt(k_e, q_e))
                d_s = (prob * dot_nt(v_e, d_e)).astype(BF16)
                dv = dv + dot_nn(prob.astype(BF16), d_w)
                dk = dk + dot_nn(d_s, q_w)
                dq.append(dot_tn(d_s, k_pair))
            dks.append(dk)
            dvs.append(dv)
            dqs.append(jnp.concatenate(dq, axis=0))
        dk = choose(first, dks[0], dks[1])
        dv = choose(first, dvs[0], dvs[1])
        big3[:, pair] = (choose(first, dqs[0], dqs[1]).astype(F32) * HD ** (-0.5)).astype(BF16)
        for d in range(2):
            big2[:, lanes(2048 * d + 128 * h, 128)] = dk[512 * d : 512 * d + 512]
            big2[:, lanes(2048 * d + 1024 + 128 * h, 128)] = dv[512 * d : 512 * d + 512]

    exchanges = []
    plan = (
        (lambda: step2(4),),
        (lambda: step2(5), lambda: step3(2)),
        (lambda: step2(6), lambda: step3(3)),
        (lambda: step2(7), lambda: step3(4)),
        (lambda: step2(8), lambda: step3(5)),
        (lambda: step3(6),),
        (lambda: step3(7),),
        (),
    )
    for h in range(8):
        if h % 4 == 0:
            pass
        lax.fori_loop(h, h + 1, lambda n, t: (heads(n), t)[1], 0)
        if h % 4 == 3:
            for part in range(2):
                at = 1024 * part + 512 * (h // 4)
                s = len(exchanges)
                exchanges.append(
                    remote(
                        big2.at[:, lanes(2048 * (1 - c) + at, 512)],
                        kv_got.at[:, pl.ds(at, 512)],
                        xsend.at[s],
                        xrecv.at[s],
                        at_c,
                    )
                )
        for act in plan[h]:
            act()

    h1_l.wait()
    emit(9, wb[0], big3.at[:, 0:1024])
    for copy in exchanges:
        copy.wait_recv()
    for part in range(2):

        def join(i, carry, part=part):
            rows = pl.ds(pl.multiple_of(i * 64, 64), 64)
            value = big2[rows, lanes(2048 * c + 1024 * part, 1024)].astype(F32) + kv_got[
                rows, 1024 * part : 1024 * part + 1024
            ].astype(F32)
            big3[rows, 1024 + 1024 * part : 2048 + 1024 * part] = value.astype(BF16)
            return carry

        lax.fori_loop(0, 8, join, 0)
        emit(10 + part, wb[0], big3.at[:, 1024 + 1024 * part : 2048 + 1024 * part])
        step1(9 + part)
    step3(8)
    for t in range(6):
        part = dot_nt(big3[:, 512 * t : 512 * t + 512], tile(in_tiles, wa, 8 + t))
        f1[...] = part if t == 0 else f1[...] + part
        fetch(in_tiles, wa, asem, 8 + t + 2)
        if t == 0:
            step1(11)
        if t == 3:
            step2(9)

    tok_l.wait()
    for p in range(4):
        scale = mod_row(1, p)

        def back_one(rows, d_scale, d_shift, scale=scale):
            normed, inv_std = norm_rows(wb[1, rows, :].astype(F32))
            d_h = f1[rows, :]
            s1[rows, :] = (f2[rows, :] + norm_back(d_h * (1.0 + scale), normed, inv_std)).astype(BF16)
            return d_scale + fold_rows(d_h * normed), d_shift + fold_rows(d_h)

        d_scale, d_shift = by_rows(p, back_one, 2)
        dmv[pl.ds(4 + p, 1), :] = d_scale
        dmv[pl.ds(p, 1), :] = d_shift
    grad_l = load(s1, grad_o, 0)
    for j in range(6):
        for fr in range(4):
            value = sel[0, fr] * dmv[pl.ds(4 * j, 1), :]
            for p in range(1, 4):
                value = value + sel[p, fr] * dmv[pl.ds(4 * j + p, 1), :]
            dmf[pl.ds(4 * j + fr, 1), :] = value

    def mod_group(k, start):
        other = (me + k) % total
        of, oz = other // batch, other % batch
        copy = pltpu.make_async_remote_copy(
            src_ref=dmf.at[:, lanes(128 * strip_of(of), 128)],
            dst_ref=dmod_out.at[me],
            send_sem=msend.at[k],
            recv_sem=mrecv.at[k],
            device_id=(of, oz),
            device_id_type=MESH,
        )
        if start:
            copy.start()
        else:
            copy.wait()

    lax.fori_loop(1, total, lambda k, u: (mod_group(k, True), u)[1], 0)
    mod_own = load(dmf.at[:, lanes(128 * strip_of(f), 128)], dmod_out.at[me], 1)

    out[pl.ds(0, 96), :] = jnp.zeros((96, 128), BF16)
    step2(10)
    step3(9)
    for d in (5, 6, 7, 8):
        last(d)
    step2(11)
    step3(10)
    last(4)
    last(3)
    step3(11)
    for d in (0, 1, 2):
        last(d)
    for n, copies in slots.items():
        if n[1] > 0:
            for copy in copies:
                copy.wait_send()
    for d in range(len(DEALS)):
        for k in range(1, batch):
            pltpu.make_async_copy(whole(d, k), whole(d, k), zsend.at[d, k]).wait()
    for copy in exchanges:
        copy.wait_send()
    for copy in videos:
        copy.wait()
    grad_l.wait()
    mod_own.wait()
    lax.fori_loop(1, total, lambda k, u: (mod_group(k, False), u)[1], 0)


def backward(sel, pm, dg, arrays, total, batch, piece, per):
    def sums(width):
        return [pltpu.VMEM((depth, blocks * width), BF16) for _, depth, blocks in KINDS]

    def buf(*shape, dtype=BF16):
        return pltpu.VMEM(shape, dtype)

    whole = pl.BlockSpec(memory_space=pltpu.VMEM)
    dma = pltpu.SemaphoreType.DMA
    return pl.pallas_call(
        partial(backward_kernel, total, batch, piece, per),
        out_shape=[
            jax.ShapeDtypeStruct((HELD, 128), BF16),
            jax.ShapeDtypeStruct((total, 24, 128), F32),
            jax.ShapeDtypeStruct((512, 1024), BF16),
            jax.ShapeDtypeStruct((4, piece, 1024), BF16),
        ],
        in_specs=[pl.BlockSpec(memory_space=pltpu.SMEM), whole, whole] + [ANY] * len(arrays),
        out_specs=[whole, ANY, ANY, ANY],
        scratch_shapes=[buf(512, 4096) for _ in range(3)]
        + [buf(2, 1024, 512), buf(2, 512, 1024)]
        + [buf(512, 1024, dtype=F32) for _ in range(2)]
        + [buf(512, 1024) for _ in range(4)]
        + [buf(512, 2048), buf(24, 1024, dtype=F32), buf(24, 1024, dtype=F32), buf(1024, 128), buf(2, 1024, 1024)]
        + sums(512)
        + sums(256)
        + sums(128)
        + [buf(batch - 1, HELD, 128)]
        + [
            dma((72,)),
            dma((72,)),
            dma((len(DEALS), batch)),
            dma((len(DEALS), batch)),
            dma((total,)),
            dma((total,)),
            dma((4,)),
            dma((4,)),
            dma((4,)),
            dma((4,)),
            dma((13,)),
            dma((2,)),
            dma((2,)),
        ],
        compiler_params=pltpu.CompilerParams(
            collective_id=2, has_side_effects=True, vmem_limit_bytes=VMEM_LIMIT
        ),
        name="backward",
    )(sel, pm, dg, *arrays)


def pick_kernel(index, src, dst):
    def body(i, carry):
        dst[i] = src[index[i]]
        return carry

    lax.fori_loop(0, dst.shape[0], body, 0)


def pick_blocks(index, src):
    whole = pl.BlockSpec(memory_space=pltpu.VMEM)
    return pl.pallas_call(
        pick_kernel,
        out_shape=jax.ShapeDtypeStruct((index.shape[0],) + src.shape[1:], src.dtype),
        in_specs=[pl.BlockSpec(memory_space=pltpu.SMEM), whole],
        out_specs=whole,
        name="pick_blocks",
    )(index, src)


def cut_kernel(rows, master, out):
    swap = (rows[...] == lax.broadcasted_iota(jnp.int32, (ROWS, ROWS), 1)).astype(BF16)
    for s in range(8):
        strip = master[pl.ds(s, ROWS, stride=8), :].astype(BF16)
        out[:, 128 * s : 128 * s + 128] = jnp.dot(swap, strip, preferred_element_type=F32).astype(BF16)


def cut_owned(rows, master):
    whole = pl.BlockSpec(memory_space=pltpu.VMEM)
    return pl.pallas_call(
        cut_kernel,
        out_shape=jax.ShapeDtypeStruct((ROWS, 1024), BF16),
        in_specs=[whole, whole],
        out_specs=whole,
        compiler_params=pltpu.CompilerParams(vmem_limit_bytes=VMEM_LIMIT),
        name="cut_owned",
    )(rows, master)


def adam(grad, master, first, second):
    new_first = BETA_ONE * first + (1.0 - BETA_ONE) * grad
    new_second = BETA_TWO * second + (1.0 - BETA_TWO) * grad * grad
    fix_one = 1.0 - BETA_ONE**STEP
    fix_two = 1.0 - BETA_TWO**STEP
    update = new_first / fix_one / (jnp.sqrt(new_second / fix_two) + ADAM_EPS)
    return master - LEARN_RATE * (update + WEIGHT_DECAY * master), new_first, new_second


def update_kernel(rows, grad, master, first, second, new_master, new_first, new_second):
    base = pl.program_id(0) * GROUP
    swap = (rows[...] == base + lax.broadcasted_iota(jnp.int32, (GROUP, ROWS), 0)).astype(BF16)
    for s in range(8):
        at = pl.ds(s, GROUP, stride=8)
        value = jnp.dot(swap, grad[:, 128 * s : 128 * s + 128], preferred_element_type=F32)
        new_master[at, :], new_first[at, :], new_second[at, :] = adam(
            value, master[at, :], first[at, :], second[at, :]
        )


def update_owned(rows, grad, master, first, second):
    part = pl.BlockSpec((8 * GROUP, 128), lambda i: (i, 0))
    return pl.pallas_call(
        update_kernel,
        grid=(ROWS // GROUP,),
        out_shape=[jax.ShapeDtypeStruct(master.shape, F32)] * 3,
        in_specs=[
            pl.BlockSpec((1, ROWS), lambda i: (0, 0)),
            pl.BlockSpec((ROWS, 1024), lambda i: (0, 0)),
            part,
            part,
            part,
        ],
        out_specs=[part] * 3,
        compiler_params=pltpu.CompilerParams(vmem_limit_bytes=VMEM_LIMIT),
        name="update_owned",
    )(rows, grad, master, first, second)


def key_positions(rows, piece, per):
    i = lax.broadcasted_iota(jnp.int32, (rows, 1), 0)
    local_rows = rows // per
    return ((i % local_rows) // piece * per + i // local_rows) * piece + i % piece


def scores_t(k, q, ends, piece, per):
    s = lax.dot_general(k, q, (((1,), (1,)), ((), ())), preferred_element_type=F32)
    pos = key_positions(k.shape[0], piece, per)
    cols = []
    for t in range(q.shape[0] // piece):
        part = s[:, t * piece : (t + 1) * piece]
        cols.append(jnp.where(pos < ends[t], part, NEG_FILL))
    return jnp.concatenate(cols, axis=1)


def attend_kernel(piece, per, ends, q, k, v, o):
    outs = []
    for a in range(2):
        cut = slice(64 * a, 64 * a + 64)
        s = scores_t(k[:, cut], q[:, cut], ends, piece, per)
        peak = jnp.max(s, axis=0, keepdims=True)
        e = jnp.exp(s - peak)
        p = (e * (1.0 / jnp.sum(e, axis=0, keepdims=True))).astype(BF16)
        outs.append(lax.dot_general(p, v[:, cut], (((0,), (0,)), ((), ())), preferred_element_type=F32))
    o[...] = jnp.concatenate(outs, axis=1).astype(BF16)


def attend(ends, q, kv, piece, per):
    rows, width = q.shape
    keys = kv.shape[0]
    pairs = width // 128
    return pl.pallas_call(
        partial(attend_kernel, piece, per),
        grid_spec=pltpu.PrefetchScalarGridSpec(
            num_scalar_prefetch=1,
            grid=(pairs,),
            in_specs=[
                pl.BlockSpec((rows, 128), lambda h, e: (0, h)),
                pl.BlockSpec((keys, 128), lambda h, e: (0, h)),
                pl.BlockSpec((keys, 128), lambda h, e: (0, h + pairs)),
            ],
            out_specs=pl.BlockSpec((rows, 128), lambda h, e: (0, h)),
        ),
        out_shape=jax.ShapeDtypeStruct((rows, width), BF16),
        compiler_params=pltpu.CompilerParams(vmem_limit_bytes=VMEM_LIMIT),
        cost_estimate=pl.CostEstimate(
            flops=4 * rows * keys * width, bytes_accessed=4 * (rows + keys) * width, transcendentals=rows * keys * H
        ),
        name="attend",
    )(ends, q, kv, kv)


def attend_back_kernel(piece, per, ends, q, k, v, do, dq, dk, dv):
    dqs, dks, dvs = [], [], []
    for a in range(2):
        cut = slice(64 * a, 64 * a + 64)
        qa, ka, va, da = q[:, cut], k[:, cut], v[:, cut], do[:, cut]
        s = scores_t(ka, qa, ends, piece, per)
        peak = jnp.max(s, axis=0, keepdims=True)
        e = jnp.exp(s - peak)
        p = e * (1.0 / jnp.sum(e, axis=0, keepdims=True))
        dvs.append(jnp.dot(p.astype(BF16), da, preferred_element_type=F32))
        dp = lax.dot_general(va, da, (((1,), (1,)), ((), ())), preferred_element_type=F32)
        pdp = p * dp
        row = jnp.sum(pdp, axis=0, keepdims=True)
        ds = (pdp - p * row).astype(BF16)
        dks.append(jnp.dot(ds, qa, preferred_element_type=F32))
        dqs.append(lax.dot_general(ds, ka, (((0,), (0,)), ((), ())), preferred_element_type=F32))
    dq[...] = jnp.concatenate(dqs, axis=1).astype(BF16)
    dk[...] = jnp.concatenate(dks, axis=1).astype(BF16)
    dv[...] = jnp.concatenate(dvs, axis=1).astype(BF16)


def attend_back(ends, q, kv, do, piece, per):
    rows, width = q.shape
    keys = kv.shape[0]
    pairs = width // 128
    mine = pl.BlockSpec((rows, 128), lambda h, e: (0, h))
    allk = pl.BlockSpec((keys, 128), lambda h, e: (0, h))
    return pl.pallas_call(
        partial(attend_back_kernel, piece, per),
        grid_spec=pltpu.PrefetchScalarGridSpec(
            num_scalar_prefetch=1,
            grid=(pairs,),
            in_specs=[mine, allk, pl.BlockSpec((keys, 128), lambda h, e: (0, h + pairs)), mine],
            out_specs=[mine, allk, allk],
        ),
        out_shape=[
            jax.ShapeDtypeStruct((rows, width), BF16),
            jax.ShapeDtypeStruct((keys, width), BF16),
            jax.ShapeDtypeStruct((keys, width), BF16),
        ],
        compiler_params=pltpu.CompilerParams(vmem_limit_bytes=VMEM_LIMIT),
        cost_estimate=pl.CostEstimate(
            flops=10 * rows * keys * width, bytes_accessed=6 * (rows + keys) * width, transcendentals=rows * keys * H
        ),
        name="attend_back",
    )(ends, q, kv, kv, do)


def layer_stats(values):
    centre = values - jnp.mean(values, axis=-1, keepdims=True)
    inv_std = lax.rsqrt(jnp.mean(centre * centre, axis=-1, keepdims=True) + 1e-06)
    return (centre * inv_std, inv_std)


def norm_back(upstream, normed, inv_std):
    mean_grad = jnp.mean(upstream, axis=-1, keepdims=True)
    mean_cross = jnp.mean(upstream * normed, axis=-1, keepdims=True)
    return inv_std * (upstream - mean_grad - normed * mean_cross)


def noise_embedding(levels, feature_width):
    half_width = feature_width // 2
    frequencies = jnp.exp(
        -math.log(10000.0) * jnp.arange(half_width, dtype=jnp.float32) / half_width
    )
    angles = levels.astype(jnp.float32)[:, None] * frequencies[None, :]
    return jnp.concatenate([jnp.cos(angles), jnp.sin(angles)], axis=1)


def silu_embedding(levels, width):
    return jax.nn.silu(noise_embedding(levels, width)).astype(BF16)


def split_flat(flat_values, model_width, hidden_width):
    matrix_shapes = (
        (model_width, 6 * model_width),
        (model_width, 3 * model_width),
        (model_width, model_width),
        (model_width, hidden_width),
        (hidden_width, model_width),
    )
    matrices = []
    offset_now = 0
    for matrix_shape in matrix_shapes:
        entry_count = matrix_shape[0] * matrix_shape[1]
        matrices.append(flat_values[offset_now : offset_now + entry_count].reshape(matrix_shape))
        offset_now = offset_now + entry_count
    return matrices


def shards(
    frame_size,
    batch_size,
    tokens,
    out_cotangent,
    buckets,
    noise_levels,
    owned_block,
    master,
    first_moment,
    second_moment,
):
    micro_count, piece, width = tokens.shape
    block_size = master.shape[1]
    frame_count = noise_levels.shape[1]
    total = frame_size * batch_size
    videos = micro_count
    per = frame_size // videos
    rows = videos * piece
    keys = rows * per
    q_scale = HD ** (-0.5)
    f, z = frame_index()
    me = f * batch_size + z
    mine, g = f // per, f % per
    direct = frame_size == 8 and batch_size == 4 and block_size == ROWS * 1024 and videos == 4 and frame_count == 4

    if direct:
        inverse = jnp.argsort(owned_block).astype(jnp.int32)
        table = jnp.asarray(np.stack([block_rows(b) for b in range(total)]).astype(np.int32))
        own_rows = lax.dynamic_index_in_dim(table, owned_block[me], 0, keepdims=False)
        cut_block = cut_owned(own_rows[:, None], master.reshape(-1, 128))
        levels = jnp.zeros((8, 128), jnp.int32).at[:4, :4].set(noise_levels)
        cut, all_levels, tok, cot = scatter_blocks(cut_block, levels, tokens, out_cotangent, total, batch_size)
        ordered = pick_blocks(inverse, cut)
        held = ordered[FIRST:].reshape(HELD, 128)
        cond = silu_embedding(all_levels[:, :4, :4].reshape(64), width)
        ada_row, ada_col = ada_rows(z)
        spread = (ada_row[None, :] == jnp.arange(width, dtype=jnp.int32)[:, None]).astype(BF16)
        cond_rows = jnp.dot(cond, spread, preferred_element_type=F32).astype(BF16)
        six = (ada_col[None, :] == jnp.arange(6, dtype=jnp.int32)[:, None]).astype(BF16)
        cond_all = (cond_rows.reshape(16, 1, 4, -1) * six[None, :, None, :]).reshape(384, -1)
        mod_part = jnp.dot(
            cond_all, ordered[: FIRST + 1].reshape(-1, 128), preferred_element_type=F32
        ).reshape(16, 24, 128)
    else:
        tok, cot = swap_videos([tokens, out_cotangent], videos, per, 0)
        gathered = lax.all_gather(master.astype(BF16), ("frame", "batch"), axis=0, tiled=True)
        placed = jnp.take(gathered, jnp.argsort(owned_block), axis=0).reshape(-1)
        w_ada, w_qkv, w_out, w_in, w_down = split_flat(placed, width, FF)
        cond = silu_embedding(lax.dynamic_index_in_dim(noise_levels, mine, 0, keepdims=False), width)
        modulation = jnp.dot(cond, w_ada, preferred_element_type=F32).reshape(frame_count, 6, width)

    frame_len = FRAME_LO * (1 + 3 * buckets[mine])
    piece_at = (jnp.arange(videos, dtype=jnp.int32) * per + g) * piece
    piece_frame = piece_at // frame_len
    ends = (piece_frame + 1) * frame_len
    selector = (piece_frame[:, None] == jnp.arange(frame_count, dtype=jnp.int32)[None, :]).astype(F32)

    def flat(a):
        return a.reshape(rows, a.shape[-1])

    def cube(a):
        return a.reshape(videos, piece, a.shape[-1])

    def partners(k):
        return [(i, i // per * per + (i + k) % per) for i in range(frame_size)]

    def split_mod(piece_mod):
        return [piece_mod[j][:, None, :] for j in range(6)]

    if direct:
        saved = forward(
            selector, ends, tok.reshape(rows, width), cot.reshape(rows, width), held, mod_part, total, batch_size, piece, per
        )
        *saved, block_output, piece_mod, d_gate = saved
        held_grad, dmod_parts, input_grad, outputs = backward(
            selector,
            piece_mod,
            d_gate,
            [*saved, cube(block_output), tok.reshape(rows, width), cot.reshape(rows, width)],
            total,
            batch_size,
            piece,
            per,
        )
        input_grad = cube(input_grad)
    else:
        x_float = tok.astype(F32)
        normed_one, inv_one = layer_stats(x_float)
        piece_mod = jnp.einsum("pf,fjd->jpd", selector, modulation, precision=HIGHEST)
        shift_one, scale_one, gate_one, shift_two, scale_two, gate_two = split_mod(piece_mod)

        h_one = flat((normed_one * (1.0 + scale_one) + shift_one).astype(BF16))
        projected = jnp.dot(h_one, w_qkv, preferred_element_type=F32)
        queries = (projected[:, :width] * q_scale).astype(BF16)
        kv_own = projected[:, width:].astype(BF16)

        kv_all = jnp.zeros((per, rows, 2 * width), BF16)
        kv_all = lax.dynamic_update_index_in_dim(kv_all, kv_own, g, 0)
        for k in range(1, per):
            kv_all = lax.dynamic_update_index_in_dim(
                kv_all, lax.ppermute(kv_own, "frame", partners(k)), (g + per - k) % per, 0
            )
        kv_all = kv_all.reshape(keys, 2 * width)
        attended = attend(ends, queries, kv_all, piece, per)
        attn_out = jnp.dot(attended, w_out, preferred_element_type=F32)
        middle = x_float + gate_one * cube(attn_out)
        normed_two, inv_two = layer_stats(middle)
        h_two = flat((normed_two * (1.0 + scale_two) + shift_two).astype(BF16))
        pre_act = jnp.dot(h_two, w_in, preferred_element_type=F32)
        activated, gelu_back = jax.vjp(partial(jax.nn.gelu, approximate=True), pre_act)
        act_low = activated.astype(BF16)
        slope = gelu_back(jnp.ones_like(pre_act))[0]
        mlp_out = jnp.dot(act_low, w_down, preferred_element_type=F32)
        block_output = (middle + gate_two * cube(mlp_out)).astype(BF16)

        grad_out = cot.astype(F32)
        d_mlp = flat((gate_two * grad_out).astype(BF16))
        g_down = jnp.dot(act_low.T, d_mlp, preferred_element_type=F32).astype(BF16)
        d_act = jnp.dot(d_mlp, w_down.T, preferred_element_type=F32)
        d_pre = (d_act * slope.astype(F32)).astype(BF16)
        g_in = jnp.dot(h_two.T, d_pre, preferred_element_type=F32).astype(BF16)
        d_htwo = cube(jnp.dot(d_pre, w_in.T, preferred_element_type=F32))
        d_gate_two = jnp.sum(grad_out * cube(mlp_out), axis=1)
        d_scale_two = jnp.sum(d_htwo * normed_two, axis=1)
        d_shift_two = jnp.sum(d_htwo, axis=1)
        d_middle = grad_out + norm_back(d_htwo * (1.0 + scale_two), normed_two, inv_two)
        d_attn = flat((gate_one * d_middle).astype(BF16))
        d_gate_one = jnp.sum(d_middle * cube(attn_out), axis=1)
        g_out = jnp.dot(attended.T, d_attn, preferred_element_type=F32).astype(BF16)
        d_attended = jnp.dot(d_attn, w_out.T, preferred_element_type=F32).astype(BF16)
        dq, dk, dv = attend_back(ends, queries, kv_all, d_attended, piece, per)
        dkv = jnp.concatenate([dk, dv], axis=1).reshape(per, rows, 2 * width)
        dkv_own = lax.dynamic_index_in_dim(dkv, g, 0, keepdims=False).astype(F32)
        for k in range(1, per):
            sent = lax.dynamic_index_in_dim(dkv, (g + k) % per, 0, keepdims=False)
            dkv_own = dkv_own + lax.ppermute(sent, "frame", partners(k)).astype(F32)
        d_proj = jnp.concatenate([dq * jnp.asarray(q_scale, BF16), dkv_own.astype(BF16)], axis=1)
        g_qkv = jnp.dot(h_one.T, d_proj, preferred_element_type=F32).astype(BF16)
        d_hone = cube(jnp.dot(d_proj, w_qkv.T, preferred_element_type=F32))
        d_scale_one = jnp.sum(d_hone * normed_one, axis=1)
        d_shift_one = jnp.sum(d_hone, axis=1)
        d_input = d_middle + norm_back(d_hone * (1.0 + scale_one), normed_one, inv_one)
        input_grad = d_input.astype(BF16)
        piece_dmod = jnp.stack([d_shift_one, d_scale_one, d_gate_one, d_shift_two, d_scale_two, d_gate_two])
        frame_dmod = jnp.einsum("pf,jpd->jfd", selector, piece_dmod, precision=HIGHEST)

    if direct:
        dmod_all = jnp.sum(dmod_parts.reshape(4, 2, 4, 24, 128), axis=1).transpose(1, 0, 2, 3).reshape(384, 128)
        ada_grad = lax.dot_general(
            cond_all.astype(F32), dmod_all, (((0,), (0,)), ((), ())), precision=HIGHEST
        ).astype(BF16)
        edge = jnp.concatenate([ada_grad[FIRST * GROUP : FIRST * GROUP + 96], held_grad[96:GROUP]], axis=0)
        ordered_grad = jnp.concatenate([ada_grad[: FIRST * GROUP], edge, held_grad[GROUP:]], axis=0)
        cut_grad = pick_blocks(owned_block, ordered_grad.reshape(total, GROUP, 128))
        grad_block, input_grads = collect_blocks(cut_grad, input_grad, total, batch_size)
        updated = update_owned(
            own_rows[None, :],
            grad_block,
            master.reshape(-1, 128),
            first_moment.reshape(-1, 128),
            second_moment.reshape(-1, 128),
        )
        new_master, new_first, new_second = [a.reshape(1, block_size) for a in updated]
    else:
        outputs, input_grads = swap_videos([block_output, input_grad], videos, per, 1)
        g_ada = lax.dot_general(
            cond.astype(F32),
            frame_dmod.transpose(1, 0, 2).reshape(frame_count, 6 * width),
            (((0,), (0,)), ((), ())),
            precision=HIGHEST,
        )
        flat_grads = jnp.concatenate(
            [piece_grad.astype(F32).reshape(-1) for piece_grad in (g_ada, g_qkv, g_out, g_in, g_down)]
        )
        arranged = jnp.take(flat_grads.reshape(-1, block_size), owned_block, axis=0).reshape(-1)
        shard_total = lax.psum_scatter(
            arranged, ("frame", "batch"), scatter_dimension=0, tiled=True
        ).reshape(1, block_size)
        new_master, new_first, new_second = adam(shard_total, master, first_moment, second_moment)
    return (outputs, input_grads, new_master, new_first, new_second)


def solution(mesh):
    placed = (
        P("batch", "frame", None),
        P("batch", "frame", None),
        P("batch"),
        P("batch", None),
        P(),
        P(("frame", "batch"), None),
        P(("frame", "batch"), None),
        P(("frame", "batch"), None),
    )
    return jax.shard_map(
        partial(shards, mesh.shape["frame"], mesh.shape["batch"]),
        mesh=mesh,
        in_specs=placed,
        out_specs=(
            P("batch", "frame", None),
            P("batch", "frame", None),
            P(("frame", "batch"), None),
            P(("frame", "batch"), None),
            P(("frame", "batch"), None),
        ),
        check_vma=False,
    )
```

```python
from functools import partial
import math

import jax
import jax.numpy as jnp
import numpy as np
from jax import lax
from jax.experimental import pallas as pl
from jax.experimental.pallas import tpu as pltpu
from jax.sharding import PartitionSpec as P

H = 16
HD = 64
FF = 4096
FRAME_LO = 256
STEP = 10

HIGHEST = lax.Precision.HIGHEST
NEG_FILL = -1e30
BETA_ONE = 0.5
BETA_TWO = 0.5
LEARN_RATE = 0.05
WEIGHT_DECAY = 0.1
ADAM_EPS = 1e-08
MESH = pl.DeviceIdType.MESH
F32 = jnp.float32
BF16 = jnp.bfloat16
ANY = pl.BlockSpec(memory_space=pl.ANY)
VMEM_LIMIT = 63 * 1024 * 1024

ROWS = 576
GROUP = 144
FIRST = 10
KINDS = (("qkv", 1024, 3), ("out", 1024, 1), ("in", 1024, 4), ("down", 4096, 1))
HELD = 3168
THIRD = 48
ADA = 1664


def pieces(kind, z):
    if kind == "qkv":
        found = [(48 * j, 16, 16 * z, j) for j in range(3)]
        for k in range(5):
            found += [(144 + 144 * k + 48 * j, 48, 64 + 192 * k + 48 * z, j) for j in range(3)]
        return found
    if kind == "out":
        return [(864, 144, 144 * z, 0), (1008, 112, 576 + 112 * z, 0)]
    if kind == "in":
        return [(1120, 1024, 0, z)]
    found = [(2144, 16, 16 * z, 0)]
    return found + [(2160 + 144 * k, 144, 64 + 576 * k + 144 * z, 0) for k in range(7)]


def block_rows(block):
    t = np.arange(GROUP)
    groups = []
    for z in range(4):
        if block == 10:
            i, j = t % THIRD, t // THIRD
            rows = np.where(i < 16, 384 + 3 * (16 * z + i) + j, 96 * z + 32 * j + i - 16)
        elif 11 <= block <= 15:
            rows = 3 * (48 * z + t % 48) + t // 48
        elif block == 17:
            rows = np.where(t < 112, 112 * z + t, 448 + 4 * (t - 112) + z)
        elif 18 <= block <= 23:
            rows = 4 * t + z
        elif block == 24:
            rows = np.where(t < 128, 4 * t + z, 512 + 16 * z + t - 128)
        else:
            rows = GROUP * z + t
        groups.append(rows)
    return np.concatenate(groups)


def ada_place(n, z):
    b, t = n // GROUP, n % GROUP
    i = t % THIRD - 16
    a = 32 * (t // THIRD) + i
    row = jnp.where(b < 10, 96 * b + 24 * z + t // 6, 960 + 16 * z + a // 6)
    col = jnp.where(b < 10, t % 6, a % 6)
    none = (b > 10) | ((b == 10) & (i < 0))
    return jnp.where(none, -1, row), col


def frame_index():
    return lax.axis_index("frame"), lax.axis_index("batch")


def strip_of(f):
    return 4 * (f % 2) + f // 2


def greet(devices):
    barrier = pltpu.get_barrier_semaphore()
    for device in devices:
        pl.semaphore_signal(barrier, inc=1, device_id=device, device_id_type=MESH)
    pl.semaphore_wait(barrier, len(devices))


def greet_all(total, batch):
    f, z = frame_index()
    me = f * batch + z
    barrier = pltpu.get_barrier_semaphore()

    def hail(k, carry):
        other = (me + k) % total
        pl.semaphore_signal(barrier, inc=1, device_id=(other // batch, other % batch), device_id_type=MESH)
        return carry

    lax.fori_loop(1, total, hail, 0)
    pl.semaphore_wait(barrier, total - 1)


def remote(src, dst, send, recv, device):
    copy = pltpu.make_async_remote_copy(
        src_ref=src, dst_ref=dst, send_sem=send, recv_sem=recv, device_id=device, device_id_type=MESH
    )
    copy.start()
    return copy


def local(src, dst, sem):
    copy = pltpu.make_async_copy(src, dst, sem)
    copy.start()
    return copy


def video_kernel(videos, per, arrays, *refs):
    ins, outs = refs[:arrays], refs[arrays : 2 * arrays]
    send, recv, own = refs[2 * arrays :]
    f, z = frame_index()
    mine, g = f // per, f % per
    others = [((mine + k) % videos, k) for k in range(1, videos)]
    greet([(v * per + g, z) for v, k in others])
    copies = []
    for a in range(arrays):
        for v, k in others:
            copies.append(
                remote(ins[a].at[v], outs[a].at[mine], send.at[a, k], recv.at[a, k], (v * per + g, z))
            )
        copies.append(local(ins[a].at[mine], outs[a].at[mine], own.at[a]))
    for copy in copies:
        copy.wait()


def swap_videos(arrays, videos, per, ident):
    count = len(arrays)
    return pl.pallas_call(
        partial(video_kernel, videos, per, count),
        out_shape=[jax.ShapeDtypeStruct(a.shape, a.dtype) for a in arrays],
        in_specs=[ANY] * count,
        out_specs=[ANY] * count,
        scratch_shapes=[
            pltpu.SemaphoreType.DMA((count, videos)),
            pltpu.SemaphoreType.DMA((count, videos)),
            pltpu.SemaphoreType.DMA((count,)),
        ],
        compiler_params=pltpu.CompilerParams(collective_id=ident, has_side_effects=True),
        name="swap_videos",
    )(*arrays)


def collect_kernel(total, batch, cut, grad, blk, grad_out, send, recv, vsend, vrecv, own):
    f, z = frame_index()
    me = f * batch + z
    greet_all(total, batch)
    mine, g = f // 2, f % 2

    def spot(of, oz):
        return blk.at[pl.ds(pl.multiple_of(GROUP * oz, 16), GROUP), pl.ds(pl.multiple_of(128 * strip_of(of), 128), 128)]

    def group(k, start):
        other = (me + k) % total
        copy = pltpu.make_async_remote_copy(
            src_ref=cut.at[other],
            dst_ref=spot(f, z),
            send_sem=send.at[k],
            recv_sem=recv.at[k],
            device_id=(other // batch, other % batch),
            device_id_type=MESH,
        )
        if start:
            copy.start()
        else:
            copy.wait()

    lax.fori_loop(1, total, lambda k, c: (group(k, True), c)[1], 0)
    copies = [local(cut.at[me], spot(f, z), own.at[0])]
    for a, (src, dst) in enumerate(((grad, grad_out),)):
        for k in range(1, 4):
            v = (mine + k) % 4
            copies.append(remote(src.at[v], dst.at[mine], vsend.at[a, k], vrecv.at[a, k], (v * 2 + g, z)))
        copies.append(local(src.at[mine], dst.at[mine], own.at[1 + a]))
    for copy in copies:
        copy.wait()
    lax.fori_loop(1, total, lambda k, c: (group(k, False), c)[1], 0)


def collect_blocks(cut, grad, total, batch):
    return pl.pallas_call(
        partial(collect_kernel, total, batch),
        out_shape=[
            jax.ShapeDtypeStruct((ROWS, 1024), BF16),
            jax.ShapeDtypeStruct(grad.shape, grad.dtype),
        ],
        in_specs=[ANY] * 2,
        out_specs=[ANY] * 2,
        scratch_shapes=[
            pltpu.SemaphoreType.DMA((total,)),
            pltpu.SemaphoreType.DMA((total,)),
            pltpu.SemaphoreType.DMA((2, 4)),
            pltpu.SemaphoreType.DMA((2, 4)),
            pltpu.SemaphoreType.DMA((3,)),
        ],
        compiler_params=pltpu.CompilerParams(collective_id=3, has_side_effects=True),
        name="collect_blocks",
    )(cut, grad)


def plane():
    f, z = frame_index()
    y, x, c = f // 4, (f // 2) % 2, f % 2
    at_x = (4 * y + 2 * (1 - x) + c, z)
    at_y = (4 * (1 - y) + 2 * x + c, z)
    at_c = (4 * y + 2 * x + 1 - c, z)
    return y, x, c, z, at_x, at_y, at_c


def lanes(first, count):
    return pl.ds(pl.multiple_of(first, 128), count)


UNITS = (
    [("qkv", 0, 1024, 1024 * j) for j in range(3)]
    + [("out", 0, 1024, 0), ("down", 0, 1024, 0)]
    + [("in", 0, 1024, 1024 * j) for j in range(4)]
    + [("down", 1024 * n, 1024, 0) for n in range(1, 4)]
)
PLACE = {"qkv": (0, 1, 2), "out": (3,), "in": (5, 6, 7, 8), "down": (4, 9, 10, 11)}
AHEAD = 2
DEALS = (
    [("qkv", j, 0, 1024) for j in range(3)]
    + [("out", 0, 0, 1024), ("down", 0, 0, 1216), ("in", None, 0, 1024)]
    + [("down", 0, first, count) for first, count in ((1216, 1152), (2368, 1152), (3520, 576))]
)
IN_DEAL = 5
DEAL_OF = (0, 1, 2, 3, 4, 5, 5, 5, 5, 6, 7, 8)
DEAL_ROWS = (256, 256, 256, 256, 304, 1024, 288, 288, 144)


def deal_pieces(d, z):
    kind, j, first, count = DEALS[d]
    last = first + count
    found = []
    for row, rows, to, col in pieces(kind, z):
        base = pieces(kind, 0)[len(found)][2] if kind == "down" else None
        found.append((row, rows, to, col, base))
    if kind == "down":
        return [p[:4] for p in found if first <= p[4] < last]
    if kind == "qkv":
        return [p[:4] for p in found if p[3] == j]
    return [p[:4] for p in found]


GELU_A = math.sqrt(2.0 / math.pi)
GELU_B = 0.044715


def row_loop(count, step, body):
    def one(i, carry):
        body(pl.multiple_of(i * step, step))
        return carry

    lax.fori_loop(0, count // step, one, 0)


def norm_rows(values):
    centre = values - jnp.mean(values, axis=-1, keepdims=True)
    inv_std = lax.rsqrt(jnp.mean(centre * centre, axis=-1, keepdims=True) + 1e-06)
    return centre * inv_std, inv_std


def lane_half(e):
    return lax.broadcasted_iota(jnp.int32, (1, 128), 1) // 64 == e


def choose(mask, one, other):
    return jnp.where(mask, one.astype(F32), other.astype(F32)).astype(BF16)


def three_parts(value):
    high = value.astype(BF16).astype(F32)
    rest = value - high
    middle = rest.astype(BF16).astype(F32)
    return high, middle, rest - middle


def in_lanes(parts, first):
    lane = lax.broadcasted_iota(jnp.int32, (1, 128), 1) % 64
    total = 0.0
    for n, part in enumerate(parts):
        total = total + jnp.where(lane == first + n, part, 0.0)
    return total


def query_mask(ends, piece):
    lane = lax.broadcasted_iota(jnp.int32, (piece, 128), 1) % 64
    found = []
    for t in range(4):
        hidden = (lane < 4) & (lane * FRAME_LO >= ends[t])
        found.append(jnp.where(hidden, NEG_FILL, 0.0))
    return jnp.concatenate(found, axis=0)


def key_mask(keys, piece, per):
    lane = lax.broadcasted_iota(jnp.int32, (keys, 128), 1) % 64
    quarter = key_positions(keys, piece, per) // FRAME_LO
    return jnp.where((lane == quarter) | ((lane >= 4) & (lane < 7)), 1.0, 0.0)


def dot_nt(a, b):
    return lax.dot_general(a, b, (((1,), (1,)), ((), ())), preferred_element_type=F32)


def dot_tn(a, b):
    return lax.dot_general(a, b, (((0,), (0,)), ((), ())), preferred_element_type=F32)


def dot_nn(a, b):
    return jnp.dot(a, b, preferred_element_type=F32)


def fold_rows(values):
    return values[:8] + values[8:]


def frames_of(buckets, mine, g, piece, per):
    large = buckets[mine] > 0
    sel, ends = [], []
    for p in range(4):
        at = (p * per + g) * piece
        frame = jnp.where(large, at // (4 * FRAME_LO), at // FRAME_LO)
        sel.append([jnp.where(frame == fr, 1.0, 0.0) for fr in range(4)])
        ends.append((frame + 1) * jnp.where(large, 4 * FRAME_LO, FRAME_LO))
    return sel, ends


def forward_kernel(total, batch, piece, per, inverse, buckets, blk, cond_i, tok_i, cot_i, *refs):
    hbm, vm, sems = refs[:20], refs[20:48], refs[48:]
    wq_o, wo_o, wi_o, wd_o, h1_o, q_o, qb_o, kv_o, att_o, a_o, x1_o, h2_o, gp_o, u_o, y_o, pm_o, dg_o, cot_o, spread_o, tok_o = hbm
    wq, wo, wi, wd, h1, q, qb, kv, att, a, x1, h2, gp, u, acc, pm, mod_v, dg, kmask, cot = vm[:20]
    tok, held, cond, spread, mod, *cut = vm[20:]
    zsend, zrecv, psend, precv, msend, mrecv, own, wsem, osem, kvsend, kvrecv, vsend, vrecv = sems[:13]
    csend, crecv, lsend, lrecv = sems[13:]
    mats = {"qkv": wq, "out": wo, "in": wi, "down": wd}
    mats_o = {"qkv": wq_o, "out": wo_o, "in": wi_o, "down": wd_o}
    y, x, c, z, at_x, at_y, at_c = plane()
    f = 4 * y + 2 * x + c
    me = f * batch + z
    strip = 4 * c + 2 * y + x
    mine, g = f // per, f % per
    sel, ends = frames_of(buckets, mine, g, piece, per)
    greet_all(total, batch)

    def third_of(n, of, oz):
        return blk.at[
            pl.ds(pl.multiple_of(GROUP * oz + THIRD * n, 16), THIRD), lanes(128 * strip_of(of), 128)
        ]

    def send_third(n):
        def one(k, carry):
            other = (me + k) % total
            of, oz = other // batch, other % batch
            pltpu.make_async_remote_copy(
                src_ref=third_of(n, of, oz),
                dst_ref=cut[n].at[me],
                send_sem=csend.at[n],
                recv_sem=crecv.at[n],
                device_id=(of, oz),
                device_id_type=MESH,
            ).start()
            return carry

        lax.fori_loop(1, total, one, 0)

    def others(n):
        return cut[n].at[pl.ds(0, total - 1)]

    def take_third(n):
        pltpu.make_async_copy(others(n), others(n), crecv.at[n]).wait()
        own_thirds[n].wait()
        if n + 1 < 3:
            send_third(n + 1)

        def one(b, carry):
            held[pl.ds(pl.multiple_of(GROUP * b + THIRD * n, 16), THIRD), :] = cut[n][inverse[b]]
            return carry

        lax.fori_loop(0, total, one, 0)

    def send_video(src, dst, s, sem):
        for k in range(1, 4):
            v = (mine + k) % 4
            videos[s].append(
                remote(
                    src.at[v],
                    dst.at[pl.ds(pl.multiple_of(mine * piece, piece), piece)],
                    vsend.at[s, k],
                    vrecv.at[s, k],
                    (v * per + g, z),
                )
            )
        videos[s].append(local(src.at[mine], dst.at[pl.ds(pl.multiple_of(mine * piece, piece), piece)], sem))

    videos = ([], [])
    send_third(0)
    levels = [
        remote(cond_i, cond.at[pl.ds(pl.multiple_of(16 * z, 16), 16)], lsend.at[k], lrecv.at[k], (f, (z + k) % batch))
        for k in range(1, batch)
    ]
    levels.append(local(cond_i, cond.at[pl.ds(pl.multiple_of(16 * z, 16), 16)], own.at[len(DEALS)]))
    own_thirds = [local(third_of(n, f, z), cut[n].at[me], own.at[len(DEALS) + 1 + n]) for n in range(3)]
    send_video(tok_i, tok, 0, own.at[len(DEALS) + 4])

    def mod_group(k, start):
        other = (me + k) % total
        of, oz = other // batch, other % batch
        copy = pltpu.make_async_remote_copy(
            src_ref=mod.at[4 * oz + of // 2],
            dst_ref=mod_v.at[z, :, lanes(128 * strip, 128)],
            send_sem=msend.at[k],
            recv_sem=mrecv.at[k],
            device_id=(of, oz),
            device_id_type=MESH,
        )
        if start:
            copy.start()
        else:
            copy.wait()

    def spot(kind, to, count, j):
        return mats[kind].at[pl.ds(pl.multiple_of(to, 16), count), lanes(1024 * j + 128 * strip, 128)]

    base = FIRST * GROUP

    def deal(d):
        kind = DEALS[d][0]
        for k in range(1, batch):
            for row, count, to, j in deal_pieces(d, z):
                remote(
                    held.at[pl.ds(base + row, count)], spot(kind, to, count, j), zsend.at[d, k], zrecv.at[d, k],
                    (f, (z + k) % batch),
                )
        for row, count, to, j in deal_pieces(d, z):
            local(held.at[pl.ds(base + row, count)], spot(kind, to, count, j), own.at[d])

    def whole(d):
        return held.at[pl.ds(0, DEAL_ROWS[d])]

    dealt = set()
    following = [4]

    def deal_wait(d):
        if d in dealt:
            return
        dealt.add(d)
        for k in range(1, batch):
            pltpu.make_async_copy(whole(d), whole(d), zrecv.at[d, k]).wait()
        pltpu.make_async_copy(whole(d), whole(d), own.at[d]).wait()
        if d >= 1 and following[0] < len(DEALS):
            deal(following[0])
            following[0] += 1

    slots = {}
    counter = [0]

    def push(key, mat, row, count, col, width, device):
        s = counter[0]
        counter[0] += 1
        ref = mat.at[pl.ds(row, count), lanes(col, width)]
        slots.setdefault(key, []).append(remote(ref, ref, psend.at[s], precv.at[s], device))

    def stage_a(n):
        kind, row, rows, col = UNITS[n]
        half = rows // 2
        deal_wait(DEAL_OF[n])
        push((n, 1), mats[kind], row, half, col + 128 * strip, 128, at_x)
        push((n, 1), mats[kind], row + half, half, col + 128 * strip, 128, at_y)

    def stage_b(n):
        kind, row, rows, col = UNITS[n]
        half = rows // 2
        for copy in slots[(n, 1)]:
            copy.wait_recv()
        push((n, 2), mats[kind], row, half, col + 512 * c + 256 * y, 256, at_y)
        for yy in range(2):
            push((n, 2), mats[kind], row + half, half, col + 512 * c + 256 * yy + 128 * x, 128, at_x)

    def stage_c(n):
        kind, row, rows, col = UNITS[n]
        for copy in slots[(n, 2)]:
            copy.wait_recv()
        push((n, 3), mats[kind], row, rows, col + 512 * c, 512, at_c)

    saves = []

    def ready(n):
        kind, row, rows, col = UNITS[n]
        for copy in slots[(n, 3)]:
            copy.wait_recv()
        ref = (pl.ds(row, rows), pl.ds(col, 1024))
        saves.append(local(mats[kind].at[ref], mats_o[kind].at[ref], wsem.at[n]))

    pumped = [0]
    last_unit = len(UNITS)

    def pump():
        s = pumped[0]
        pumped[0] += 1
        if 0 <= s - 2 < last_unit:
            stage_b(s - 2)
        if s < last_unit:
            stage_a(s)
        if 0 <= s - 3 < last_unit:
            stage_c(s - 3)

    def pump_to(s):
        while pumped[0] <= s:
            pump()

    def save(src, dst, n):
        saves.append(local(src, dst, osem.at[n]))

    take_third(0)
    deal(0)
    send_video(cot_i, cot, 1, own.at[len(DEALS) + 5])
    take_third(1)
    deal(1)
    take_third(2)
    deal(2)
    pump_to(0)
    for copy in levels:
        copy.wait()
    row_id = lax.broadcasted_iota(jnp.int32, (384, 1), 0)
    expand = (
        lax.broadcasted_iota(jnp.int32, (384, 64), 1) == 4 * (row_id // 24) + row_id % 4
    ).astype(F32).astype(BF16)

    def mod_tile(n, carry):
        index = 128 * n + lax.broadcasted_iota(jnp.int32, (1, 128), 1)
        row, col = ada_place(index, z)
        pick = (lax.broadcasted_iota(jnp.int32, (1024, 128), 0) == row).astype(F32).astype(BF16)
        wide = dot_nn(expand, dot_nn(cond[...], pick).astype(BF16))
        wide = jnp.where(col == (row_id % 24) // 4, wide, 0.0).astype(BF16)
        spread[:, lanes(128 * n, 128)] = wide
        part = dot_nn(wide, held[pl.ds(pl.multiple_of(128 * n, 128), 128), :])
        return carry + part

    part = lax.fori_loop(0, ADA // 128, mod_tile, jnp.zeros((384, 128), F32))
    for v in range(16):
        mod[v] = part[24 * v : 24 * v + 24]
    lax.fori_loop(1, total, lambda k, t: (mod_group(k, True), t)[1], 0)
    mod_own = local(mod.at[4 * z + f // 2], mod_v.at[z, :, lanes(128 * strip, 128)], own.at[len(DEALS) + 6])
    deal(3)
    pump_to(1)
    lax.fori_loop(1, total, lambda k, t: (mod_group(k, False), t)[1], 0)
    mod_own.wait()
    save(spread, spread_o, 14)
    for copy in videos[0]:
        copy.wait()
    save(tok, tok_o, 15)
    for j in range(6):
        for p in range(4):
            value = jnp.zeros((1, 1024), F32)
            for fr in range(4):
                row = mod_v[0, pl.ds(4 * j + fr, 1), :]
                for s in range(1, batch):
                    row = row + mod_v[s, pl.ds(4 * j + fr, 1), :]
                value = value + sel[p][fr] * row
            pm[pl.ds(4 * j + p, 1), :] = value
    save(pm, pm_o, 0)

    def mod_row(j, p):
        return pm[pl.ds(4 * j + p, 1), :]

    step = 32
    for p in range(4):
        shift, scale = mod_row(0, p), mod_row(1, p)

        def one(i, p=p, shift=shift, scale=scale):
            rows = pl.ds(pl.multiple_of(p * piece + i, step), step)
            normed, _ = norm_rows(tok[rows, :].astype(F32))
            h1[rows, :] = (normed * (1.0 + scale) + shift).astype(BF16)

        row_loop(piece, step, one)
    save(h1, h1_o, 1)
    saves_h1 = saves[-1]

    pump_to(4)
    for j in range(3):
        pump_to(3 + j)
        ready(j)

        def cols(n, j=j):
            value = jnp.dot(h1[...], wq[:, lanes(1024 * j + n, 512)], preferred_element_type=F32)
            if j == 0:
                q[:, lanes(n, 512)] = (value * HD ** (-0.5)).astype(BF16)
            else:
                kv[c, :, lanes(1024 * (j - 1) + n, 512)] = value.astype(BF16)

        row_loop(1024, 512, cols)
    save(q, q_o, 2)
    kv_copy = remote(kv.at[c], kv.at[c], kvsend, kvrecv, at_c)
    pump_to(6)
    kv_copy.wait_recv()
    save(kv, kv_o, 3)

    keys = 2 * 4 * piece
    qb_mask = query_mask(ends, piece)
    acc[:, 0:128] = qb_mask
    kmask[...] = key_mask(keys, piece, per).astype(BF16)

    def heads(h):
        pair = lanes(128 * h, 128)
        k_pair = kv[:, :, pair].reshape(keys, 128)
        v_pair = kv[:, :, lanes(1024 + 128 * h, 128)].reshape(keys, 128)
        q_pair = q[:, pair]
        outs, parts = [], []
        for e in range(2):
            mine = lane_half(e)
            s = dot_nt(choose(mine, q_pair, acc[:, 0:128]), choose(mine, k_pair, kmask[...]))
            peak = jnp.max(s, axis=1, keepdims=True)
            w = jnp.exp(s - peak).astype(BF16)
            o = dot_nn(w, choose(mine, v_pair, jnp.ones_like(v_pair)))
            outs.append(o / pltpu.roll(o, 64, 1))
            parts.append(-(peak + jnp.log(jnp.where(mine, 1.0, o))))
        att[:, pair] = choose(lane_half(0), outs[0], outs[1])
        level = jnp.where(lane_half(1), parts[0], parts[1])
        qb[:, pair] = (acc[:, 0:128] + in_lanes(three_parts(level), 4)).astype(BF16)

    for n in range(4):
        lax.fori_loop(2 * n, 2 * n + 2, lambda h, t: (heads(h), t)[1], 0)
        pump_to(7 + n)
    save(att, att_o, 4)
    save(qb, qb_o, 12)

    ready(3)

    def out_cols(n):
        value = dot_nn(att[...], wo[:, lanes(n, 512)])
        acc[:, lanes(n, 512)] = value
        a[:, lanes(n, 512)] = value.astype(BF16)

    row_loop(1024, 512, out_cols)
    save(a, a_o, 5)
    for p in range(4):
        gate, shift, scale = mod_row(2, p), mod_row(3, p), mod_row(4, p)

        def two(i, p=p, gate=gate, shift=shift, scale=scale):
            rows = pl.ds(pl.multiple_of(p * piece + i, step), step)
            middle = tok[rows, :].astype(F32) + gate * acc[rows, :]
            x1[rows, :] = middle
            normed, _ = norm_rows(middle)
            h2[rows, :] = (normed * (1.0 + scale) + shift).astype(BF16)

        row_loop(piece, step, two)
    save(x1, x1_o, 6)
    save(h2, h2_o, 7)

    for j in range(4):
        pump_to(11 + j)
        ready(PLACE["in"][j])

        def in_cols(n, j=j):
            col = 1024 * j + n
            pre = jnp.dot(h2[...], wi[:, lanes(col, 512)], preferred_element_type=F32)
            square = pre * pre
            t = jnp.tanh(GELU_A * (pre + GELU_B * (square * pre)))
            lift = 0.5 * (1.0 + t)
            u[:, lanes(col, 512)] = (pre * lift).astype(BF16)
            slope = lift + (0.5 * GELU_A) * pre * (1.0 - t * t) * (1.0 + 3.0 * GELU_B * square)
            gp[:, lanes(col, 512)] = slope.astype(BF16)

        row_loop(1024, 512, in_cols)
    save(u, u_o, 8)
    save(gp, gp_o, 9)
    for n in range(4):
        ready(PLACE["down"][n])

        def down_cols(col, n=n):
            part = dot_nn(u[:, 1024 * n : 1024 * n + 1024], wd[1024 * n : 1024 * n + 1024, lanes(col, 512)])
            if n == 0:
                acc[:, lanes(col, 512)] = part
            else:
                acc[:, lanes(col, 512)] = acc[:, lanes(col, 512)] + part

        row_loop(1024, 512, down_cols)
    saves_h1.wait()
    for copy in videos[1]:
        copy.wait()
    save(cot, cot_o, 13)
    for p in range(4):
        gate = mod_row(5, p)

        def three(i, total_grad, p=p, gate=gate):
            rows = pl.ds(pl.multiple_of(p * piece + i * 16, 16), 16)
            value = acc[rows, :]
            h1[rows, :] = (x1[rows, :] + gate * value).astype(BF16)
            return total_grad + fold_rows(cot[rows, :].astype(F32) * value)

        part = lax.fori_loop(0, piece // 16, three, jnp.zeros((8, 1024), F32))
        dg[pl.ds(p, 1), :] = jnp.sum(part, axis=0, keepdims=True)
    dg[pl.ds(4, 4), :] = jnp.zeros((4, 1024), F32)
    save(dg, dg_o, 10)
    save(h1, y_o, 11)
    for copy in saves:
        if copy is not saves_h1:
            copy.wait()
    kv_copy.wait_send()
    for copies in slots.values():
        for copy in copies:
            copy.wait_send()
    for n in range(3):
        pltpu.make_async_copy(others(n), others(n), csend.at[n]).wait()
    for d in range(len(DEALS)):
        for k in range(1, batch):
            pltpu.make_async_copy(whole(d), whole(d), zsend.at[d, k]).wait()


def forward(inverse, buckets, blk, cond, tok, cot, total, batch, piece, per):
    def out(*shape, dtype=BF16):
        return jax.ShapeDtypeStruct(shape, dtype)

    outs = [out(depth, 1024 * blocks) for _, depth, blocks in KINDS] + [
        out(512, 1024),
        out(512, 1024),
        out(512, 1024),
        out(2, 512, 2048),
        out(512, 1024),
        out(512, 1024),
        out(512, 1024, dtype=F32),
        out(512, 1024),
        out(512, 4096),
        out(512, 4096),
        out(512, 1024),
        out(24, 1024, dtype=F32),
        out(8, 1024, dtype=F32),
        out(512, 1024),
        out(384, ADA),
        out(512, 1024),
    ]
    bufs = [pltpu.VMEM(o.shape, o.dtype) for o in outs[:14]] + [
        pltpu.VMEM((512, 1024), F32),
        pltpu.VMEM((24, 1024), F32),
        pltpu.VMEM((batch, 24, 1024), F32),
        pltpu.VMEM((8, 1024), F32),
        pltpu.VMEM((1024, 128), BF16),
        pltpu.VMEM((512, 1024), BF16),
        pltpu.VMEM((512, 1024), BF16),
        pltpu.VMEM((total * GROUP, 128), BF16),
        pltpu.VMEM((64, 1024), BF16),
        pltpu.VMEM((384, ADA), BF16),
        pltpu.VMEM((16, 24, 128), F32),
    ] + [pltpu.VMEM((total, THIRD, 128), BF16) for _ in range(3)]
    smem = pl.BlockSpec(memory_space=pltpu.SMEM)
    dma = pltpu.SemaphoreType.DMA
    return pl.pallas_call(
        partial(forward_kernel, total, batch, piece, per),
        out_shape=outs,
        in_specs=[smem, smem] + [ANY] * 4,
        out_specs=[ANY] * len(outs),
        scratch_shapes=bufs
        + [
            dma((len(DEALS), batch)),
            dma((len(DEALS), batch)),
            dma((6 * len(UNITS),)),
            dma((6 * len(UNITS),)),
            dma((total,)),
            dma((total,)),
            dma((len(DEALS) + 7,)),
            dma((len(UNITS),)),
            dma((16,)),
            dma,
            dma,
            dma((2, 4)),
            dma((2, 4)),
            dma((3,)),
            dma((3,)),
            dma((batch,)),
            dma((batch,)),
        ],
        compiler_params=pltpu.CompilerParams(
            collective_id=1, has_side_effects=True, vmem_limit_bytes=VMEM_LIMIT
        ),
        name="forward",
    )(inverse, buckets, blk, cond, tok, cot)


LEAVES = (
    [(3, 1024 * n, 0) for n in range(4)] + [(2, 0, j) for j in range(4)] + [(1, 0, 0)] + [(0, 0, j) for j in range(3)]
)
DEALS_AFTER = ((), (4,), (6,), (7, 8), (), (), (), (), (3,), (0,), (1,), (2,))


def backward_kernel(total, batch, piece, per, buckets, pm, dg, *refs):
    wq, wo, wi, wd, h1_i, q_i, qb_i, kv_i, att_i, a_i, x1_i, h2_i, gp_i, u_i, y_i, tok_i, cot_i = refs[:17]
    out, dmod_out, grad_o, act_o = refs[17:21]
    big1, big2, big3, wa, wb, f1, f2, s1, s2, s3, s4, kv_got, dmv, dmf, kmask, ring = refs[21:37]
    got, half_sum, strip_sum, zgot = refs[37:41], refs[41:45], refs[45:49], refs[49]
    psend, precv, zsend, zrecv, msend, mrecv, vsend, vrecv, xsend, xrecv, lsem, asem, bsem = refs[50:]
    y, x, c, z, at_x, at_y, at_c = plane()
    f = 4 * y + 2 * x + c
    me = f * batch + z

    def load(src, dst, n):
        return local(src, dst, lsem.at[n])

    cot_l = load(cot_i, s3, 0)
    u_l = [load(u_i.at[:, pl.ds(1024 * n, 1024)], big1.at[:, pl.ds(1024 * n, 1024)], 1 + n) for n in range(4)]
    h2_l = load(h2_i, s2, 5)
    gp_l = load(gp_i, big2, 6)
    x1_l = load(x1_i, f2, 7)
    a_l = load(a_i, s4, 8)
    down_tiles = [wd.at[pl.ds(512 * t, 512)] for t in range(8)] + [wo.at[pl.ds(512 * t, 512)] for t in range(2)]
    in_tiles = [wi.at[:, pl.ds(512 * t, 512)] for t in range(8)] + [wq.at[:, pl.ds(512 * t, 512)] for t in range(6)]
    fetched = {}

    def fetch(tiles, buf, sem, t):
        if t < len(tiles):
            fetched[id(tiles), t] = local(tiles[t], buf.at[t % 2], sem.at[t % 2])

    for t in range(2):
        fetch(down_tiles, wb, bsem, t)
        fetch(in_tiles, wa, asem, t)

    def tile(tiles, buf, t):
        fetched[id(tiles), t].wait()
        return buf[t % 2]

    greet_all(total, batch)
    mine, g = f // per, f % per
    sel, _ = frames_of(buckets, mine, g, piece, per)
    videos = []
    for k in range(1, 4):
        v = (mine + k) % 4
        videos.append(remote(y_i.at[v], act_o.at[mine], vsend.at[k], vrecv.at[k], (v * per + g, z)))
    videos.append(local(y_i.at[mine], act_o.at[mine], lsem.at[9]))

    slots = {}
    counter = [0]

    def push(key, src, dst, device):
        s = counter[0]
        counter[0] += 1
        slots.setdefault(key, []).append(remote(src, dst, psend.at[s], precv.at[s], device))

    def arrive(key):
        for copy in slots[key]:
            copy.wait_recv()

    def emit(n, left, right):
        m, row, j = LEAVES[n]
        for w in range(2):
            ring[n % 2, :, 512 * w : 512 * w + 512] = dot_tn(left, right[:, 512 * w : 512 * w + 512]).astype(BF16)
        push(
            (n, 0),
            ring.at[n % 2, :, lanes(512 * (1 - c), 512)],
            got[m].at[pl.ds(row, 1024), pl.ds(512 * j, 512)],
            at_c,
        )

    def add_block(dst, dst_row, dst_col, src, src_row, src_col, width, count):
        def body(i, carry):
            to = pl.ds(pl.multiple_of(dst_row + i * 128, 128), 128)
            at = pl.ds(pl.multiple_of(src_row + i * 128, 128), 128)
            dst[to, lanes(dst_col, width)] = dst[to, lanes(dst_col, width)] + src[at, lanes(src_col, width)]
            return carry

        lax.fori_loop(0, count // 128, body, 0)

    def absorb(n):
        m, row, j = LEAVES[n]
        arrive((n, 0))
        add_block(got[m], row, 512 * j, ring.at[n % 2], 0, 512 * c, 512, 1024)
        for copy in slots[(n, 0)]:
            copy.wait_send()

    def step1(n):
        m, row, j = LEAVES[n]
        for yy in range(2):
            push(
                (n, 1),
                got[m].at[pl.ds(row, 512), lanes(512 * j + 256 * yy + 128 * (1 - x), 128)],
                half_sum[m].at[pl.ds(row, 512), lanes(256 * j + 128 * yy, 128)],
                at_x,
            )
        push(
            (n, 1),
            got[m].at[pl.ds(row + 512, 512), lanes(512 * j + 256 * (1 - y), 256)],
            half_sum[m].at[pl.ds(row + 512, 512), lanes(256 * j, 256)],
            at_y,
        )

    def step2(n):
        m, row, j = LEAVES[n]
        arrive((n, 1))
        for yy in range(2):
            add_block(half_sum[m], row, 256 * j + 128 * yy, got[m], row, 512 * j + 256 * yy + 128 * x, 128, 512)
        add_block(half_sum[m], row + 512, 256 * j, got[m], row + 512, 512 * j + 256 * y, 256, 512)
        push(
            (n, 2),
            half_sum[m].at[pl.ds(row, 512), lanes(256 * j + 128 * (1 - y), 128)],
            strip_sum[m].at[pl.ds(row, 512), lanes(128 * j, 128)],
            at_y,
        )
        push(
            (n, 2),
            half_sum[m].at[pl.ds(row + 512, 512), lanes(256 * j + 128 * (1 - x), 128)],
            strip_sum[m].at[pl.ds(row + 512, 512), lanes(128 * j, 128)],
            at_x,
        )

    def step3(n):
        m, row, j = LEAVES[n]
        arrive((n, 2))
        add_block(strip_sum[m], row, 128 * j, half_sum[m], row, 256 * j + 128 * y, 128, 512)
        add_block(strip_sum[m], row + 512, 128 * j, half_sum[m], row + 512, 256 * j + 128 * x, 128, 512)
        if m == 2:

            @pl.when(z != j)
            def _():
                k = (j - z + batch) % batch
                remote(
                    strip_sum[m].at[:, pl.ds(128 * j, 128)],
                    zgot.at[k - 1, pl.ds(1120, 1024)],
                    zsend.at[IN_DEAL, k],
                    zrecv.at[IN_DEAL, k],
                    (f, j),
                )

        for d in DEALS_AFTER[n]:
            for k in range(1, batch):
                to = (z + k) % batch
                for held_row, count, at, col in deal_pieces(d, to):
                    remote(
                        strip_sum[m].at[pl.ds(pl.multiple_of(at, 16), count), lanes(128 * col, 128)],
                        zgot.at[k - 1, pl.ds(held_row, count)],
                        zsend.at[d, k],
                        zrecv.at[d, k],
                        (f, to),
                    )

    pumped = [0]

    def pump_to(r):
        while pumped[0] <= r:
            n = pumped[0]
            pumped[0] += 1
            if 0 <= n - 2 < 12:
                step2(n - 2)
            if n < 12:
                step1(n)
            if 0 <= n - 3 < 12:
                step3(n - 3)

    def whole(d, k):
        return zgot.at[k - 1, pl.ds(0, DEAL_ROWS[d])]

    def last(d):
        m = [kind for kind, _, _ in KINDS].index(DEALS[d][0])
        for k in range(1, batch):
            pltpu.make_async_copy(whole(d, k), whole(d, k), zrecv.at[d, k]).wait()
        for row, count, at, j in deal_pieces(d, z):
            step = 128 if count == 1024 else count

            def body(i, carry, row=row, at=at, j=j, step=step):
                rows = pl.ds(pl.multiple_of(row + i * step, 16), step)
                value = strip_sum[m][pl.ds(pl.multiple_of(at + i * step, 16), step), lanes(128 * j, 128)]
                value = value.astype(F32)
                for k in range(batch - 1):
                    value = value + zgot[k, rows, :].astype(F32)
                out[rows, :] = value.astype(BF16)
                return carry

            lax.fori_loop(0, count // step, body, 0)

    def mod_row(j, p):
        return pm[pl.ds(4 * j + p, 1), :]

    def by_rows(p, body, sums):
        def one(i, carry):
            return body(pl.ds(pl.multiple_of(p * piece + i * 16, 16), 16), *carry)

        start = tuple(jnp.zeros((8, 1024), F32) for _ in range(sums))
        return [jnp.sum(s, axis=0, keepdims=True) for s in lax.fori_loop(0, piece // 16, one, start)]

    cot_l.wait()
    for p in range(4):
        gate = mod_row(5, p)

        def d_mlp(rows, gate=gate):
            s1[rows, :] = (gate * s3[rows, :].astype(F32)).astype(BF16)
            return ()

        by_rows(p, d_mlp, 0)
        dmv[pl.ds(20 + p, 1), :] = dg[pl.ds(p, 1), :]
    for n in range(4):
        u_l[n].wait()
        emit(n, big1[:, 1024 * n : 1024 * n + 1024], s1)
        if n >= 1:
            absorb(n - 1)
        if n == 1:
            pump_to(0)
    kv_l = [load(kv_i.at[d], big1.at[:, pl.ds(2048 * d, 2048)], 10 + d) for d in range(2)]
    gp_l.wait()
    for t in range(8):
        cols = slice(512 * t, 512 * t + 512)
        d_act = dot_nt(s1[...], tile(down_tiles, wb, t))
        big3[:, cols] = (d_act * big2[:, cols].astype(F32)).astype(BF16)
        fetch(down_tiles, wb, bsem, t + 2)
        if t == 0:
            absorb(3)
        if t == 3:
            pump_to(1)
    h2_l.wait()
    for j in range(4):
        emit(4 + j, s2[...], big3.at[:, 1024 * j : 1024 * j + 1024])
        if j >= 1:
            absorb(3 + j)
        if j == 1:
            pump_to(2)
    att_l = load(att_i, s2, 5)
    for t in range(8):
        part = dot_nt(big3[:, 512 * t : 512 * t + 512], tile(in_tiles, wa, t))
        f1[...] = part if t == 0 else f1[...] + part
        fetch(in_tiles, wa, asem, t + 2)
        if t == 0:
            absorb(7)
        if t == 5:
            pump_to(3)
    qb_l = load(qb_i, big3.at[:, pl.ds(3072, 1024)], 6)

    x1_l.wait()
    a_l.wait()
    for p in range(4):
        gate, scale = mod_row(2, p), mod_row(4, p)

        def back_two(rows, d_scale, d_shift, d_gate, gate=gate, scale=scale):
            normed, inv_std = norm_rows(f2[rows, :])
            d_h = f1[rows, :]
            d_mid = s3[rows, :].astype(F32) + norm_back(d_h * (1.0 + scale), normed, inv_std)
            f2[rows, :] = d_mid
            s1[rows, :] = (gate * d_mid).astype(BF16)
            return (
                d_scale + fold_rows(d_h * normed),
                d_shift + fold_rows(d_h),
                d_gate + fold_rows(d_mid * s4[rows, :].astype(F32)),
            )

        d_scale, d_shift, d_gate = by_rows(p, back_two, 3)
        dmv[pl.ds(16 + p, 1), :] = d_scale
        dmv[pl.ds(12 + p, 1), :] = d_shift
        dmv[pl.ds(8 + p, 1), :] = d_gate
    q_l = load(q_i, s4, 8)
    pump_to(4)

    att_l.wait()
    emit(8, s2[...], s1)
    for t in range(2):
        s3[:, 512 * t : 512 * t + 512] = dot_nt(s1[...], tile(down_tiles, wb, 8 + t)).astype(BF16)
    h1_l = load(h1_i, wb.at[0], 7)
    tok_l = load(tok_i, wb.at[1], 12)
    absorb(8)

    keys = 2 * 4 * piece
    kmask[...] = key_mask(keys, piece, per).astype(BF16)
    for copy in kv_l:
        copy.wait()
    qb_l.wait()
    q_l.wait()

    def heads(h):
        pair = lanes(128 * h, 128)
        k_pair = jnp.concatenate([big1[:, lanes(2048 * d + 128 * h, 128)] for d in range(2)], axis=0)
        v_pair = jnp.concatenate([big1[:, lanes(2048 * d + 1024 + 128 * h, 128)] for d in range(2)], axis=0)
        dks, dvs, dqs = [], [], []
        first = lane_half(0)
        ones = in_lanes([1.0, 1.0, 1.0], 0)
        for e in range(2):
            mask = lane_half(e)
            k_e = choose(mask, k_pair, kmask[...])
            v_e = choose(mask, v_pair, ones)
            dk = dv = 0.0
            dq = []
            for w in range(2):
                rows = slice(256 * w, 256 * w + 256)
                q_w, d_w, o_w = s4[rows, pair], s3[rows, pair], s2[rows, pair]
                q_e = choose(mask, q_w, big3[rows, lanes(3072 + 128 * h, 128)])
                dot_rows = jnp.sum(
                    jnp.where(mask, d_w.astype(F32) * o_w.astype(F32), 0.0), axis=1, keepdims=True
                )
                d_e = choose(mask, d_w, in_lanes(three_parts(-dot_rows), 0))
                prob = jnp.exp(dot_nt(k_e, q_e))
                d_s = (prob * dot_nt(v_e, d_e)).astype(BF16)
                dv = dv + dot_nn(prob.astype(BF16), d_w)
                dk = dk + dot_nn(d_s, q_w)
                dq.append(dot_tn(d_s, k_pair))
            dks.append(dk)
            dvs.append(dv)
            dqs.append(jnp.concatenate(dq, axis=0))
        dk = choose(first, dks[0], dks[1])
        dv = choose(first, dvs[0], dvs[1])
        big3[:, pair] = (choose(first, dqs[0], dqs[1]).astype(F32) * HD ** (-0.5)).astype(BF16)
        for d in range(2):
            big2[:, lanes(2048 * d + 128 * h, 128)] = dk[512 * d : 512 * d + 512]
            big2[:, lanes(2048 * d + 1024 + 128 * h, 128)] = dv[512 * d : 512 * d + 512]

    exchanges = []
    for h in range(8):
        lax.fori_loop(h, h + 1, lambda n, t: (heads(n), t)[1], 0)
        if h % 4 == 3:
            for part in range(2):
                at = 1024 * part + 512 * (h // 4)
                s = len(exchanges)
                exchanges.append(
                    remote(
                        big2.at[:, lanes(2048 * (1 - c) + at, 512)],
                        kv_got.at[:, pl.ds(at, 512)],
                        xsend.at[s],
                        xrecv.at[s],
                        at_c,
                    )
                )
        if h % 2 == 0:
            pump_to(5 + h // 2)

    h1_l.wait()
    emit(9, wb[0], big3.at[:, 0:1024])
    for copy in exchanges:
        copy.wait_recv()
    for part in range(2):

        def join(i, carry, part=part):
            rows = pl.ds(pl.multiple_of(i * 64, 64), 64)
            value = big2[rows, lanes(2048 * c + 1024 * part, 1024)].astype(F32) + kv_got[
                rows, 1024 * part : 1024 * part + 1024
            ].astype(F32)
            big3[rows, 1024 + 1024 * part : 2048 + 1024 * part] = value.astype(BF16)
            return carry

        lax.fori_loop(0, 8, join, 0)
        emit(10 + part, wb[0], big3.at[:, 1024 + 1024 * part : 2048 + 1024 * part])
        absorb(9 + part)
        pump_to(9 + part)
    for t in range(6):
        part = dot_nt(big3[:, 512 * t : 512 * t + 512], tile(in_tiles, wa, 8 + t))
        f1[...] = part if t == 0 else f1[...] + part
        fetch(in_tiles, wa, asem, 8 + t + 2)
        if t == 0:
            absorb(11)
        if t == 2:
            pump_to(11)

    tok_l.wait()
    for p in range(4):
        scale = mod_row(1, p)

        def back_one(rows, d_scale, d_shift, scale=scale):
            normed, inv_std = norm_rows(wb[1, rows, :].astype(F32))
            d_h = f1[rows, :]
            s1[rows, :] = (f2[rows, :] + norm_back(d_h * (1.0 + scale), normed, inv_std)).astype(BF16)
            return d_scale + fold_rows(d_h * normed), d_shift + fold_rows(d_h)

        d_scale, d_shift = by_rows(p, back_one, 2)
        dmv[pl.ds(4 + p, 1), :] = d_scale
        dmv[pl.ds(p, 1), :] = d_shift
    grad_l = load(s1, grad_o, 0)
    for j in range(6):
        for fr in range(4):
            value = sel[0][fr] * dmv[pl.ds(4 * j, 1), :]
            for p in range(1, 4):
                value = value + sel[p][fr] * dmv[pl.ds(4 * j + p, 1), :]
            dmf[pl.ds(4 * j + fr, 1), :] = value

    def mod_group(k, start):
        other = (me + k) % total
        of, oz = other // batch, other % batch
        copy = pltpu.make_async_remote_copy(
            src_ref=dmf.at[:, lanes(128 * strip_of(of), 128)],
            dst_ref=dmod_out.at[me],
            send_sem=msend.at[k],
            recv_sem=mrecv.at[k],
            device_id=(of, oz),
            device_id_type=MESH,
        )
        if start:
            copy.start()
        else:
            copy.wait()

    lax.fori_loop(1, total, lambda k, u: (mod_group(k, True), u)[1], 0)
    mod_own = load(dmf.at[:, lanes(128 * strip_of(f), 128)], dmod_out.at[me], 1)

    for n in range(3):
        out[pl.ds(THIRD * n + 16, 32), :] = jnp.zeros((32, 128), BF16)
    pump_to(12)
    for d in (4, 6, 7, 8):
        last(d)
    pump_to(13)
    last(IN_DEAL)
    last(3)
    last(0)
    pump_to(14)
    for d in (1, 2):
        last(d)
    for n, copies in slots.items():
        if n[1] > 0:
            for copy in copies:
                copy.wait_send()
    for d in range(len(DEALS)):
        for k in range(1, batch):
            pltpu.make_async_copy(whole(d, k), whole(d, k), zsend.at[d, k]).wait()
    for copy in exchanges:
        copy.wait_send()
    for copy in videos:
        copy.wait()
    grad_l.wait()
    mod_own.wait()
    lax.fori_loop(1, total, lambda k, u: (mod_group(k, False), u)[1], 0)


def backward(buckets, pm, dg, arrays, total, batch, piece, per):
    def sums(width):
        return [pltpu.VMEM((depth, blocks * width), BF16) for _, depth, blocks in KINDS]

    def buf(*shape, dtype=BF16):
        return pltpu.VMEM(shape, dtype)

    whole = pl.BlockSpec(memory_space=pltpu.VMEM)
    dma = pltpu.SemaphoreType.DMA
    return pl.pallas_call(
        partial(backward_kernel, total, batch, piece, per),
        out_shape=[
            jax.ShapeDtypeStruct((HELD, 128), BF16),
            jax.ShapeDtypeStruct((total, 24, 128), F32),
            jax.ShapeDtypeStruct((512, 1024), BF16),
            jax.ShapeDtypeStruct((4, piece, 1024), BF16),
        ],
        in_specs=[pl.BlockSpec(memory_space=pltpu.SMEM), whole, whole] + [ANY] * len(arrays),
        out_specs=[whole, ANY, ANY, ANY],
        scratch_shapes=[buf(512, 4096) for _ in range(3)]
        + [buf(2, 1024, 512), buf(2, 512, 1024)]
        + [buf(512, 1024, dtype=F32) for _ in range(2)]
        + [buf(512, 1024) for _ in range(4)]
        + [buf(512, 2048), buf(24, 1024, dtype=F32), buf(24, 1024, dtype=F32), buf(1024, 128), buf(2, 1024, 1024)]
        + sums(512)
        + sums(256)
        + sums(128)
        + [buf(batch - 1, HELD, 128)]
        + [
            dma((72,)),
            dma((72,)),
            dma((len(DEALS), batch)),
            dma((len(DEALS), batch)),
            dma((total,)),
            dma((total,)),
            dma((4,)),
            dma((4,)),
            dma((4,)),
            dma((4,)),
            dma((13,)),
            dma((2,)),
            dma((2,)),
        ],
        compiler_params=pltpu.CompilerParams(
            collective_id=2, has_side_effects=True, vmem_limit_bytes=VMEM_LIMIT
        ),
        name="backward",
    )(buckets, pm, dg, *arrays)


def pick_kernel(index, src, dst):
    def body(i, carry):
        dst[i] = src[index[i]]
        return carry

    lax.fori_loop(0, dst.shape[0], body, 0)


def pick_blocks(index, src):
    whole = pl.BlockSpec(memory_space=pltpu.VMEM)
    return pl.pallas_call(
        pick_kernel,
        out_shape=jax.ShapeDtypeStruct((index.shape[0],) + src.shape[1:], src.dtype),
        in_specs=[pl.BlockSpec(memory_space=pltpu.SMEM), whole],
        out_specs=whole,
        name="pick_blocks",
    )(index, src)


def own_rows_of(owned, table, me):
    return table[pl.ds(owned[me], 1), :]


def cut_kernel(batch, owned, table, master, out):
    f, z = frame_index()
    rows = own_rows_of(owned, table, f * batch + z)
    swap = (rows == lax.broadcasted_iota(jnp.int32, (ROWS, ROWS), 0)).astype(F32).astype(BF16)
    for s in range(8):
        strip = master[pl.ds(s, ROWS, stride=8), :].astype(BF16)
        out[:, 128 * s : 128 * s + 128] = dot_tn(swap, strip).astype(BF16)


def cut_owned(owned, table, master, batch):
    whole = pl.BlockSpec(memory_space=pltpu.VMEM)
    return pl.pallas_call(
        partial(cut_kernel, batch),
        out_shape=jax.ShapeDtypeStruct((ROWS, 1024), BF16),
        in_specs=[pl.BlockSpec(memory_space=pltpu.SMEM), whole, whole],
        out_specs=whole,
        compiler_params=pltpu.CompilerParams(vmem_limit_bytes=VMEM_LIMIT),
        name="cut_owned",
    )(owned, table, master)


def adam(grad, master, first, second):
    new_first = BETA_ONE * first + (1.0 - BETA_ONE) * grad
    new_second = BETA_TWO * second + (1.0 - BETA_TWO) * grad * grad
    fix_one = 1.0 - BETA_ONE**STEP
    fix_two = 1.0 - BETA_TWO**STEP
    update = new_first / fix_one / (jnp.sqrt(new_second / fix_two) + ADAM_EPS)
    return master - LEARN_RATE * (update + WEIGHT_DECAY * master), new_first, new_second


def update_kernel(batch, owned, table, grad, master, first, second, new_master, new_first, new_second):
    f, z = frame_index()
    rows = own_rows_of(owned, table, f * batch + z)
    base = pl.program_id(0) * GROUP
    swap = (rows == base + lax.broadcasted_iota(jnp.int32, (GROUP, ROWS), 0)).astype(F32).astype(BF16)
    for s in range(8):
        at = pl.ds(s, GROUP, stride=8)
        value = dot_nn(swap, grad[:, 128 * s : 128 * s + 128])
        new_master[at, :], new_first[at, :], new_second[at, :] = adam(
            value, master[at, :], first[at, :], second[at, :]
        )


def update_owned(owned, table, grad, master, first, second, batch):
    part = pl.BlockSpec((8 * GROUP, 128), lambda i: (i, 0))
    return pl.pallas_call(
        partial(update_kernel, batch),
        grid=(ROWS // GROUP,),
        out_shape=[jax.ShapeDtypeStruct(master.shape, F32)] * 3,
        in_specs=[
            pl.BlockSpec(memory_space=pltpu.SMEM),
            pl.BlockSpec(table.shape, lambda i: (0, 0)),
            pl.BlockSpec((ROWS, 1024), lambda i: (0, 0)),
            part,
            part,
            part,
        ],
        out_specs=[part] * 3,
        compiler_params=pltpu.CompilerParams(vmem_limit_bytes=VMEM_LIMIT),
        name="update_owned",
    )(owned, table, grad, master, first, second)


def key_positions(rows, piece, per):
    i = lax.broadcasted_iota(jnp.int32, (rows, 1), 0)
    local_rows = rows // per
    return ((i % local_rows) // piece * per + i // local_rows) * piece + i % piece


def scores_t(k, q, ends, piece, per):
    s = lax.dot_general(k, q, (((1,), (1,)), ((), ())), preferred_element_type=F32)
    pos = key_positions(k.shape[0], piece, per)
    cols = []
    for t in range(q.shape[0] // piece):
        part = s[:, t * piece : (t + 1) * piece]
        cols.append(jnp.where(pos < ends[t], part, NEG_FILL))
    return jnp.concatenate(cols, axis=1)


def attend_kernel(piece, per, ends, q, k, v, o):
    outs = []
    for a in range(2):
        cut = slice(64 * a, 64 * a + 64)
        s = scores_t(k[:, cut], q[:, cut], ends, piece, per)
        peak = jnp.max(s, axis=0, keepdims=True)
        e = jnp.exp(s - peak)
        p = (e * (1.0 / jnp.sum(e, axis=0, keepdims=True))).astype(BF16)
        outs.append(lax.dot_general(p, v[:, cut], (((0,), (0,)), ((), ())), preferred_element_type=F32))
    o[...] = jnp.concatenate(outs, axis=1).astype(BF16)


def attend(ends, q, kv, piece, per):
    rows, width = q.shape
    keys = kv.shape[0]
    pairs = width // 128
    return pl.pallas_call(
        partial(attend_kernel, piece, per),
        grid_spec=pltpu.PrefetchScalarGridSpec(
            num_scalar_prefetch=1,
            grid=(pairs,),
            in_specs=[
                pl.BlockSpec((rows, 128), lambda h, e: (0, h)),
                pl.BlockSpec((keys, 128), lambda h, e: (0, h)),
                pl.BlockSpec((keys, 128), lambda h, e: (0, h + pairs)),
            ],
            out_specs=pl.BlockSpec((rows, 128), lambda h, e: (0, h)),
        ),
        out_shape=jax.ShapeDtypeStruct((rows, width), BF16),
        compiler_params=pltpu.CompilerParams(vmem_limit_bytes=VMEM_LIMIT),
        cost_estimate=pl.CostEstimate(
            flops=4 * rows * keys * width, bytes_accessed=4 * (rows + keys) * width, transcendentals=rows * keys * H
        ),
        name="attend",
    )(ends, q, kv, kv)


def attend_back_kernel(piece, per, ends, q, k, v, do, dq, dk, dv):
    dqs, dks, dvs = [], [], []
    for a in range(2):
        cut = slice(64 * a, 64 * a + 64)
        qa, ka, va, da = q[:, cut], k[:, cut], v[:, cut], do[:, cut]
        s = scores_t(ka, qa, ends, piece, per)
        peak = jnp.max(s, axis=0, keepdims=True)
        e = jnp.exp(s - peak)
        p = e * (1.0 / jnp.sum(e, axis=0, keepdims=True))
        dvs.append(jnp.dot(p.astype(BF16), da, preferred_element_type=F32))
        dp = lax.dot_general(va, da, (((1,), (1,)), ((), ())), preferred_element_type=F32)
        pdp = p * dp
        row = jnp.sum(pdp, axis=0, keepdims=True)
        ds = (pdp - p * row).astype(BF16)
        dks.append(jnp.dot(ds, qa, preferred_element_type=F32))
        dqs.append(lax.dot_general(ds, ka, (((0,), (0,)), ((), ())), preferred_element_type=F32))
    dq[...] = jnp.concatenate(dqs, axis=1).astype(BF16)
    dk[...] = jnp.concatenate(dks, axis=1).astype(BF16)
    dv[...] = jnp.concatenate(dvs, axis=1).astype(BF16)


def attend_back(ends, q, kv, do, piece, per):
    rows, width = q.shape
    keys = kv.shape[0]
    pairs = width // 128
    mine = pl.BlockSpec((rows, 128), lambda h, e: (0, h))
    allk = pl.BlockSpec((keys, 128), lambda h, e: (0, h))
    return pl.pallas_call(
        partial(attend_back_kernel, piece, per),
        grid_spec=pltpu.PrefetchScalarGridSpec(
            num_scalar_prefetch=1,
            grid=(pairs,),
            in_specs=[mine, allk, pl.BlockSpec((keys, 128), lambda h, e: (0, h + pairs)), mine],
            out_specs=[mine, allk, allk],
        ),
        out_shape=[
            jax.ShapeDtypeStruct((rows, width), BF16),
            jax.ShapeDtypeStruct((keys, width), BF16),
            jax.ShapeDtypeStruct((keys, width), BF16),
        ],
        compiler_params=pltpu.CompilerParams(vmem_limit_bytes=VMEM_LIMIT),
        cost_estimate=pl.CostEstimate(
            flops=10 * rows * keys * width, bytes_accessed=6 * (rows + keys) * width, transcendentals=rows * keys * H
        ),
        name="attend_back",
    )(ends, q, kv, kv, do)


def layer_stats(values):
    centre = values - jnp.mean(values, axis=-1, keepdims=True)
    inv_std = lax.rsqrt(jnp.mean(centre * centre, axis=-1, keepdims=True) + 1e-06)
    return (centre * inv_std, inv_std)


def norm_back(upstream, normed, inv_std):
    mean_grad = jnp.mean(upstream, axis=-1, keepdims=True)
    mean_cross = jnp.mean(upstream * normed, axis=-1, keepdims=True)
    return inv_std * (upstream - mean_grad - normed * mean_cross)


def noise_embedding(levels, feature_width):
    half_width = feature_width // 2
    frequencies = jnp.exp(
        -math.log(10000.0) * jnp.arange(half_width, dtype=jnp.float32) / half_width
    )
    angles = levels.astype(jnp.float32)[:, None] * frequencies[None, :]
    return jnp.concatenate([jnp.cos(angles), jnp.sin(angles)], axis=1)


def silu_embedding(levels, width):
    return jax.nn.silu(noise_embedding(levels, width)).astype(BF16)


def split_flat(flat_values, model_width, hidden_width):
    matrix_shapes = (
        (model_width, 6 * model_width),
        (model_width, 3 * model_width),
        (model_width, model_width),
        (model_width, hidden_width),
        (hidden_width, model_width),
    )
    matrices = []
    offset_now = 0
    for matrix_shape in matrix_shapes:
        entry_count = matrix_shape[0] * matrix_shape[1]
        matrices.append(flat_values[offset_now : offset_now + entry_count].reshape(matrix_shape))
        offset_now = offset_now + entry_count
    return matrices


def shards(
    frame_size,
    batch_size,
    tokens,
    out_cotangent,
    buckets,
    noise_levels,
    owned_block,
    master,
    first_moment,
    second_moment,
):
    micro_count, piece, width = tokens.shape
    block_size = master.shape[1]
    frame_count = noise_levels.shape[1]
    total = frame_size * batch_size
    videos = micro_count
    per = frame_size // videos
    rows = videos * piece
    keys = rows * per
    q_scale = HD ** (-0.5)
    f, z = frame_index()
    me = f * batch_size + z
    mine, g = f // per, f % per
    direct = frame_size == 8 and batch_size == 4 and block_size == ROWS * 1024 and videos == 4 and frame_count == 4

    if direct:
        order = jnp.arange(total, dtype=jnp.int32)
        inverse = jnp.sum(jnp.where(owned_block[None, :] == order[:, None], order[None, :], 0), axis=1)
        table = jnp.asarray(np.stack([block_rows(b) for b in range(total)]).astype(np.int32))
        blk = cut_owned(owned_block, table, master.reshape(-1, 128), batch_size)
        cond = silu_embedding(noise_levels.reshape(16), width)
    else:
        tok, cot = swap_videos([tokens, out_cotangent], videos, per, 0)
        gathered = lax.all_gather(master.astype(BF16), ("frame", "batch"), axis=0, tiled=True)
        placed = jnp.take(gathered, jnp.argsort(owned_block), axis=0).reshape(-1)
        w_ada, w_qkv, w_out, w_in, w_down = split_flat(placed, width, FF)
        cond = silu_embedding(lax.dynamic_index_in_dim(noise_levels, mine, 0, keepdims=False), width)
        modulation = jnp.dot(cond, w_ada, preferred_element_type=F32).reshape(frame_count, 6, width)

    def flat(a):
        return a.reshape(rows, a.shape[-1])

    def cube(a):
        return a.reshape(videos, piece, a.shape[-1])

    def partners(k):
        return [(i, i // per * per + (i + k) % per) for i in range(frame_size)]

    def split_mod(piece_mod):
        return [piece_mod[j][:, None, :] for j in range(6)]

    if direct:
        saved = forward(inverse, buckets, blk, cond, tokens, out_cotangent, total, batch_size, piece, per)
        *saved, block_output, piece_mod, d_gate, cot, cond_all, tokens_own = saved
        held_grad, dmod_parts, input_grad, outputs = backward(
            buckets,
            piece_mod,
            d_gate,
            [*saved, cube(block_output), tokens_own, cot],
            total,
            batch_size,
            piece,
            per,
        )
        input_grad = cube(input_grad)
    else:
        frame_len = FRAME_LO * (1 + 3 * buckets[mine])
        piece_at = (jnp.arange(videos, dtype=jnp.int32) * per + g) * piece
        piece_frame = piece_at // frame_len
        ends = (piece_frame + 1) * frame_len
        selector = (piece_frame[:, None] == jnp.arange(frame_count, dtype=jnp.int32)[None, :]).astype(F32)
        x_float = tok.astype(F32)
        normed_one, inv_one = layer_stats(x_float)
        piece_mod = jnp.einsum("pf,fjd->jpd", selector, modulation, precision=HIGHEST)
        shift_one, scale_one, gate_one, shift_two, scale_two, gate_two = split_mod(piece_mod)

        h_one = flat((normed_one * (1.0 + scale_one) + shift_one).astype(BF16))
        projected = jnp.dot(h_one, w_qkv, preferred_element_type=F32)
        queries = (projected[:, :width] * q_scale).astype(BF16)
        kv_own = projected[:, width:].astype(BF16)

        kv_all = jnp.zeros((per, rows, 2 * width), BF16)
        kv_all = lax.dynamic_update_index_in_dim(kv_all, kv_own, g, 0)
        for k in range(1, per):
            kv_all = lax.dynamic_update_index_in_dim(
                kv_all, lax.ppermute(kv_own, "frame", partners(k)), (g + per - k) % per, 0
            )
        kv_all = kv_all.reshape(keys, 2 * width)
        attended = attend(ends, queries, kv_all, piece, per)
        attn_out = jnp.dot(attended, w_out, preferred_element_type=F32)
        middle = x_float + gate_one * cube(attn_out)
        normed_two, inv_two = layer_stats(middle)
        h_two = flat((normed_two * (1.0 + scale_two) + shift_two).astype(BF16))
        pre_act = jnp.dot(h_two, w_in, preferred_element_type=F32)
        activated, gelu_back = jax.vjp(partial(jax.nn.gelu, approximate=True), pre_act)
        act_low = activated.astype(BF16)
        slope = gelu_back(jnp.ones_like(pre_act))[0]
        mlp_out = jnp.dot(act_low, w_down, preferred_element_type=F32)
        block_output = (middle + gate_two * cube(mlp_out)).astype(BF16)

        grad_out = cot.astype(F32)
        d_mlp = flat((gate_two * grad_out).astype(BF16))
        g_down = jnp.dot(act_low.T, d_mlp, preferred_element_type=F32).astype(BF16)
        d_act = jnp.dot(d_mlp, w_down.T, preferred_element_type=F32)
        d_pre = (d_act * slope.astype(F32)).astype(BF16)
        g_in = jnp.dot(h_two.T, d_pre, preferred_element_type=F32).astype(BF16)
        d_htwo = cube(jnp.dot(d_pre, w_in.T, preferred_element_type=F32))
        d_gate_two = jnp.sum(grad_out * cube(mlp_out), axis=1)
        d_scale_two = jnp.sum(d_htwo * normed_two, axis=1)
        d_shift_two = jnp.sum(d_htwo, axis=1)
        d_middle = grad_out + norm_back(d_htwo * (1.0 + scale_two), normed_two, inv_two)
        d_attn = flat((gate_one * d_middle).astype(BF16))
        d_gate_one = jnp.sum(d_middle * cube(attn_out), axis=1)
        g_out = jnp.dot(attended.T, d_attn, preferred_element_type=F32).astype(BF16)
        d_attended = jnp.dot(d_attn, w_out.T, preferred_element_type=F32).astype(BF16)
        dq, dk, dv = attend_back(ends, queries, kv_all, d_attended, piece, per)
        dkv = jnp.concatenate([dk, dv], axis=1).reshape(per, rows, 2 * width)
        dkv_own = lax.dynamic_index_in_dim(dkv, g, 0, keepdims=False).astype(F32)
        for k in range(1, per):
            sent = lax.dynamic_index_in_dim(dkv, (g + k) % per, 0, keepdims=False)
            dkv_own = dkv_own + lax.ppermute(sent, "frame", partners(k)).astype(F32)
        d_proj = jnp.concatenate([dq * jnp.asarray(q_scale, BF16), dkv_own.astype(BF16)], axis=1)
        g_qkv = jnp.dot(h_one.T, d_proj, preferred_element_type=F32).astype(BF16)
        d_hone = cube(jnp.dot(d_proj, w_qkv.T, preferred_element_type=F32))
        d_scale_one = jnp.sum(d_hone * normed_one, axis=1)
        d_shift_one = jnp.sum(d_hone, axis=1)
        d_input = d_middle + norm_back(d_hone * (1.0 + scale_one), normed_one, inv_one)
        input_grad = d_input.astype(BF16)
        piece_dmod = jnp.stack([d_shift_one, d_scale_one, d_gate_one, d_shift_two, d_scale_two, d_gate_two])
        frame_dmod = jnp.einsum("pf,jpd->jfd", selector, piece_dmod, precision=HIGHEST)

    if direct:
        dmod_all = jnp.sum(dmod_parts.reshape(4, 2, 4, 24, 128), axis=1).transpose(1, 0, 2, 3).reshape(384, 128)
        ada_grad = lax.dot_general(
            cond_all[:, : 11 * GROUP].astype(F32), dmod_all, (((0,), (0,)), ((), ())), precision=HIGHEST
        ).astype(BF16)
        edge = jnp.concatenate(
            [ada_grad[FIRST * GROUP :].reshape(3, THIRD, 128)[:, 16:], held_grad[:GROUP].reshape(3, THIRD, 128)[:, :16]], axis=1
        )
        edge = jnp.concatenate([edge[:, 32:], edge[:, :32]], axis=1).reshape(GROUP, 128)
        ordered_grad = jnp.concatenate([ada_grad[: FIRST * GROUP], edge, held_grad[GROUP:]], axis=0)
        cut_grad = pick_blocks(owned_block, ordered_grad.reshape(total, GROUP, 128))
        grad_block, input_grads = collect_blocks(cut_grad, input_grad, total, batch_size)
        updated = update_owned(
            owned_block,
            table,
            grad_block,
            master.reshape(-1, 128),
            first_moment.reshape(-1, 128),
            second_moment.reshape(-1, 128),
            batch_size,
        )
        new_master, new_first, new_second = [a.reshape(1, block_size) for a in updated]
    else:
        outputs, input_grads = swap_videos([block_output, input_grad], videos, per, 1)
        g_ada = lax.dot_general(
            cond.astype(F32),
            frame_dmod.transpose(1, 0, 2).reshape(frame_count, 6 * width),
            (((0,), (0,)), ((), ())),
            precision=HIGHEST,
        )
        flat_grads = jnp.concatenate(
            [piece_grad.astype(F32).reshape(-1) for piece_grad in (g_ada, g_qkv, g_out, g_in, g_down)]
        )
        arranged = jnp.take(flat_grads.reshape(-1, block_size), owned_block, axis=0).reshape(-1)
        shard_total = lax.psum_scatter(
            arranged, ("frame", "batch"), scatter_dimension=0, tiled=True
        ).reshape(1, block_size)
        new_master, new_first, new_second = adam(shard_total, master, first_moment, second_moment)
    return (outputs, input_grads, new_master, new_first, new_second)


def solution(mesh):
    placed = (
        P("batch", "frame", None),
        P("batch", "frame", None),
        P("batch"),
        P("batch", None),
        P(),
        P(("frame", "batch"), None),
        P(("frame", "batch"), None),
        P(("frame", "batch"), None),
    )
    return jax.shard_map(
        partial(shards, mesh.shape["frame"], mesh.shape["batch"]),
        mesh=mesh,
        in_specs=placed,
        out_specs=(
            P("batch", "frame", None),
            P("batch", "frame", None),
            P(("frame", "batch"), None),
            P(("frame", "batch"), None),
            P(("frame", "batch"), None),
        ),
        check_vma=False,
    )
```

```python
from functools import partial
import math

import jax
import jax.numpy as jnp
import numpy as np
from jax import lax
from jax.experimental import pallas as pl
from jax.experimental.pallas import tpu as pltpu
from jax.sharding import PartitionSpec as P

H = 16
HD = 64
FF = 4096
FRAME_LO = 256
STEP = 10

HIGHEST = lax.Precision.HIGHEST
NEG_FILL = -1e30
BETA_ONE = 0.5
BETA_TWO = 0.5
LEARN_RATE = 0.05
WEIGHT_DECAY = 0.1
ADAM_EPS = 1e-08
MESH = pl.DeviceIdType.MESH
F32 = jnp.float32
BF16 = jnp.bfloat16
ANY = pl.BlockSpec(memory_space=pl.ANY)
VMEM_LIMIT = 63 * 1024 * 1024

ROWS = 576
GROUP = 144
FIRST = 10
KINDS = (("qkv", 1024, 3), ("out", 1024, 1), ("in", 1024, 4), ("down", 4096, 1))
HELD = 3168
THIRD = 48
ADA = 1664


def pieces(kind, z):
    if kind == "qkv":
        found = [(48 * j, 16, 16 * z, j) for j in range(3)]
        for k in range(5):
            found += [(144 + 144 * k + 48 * j, 48, 64 + 192 * k + 48 * z, j) for j in range(3)]
        return found
    if kind == "out":
        return [(864, 144, 144 * z, 0), (1008, 112, 576 + 112 * z, 0)]
    if kind == "in":
        return [(1120, 1024, 0, z)]
    found = [(2144, 16, 16 * z, 0)]
    return found + [(2160 + 144 * k, 144, 64 + 576 * k + 144 * z, 0) for k in range(7)]


def block_rows(block):
    t = np.arange(GROUP)
    groups = []
    for z in range(4):
        if block == 10:
            i, j = t % THIRD, t // THIRD
            rows = np.where(i < 16, 384 + 3 * (16 * z + i) + j, 96 * z + 32 * j + i - 16)
        elif 11 <= block <= 15:
            rows = 3 * (48 * z + t % 48) + t // 48
        elif block == 17:
            rows = np.where(t < 112, 112 * z + t, 448 + 4 * (t - 112) + z)
        elif 18 <= block <= 23:
            rows = 4 * t + z
        elif block == 24:
            rows = np.where(t < 128, 4 * t + z, 512 + 16 * z + t - 128)
        else:
            rows = GROUP * z + t
        groups.append(rows)
    return np.concatenate(groups)


def ada_place(n, z):
    b, t = n // GROUP, n % GROUP
    i = t % THIRD - 16
    a = 32 * (t // THIRD) + i
    row = jnp.where(b < 10, 96 * b + 24 * z + t // 6, 960 + 16 * z + a // 6)
    col = jnp.where(b < 10, t % 6, a % 6)
    none = (b > 10) | ((b == 10) & (i < 0))
    return jnp.where(none, -1, row), col


def frame_index():
    return lax.axis_index("frame"), lax.axis_index("batch")


def strip_of(f):
    return 4 * (f % 2) + f // 2


def greet(devices):
    barrier = pltpu.get_barrier_semaphore()
    for device in devices:
        pl.semaphore_signal(barrier, inc=1, device_id=device, device_id_type=MESH)
    pl.semaphore_wait(barrier, len(devices))


def greet_all(total, batch):
    f, z = frame_index()
    me = f * batch + z
    barrier = pltpu.get_barrier_semaphore()

    def hail(k, carry):
        other = (me + k) % total
        pl.semaphore_signal(barrier, inc=1, device_id=(other // batch, other % batch), device_id_type=MESH)
        return carry

    lax.fori_loop(1, total, hail, 0)
    pl.semaphore_wait(barrier, total - 1)


def remote(src, dst, send, recv, device):
    copy = pltpu.make_async_remote_copy(
        src_ref=src, dst_ref=dst, send_sem=send, recv_sem=recv, device_id=device, device_id_type=MESH
    )
    copy.start()
    return copy


def local(src, dst, sem):
    copy = pltpu.make_async_copy(src, dst, sem)
    copy.start()
    return copy


def video_kernel(videos, per, arrays, *refs):
    ins, outs = refs[:arrays], refs[arrays : 2 * arrays]
    send, recv, own = refs[2 * arrays :]
    f, z = frame_index()
    mine, g = f // per, f % per
    others = [((mine + k) % videos, k) for k in range(1, videos)]
    greet([(v * per + g, z) for v, k in others])
    copies = []
    for a in range(arrays):
        for v, k in others:
            copies.append(
                remote(ins[a].at[v], outs[a].at[mine], send.at[a, k], recv.at[a, k], (v * per + g, z))
            )
        copies.append(local(ins[a].at[mine], outs[a].at[mine], own.at[a]))
    for copy in copies:
        copy.wait()


def swap_videos(arrays, videos, per, ident):
    count = len(arrays)
    return pl.pallas_call(
        partial(video_kernel, videos, per, count),
        out_shape=[jax.ShapeDtypeStruct(a.shape, a.dtype) for a in arrays],
        in_specs=[ANY] * count,
        out_specs=[ANY] * count,
        scratch_shapes=[
            pltpu.SemaphoreType.DMA((count, videos)),
            pltpu.SemaphoreType.DMA((count, videos)),
            pltpu.SemaphoreType.DMA((count,)),
        ],
        compiler_params=pltpu.CompilerParams(collective_id=ident, has_side_effects=True),
        name="swap_videos",
    )(*arrays)


def plane():
    f, z = frame_index()
    y, x, c = f // 4, (f // 2) % 2, f % 2
    at_x = (4 * y + 2 * (1 - x) + c, z)
    at_y = (4 * (1 - y) + 2 * x + c, z)
    at_c = (4 * y + 2 * x + 1 - c, z)
    return y, x, c, z, at_x, at_y, at_c


def lanes(first, count):
    return pl.ds(pl.multiple_of(first, 128), count)


UNITS = (
    [("qkv", 0, 1024, 1024 * j) for j in range(3)]
    + [("out", 0, 1024, 0)]
    + [("down", 1024 * n, 1024, 0) for n in range(4)]
    + [("in", 0, 1024, 1024 * j) for j in range(4)]
)
AHEAD = 2
PLACE = {"qkv": (0, 1, 2), "out": (3,), "down": (4, 5, 6, 7), "in": (8, 9, 10, 11)}
DOWN_DEALS = [("down", 0, 0, 1216, 304), ("down", 0, 1216, 1152, 288), ("down", 0, 2368, 1152, 288), ("down", 0, 3520, 576, 144)]
QKV_DEALS = [("qkv", j, 0, 1024, 256) for j in range(3)]
OUT_DEAL = ("out", 0, 0, 1024, 256)
DEALS = QKV_DEALS + [OUT_DEAL]
for n in range(4):
    DEALS += [DOWN_DEALS[n], ("in", None, 256 * n, 256, 256)]
DEALS_OF = ((0,), (1,), (2,), (3,), (4,), (6,), (8,), (10,)) + ((5, 7, 9, 11),) * 4
BACK_DEALS = QKV_DEALS + [OUT_DEAL, DOWN_DEALS[0], ("in", None, 0, 1024, 1024)] + DOWN_DEALS[1:]
IN_DEAL = 5


def deal_pieces(deals, d, z):
    kind, j, first, count, _ = deals[d]
    if kind == "in":
        return [(1120 + first, count, first, z)]
    found = zip(pieces(kind, z), pieces(kind, 0))
    if kind == "down":
        return [p for p, at_zero in found if first <= at_zero[2] < first + count]
    return [p for p, _ in found if p[3] == j]


GELU_A = math.sqrt(2.0 / math.pi)
GELU_B = 0.044715


def row_loop(count, step, body):
    def one(i, carry):
        body(pl.multiple_of(i * step, step))
        return carry

    lax.fori_loop(0, count // step, one, 0)


def norm_rows(values):
    centre = values - jnp.mean(values, axis=-1, keepdims=True)
    inv_std = lax.rsqrt(jnp.mean(centre * centre, axis=-1, keepdims=True) + 1e-06)
    return centre * inv_std, inv_std


def lane_half(e):
    return lax.broadcasted_iota(jnp.int32, (1, 128), 1) // 64 == e


def choose(mask, one, other):
    return jnp.where(mask, one.astype(F32), other.astype(F32)).astype(BF16)


def three_parts(value):
    high = value.astype(BF16).astype(F32)
    rest = value - high
    middle = rest.astype(BF16).astype(F32)
    return high, middle, rest - middle


def in_lanes(parts, first):
    lane = lax.broadcasted_iota(jnp.int32, (1, 128), 1) % 64
    total = 0.0
    for n, part in enumerate(parts):
        total = total + jnp.where(lane == first + n, part, 0.0)
    return total


def query_mask(ends, piece):
    lane = lax.broadcasted_iota(jnp.int32, (piece, 128), 1) % 64
    found = []
    for t in range(4):
        hidden = (lane < 4) & (lane * FRAME_LO >= ends[t])
        found.append(jnp.where(hidden, NEG_FILL, 0.0))
    return jnp.concatenate(found, axis=0)


def key_mask(keys, piece, per):
    lane = lax.broadcasted_iota(jnp.int32, (keys, 128), 1) % 64
    quarter = key_positions(keys, piece, per) // FRAME_LO
    return jnp.where((lane == quarter) | ((lane >= 4) & (lane < 7)), 1.0, 0.0)


def dot_nt(a, b):
    return lax.dot_general(a, b, (((1,), (1,)), ((), ())), preferred_element_type=F32)


def dot_tn(a, b):
    return lax.dot_general(a, b, (((0,), (0,)), ((), ())), preferred_element_type=F32)


def dot_nn(a, b):
    return jnp.dot(a, b, preferred_element_type=F32)


def fold_rows(values):
    return values[:8] + values[8:]


def frames_of(buckets, mine, g, piece, per):
    large = buckets[mine] > 0
    sel, ends = [], []
    for p in range(4):
        at = (p * per + g) * piece
        frame = jnp.where(large, at // (4 * FRAME_LO), at // FRAME_LO)
        sel.append([jnp.where(frame == fr, 1.0, 0.0) for fr in range(4)])
        ends.append((frame + 1) * jnp.where(large, 4 * FRAME_LO, FRAME_LO))
    return sel, ends


def forward_kernel(total, batch, piece, per, inverse, buckets, blk, cond_i, tok_i, cot_i, *refs):
    hbm, vm, sems = refs[:20], refs[20:49], refs[49:]
    wq_o, wo_o, wi_o, wd_o, h1_o, q_o, qb_o, kv_o, att_o, a_o, x1_o, h2_o, gp_o, u_o, y_o, pm_o, dg_o, cot_o, spread_o, tok_o = hbm
    wq, wo, wi, wd, h1, q, qb, kv, att, a, x1, h2, gp, u, acc, pm, mod_v, dg, kmask, cot = vm[:20]
    tok, held, cond, spread, mod, *cut, mod_half = vm[20:]
    zsend, zrecv, psend, precv, msend, mrecv, own, wsem, osem, kvsend, kvrecv, vsend, vrecv = sems[:13]
    csend, crecv, lsend, lrecv, hsend, hrecv = sems[13:]
    mats = {"qkv": wq, "out": wo, "in": wi, "down": wd}
    mats_o = {"qkv": wq_o, "out": wo_o, "in": wi_o, "down": wd_o}
    y, x, c, z, at_x, at_y, at_c = plane()
    f = 4 * y + 2 * x + c
    me = f * batch + z
    strip = 4 * c + 2 * y + x
    mine, g = f // per, f % per
    sel, ends = frames_of(buckets, mine, g, piece, per)
    greet_all(total, batch)

    def third_of(n, of, oz):
        return blk.at[
            pl.ds(pl.multiple_of(GROUP * oz + THIRD * n, 16), THIRD), lanes(128 * strip_of(of), 128)
        ]

    def send_third(n):
        def one(k, carry):
            other = (me + k) % total
            of, oz = other // batch, other % batch
            pltpu.make_async_remote_copy(
                src_ref=third_of(n, of, oz),
                dst_ref=cut[n].at[me],
                send_sem=csend.at[n],
                recv_sem=crecv.at[n],
                device_id=(of, oz),
                device_id_type=MESH,
            ).start()
            return carry

        lax.fori_loop(1, total, one, 0)

    def others(n):
        return cut[n].at[pl.ds(0, total - 1)]

    def take_third(n):
        pltpu.make_async_copy(others(n), others(n), crecv.at[n]).wait()
        own_thirds[n].wait()
        if n + 2 < 3:
            send_third(n + 2)

        def one(b, carry):
            held[pl.ds(pl.multiple_of(GROUP * b + THIRD * n, 16), THIRD), :] = cut[n][inverse[b]]
            return carry

        lax.fori_loop(0, total, one, 0)

    def send_video(src, dst, s, sem):
        for k in range(1, 4):
            v = (mine + k) % 4
            videos[s].append(
                remote(
                    src.at[v],
                    dst.at[pl.ds(pl.multiple_of(mine * piece, piece), piece)],
                    vsend.at[s, k],
                    vrecv.at[s, k],
                    (v * per + g, z),
                )
            )
        videos[s].append(local(src.at[mine], dst.at[pl.ds(pl.multiple_of(mine * piece, piece), piece)], sem))

    videos = ([], [])
    send_third(0)
    send_third(1)
    levels = [
        remote(cond_i, cond.at[pl.ds(pl.multiple_of(16 * z, 16), 16)], lsend.at[k], lrecv.at[k], (f, (z + k) % batch))
        for k in range(1, batch)
    ]
    levels.append(local(cond_i, cond.at[pl.ds(pl.multiple_of(16 * z, 16), 16)], own.at[len(DEALS)]))
    own_thirds = [local(third_of(n, f, z), cut[n].at[me], own.at[len(DEALS) + 1 + n]) for n in range(3)]
    send_video(tok_i, tok, 0, own.at[len(DEALS) + 4])

    def mod_group(k, start):
        other = (f // 2 * batch + z + k) % (4 * batch)
        chip, oz = other // batch, other % batch
        copy = pltpu.make_async_remote_copy(
            src_ref=mod.at[4 * oz + chip],
            dst_ref=mod_v.at[z, :, lanes(128 * (f // 2), 128)],
            send_sem=msend.at[k],
            recv_sem=mrecv.at[k],
            device_id=(2 * chip + c, oz),
            device_id_type=MESH,
        )
        if start:
            copy.start()
        else:
            copy.wait()

    def spot(kind, to, count, j):
        return mats[kind].at[pl.ds(pl.multiple_of(to, 16), count), lanes(1024 * j + 128 * strip, 128)]

    base = FIRST * GROUP

    def deal(d):
        kind = DEALS[d][0]
        for k in range(1, batch):
            for row, count, to, j in deal_pieces(DEALS, d, z):
                remote(
                    held.at[pl.ds(base + row, count)], spot(kind, to, count, j), zsend.at[d, k], zrecv.at[d, k],
                    (f, (z + k) % batch),
                )
        for row, count, to, j in deal_pieces(DEALS, d, z):
            local(held.at[pl.ds(base + row, count)], spot(kind, to, count, j), own.at[d])

    def whole(d):
        return held.at[pl.ds(0, DEALS[d][4])]

    dealt = set()
    following = [2]

    def deal_wait(d):
        if d in dealt:
            return
        dealt.add(d)
        for k in range(1, batch):
            pltpu.make_async_copy(whole(d), whole(d), zrecv.at[d, k]).wait()
        pltpu.make_async_copy(whole(d), whole(d), own.at[d]).wait()
        while following[0] <= min(d + AHEAD, len(DEALS) - 1):
            deal(following[0])
            following[0] += 1

    slots = {}
    counter = [0]

    def push(key, mat, row, count, col, width, device):
        s = counter[0]
        counter[0] += 1
        ref = mat.at[pl.ds(row, count), lanes(col, width)]
        slots.setdefault(key, []).append(remote(ref, ref, psend.at[s], precv.at[s], device))

    def stage_a(n):
        kind, row, rows, col = UNITS[n]
        half = rows // 2
        for d in DEALS_OF[n]:
            deal_wait(d)
        push((n, 1), mats[kind], row, half, col + 128 * strip, 128, at_x)
        push((n, 1), mats[kind], row + half, half, col + 128 * strip, 128, at_y)

    def stage_b(n):
        kind, row, rows, col = UNITS[n]
        half = rows // 2
        for copy in slots[(n, 1)]:
            copy.wait_recv()
        push((n, 2), mats[kind], row, half, col + 512 * c + 256 * y, 256, at_y)
        for yy in range(2):
            push((n, 2), mats[kind], row + half, half, col + 512 * c + 256 * yy + 128 * x, 128, at_x)

    def stage_c(n):
        kind, row, rows, col = UNITS[n]
        for copy in slots[(n, 2)]:
            copy.wait_recv()
        push((n, 3), mats[kind], row, rows, col + 512 * c, 512, at_c)

    saves = []

    def ready(n):
        kind, row, rows, col = UNITS[n]
        for copy in slots[(n, 3)]:
            copy.wait_recv()
        ref = (pl.ds(row, rows), pl.ds(col, 1024))
        saves.append(local(mats[kind].at[ref], mats_o[kind].at[ref], wsem.at[n]))

    pumped = [0]
    last_unit = len(UNITS)

    def pump():
        s = pumped[0]
        pumped[0] += 1
        if 0 <= s - 2 < last_unit:
            stage_b(s - 2)
        if s < last_unit:
            stage_a(s)
        if 0 <= s - 3 < last_unit:
            stage_c(s - 3)

    def pump_to(s):
        while pumped[0] <= s:
            pump()

    def save(src, dst, n):
        saves.append(local(src, dst, osem.at[n]))

    take_third(0)
    deal(0)
    send_video(cot_i, cot, 1, own.at[len(DEALS) + 5])
    take_third(1)
    deal(1)
    take_third(2)
    pump_to(0)
    for copy in levels:
        copy.wait()
    row_id = lax.broadcasted_iota(jnp.int32, (384, 1), 0)
    expand = (
        lax.broadcasted_iota(jnp.int32, (384, 64), 1) == 4 * (row_id // 24) + row_id % 4
    ).astype(F32).astype(BF16)

    def mod_tile(n, carry):
        index = 128 * n + lax.broadcasted_iota(jnp.int32, (1, 128), 1)
        row, col = ada_place(index, z)
        pick = (lax.broadcasted_iota(jnp.int32, (1024, 128), 0) == row).astype(F32).astype(BF16)
        wide = dot_nn(expand, dot_nn(cond[...], pick).astype(BF16))
        wide = jnp.where(col == (row_id % 24) // 4, wide, 0.0).astype(BF16)
        spread[:, lanes(128 * n, 128)] = wide
        part = dot_nn(wide, held[pl.ds(pl.multiple_of(128 * n, 128), 128), :])
        return carry + part

    part = jnp.zeros((384, 128), F32)
    part = lax.fori_loop(0, 7, mod_tile, part)
    pump_to(1)
    part = lax.fori_loop(7, 13, mod_tile, part)
    for v in range(16):
        mod[v] = part[24 * v : 24 * v + 24]
    lax.fori_loop(1, 4 * batch, lambda k, t: (mod_group(k, True), t)[1], 0)
    mod_own = local(mod.at[4 * z + f // 2], mod_v.at[z, :, lanes(128 * (f // 2), 128)], own.at[len(DEALS) + 6])
    pump_to(2)
    lax.fori_loop(1, 4 * batch, lambda k, t: (mod_group(k, False), t)[1], 0)
    mod_own.wait()
    half_row = mod_v[0]
    for s in range(1, batch):
        half_row = half_row + mod_v[s]
    mod_half[c] = half_row
    half_copy = remote(mod_half.at[c], mod_half.at[c], hsend, hrecv, at_c)
    save(spread, spread_o, 14)
    half_copy.wait()
    for copy in videos[0]:
        copy.wait()
    save(tok, tok_o, 15)
    for j in range(6):
        for p in range(4):
            value = jnp.zeros((1, 1024), F32)
            for fr in range(4):
                row = [mod_half[e, pl.ds(4 * j + fr, 1), :] for e in range(2)]
                value = value + sel[p][fr] * jnp.concatenate(row, axis=1)
            pm[pl.ds(4 * j + p, 1), :] = value
    save(pm, pm_o, 0)

    def mod_row(j, p):
        return pm[pl.ds(4 * j + p, 1), :]

    step = 32
    for p in range(4):
        shift, scale = mod_row(0, p), mod_row(1, p)

        def one(i, p=p, shift=shift, scale=scale):
            rows = pl.ds(pl.multiple_of(p * piece + i, step), step)
            normed, _ = norm_rows(tok[rows, :].astype(F32))
            h1[rows, :] = (normed * (1.0 + scale) + shift).astype(BF16)

        row_loop(piece, step, one)
    save(h1, h1_o, 1)
    saves_h1 = saves[-1]

    pump_to(4)
    for j in range(3):
        pump_to(3 + j)
        ready(j)

        def cols(n, j=j):
            value = jnp.dot(h1[...], wq[:, lanes(1024 * j + n, 512)], preferred_element_type=F32)
            if j == 0:
                q[:, lanes(n, 512)] = (value * HD ** (-0.5)).astype(BF16)
            else:
                kv[c, :, lanes(1024 * (j - 1) + n, 512)] = value.astype(BF16)

        row_loop(1024, 512, cols)
    save(q, q_o, 2)
    kv_copy = remote(kv.at[c], kv.at[c], kvsend, kvrecv, at_c)
    pump_to(6)
    kv_copy.wait_recv()
    save(kv, kv_o, 3)

    keys = 2 * 4 * piece
    qb_mask = query_mask(ends, piece)
    acc[:, 0:128] = qb_mask
    kmask[...] = key_mask(keys, piece, per).astype(BF16)

    def heads(h):
        pair = lanes(128 * h, 128)
        k_pair = kv[:, :, pair].reshape(keys, 128)
        v_pair = kv[:, :, lanes(1024 + 128 * h, 128)].reshape(keys, 128)
        q_pair = q[:, pair]
        outs, parts = [], []
        for e in range(2):
            mine = lane_half(e)
            s = dot_nt(choose(mine, q_pair, acc[:, 0:128]), choose(mine, k_pair, kmask[...]))
            peak = jnp.max(s, axis=1, keepdims=True)
            w = jnp.exp(s - peak).astype(BF16)
            o = dot_nn(w, choose(mine, v_pair, jnp.ones_like(v_pair)))
            outs.append(o / pltpu.roll(o, 64, 1))
            parts.append(-(peak + jnp.log(jnp.where(mine, 1.0, o))))
        att[:, pair] = choose(lane_half(0), outs[0], outs[1])
        level = jnp.where(lane_half(1), parts[0], parts[1])
        qb[:, pair] = (acc[:, 0:128] + in_lanes(three_parts(level), 4)).astype(BF16)

    for n in range(4):
        lax.fori_loop(2 * n, 2 * n + 2, lambda h, t: (heads(h), t)[1], 0)
        pump_to(7 + n)
    save(att, att_o, 4)
    save(qb, qb_o, 12)

    ready(3)

    def out_cols(n):
        value = dot_nn(att[...], wo[:, lanes(n, 512)])
        acc[:, lanes(n, 512)] = value
        a[:, lanes(n, 512)] = value.astype(BF16)

    row_loop(1024, 512, out_cols)
    save(a, a_o, 5)
    for p in range(4):
        gate, shift, scale = mod_row(2, p), mod_row(3, p), mod_row(4, p)

        def two(i, p=p, gate=gate, shift=shift, scale=scale):
            rows = pl.ds(pl.multiple_of(p * piece + i, step), step)
            middle = tok[rows, :].astype(F32) + gate * acc[rows, :]
            x1[rows, :] = middle
            normed, _ = norm_rows(middle)
            h2[rows, :] = (normed * (1.0 + scale) + shift).astype(BF16)

        row_loop(piece, step, two)
    save(x1, x1_o, 6)
    save(h2, h2_o, 7)

    for j in range(4):
        pump_to(11 + j)
        ready(PLACE["in"][j])

        def in_cols(n, j=j):
            col = 1024 * j + n
            pre = jnp.dot(h2[...], wi[:, lanes(col, 512)], preferred_element_type=F32)
            square = pre * pre
            t = jnp.tanh(GELU_A * (pre + GELU_B * (square * pre)))
            lift = 0.5 * (1.0 + t)
            u[:, lanes(col, 512)] = (pre * lift).astype(BF16)
            slope = lift + (0.5 * GELU_A) * pre * (1.0 - t * t) * (1.0 + 3.0 * GELU_B * square)
            gp[:, lanes(col, 512)] = slope.astype(BF16)

        row_loop(1024, 512, in_cols)
        if j == 0:
            for n in PLACE["down"]:
                ready(n)

        def down_cols(col, j=j):
            part = dot_nn(u[:, 1024 * j : 1024 * j + 1024], wd[1024 * j : 1024 * j + 1024, lanes(col, 512)])
            if j == 0:
                acc[:, lanes(col, 512)] = part
            else:
                acc[:, lanes(col, 512)] = acc[:, lanes(col, 512)] + part

        row_loop(1024, 512, down_cols)
    save(u, u_o, 8)
    save(gp, gp_o, 9)
    saves_h1.wait()
    for copy in videos[1]:
        copy.wait()
    save(cot, cot_o, 13)
    for p in range(4):
        gate = mod_row(5, p)

        def three(i, total_grad, p=p, gate=gate):
            rows = pl.ds(pl.multiple_of(p * piece + i * 16, 16), 16)
            value = acc[rows, :]
            h1[rows, :] = (x1[rows, :] + gate * value).astype(BF16)
            return total_grad + fold_rows(cot[rows, :].astype(F32) * value)

        part = lax.fori_loop(0, piece // 16, three, jnp.zeros((8, 1024), F32))
        dg[pl.ds(p, 1), :] = jnp.sum(part, axis=0, keepdims=True)
    dg[pl.ds(4, 4), :] = jnp.zeros((4, 1024), F32)
    save(dg, dg_o, 10)
    save(h1, y_o, 11)
    for copy in saves:
        if copy is not saves_h1:
            copy.wait()
    kv_copy.wait_send()
    for copies in slots.values():
        for copy in copies:
            copy.wait_send()
    for n in range(3):
        pltpu.make_async_copy(others(n), others(n), csend.at[n]).wait()
    for d in range(len(DEALS)):
        for k in range(1, batch):
            pltpu.make_async_copy(whole(d), whole(d), zsend.at[d, k]).wait()


def forward(inverse, buckets, blk, cond, tok, cot, total, batch, piece, per):
    def out(*shape, dtype=BF16):
        return jax.ShapeDtypeStruct(shape, dtype)

    outs = [out(depth, 1024 * blocks) for _, depth, blocks in KINDS] + [
        out(512, 1024),
        out(512, 1024),
        out(512, 1024),
        out(2, 512, 2048),
        out(512, 1024),
        out(512, 1024),
        out(512, 1024, dtype=F32),
        out(512, 1024),
        out(512, 4096),
        out(512, 4096),
        out(512, 1024),
        out(24, 1024, dtype=F32),
        out(8, 1024, dtype=F32),
        out(512, 1024),
        out(384, ADA),
        out(512, 1024),
    ]
    bufs = [pltpu.VMEM(o.shape, o.dtype) for o in outs[:14]] + [
        pltpu.VMEM((512, 1024), F32),
        pltpu.VMEM((24, 1024), F32),
        pltpu.VMEM((batch, 24, 512), F32),
        pltpu.VMEM((8, 1024), F32),
        pltpu.VMEM((1024, 128), BF16),
        pltpu.VMEM((512, 1024), BF16),
        pltpu.VMEM((512, 1024), BF16),
        pltpu.VMEM((total * GROUP, 128), BF16),
        pltpu.VMEM((64, 1024), BF16),
        pltpu.VMEM((384, ADA), BF16),
        pltpu.VMEM((16, 24, 128), F32),
    ] + [pltpu.VMEM((total, THIRD, 128), BF16) for _ in range(3)]
    bufs.append(pltpu.VMEM((2, 24, 512), F32))
    smem = pl.BlockSpec(memory_space=pltpu.SMEM)
    dma = pltpu.SemaphoreType.DMA
    return pl.pallas_call(
        partial(forward_kernel, total, batch, piece, per),
        out_shape=outs,
        in_specs=[smem, smem] + [ANY] * 4,
        out_specs=[ANY] * len(outs),
        scratch_shapes=bufs
        + [
            dma((len(DEALS), batch)),
            dma((len(DEALS), batch)),
            dma((6 * len(UNITS),)),
            dma((6 * len(UNITS),)),
            dma((total,)),
            dma((total,)),
            dma((len(DEALS) + 7,)),
            dma((len(UNITS),)),
            dma((16,)),
            dma,
            dma,
            dma((2, 4)),
            dma((2, 4)),
            dma((3,)),
            dma((3,)),
            dma((batch,)),
            dma((batch,)),
            dma,
            dma,
        ],
        compiler_params=pltpu.CompilerParams(
            collective_id=1, has_side_effects=True, vmem_limit_bytes=VMEM_LIMIT
        ),
        name="forward",
    )(inverse, buckets, blk, cond, tok, cot)


LEAVES = (
    [(3, 1024 * n, 0) for n in range(4)] + [(2, 0, j) for j in range(4)] + [(1, 0, 0)] + [(0, 0, j) for j in range(3)]
)
DEALS_AFTER = ((), (4,), (6,), (7, 8), (), (), (), (), (3,), (0,), (1,), (2,))


def by_block(row, count):
    found, done = [], 0
    while done < count:
        b, first = divmod(row + done, GROUP)
        rows = min(count - done, GROUP - first)
        found.append((b, first, rows, done))
        done += rows
    return found


def backward_kernel(total, batch, piece, per, buckets, owned, pm, dg, *refs):
    wq, wo, wi, wd, h1_i, q_i, qb_i, kv_i, att_i, a_i, x1_i, h2_i, gp_i, u_i, y_i, cot_i, spread_i, tok_i = refs[:18]
    blk, grad_o, act_o = refs[18:21]
    big1, big2, big3, wa, wb, f1, f2, s1, s2, s3, s4, kv_got, dmv, dmf, kmask, ring = refs[21:37]
    got, half_sum, strip_sum, zgot = refs[37:41], refs[41:45], refs[45:49], refs[49]
    ordered, picked, dmf_got, dmod = refs[50:54]
    psend, precv, zsend, zrecv, msend, mrecv, vsend, vrecv, xsend, xrecv, lsem, asem, bsem = refs[54:67]
    gsend, grecv, hsend, hrecv = refs[67:]
    y, x, c, z, at_x, at_y, at_c = plane()
    f = 4 * y + 2 * x + c
    me = f * batch + z

    def load(src, dst, n):
        return local(src, dst, lsem.at[n])

    cot_l = load(cot_i, s3, 0)
    u_l = [load(u_i.at[:, pl.ds(1024 * n, 1024)], big1.at[:, pl.ds(1024 * n, 1024)], 1 + n) for n in range(4)]
    h2_l = load(h2_i, s2, 5)
    gp_l = load(gp_i, big2, 6)
    x1_l = load(x1_i, f2, 7)
    a_l = load(a_i, s4, 8)
    down_tiles = [wd.at[pl.ds(512 * t, 512)] for t in range(8)] + [wo.at[pl.ds(512 * t, 512)] for t in range(2)]
    in_tiles = [wi.at[:, pl.ds(512 * t, 512)] for t in range(8)] + [wq.at[:, pl.ds(512 * t, 512)] for t in range(6)]
    fetched = {}

    def fetch(tiles, buf, sem, t):
        if t < len(tiles):
            fetched[id(tiles), t] = local(tiles[t], buf.at[t % 2], sem.at[t % 2])

    for t in range(2):
        fetch(down_tiles, wb, bsem, t)
        fetch(in_tiles, wa, asem, t)

    def tile(tiles, buf, t):
        fetched[id(tiles), t].wait()
        return buf[t % 2]

    greet_all(total, batch)
    mine, g = f // per, f % per
    sel, _ = frames_of(buckets, mine, g, piece, per)
    videos = []

    def send_video(s, part, dst, n):
        for k in range(1, 4):
            v = (mine + k) % 4
            videos.append(remote(part(v), dst.at[mine], vsend.at[s, k], vrecv.at[s, k], (v * per + g, z)))
        videos.append(local(part(mine), dst.at[mine], lsem.at[n]))

    slots = {}
    counter = [0]

    def push(key, src, dst, device):
        s = counter[0]
        counter[0] += 1
        slots.setdefault(key, []).append(remote(src, dst, psend.at[s], precv.at[s], device))

    def arrive(key):
        for copy in slots[key]:
            copy.wait_recv()

    def emit(n, left, right):
        m, row, j = LEAVES[n]
        for w in range(2):
            ring[n % 2, :, 512 * w : 512 * w + 512] = dot_tn(left, right[:, 512 * w : 512 * w + 512]).astype(BF16)
        push(
            (n, 0),
            ring.at[n % 2, :, lanes(512 * (1 - c), 512)],
            got[m].at[pl.ds(row, 1024), pl.ds(512 * j, 512)],
            at_c,
        )

    def add_block(dst, dst_row, dst_col, src, src_row, src_col, width, count):
        def body(i, carry):
            to = pl.ds(pl.multiple_of(dst_row + i * 128, 128), 128)
            at = pl.ds(pl.multiple_of(src_row + i * 128, 128), 128)
            dst[to, lanes(dst_col, width)] = dst[to, lanes(dst_col, width)] + src[at, lanes(src_col, width)]
            return carry

        lax.fori_loop(0, count // 128, body, 0)

    def absorb(n):
        m, row, j = LEAVES[n]
        arrive((n, 0))
        add_block(got[m], row, 512 * j, ring.at[n % 2], 0, 512 * c, 512, 1024)
        for copy in slots[(n, 0)]:
            copy.wait_send()

    def step1(n):
        m, row, j = LEAVES[n]
        for yy in range(2):
            push(
                (n, 1),
                got[m].at[pl.ds(row, 512), lanes(512 * j + 256 * yy + 128 * (1 - x), 128)],
                half_sum[m].at[pl.ds(row, 512), lanes(256 * j + 128 * yy, 128)],
                at_x,
            )
        push(
            (n, 1),
            got[m].at[pl.ds(row + 512, 512), lanes(512 * j + 256 * (1 - y), 256)],
            half_sum[m].at[pl.ds(row + 512, 512), lanes(256 * j, 256)],
            at_y,
        )

    def step2(n):
        m, row, j = LEAVES[n]
        arrive((n, 1))
        for yy in range(2):
            add_block(half_sum[m], row, 256 * j + 128 * yy, got[m], row, 512 * j + 256 * yy + 128 * x, 128, 512)
        add_block(half_sum[m], row + 512, 256 * j, got[m], row + 512, 512 * j + 256 * y, 256, 512)
        push(
            (n, 2),
            half_sum[m].at[pl.ds(row, 512), lanes(256 * j + 128 * (1 - y), 128)],
            strip_sum[m].at[pl.ds(row, 512), lanes(128 * j, 128)],
            at_y,
        )
        push(
            (n, 2),
            half_sum[m].at[pl.ds(row + 512, 512), lanes(256 * j + 128 * (1 - x), 128)],
            strip_sum[m].at[pl.ds(row + 512, 512), lanes(128 * j, 128)],
            at_x,
        )

    def step3(n):
        m, row, j = LEAVES[n]
        arrive((n, 2))
        add_block(strip_sum[m], row, 128 * j, half_sum[m], row, 256 * j + 128 * y, 128, 512)
        add_block(strip_sum[m], row + 512, 128 * j, half_sum[m], row + 512, 256 * j + 128 * x, 128, 512)
        if m == 2:

            @pl.when(z != j)
            def _():
                k = (j - z + batch) % batch
                remote(
                    strip_sum[m].at[:, pl.ds(128 * j, 128)],
                    zgot.at[k - 1, pl.ds(1120, 1024)],
                    zsend.at[IN_DEAL, k],
                    zrecv.at[IN_DEAL, k],
                    (f, j),
                )

        for d in DEALS_AFTER[n]:
            for k in range(1, batch):
                to = (z + k) % batch
                for held_row, count, at, col in deal_pieces(BACK_DEALS, d, to):
                    remote(
                        strip_sum[m].at[pl.ds(pl.multiple_of(at, 16), count), lanes(128 * col, 128)],
                        zgot.at[k - 1, pl.ds(held_row, count)],
                        zsend.at[d, k],
                        zrecv.at[d, k],
                        (f, to),
                    )

    pumped = [0]

    def pump_to(r):
        while pumped[0] <= r:
            n = pumped[0]
            pumped[0] += 1
            if 0 <= n - 2 < 12:
                step2(n - 2)
            if n < 12:
                step1(n)
            if 0 <= n - 3 < 12:
                step3(n - 3)

    def whole(d, k):
        return zgot.at[k - 1, pl.ds(0, BACK_DEALS[d][4])]

    def last(d):
        m = [kind for kind, _, _ in KINDS].index(BACK_DEALS[d][0])
        for k in range(1, batch):
            pltpu.make_async_copy(whole(d, k), whole(d, k), zrecv.at[d, k]).wait()
        for row, count, at, j in deal_pieces(BACK_DEALS, d, z):
            for b, first, rows, skip in by_block(row, count):
                value = strip_sum[m][pl.ds(pl.multiple_of(at + skip, 16), rows), lanes(128 * j, 128)].astype(F32)
                for k in range(batch - 1):
                    value = value + zgot[k, row + skip : row + skip + rows, :].astype(F32)
                ordered[FIRST + b, first : first + rows, :] = value.astype(BF16)

    def mod_row(j, p):
        return pm[pl.ds(4 * j + p, 1), :]

    def by_rows(p, body, sums):
        def one(i, carry):
            return body(pl.ds(pl.multiple_of(p * piece + i * 16, 16), 16), *carry)

        start = tuple(jnp.zeros((8, 1024), F32) for _ in range(sums))
        return [jnp.sum(s, axis=0, keepdims=True) for s in lax.fori_loop(0, piece // 16, one, start)]

    cot_l.wait()
    for p in range(4):
        gate = mod_row(5, p)

        def d_mlp(rows, gate=gate):
            s1[rows, :] = (gate * s3[rows, :].astype(F32)).astype(BF16)
            return ()

        by_rows(p, d_mlp, 0)
        dmv[pl.ds(20 + p, 1), :] = dg[pl.ds(p, 1), :]
    for n in range(4):
        u_l[n].wait()
        emit(n, big1[:, 1024 * n : 1024 * n + 1024], s1)
        if n >= 1:
            absorb(n - 1)
        if n == 1:
            pump_to(0)
    kv_l = [load(kv_i.at[d], big1.at[:, pl.ds(2048 * d, 2048)], 10 + d) for d in range(2)]
    gp_l.wait()
    for t in range(8):
        cols = slice(512 * t, 512 * t + 512)
        d_act = dot_nt(s1[...], tile(down_tiles, wb, t))
        big3[:, cols] = (d_act * big2[:, cols].astype(F32)).astype(BF16)
        fetch(down_tiles, wb, bsem, t + 2)
        if t == 0:
            absorb(3)
        if t == 3:
            pump_to(1)
    h2_l.wait()
    for j in range(4):
        emit(4 + j, s2[...], big3.at[:, 1024 * j : 1024 * j + 1024])
        if j >= 1:
            absorb(3 + j)
        if j == 1:
            pump_to(2)
    att_l = load(att_i, s2, 5)
    for t in range(8):
        part = dot_nt(big3[:, 512 * t : 512 * t + 512], tile(in_tiles, wa, t))
        f1[...] = part if t == 0 else f1[...] + part
        fetch(in_tiles, wa, asem, t + 2)
        if t == 0:
            absorb(7)
        if t == 5:
            pump_to(3)
    qb_l = load(qb_i, big3.at[:, pl.ds(3072, 1024)], 6)

    x1_l.wait()
    a_l.wait()
    for p in range(4):
        gate, scale = mod_row(2, p), mod_row(4, p)

        def back_two(rows, d_scale, d_shift, d_gate, gate=gate, scale=scale):
            normed, inv_std = norm_rows(f2[rows, :])
            d_h = f1[rows, :]
            d_mid = s3[rows, :].astype(F32) + norm_back(d_h * (1.0 + scale), normed, inv_std)
            f2[rows, :] = d_mid
            s1[rows, :] = (gate * d_mid).astype(BF16)
            return (
                d_scale + fold_rows(d_h * normed),
                d_shift + fold_rows(d_h),
                d_gate + fold_rows(d_mid * s4[rows, :].astype(F32)),
            )

        d_scale, d_shift, d_gate = by_rows(p, back_two, 3)
        dmv[pl.ds(16 + p, 1), :] = d_scale
        dmv[pl.ds(12 + p, 1), :] = d_shift
        dmv[pl.ds(8 + p, 1), :] = d_gate
    q_l = load(q_i, s4, 8)
    pump_to(4)

    att_l.wait()
    emit(8, s2[...], s1)
    for t in range(2):
        s3[:, 512 * t : 512 * t + 512] = dot_nt(s1[...], tile(down_tiles, wb, 8 + t)).astype(BF16)
    h1_l = load(h1_i, wb.at[0], 7)
    tok_l = load(tok_i, wb.at[1], 12)
    absorb(8)

    keys = 2 * 4 * piece
    kmask[...] = key_mask(keys, piece, per).astype(BF16)
    for copy in kv_l:
        copy.wait()
    qb_l.wait()
    q_l.wait()

    def heads(h):
        pair = lanes(128 * h, 128)
        k_pair = jnp.concatenate([big1[:, lanes(2048 * d + 128 * h, 128)] for d in range(2)], axis=0)
        v_pair = jnp.concatenate([big1[:, lanes(2048 * d + 1024 + 128 * h, 128)] for d in range(2)], axis=0)
        dks, dvs, dqs = [], [], []
        first = lane_half(0)
        ones = in_lanes([1.0, 1.0, 1.0], 0)
        for e in range(2):
            mask = lane_half(e)
            k_e = choose(mask, k_pair, kmask[...])
            v_e = choose(mask, v_pair, ones)
            dk = dv = 0.0
            dq = []
            for w in range(2):
                rows = slice(256 * w, 256 * w + 256)
                q_w, d_w, o_w = s4[rows, pair], s3[rows, pair], s2[rows, pair]
                q_e = choose(mask, q_w, big3[rows, lanes(3072 + 128 * h, 128)])
                dot_rows = jnp.sum(
                    jnp.where(mask, d_w.astype(F32) * o_w.astype(F32), 0.0), axis=1, keepdims=True
                )
                d_e = choose(mask, d_w, in_lanes(three_parts(-dot_rows), 0))
                prob = jnp.exp(dot_nt(k_e, q_e))
                d_s = (prob * dot_nt(v_e, d_e)).astype(BF16)
                dv = dv + dot_nn(prob.astype(BF16), d_w)
                dk = dk + dot_nn(d_s, q_w)
                dq.append(dot_tn(d_s, k_pair))
            dks.append(dk)
            dvs.append(dv)
            dqs.append(jnp.concatenate(dq, axis=0))
        dk = choose(first, dks[0], dks[1])
        dv = choose(first, dvs[0], dvs[1])
        big3[:, pair] = (choose(first, dqs[0], dqs[1]).astype(F32) * HD ** (-0.5)).astype(BF16)
        for d in range(2):
            big2[:, lanes(2048 * d + 128 * h, 128)] = dk[512 * d : 512 * d + 512]
            big2[:, lanes(2048 * d + 1024 + 128 * h, 128)] = dv[512 * d : 512 * d + 512]

    exchanges = []
    for h in range(8):
        lax.fori_loop(h, h + 1, lambda n, t: (heads(n), t)[1], 0)
        if h % 4 == 3:
            for part in range(2):
                at = 1024 * part + 512 * (h // 4)
                s = len(exchanges)
                exchanges.append(
                    remote(
                        big2.at[:, lanes(2048 * (1 - c) + at, 512)],
                        kv_got.at[:, pl.ds(at, 512)],
                        xsend.at[s],
                        xrecv.at[s],
                        at_c,
                    )
                )
        if h % 2 == 0:
            pump_to(5 + h // 2)

    spread_l = load(spread_i, big1.at[pl.ds(0, 384), pl.ds(0, ADA)], 10)
    h1_l.wait()
    emit(9, wb[0], big3.at[:, 0:1024])
    for copy in exchanges:
        copy.wait_recv()
    for part in range(2):

        def join(i, carry, part=part):
            rows = pl.ds(pl.multiple_of(i * 64, 64), 64)
            value = big2[rows, lanes(2048 * c + 1024 * part, 1024)].astype(F32) + kv_got[
                rows, 1024 * part : 1024 * part + 1024
            ].astype(F32)
            big3[rows, 1024 + 1024 * part : 2048 + 1024 * part] = value.astype(BF16)
            return carry

        lax.fori_loop(0, 8, join, 0)
        emit(10 + part, wb[0], big3.at[:, 1024 + 1024 * part : 2048 + 1024 * part])
        absorb(9 + part)
        pump_to(9 + part)
    for t in range(6):
        part = dot_nt(big3[:, 512 * t : 512 * t + 512], tile(in_tiles, wa, 8 + t))
        f1[...] = part if t == 0 else f1[...] + part
        fetch(in_tiles, wa, asem, 8 + t + 2)
        if t == 0:
            absorb(11)
        if t == 2:
            pump_to(11)

    tok_l.wait()
    for p in range(4):
        scale = mod_row(1, p)

        def back_one(rows, d_scale, d_shift, scale=scale):
            normed, inv_std = norm_rows(wb[1, rows, :].astype(F32))
            d_h = f1[rows, :]
            s1[rows, :] = (f2[rows, :] + norm_back(d_h * (1.0 + scale), normed, inv_std)).astype(BF16)
            return d_scale + fold_rows(d_h * normed), d_shift + fold_rows(d_h)

        d_scale, d_shift = by_rows(p, back_one, 2)
        dmv[pl.ds(4 + p, 1), :] = d_scale
        dmv[pl.ds(p, 1), :] = d_shift
    send_video(0, lambda v: s1.at[pl.ds(pl.multiple_of(v * piece, piece), piece)], grad_o, 0)
    for j in range(6):
        for fr in range(4):
            value = sel[0][fr] * dmv[pl.ds(4 * j, 1), :]
            for p in range(1, 4):
                value = value + sel[p][fr] * dmv[pl.ds(4 * j + p, 1), :]
            dmf[pl.ds(4 * j + fr, 1), :] = value
    half_copy = remote(dmf, dmf_got, hsend, hrecv, at_c)

    def mod_group(k, start):
        other = (f // 2 * batch + z + k) % (4 * batch)
        chip, oz = other // batch, other % batch
        copy = pltpu.make_async_remote_copy(
            src_ref=dmf_got.at[:, lanes(512 * c + 128 * chip, 128)],
            dst_ref=dmod.at[4 * z + f // 2],
            send_sem=msend.at[k],
            recv_sem=mrecv.at[k],
            device_id=(2 * chip + c, oz),
            device_id_type=MESH,
        )
        if start:
            copy.start()
        else:
            copy.wait()

    pump_to(12)
    half_copy.wait()
    dmf_got[...] = dmf_got[...] + dmf[...]
    lax.fori_loop(1, 4 * batch, lambda k, u: (mod_group(k, True), u)[1], 0)
    dmod[4 * z + f // 2] = dmf_got[:, lanes(512 * c + 128 * (f // 2), 128)]
    for d in (4, 6, 7, 8):
        last(d)
    pump_to(13)
    send_video(1, lambda v: y_i.at[v], act_o, 1)
    last(IN_DEAL)
    last(3)
    last(0)
    pump_to(14)

    spread_l.wait()
    lax.fori_loop(1, 4 * batch, lambda k, u: (mod_group(k, False), u)[1], 0)
    parts = [part.astype(BF16) for part in three_parts(dmod[...].reshape(384, 128))]
    for n in range(ADA // 128):
        wide = big1[0:384, 128 * n : 128 * n + 128]
        value = (dot_tn(wide, parts[0]) + dot_tn(wide, parts[1]) + dot_tn(wide, parts[2])).astype(BF16)
        spans = [(0, FIRST * GROUP)]
        spans += [(FIRST * GROUP + THIRD * q + 16, FIRST * GROUP + THIRD * q + THIRD) for q in range(3)]
        for lo, hi in spans:
            lo, hi = max(lo, 128 * n), min(hi, 128 * n + 128)
            for b, first, rows, skip in by_block(lo, max(hi - lo, 0)):
                ordered[b, first : first + rows, :] = value[lo - 128 * n + skip : lo - 128 * n + skip + rows]
    for d in (1, 2):
        last(d)

    def spot(of, oz):
        return blk.at[pl.ds(pl.multiple_of(GROUP * oz, 16), GROUP), lanes(128 * strip_of(of), 128)]

    def to_owner(k, start):
        other = (me + k) % total
        copy = pltpu.make_async_remote_copy(
            src_ref=picked.at[other],
            dst_ref=spot(f, z),
            send_sem=gsend.at[k],
            recv_sem=grecv.at[k],
            device_id=(other // batch, other % batch),
            device_id_type=MESH,
        )
        if start:
            copy.start()
        else:
            copy.wait()

    def pick(d, carry):
        picked[d] = ordered[owned[d]]
        return carry

    lax.fori_loop(0, total, pick, 0)
    lax.fori_loop(1, total, lambda k, u: (to_owner(k, True), u)[1], 0)
    blk_own = local(picked.at[me], spot(f, z), lsem.at[2])
    for n, copies in slots.items():
        if n[1] > 0:
            for copy in copies:
                copy.wait_send()
    for d in range(len(BACK_DEALS)):
        for k in range(1, batch):
            pltpu.make_async_copy(whole(d, k), whole(d, k), zsend.at[d, k]).wait()
    for copy in exchanges:
        copy.wait_send()
    for copy in videos:
        copy.wait()
    blk_own.wait()
    lax.fori_loop(1, total, lambda k, u: (to_owner(k, False), u)[1], 0)


def backward(buckets, owned, pm, dg, arrays, total, batch, piece, per):
    def sums(width):
        return [pltpu.VMEM((depth, blocks * width), BF16) for _, depth, blocks in KINDS]

    def buf(*shape, dtype=BF16):
        return pltpu.VMEM(shape, dtype)

    whole = pl.BlockSpec(memory_space=pltpu.VMEM)
    dma = pltpu.SemaphoreType.DMA
    return pl.pallas_call(
        partial(backward_kernel, total, batch, piece, per),
        out_shape=[
            jax.ShapeDtypeStruct((ROWS, 1024), BF16),
            jax.ShapeDtypeStruct((4, piece, 1024), BF16),
            jax.ShapeDtypeStruct((4, piece, 1024), BF16),
        ],
        in_specs=[pl.BlockSpec(memory_space=pltpu.SMEM)] * 2 + [whole, whole] + [ANY] * len(arrays),
        out_specs=[ANY, ANY, ANY],
        scratch_shapes=[buf(512, 4096) for _ in range(3)]
        + [buf(2, 1024, 512), buf(2, 512, 1024)]
        + [buf(512, 1024, dtype=F32) for _ in range(2)]
        + [buf(512, 1024) for _ in range(4)]
        + [buf(512, 2048), buf(24, 1024, dtype=F32), buf(24, 1024, dtype=F32), buf(1024, 128), buf(2, 1024, 1024)]
        + sums(512)
        + sums(256)
        + sums(128)
        + [buf(batch - 1, HELD, 128), buf(total, GROUP, 128), buf(total, GROUP, 128)]
        + [buf(24, 1024, dtype=F32), buf(16, 24, 128, dtype=F32)]
        + [
            dma((72,)),
            dma((72,)),
            dma((len(BACK_DEALS), batch)),
            dma((len(BACK_DEALS), batch)),
            dma((4 * batch,)),
            dma((4 * batch,)),
            dma((2, 4)),
            dma((2, 4)),
            dma((4,)),
            dma((4,)),
            dma((13,)),
            dma((2,)),
            dma((2,)),
            dma((total,)),
            dma((total,)),
            dma,
            dma,
        ],
        compiler_params=pltpu.CompilerParams(
            collective_id=2, has_side_effects=True, vmem_limit_bytes=VMEM_LIMIT
        ),
        name="backward",
    )(buckets, owned, pm, dg, *arrays)


def own_rows_of(owned, table, me):
    return table[pl.ds(owned[me], 1), :]


def cut_kernel(batch, owned, table, master, out):
    f, z = frame_index()
    rows = own_rows_of(owned, table, f * batch + z)
    swap = (rows == lax.broadcasted_iota(jnp.int32, (ROWS, ROWS), 0)).astype(F32).astype(BF16)
    for s in range(8):
        strip = master[pl.ds(s, ROWS, stride=8), :].astype(BF16)
        out[:, 128 * s : 128 * s + 128] = dot_tn(swap, strip).astype(BF16)


def cut_owned(owned, table, master, batch):
    whole = pl.BlockSpec(memory_space=pltpu.VMEM)
    return pl.pallas_call(
        partial(cut_kernel, batch),
        out_shape=jax.ShapeDtypeStruct((ROWS, 1024), BF16),
        in_specs=[pl.BlockSpec(memory_space=pltpu.SMEM), whole, whole],
        out_specs=whole,
        compiler_params=pltpu.CompilerParams(vmem_limit_bytes=VMEM_LIMIT),
        name="cut_owned",
    )(owned, table, master)


def adam(grad, master, first, second):
    new_first = BETA_ONE * first + (1.0 - BETA_ONE) * grad
    new_second = BETA_TWO * second + (1.0 - BETA_TWO) * grad * grad
    fix_one = 1.0 - BETA_ONE**STEP
    fix_two = 1.0 - BETA_TWO**STEP
    update = new_first / fix_one / (jnp.sqrt(new_second / fix_two) + ADAM_EPS)
    return master - LEARN_RATE * (update + WEIGHT_DECAY * master), new_first, new_second


def update_kernel(batch, owned, table, grad, master, first, second, new_master, new_first, new_second):
    f, z = frame_index()
    rows = own_rows_of(owned, table, f * batch + z)
    base = pl.program_id(0) * GROUP
    swap = (rows == base + lax.broadcasted_iota(jnp.int32, (GROUP, ROWS), 0)).astype(F32).astype(BF16)
    for s in range(8):
        at = pl.ds(s, GROUP, stride=8)
        value = dot_nn(swap, grad[:, 128 * s : 128 * s + 128])
        new_master[at, :], new_first[at, :], new_second[at, :] = adam(
            value, master[at, :], first[at, :], second[at, :]
        )


def update_owned(owned, table, grad, master, first, second, batch):
    part = pl.BlockSpec((8 * GROUP, 128), lambda i: (i, 0))
    return pl.pallas_call(
        partial(update_kernel, batch),
        grid=(ROWS // GROUP,),
        out_shape=[jax.ShapeDtypeStruct(master.shape, F32)] * 3,
        in_specs=[
            pl.BlockSpec(memory_space=pltpu.SMEM),
            pl.BlockSpec(table.shape, lambda i: (0, 0)),
            pl.BlockSpec((ROWS, 1024), lambda i: (0, 0)),
            part,
            part,
            part,
        ],
        out_specs=[part] * 3,
        compiler_params=pltpu.CompilerParams(vmem_limit_bytes=VMEM_LIMIT),
        name="update_owned",
    )(owned, table, grad, master, first, second)


def key_positions(rows, piece, per):
    i = lax.broadcasted_iota(jnp.int32, (rows, 1), 0)
    local_rows = rows // per
    return ((i % local_rows) // piece * per + i // local_rows) * piece + i % piece


def scores_t(k, q, ends, piece, per):
    s = lax.dot_general(k, q, (((1,), (1,)), ((), ())), preferred_element_type=F32)
    pos = key_positions(k.shape[0], piece, per)
    cols = []
    for t in range(q.shape[0] // piece):
        part = s[:, t * piece : (t + 1) * piece]
        cols.append(jnp.where(pos < ends[t], part, NEG_FILL))
    return jnp.concatenate(cols, axis=1)


def attend_kernel(piece, per, ends, q, k, v, o):
    outs = []
    for a in range(2):
        cut = slice(64 * a, 64 * a + 64)
        s = scores_t(k[:, cut], q[:, cut], ends, piece, per)
        peak = jnp.max(s, axis=0, keepdims=True)
        e = jnp.exp(s - peak)
        p = (e * (1.0 / jnp.sum(e, axis=0, keepdims=True))).astype(BF16)
        outs.append(lax.dot_general(p, v[:, cut], (((0,), (0,)), ((), ())), preferred_element_type=F32))
    o[...] = jnp.concatenate(outs, axis=1).astype(BF16)


def attend(ends, q, kv, piece, per):
    rows, width = q.shape
    keys = kv.shape[0]
    pairs = width // 128
    return pl.pallas_call(
        partial(attend_kernel, piece, per),
        grid_spec=pltpu.PrefetchScalarGridSpec(
            num_scalar_prefetch=1,
            grid=(pairs,),
            in_specs=[
                pl.BlockSpec((rows, 128), lambda h, e: (0, h)),
                pl.BlockSpec((keys, 128), lambda h, e: (0, h)),
                pl.BlockSpec((keys, 128), lambda h, e: (0, h + pairs)),
            ],
            out_specs=pl.BlockSpec((rows, 128), lambda h, e: (0, h)),
        ),
        out_shape=jax.ShapeDtypeStruct((rows, width), BF16),
        compiler_params=pltpu.CompilerParams(vmem_limit_bytes=VMEM_LIMIT),
        cost_estimate=pl.CostEstimate(
            flops=4 * rows * keys * width, bytes_accessed=4 * (rows + keys) * width, transcendentals=rows * keys * H
        ),
        name="attend",
    )(ends, q, kv, kv)


def attend_back_kernel(piece, per, ends, q, k, v, do, dq, dk, dv):
    dqs, dks, dvs = [], [], []
    for a in range(2):
        cut = slice(64 * a, 64 * a + 64)
        qa, ka, va, da = q[:, cut], k[:, cut], v[:, cut], do[:, cut]
        s = scores_t(ka, qa, ends, piece, per)
        peak = jnp.max(s, axis=0, keepdims=True)
        e = jnp.exp(s - peak)
        p = e * (1.0 / jnp.sum(e, axis=0, keepdims=True))
        dvs.append(jnp.dot(p.astype(BF16), da, preferred_element_type=F32))
        dp = lax.dot_general(va, da, (((1,), (1,)), ((), ())), preferred_element_type=F32)
        pdp = p * dp
        row = jnp.sum(pdp, axis=0, keepdims=True)
        ds = (pdp - p * row).astype(BF16)
        dks.append(jnp.dot(ds, qa, preferred_element_type=F32))
        dqs.append(lax.dot_general(ds, ka, (((0,), (0,)), ((), ())), preferred_element_type=F32))
    dq[...] = jnp.concatenate(dqs, axis=1).astype(BF16)
    dk[...] = jnp.concatenate(dks, axis=1).astype(BF16)
    dv[...] = jnp.concatenate(dvs, axis=1).astype(BF16)


def attend_back(ends, q, kv, do, piece, per):
    rows, width = q.shape
    keys = kv.shape[0]
    pairs = width // 128
    mine = pl.BlockSpec((rows, 128), lambda h, e: (0, h))
    allk = pl.BlockSpec((keys, 128), lambda h, e: (0, h))
    return pl.pallas_call(
        partial(attend_back_kernel, piece, per),
        grid_spec=pltpu.PrefetchScalarGridSpec(
            num_scalar_prefetch=1,
            grid=(pairs,),
            in_specs=[mine, allk, pl.BlockSpec((keys, 128), lambda h, e: (0, h + pairs)), mine],
            out_specs=[mine, allk, allk],
        ),
        out_shape=[
            jax.ShapeDtypeStruct((rows, width), BF16),
            jax.ShapeDtypeStruct((keys, width), BF16),
            jax.ShapeDtypeStruct((keys, width), BF16),
        ],
        compiler_params=pltpu.CompilerParams(vmem_limit_bytes=VMEM_LIMIT),
        cost_estimate=pl.CostEstimate(
            flops=10 * rows * keys * width, bytes_accessed=6 * (rows + keys) * width, transcendentals=rows * keys * H
        ),
        name="attend_back",
    )(ends, q, kv, kv, do)


def layer_stats(values):
    centre = values - jnp.mean(values, axis=-1, keepdims=True)
    inv_std = lax.rsqrt(jnp.mean(centre * centre, axis=-1, keepdims=True) + 1e-06)
    return (centre * inv_std, inv_std)


def norm_back(upstream, normed, inv_std):
    mean_grad = jnp.mean(upstream, axis=-1, keepdims=True)
    mean_cross = jnp.mean(upstream * normed, axis=-1, keepdims=True)
    return inv_std * (upstream - mean_grad - normed * mean_cross)


def noise_embedding(levels, feature_width):
    half_width = feature_width // 2
    frequencies = jnp.exp(
        -math.log(10000.0) * jnp.arange(half_width, dtype=jnp.float32) / half_width
    )
    angles = levels.astype(jnp.float32)[:, None] * frequencies[None, :]
    return jnp.concatenate([jnp.cos(angles), jnp.sin(angles)], axis=1)


def silu_embedding(levels, width):
    return jax.nn.silu(noise_embedding(levels, width)).astype(BF16)


def split_flat(flat_values, model_width, hidden_width):
    matrix_shapes = (
        (model_width, 6 * model_width),
        (model_width, 3 * model_width),
        (model_width, model_width),
        (model_width, hidden_width),
        (hidden_width, model_width),
    )
    matrices = []
    offset_now = 0
    for matrix_shape in matrix_shapes:
        entry_count = matrix_shape[0] * matrix_shape[1]
        matrices.append(flat_values[offset_now : offset_now + entry_count].reshape(matrix_shape))
        offset_now = offset_now + entry_count
    return matrices


def shards(
    frame_size,
    batch_size,
    tokens,
    out_cotangent,
    buckets,
    noise_levels,
    owned_block,
    master,
    first_moment,
    second_moment,
):
    micro_count, piece, width = tokens.shape
    block_size = master.shape[1]
    frame_count = noise_levels.shape[1]
    total = frame_size * batch_size
    videos = micro_count
    per = frame_size // videos
    rows = videos * piece
    keys = rows * per
    q_scale = HD ** (-0.5)
    f, z = frame_index()
    me = f * batch_size + z
    mine, g = f // per, f % per
    direct = frame_size == 8 and batch_size == 4 and block_size == ROWS * 1024 and videos == 4 and frame_count == 4

    if direct:
        order = jnp.arange(total, dtype=jnp.int32)
        inverse = jnp.sum(jnp.where(owned_block[None, :] == order[:, None], order[None, :], 0), axis=1)
        table = jnp.asarray(np.stack([block_rows(b) for b in range(total)]).astype(np.int32))
        blk = cut_owned(owned_block, table, master.reshape(-1, 128), batch_size)
        cond = silu_embedding(noise_levels.reshape(16), width)
    else:
        tok, cot = swap_videos([tokens, out_cotangent], videos, per, 0)
        gathered = lax.all_gather(master.astype(BF16), ("frame", "batch"), axis=0, tiled=True)
        placed = jnp.take(gathered, jnp.argsort(owned_block), axis=0).reshape(-1)
        w_ada, w_qkv, w_out, w_in, w_down = split_flat(placed, width, FF)
        cond = silu_embedding(lax.dynamic_index_in_dim(noise_levels, mine, 0, keepdims=False), width)
        modulation = jnp.dot(cond, w_ada, preferred_element_type=F32).reshape(frame_count, 6, width)

    def flat(a):
        return a.reshape(rows, a.shape[-1])

    def cube(a):
        return a.reshape(videos, piece, a.shape[-1])

    def partners(k):
        return [(i, i // per * per + (i + k) % per) for i in range(frame_size)]

    def split_mod(piece_mod):
        return [piece_mod[j][:, None, :] for j in range(6)]

    if direct:
        saved = forward(inverse, buckets, blk, cond, tokens, out_cotangent, total, batch_size, piece, per)
        *saved, block_output, piece_mod, d_gate, cot, cond_all, tokens_own = saved
        grad_block, input_grads, outputs = backward(
            buckets,
            owned_block,
            piece_mod,
            d_gate,
            [*saved, cube(block_output), cot, cond_all, tokens_own],
            total,
            batch_size,
            piece,
            per,
        )
    else:
        frame_len = FRAME_LO * (1 + 3 * buckets[mine])
        piece_at = (jnp.arange(videos, dtype=jnp.int32) * per + g) * piece
        piece_frame = piece_at // frame_len
        ends = (piece_frame + 1) * frame_len
        selector = (piece_frame[:, None] == jnp.arange(frame_count, dtype=jnp.int32)[None, :]).astype(F32)
        x_float = tok.astype(F32)
        normed_one, inv_one = layer_stats(x_float)
        piece_mod = jnp.einsum("pf,fjd->jpd", selector, modulation, precision=HIGHEST)
        shift_one, scale_one, gate_one, shift_two, scale_two, gate_two = split_mod(piece_mod)

        h_one = flat((normed_one * (1.0 + scale_one) + shift_one).astype(BF16))
        projected = jnp.dot(h_one, w_qkv, preferred_element_type=F32)
        queries = (projected[:, :width] * q_scale).astype(BF16)
        kv_own = projected[:, width:].astype(BF16)

        kv_all = jnp.zeros((per, rows, 2 * width), BF16)
        kv_all = lax.dynamic_update_index_in_dim(kv_all, kv_own, g, 0)
        for k in range(1, per):
            kv_all = lax.dynamic_update_index_in_dim(
                kv_all, lax.ppermute(kv_own, "frame", partners(k)), (g + per - k) % per, 0
            )
        kv_all = kv_all.reshape(keys, 2 * width)
        attended = attend(ends, queries, kv_all, piece, per)
        attn_out = jnp.dot(attended, w_out, preferred_element_type=F32)
        middle = x_float + gate_one * cube(attn_out)
        normed_two, inv_two = layer_stats(middle)
        h_two = flat((normed_two * (1.0 + scale_two) + shift_two).astype(BF16))
        pre_act = jnp.dot(h_two, w_in, preferred_element_type=F32)
        activated, gelu_back = jax.vjp(partial(jax.nn.gelu, approximate=True), pre_act)
        act_low = activated.astype(BF16)
        slope = gelu_back(jnp.ones_like(pre_act))[0]
        mlp_out = jnp.dot(act_low, w_down, preferred_element_type=F32)
        block_output = (middle + gate_two * cube(mlp_out)).astype(BF16)

        grad_out = cot.astype(F32)
        d_mlp = flat((gate_two * grad_out).astype(BF16))
        g_down = jnp.dot(act_low.T, d_mlp, preferred_element_type=F32).astype(BF16)
        d_act = jnp.dot(d_mlp, w_down.T, preferred_element_type=F32)
        d_pre = (d_act * slope.astype(F32)).astype(BF16)
        g_in = jnp.dot(h_two.T, d_pre, preferred_element_type=F32).astype(BF16)
        d_htwo = cube(jnp.dot(d_pre, w_in.T, preferred_element_type=F32))
        d_gate_two = jnp.sum(grad_out * cube(mlp_out), axis=1)
        d_scale_two = jnp.sum(d_htwo * normed_two, axis=1)
        d_shift_two = jnp.sum(d_htwo, axis=1)
        d_middle = grad_out + norm_back(d_htwo * (1.0 + scale_two), normed_two, inv_two)
        d_attn = flat((gate_one * d_middle).astype(BF16))
        d_gate_one = jnp.sum(d_middle * cube(attn_out), axis=1)
        g_out = jnp.dot(attended.T, d_attn, preferred_element_type=F32).astype(BF16)
        d_attended = jnp.dot(d_attn, w_out.T, preferred_element_type=F32).astype(BF16)
        dq, dk, dv = attend_back(ends, queries, kv_all, d_attended, piece, per)
        dkv = jnp.concatenate([dk, dv], axis=1).reshape(per, rows, 2 * width)
        dkv_own = lax.dynamic_index_in_dim(dkv, g, 0, keepdims=False).astype(F32)
        for k in range(1, per):
            sent = lax.dynamic_index_in_dim(dkv, (g + k) % per, 0, keepdims=False)
            dkv_own = dkv_own + lax.ppermute(sent, "frame", partners(k)).astype(F32)
        d_proj = jnp.concatenate([dq * jnp.asarray(q_scale, BF16), dkv_own.astype(BF16)], axis=1)
        g_qkv = jnp.dot(h_one.T, d_proj, preferred_element_type=F32).astype(BF16)
        d_hone = cube(jnp.dot(d_proj, w_qkv.T, preferred_element_type=F32))
        d_scale_one = jnp.sum(d_hone * normed_one, axis=1)
        d_shift_one = jnp.sum(d_hone, axis=1)
        d_input = d_middle + norm_back(d_hone * (1.0 + scale_one), normed_one, inv_one)
        input_grad = d_input.astype(BF16)
        piece_dmod = jnp.stack([d_shift_one, d_scale_one, d_gate_one, d_shift_two, d_scale_two, d_gate_two])
        frame_dmod = jnp.einsum("pf,jpd->jfd", selector, piece_dmod, precision=HIGHEST)

    if direct:
        updated = update_owned(
            owned_block,
            table,
            grad_block,
            master.reshape(-1, 128),
            first_moment.reshape(-1, 128),
            second_moment.reshape(-1, 128),
            batch_size,
        )
        new_master, new_first, new_second = [a.reshape(1, block_size) for a in updated]
    else:
        outputs, input_grads = swap_videos([block_output, input_grad], videos, per, 1)
        g_ada = lax.dot_general(
            cond.astype(F32),
            frame_dmod.transpose(1, 0, 2).reshape(frame_count, 6 * width),
            (((0,), (0,)), ((), ())),
            precision=HIGHEST,
        )
        flat_grads = jnp.concatenate(
            [piece_grad.astype(F32).reshape(-1) for piece_grad in (g_ada, g_qkv, g_out, g_in, g_down)]
        )
        arranged = jnp.take(flat_grads.reshape(-1, block_size), owned_block, axis=0).reshape(-1)
        shard_total = lax.psum_scatter(
            arranged, ("frame", "batch"), scatter_dimension=0, tiled=True
        ).reshape(1, block_size)
        new_master, new_first, new_second = adam(shard_total, master, first_moment, second_moment)
    return (outputs, input_grads, new_master, new_first, new_second)


def solution(mesh):
    placed = (
        P("batch", "frame", None),
        P("batch", "frame", None),
        P("batch"),
        P("batch", None),
        P(),
        P(("frame", "batch"), None),
        P(("frame", "batch"), None),
        P(("frame", "batch"), None),
    )
    return jax.shard_map(
        partial(shards, mesh.shape["frame"], mesh.shape["batch"]),
        mesh=mesh,
        in_specs=placed,
        out_specs=(
            P("batch", "frame", None),
            P("batch", "frame", None),
            P(("frame", "batch"), None),
            P(("frame", "batch"), None),
            P(("frame", "batch"), None),
        ),
        check_vma=False,
    )
```

```python
from functools import partial
import math

import jax
import jax.numpy as jnp
import numpy as np
from jax import lax
from jax.experimental import pallas as pl
from jax.experimental.pallas import tpu as pltpu
from jax.sharding import PartitionSpec as P

H = 16
HD = 64
FF = 4096
FRAME_LO = 256
STEP = 10

HIGHEST = lax.Precision.HIGHEST
NEG_FILL = -1e30
BETA_ONE = 0.5
BETA_TWO = 0.5
LEARN_RATE = 0.05
WEIGHT_DECAY = 0.1
ADAM_EPS = 1e-08
MESH = pl.DeviceIdType.MESH
F32 = jnp.float32
BF16 = jnp.bfloat16
ANY = pl.BlockSpec(memory_space=pl.ANY)
VMEM_LIMIT = 63 * 1024 * 1024

ROWS = 576
GROUP = 144
FIRST = 10
KINDS = (("qkv", 1024, 3), ("out", 1024, 1), ("in", 1024, 4), ("down", 4096, 1))
HELD = 3168
THIRD = 48
ADA = 1664


def pieces(kind, z):
    if kind == "qkv":
        found = [(48 * j, 16, 16 * z, j) for j in range(3)]
        for k in range(5):
            found += [(144 + 144 * k + 48 * j, 48, 64 + 192 * k + 48 * z, j) for j in range(3)]
        return found
    if kind == "out":
        return [(864, 144, 144 * z, 0), (1008, 112, 576 + 112 * z, 0)]
    if kind == "in":
        return [(1120, 1024, 0, z)]
    found = [(2144, 16, 16 * z, 0)]
    return found + [(2160 + 144 * k, 144, 64 + 576 * k + 144 * z, 0) for k in range(7)]


def block_rows(block):
    t = np.arange(GROUP)
    groups = []
    for z in range(4):
        if block == 10:
            i, j = t % THIRD, t // THIRD
            rows = np.where(i < 16, 384 + 3 * (16 * z + i) + j, 96 * z + 32 * j + i - 16)
        elif 11 <= block <= 15:
            rows = 3 * (48 * z + t % 48) + t // 48
        elif block == 17:
            rows = np.where(t < 112, 112 * z + t, 448 + 4 * (t - 112) + z)
        elif 18 <= block <= 23:
            rows = 4 * t + z
        elif block == 24:
            rows = np.where(t < 128, 4 * t + z, 512 + 16 * z + t - 128)
        else:
            rows = GROUP * z + t
        groups.append(rows)
    return np.concatenate(groups)


def ada_place(n, z):
    b, t = n // GROUP, n % GROUP
    i = t % THIRD - 16
    a = 32 * (t // THIRD) + i
    row = jnp.where(b < 10, 96 * b + 24 * z + t // 6, 960 + 16 * z + a // 6)
    col = jnp.where(b < 10, t % 6, a % 6)
    none = (b > 10) | ((b == 10) & (i < 0))
    return jnp.where(none, -1, row), col


def frame_index():
    return lax.axis_index("frame"), lax.axis_index("batch")


def strip_of(f):
    return 4 * (f % 2) + f // 2


def greet(devices):
    barrier = pltpu.get_barrier_semaphore()
    for device in devices:
        pl.semaphore_signal(barrier, inc=1, device_id=device, device_id_type=MESH)
    pl.semaphore_wait(barrier, len(devices))


def greet_all(total, batch):
    f, z = frame_index()
    me = f * batch + z
    barrier = pltpu.get_barrier_semaphore()

    def hail(k, carry):
        other = (me + k) % total
        pl.semaphore_signal(barrier, inc=1, device_id=(other // batch, other % batch), device_id_type=MESH)
        return carry

    lax.fori_loop(1, total, hail, 0)
    pl.semaphore_wait(barrier, total - 1)


def remote(src, dst, send, recv, device):
    copy = pltpu.make_async_remote_copy(
        src_ref=src, dst_ref=dst, send_sem=send, recv_sem=recv, device_id=device, device_id_type=MESH
    )
    copy.start()
    return copy


def local(src, dst, sem):
    copy = pltpu.make_async_copy(src, dst, sem)
    copy.start()
    return copy


def video_kernel(videos, per, arrays, *refs):
    ins, outs = refs[:arrays], refs[arrays : 2 * arrays]
    send, recv, own = refs[2 * arrays :]
    f, z = frame_index()
    mine, g = f // per, f % per
    others = [((mine + k) % videos, k) for k in range(1, videos)]
    greet([(v * per + g, z) for v, k in others])
    copies = []
    for a in range(arrays):
        for v, k in others:
            copies.append(
                remote(ins[a].at[v], outs[a].at[mine], send.at[a, k], recv.at[a, k], (v * per + g, z))
            )
        copies.append(local(ins[a].at[mine], outs[a].at[mine], own.at[a]))
    for copy in copies:
        copy.wait()


def swap_videos(arrays, videos, per, ident):
    count = len(arrays)
    return pl.pallas_call(
        partial(video_kernel, videos, per, count),
        out_shape=[jax.ShapeDtypeStruct(a.shape, a.dtype) for a in arrays],
        in_specs=[ANY] * count,
        out_specs=[ANY] * count,
        scratch_shapes=[
            pltpu.SemaphoreType.DMA((count, videos)),
            pltpu.SemaphoreType.DMA((count, videos)),
            pltpu.SemaphoreType.DMA((count,)),
        ],
        compiler_params=pltpu.CompilerParams(collective_id=ident, has_side_effects=True),
        name="swap_videos",
    )(*arrays)


def plane():
    f, z = frame_index()
    y, x, c = f // 4, (f // 2) % 2, f % 2
    at_x = (4 * y + 2 * (1 - x) + c, z)
    at_y = (4 * (1 - y) + 2 * x + c, z)
    at_c = (4 * y + 2 * x + 1 - c, z)
    return y, x, c, z, at_x, at_y, at_c


def lanes(first, count):
    return pl.ds(pl.multiple_of(first, 128), count)


UNITS = (
    [("qkv", 0, 1024, 1024 * j) for j in range(3)]
    + [("out", 0, 1024, 0)]
    + [("down", 1024 * n, 1024, 0) for n in range(4)]
    + [("in", 0, 1024, 1024 * j) for j in range(4)]
)
AHEAD = 2
PLACE = {"qkv": (0, 1, 2), "out": (3,), "down": (4, 5, 6, 7), "in": (8, 9, 10, 11)}
DOWN_DEALS = [("down", 0, 0, 1216, 304), ("down", 0, 1216, 1152, 288), ("down", 0, 2368, 1152, 288), ("down", 0, 3520, 576, 144)]
QKV_DEALS = [("qkv", j, 0, 1024, 256) for j in range(3)]
OUT_DEAL = ("out", 0, 0, 1024, 256)
DEALS = QKV_DEALS + [OUT_DEAL]
for n in range(4):
    DEALS += [DOWN_DEALS[n], ("in", None, 256 * n, 256, 256)]
DEALS_OF = ((0,), (1,), (2,), (3,), (4,), (6,), (8,), (10,)) + ((5, 7, 9, 11),) * 4
BACK_DEALS = QKV_DEALS + [OUT_DEAL, DOWN_DEALS[0], ("in", None, 0, 1024, 1024)] + DOWN_DEALS[1:]
IN_DEAL = 5


def deal_pieces(deals, d, z):
    kind, j, first, count, _ = deals[d]
    if kind == "in":
        return [(1120 + first, count, first, z)]
    found = zip(pieces(kind, z), pieces(kind, 0))
    if kind == "down":
        return [p for p, at_zero in found if first <= at_zero[2] < first + count]
    return [p for p, _ in found if p[3] == j]


GELU_A = math.sqrt(2.0 / math.pi)
GELU_B = 0.044715


def row_loop(count, step, body):
    def one(i, carry):
        body(pl.multiple_of(i * step, step))
        return carry

    lax.fori_loop(0, count // step, one, 0)


def norm_rows(values):
    centre = values - jnp.mean(values, axis=-1, keepdims=True)
    inv_std = lax.rsqrt(jnp.mean(centre * centre, axis=-1, keepdims=True) + 1e-06)
    return centre * inv_std, inv_std


def lane_half(e):
    return lax.broadcasted_iota(jnp.int32, (1, 128), 1) // 64 == e


def choose(mask, one, other):
    return jnp.where(mask, one.astype(F32), other.astype(F32)).astype(BF16)


def three_parts(value):
    high = value.astype(BF16).astype(F32)
    rest = value - high
    middle = rest.astype(BF16).astype(F32)
    return high, middle, rest - middle


def in_lanes(parts, first):
    lane = lax.broadcasted_iota(jnp.int32, (1, 128), 1) % 64
    total = 0.0
    for n, part in enumerate(parts):
        total = total + jnp.where(lane == first + n, part, 0.0)
    return total


def query_mask(ends, piece):
    lane = lax.broadcasted_iota(jnp.int32, (piece, 128), 1) % 64
    found = []
    for t in range(4):
        hidden = (lane < 4) & (lane * FRAME_LO >= ends[t])
        found.append(jnp.where(hidden, NEG_FILL, 0.0))
    return jnp.concatenate(found, axis=0)


def key_mask(keys, piece, per):
    lane = lax.broadcasted_iota(jnp.int32, (keys, 128), 1) % 64
    quarter = key_positions(keys, piece, per) // FRAME_LO
    return jnp.where((lane == quarter) | ((lane >= 4) & (lane < 7)), 1.0, 0.0)


def dot_nt(a, b):
    return lax.dot_general(a, b, (((1,), (1,)), ((), ())), preferred_element_type=F32)


def dot_tn(a, b):
    return lax.dot_general(a, b, (((0,), (0,)), ((), ())), preferred_element_type=F32)


def dot_nn(a, b):
    return jnp.dot(a, b, preferred_element_type=F32)


def fold_rows(values):
    return values[:8] + values[8:]


def frames_of(buckets, mine, g, piece, per):
    large = buckets[mine] > 0
    sel, ends = [], []
    for p in range(4):
        at = (p * per + g) * piece
        frame = jnp.where(large, at // (4 * FRAME_LO), at // FRAME_LO)
        sel.append([jnp.where(frame == fr, 1.0, 0.0) for fr in range(4)])
        ends.append((frame + 1) * jnp.where(large, 4 * FRAME_LO, FRAME_LO))
    return sel, ends


def forward_kernel(total, batch, piece, per, inverse, buckets, blk, cond_i, tok_i, cot_i, *refs):
    hbm, vm, sems = refs[:20], refs[20:49], refs[49:]
    wq_o, wo_o, wi_o, wd_o, h1_o, q_o, qb_o, kv_o, att_o, a_o, x1_o, h2_o, gp_o, u_o, y_o, pm_o, dg_o, cot_o, spread_o, tok_o = hbm
    wq, wo, wi, wd, h1, q, qb, kv, att, a, x1, h2, gp, u, acc, pm, mod_v, dg, kmask, cot = vm[:20]
    tok, held, cond, spread, mod, *cut, mod_half = vm[20:]
    zsend, zrecv, psend, precv, msend, mrecv, own, wsem, osem, kvsend, kvrecv, vsend, vrecv = sems[:13]
    csend, crecv, lsend, lrecv, hsend, hrecv = sems[13:]
    mats = {"qkv": wq, "out": wo, "in": wi, "down": wd}
    mats_o = {"qkv": wq_o, "out": wo_o, "in": wi_o, "down": wd_o}
    y, x, c, z, at_x, at_y, at_c = plane()
    f = 4 * y + 2 * x + c
    me = f * batch + z
    strip = 4 * c + 2 * y + x
    mine, g = f // per, f % per
    sel, ends = frames_of(buckets, mine, g, piece, per)
    greet_all(total, batch)

    def third_of(n, of, oz):
        return blk.at[
            pl.ds(pl.multiple_of(GROUP * oz + THIRD * n, 16), THIRD), lanes(128 * strip_of(of), 128)
        ]

    def send_third(n):
        def one(k, carry):
            other = (me + k) % total
            of, oz = other // batch, other % batch
            pltpu.make_async_remote_copy(
                src_ref=third_of(n, of, oz),
                dst_ref=cut[n].at[me],
                send_sem=csend.at[n],
                recv_sem=crecv.at[n],
                device_id=(of, oz),
                device_id_type=MESH,
            ).start()
            return carry

        lax.fori_loop(1, total, one, 0)

    def others(n):
        return cut[n].at[pl.ds(0, total - 1)]

    def take_third(n):
        pltpu.make_async_copy(others(n), others(n), crecv.at[n]).wait()
        own_thirds[n].wait()
        if n + 2 < 3:
            send_third(n + 2)

        def one(b, carry):
            held[pl.ds(pl.multiple_of(GROUP * b + THIRD * n, 16), THIRD), :] = cut[n][inverse[b]]
            return carry

        lax.fori_loop(0, total, one, 0)

    def send_video(src, dst, s, sem):
        for k in range(1, 4):
            v = (mine + k) % 4
            videos[s].append(
                remote(
                    src.at[v],
                    dst.at[pl.ds(pl.multiple_of(mine * piece, piece), piece)],
                    vsend.at[s, k],
                    vrecv.at[s, k],
                    (v * per + g, z),
                )
            )
        videos[s].append(local(src.at[mine], dst.at[pl.ds(pl.multiple_of(mine * piece, piece), piece)], sem))

    videos = ([], [])
    send_third(0)
    send_third(1)
    levels = [
        remote(cond_i, cond.at[pl.ds(pl.multiple_of(16 * z, 16), 16)], lsend.at[k], lrecv.at[k], (f, (z + k) % batch))
        for k in range(1, batch)
    ]
    levels.append(local(cond_i, cond.at[pl.ds(pl.multiple_of(16 * z, 16), 16)], own.at[len(DEALS)]))
    own_thirds = [local(third_of(n, f, z), cut[n].at[me], own.at[len(DEALS) + 1 + n]) for n in range(3)]
    send_video(tok_i, tok, 0, own.at[len(DEALS) + 4])

    def mod_group(k, start):
        other = (f // 2 * batch + z + k) % (4 * batch)
        chip, oz = other // batch, other % batch
        copy = pltpu.make_async_remote_copy(
            src_ref=mod.at[4 * oz + chip],
            dst_ref=mod_v.at[z, :, lanes(128 * (f // 2), 128)],
            send_sem=msend.at[k],
            recv_sem=mrecv.at[k],
            device_id=(2 * chip + c, oz),
            device_id_type=MESH,
        )
        if start:
            copy.start()
        else:
            copy.wait()

    def spot(kind, to, count, j):
        return mats[kind].at[pl.ds(pl.multiple_of(to, 16), count), lanes(1024 * j + 128 * strip, 128)]

    base = FIRST * GROUP

    def deal(d):
        kind = DEALS[d][0]
        for k in range(1, batch):
            for row, count, to, j in deal_pieces(DEALS, d, z):
                remote(
                    held.at[pl.ds(base + row, count)], spot(kind, to, count, j), zsend.at[d, k], zrecv.at[d, k],
                    (f, (z + k) % batch),
                )
        for row, count, to, j in deal_pieces(DEALS, d, z):
            local(held.at[pl.ds(base + row, count)], spot(kind, to, count, j), own.at[d])

    def whole(d):
        return held.at[pl.ds(0, DEALS[d][4])]

    dealt = set()
    following = [2]

    def deal_wait(d):
        if d in dealt:
            return
        dealt.add(d)
        for k in range(1, batch):
            pltpu.make_async_copy(whole(d), whole(d), zrecv.at[d, k]).wait()
        pltpu.make_async_copy(whole(d), whole(d), own.at[d]).wait()
        while following[0] <= min(d + AHEAD, len(DEALS) - 1):
            deal(following[0])
            following[0] += 1

    slots = {}
    counter = [0]

    def push(key, mat, row, count, col, width, device):
        s = counter[0]
        counter[0] += 1
        ref = mat.at[pl.ds(row, count), lanes(col, width)]
        slots.setdefault(key, []).append(remote(ref, ref, psend.at[s], precv.at[s], device))

    def stage_a(n):
        kind, row, rows, col = UNITS[n]
        half = rows // 2
        for d in DEALS_OF[n]:
            deal_wait(d)
        push((n, 1), mats[kind], row, half, col + 128 * strip, 128, at_x)
        push((n, 1), mats[kind], row + half, half, col + 128 * strip, 128, at_y)

    def stage_b(n):
        kind, row, rows, col = UNITS[n]
        half = rows // 2
        for copy in slots[(n, 1)]:
            copy.wait_recv()
        push((n, 2), mats[kind], row, half, col + 512 * c + 256 * y, 256, at_y)
        for yy in range(2):
            push((n, 2), mats[kind], row + half, half, col + 512 * c + 256 * yy + 128 * x, 128, at_x)

    def stage_c(n):
        kind, row, rows, col = UNITS[n]
        for copy in slots[(n, 2)]:
            copy.wait_recv()
        push((n, 3), mats[kind], row, rows, col + 512 * c, 512, at_c)

    saves = []

    def ready(n):
        kind, row, rows, col = UNITS[n]
        for copy in slots[(n, 3)]:
            copy.wait_recv()
        ref = (pl.ds(row, rows), pl.ds(col, 1024))
        saves.append(local(mats[kind].at[ref], mats_o[kind].at[ref], wsem.at[n]))

    pumped = [0]
    last_unit = len(UNITS)

    def pump():
        s = pumped[0]
        pumped[0] += 1
        if 0 <= s - 2 < last_unit:
            stage_b(s - 2)
        if s < last_unit:
            stage_a(s)
        if 0 <= s - 3 < last_unit:
            stage_c(s - 3)

    def pump_to(s):
        while pumped[0] <= s:
            pump()

    def save(src, dst, n):
        saves.append(local(src, dst, osem.at[n]))

    take_third(0)
    deal(0)
    send_video(cot_i, cot, 1, own.at[len(DEALS) + 5])
    take_third(1)
    deal(1)
    take_third(2)
    pump_to(0)
    for copy in levels:
        copy.wait()
    row_id = lax.broadcasted_iota(jnp.int32, (384, 1), 0)
    expand = (
        lax.broadcasted_iota(jnp.int32, (384, 64), 1) == 4 * (row_id // 24) + row_id % 4
    ).astype(F32).astype(BF16)

    def mod_tile(n, carry):
        index = 128 * n + lax.broadcasted_iota(jnp.int32, (1, 128), 1)
        row, col = ada_place(index, z)
        pick = (lax.broadcasted_iota(jnp.int32, (1024, 128), 0) == row).astype(F32).astype(BF16)
        wide = dot_nn(expand, dot_nn(cond[...], pick).astype(BF16))
        wide = jnp.where(col == (row_id % 24) // 4, wide, 0.0).astype(BF16)
        spread[:, lanes(128 * n, 128)] = wide
        part = dot_nn(wide, held[pl.ds(pl.multiple_of(128 * n, 128), 128), :])
        return carry + part

    part = jnp.zeros((384, 128), F32)
    part = lax.fori_loop(0, 7, mod_tile, part)
    pump_to(1)
    part = lax.fori_loop(7, 13, mod_tile, part)
    for v in range(16):
        mod[v] = part[24 * v : 24 * v + 24]
    lax.fori_loop(1, 4 * batch, lambda k, t: (mod_group(k, True), t)[1], 0)
    mod_own = local(mod.at[4 * z + f // 2], mod_v.at[z, :, lanes(128 * (f // 2), 128)], own.at[len(DEALS) + 6])
    pump_to(2)
    lax.fori_loop(1, 4 * batch, lambda k, t: (mod_group(k, False), t)[1], 0)
    mod_own.wait()
    half_row = mod_v[0]
    for s in range(1, batch):
        half_row = half_row + mod_v[s]
    mod_half[c] = half_row
    half_copy = remote(mod_half.at[c], mod_half.at[c], hsend, hrecv, at_c)
    save(spread, spread_o, 14)
    half_copy.wait()
    for copy in videos[0]:
        copy.wait()
    save(tok, tok_o, 15)
    for j in range(6):
        for p in range(4):
            value = jnp.zeros((1, 1024), F32)
            for fr in range(4):
                row = [mod_half[e, pl.ds(4 * j + fr, 1), :] for e in range(2)]
                value = value + sel[p][fr] * jnp.concatenate(row, axis=1)
            pm[pl.ds(4 * j + p, 1), :] = value
    save(pm, pm_o, 0)

    def mod_row(j, p):
        return pm[pl.ds(4 * j + p, 1), :]

    step = 32
    for p in range(4):
        shift, scale = mod_row(0, p), mod_row(1, p)

        def one(i, p=p, shift=shift, scale=scale):
            rows = pl.ds(pl.multiple_of(p * piece + i, step), step)
            normed, _ = norm_rows(tok[rows, :].astype(F32))
            h1[rows, :] = (normed * (1.0 + scale) + shift).astype(BF16)

        row_loop(piece, step, one)
    save(h1, h1_o, 1)
    saves_h1 = saves[-1]

    pump_to(4)
    for j in range(3):
        pump_to(3 + j)
        ready(j)

        def cols(n, j=j):
            value = jnp.dot(h1[...], wq[:, lanes(1024 * j + n, 512)], preferred_element_type=F32)
            if j == 0:
                q[:, lanes(n, 512)] = (value * HD ** (-0.5)).astype(BF16)
            else:
                kv[c, :, lanes(1024 * (j - 1) + n, 512)] = value.astype(BF16)

        row_loop(1024, 512, cols)
    save(q, q_o, 2)
    kv_copy = remote(kv.at[c], kv.at[c], kvsend, kvrecv, at_c)
    pump_to(6)
    kv_copy.wait_recv()
    save(kv, kv_o, 3)

    keys = 2 * 4 * piece
    qb_mask = query_mask(ends, piece)
    acc[:, 0:128] = qb_mask
    kmask[...] = key_mask(keys, piece, per).astype(BF16)

    def heads(h):
        pair = lanes(128 * h, 128)
        k_pair = kv[:, :, pair].reshape(keys, 128)
        v_pair = kv[:, :, lanes(1024 + 128 * h, 128)].reshape(keys, 128)
        q_pair = q[:, pair]
        outs, parts = [], []
        for e in range(2):
            mine = lane_half(e)
            s = dot_nt(choose(mine, q_pair, acc[:, 0:128]), choose(mine, k_pair, kmask[...]))
            peak = jnp.max(s, axis=1, keepdims=True)
            w = jnp.exp(s - peak).astype(BF16)
            o = dot_nn(w, choose(mine, v_pair, jnp.ones_like(v_pair)))
            outs.append(o / pltpu.roll(o, 64, 1))
            parts.append(-(peak + jnp.log(jnp.where(mine, 1.0, o))))
        att[:, pair] = choose(lane_half(0), outs[0], outs[1])
        level = jnp.where(lane_half(1), parts[0], parts[1])
        qb[:, pair] = (acc[:, 0:128] + in_lanes(three_parts(level), 4)).astype(BF16)

    for n in range(4):
        lax.fori_loop(2 * n, 2 * n + 2, lambda h, t: (heads(h), t)[1], 0)
        pump_to(7 + n)
    save(att, att_o, 4)
    save(qb, qb_o, 12)

    ready(3)

    def out_cols(n):
        value = dot_nn(att[...], wo[:, lanes(n, 512)])
        acc[:, lanes(n, 512)] = value
        a[:, lanes(n, 512)] = value.astype(BF16)

    row_loop(1024, 512, out_cols)
    save(a, a_o, 5)
    for p in range(4):
        gate, shift, scale = mod_row(2, p), mod_row(3, p), mod_row(4, p)

        def two(i, p=p, gate=gate, shift=shift, scale=scale):
            rows = pl.ds(pl.multiple_of(p * piece + i, step), step)
            middle = tok[rows, :].astype(F32) + gate * acc[rows, :]
            x1[rows, :] = middle
            normed, _ = norm_rows(middle)
            h2[rows, :] = (normed * (1.0 + scale) + shift).astype(BF16)

        row_loop(piece, step, two)
    save(x1, x1_o, 6)
    save(h2, h2_o, 7)

    for j in range(4):
        pump_to(11 + j)
        ready(PLACE["in"][j])

        def in_cols(n, j=j):
            col = 1024 * j + n
            pre = jnp.dot(h2[...], wi[:, lanes(col, 512)], preferred_element_type=F32)
            square = pre * pre
            t = jnp.tanh(GELU_A * (pre + GELU_B * (square * pre)))
            lift = 0.5 * (1.0 + t)
            u[:, lanes(col, 512)] = (pre * lift).astype(BF16)
            slope = lift + (0.5 * GELU_A) * pre * (1.0 - t * t) * (1.0 + 3.0 * GELU_B * square)
            gp[:, lanes(col, 512)] = slope.astype(BF16)

        row_loop(1024, 512, in_cols)
        if j == 0:
            for n in PLACE["down"]:
                ready(n)

        def down_cols(col, j=j):
            part = dot_nn(u[:, 1024 * j : 1024 * j + 1024], wd[1024 * j : 1024 * j + 1024, lanes(col, 512)])
            if j == 0:
                acc[:, lanes(col, 512)] = part
            else:
                acc[:, lanes(col, 512)] = acc[:, lanes(col, 512)] + part

        row_loop(1024, 512, down_cols)
    save(u, u_o, 8)
    save(gp, gp_o, 9)
    saves_h1.wait()
    for copy in videos[1]:
        copy.wait()
    save(cot, cot_o, 13)
    for p in range(4):
        gate = mod_row(5, p)

        def three(i, total_grad, p=p, gate=gate):
            rows = pl.ds(pl.multiple_of(p * piece + i * 16, 16), 16)
            value = acc[rows, :]
            h1[rows, :] = (x1[rows, :] + gate * value).astype(BF16)
            return total_grad + fold_rows(cot[rows, :].astype(F32) * value)

        part = lax.fori_loop(0, piece // 16, three, jnp.zeros((8, 1024), F32))
        dg[pl.ds(p, 1), :] = jnp.sum(part, axis=0, keepdims=True)
    dg[pl.ds(4, 4), :] = jnp.zeros((4, 1024), F32)
    save(dg, dg_o, 10)
    save(h1, y_o, 11)
    for copy in saves:
        if copy is not saves_h1:
            copy.wait()
    kv_copy.wait_send()
    for copies in slots.values():
        for copy in copies:
            copy.wait_send()
    for n in range(3):
        pltpu.make_async_copy(others(n), others(n), csend.at[n]).wait()
    for d in range(len(DEALS)):
        for k in range(1, batch):
            pltpu.make_async_copy(whole(d), whole(d), zsend.at[d, k]).wait()


def forward(inverse, buckets, blk, cond, tok, cot, total, batch, piece, per):
    def out(*shape, dtype=BF16):
        return jax.ShapeDtypeStruct(shape, dtype)

    outs = [out(depth, 1024 * blocks) for _, depth, blocks in KINDS] + [
        out(512, 1024),
        out(512, 1024),
        out(512, 1024),
        out(2, 512, 2048),
        out(512, 1024),
        out(512, 1024),
        out(512, 1024, dtype=F32),
        out(512, 1024),
        out(512, 4096),
        out(512, 4096),
        out(512, 1024),
        out(24, 1024, dtype=F32),
        out(8, 1024, dtype=F32),
        out(512, 1024),
        out(384, ADA),
        out(512, 1024),
    ]
    bufs = [pltpu.VMEM(o.shape, o.dtype) for o in outs[:14]] + [
        pltpu.VMEM((512, 1024), F32),
        pltpu.VMEM((24, 1024), F32),
        pltpu.VMEM((batch, 24, 512), F32),
        pltpu.VMEM((8, 1024), F32),
        pltpu.VMEM((1024, 128), BF16),
        pltpu.VMEM((512, 1024), BF16),
        pltpu.VMEM((512, 1024), BF16),
        pltpu.VMEM((total * GROUP, 128), BF16),
        pltpu.VMEM((64, 1024), BF16),
        pltpu.VMEM((384, ADA), BF16),
        pltpu.VMEM((16, 24, 128), F32),
    ] + [pltpu.VMEM((total, THIRD, 128), BF16) for _ in range(3)]
    bufs.append(pltpu.VMEM((2, 24, 512), F32))
    smem = pl.BlockSpec(memory_space=pltpu.SMEM)
    dma = pltpu.SemaphoreType.DMA
    return pl.pallas_call(
        partial(forward_kernel, total, batch, piece, per),
        out_shape=outs,
        in_specs=[smem, smem] + [ANY] * 4,
        out_specs=[ANY] * len(outs),
        scratch_shapes=bufs
        + [
            dma((len(DEALS), batch)),
            dma((len(DEALS), batch)),
            dma((6 * len(UNITS),)),
            dma((6 * len(UNITS),)),
            dma((total,)),
            dma((total,)),
            dma((len(DEALS) + 7,)),
            dma((len(UNITS),)),
            dma((16,)),
            dma,
            dma,
            dma((2, 4)),
            dma((2, 4)),
            dma((3,)),
            dma((3,)),
            dma((batch,)),
            dma((batch,)),
            dma,
            dma,
        ],
        compiler_params=pltpu.CompilerParams(
            collective_id=1, has_side_effects=True, vmem_limit_bytes=VMEM_LIMIT
        ),
        name="forward",
    )(inverse, buckets, blk, cond, tok, cot)


LEAVES = (
    [(3, 1024 * n, 0) for n in range(4)] + [(2, 0, j) for j in range(4)] + [(1, 0, 0)] + [(0, 0, j) for j in range(3)]
)
DEALS_AFTER = ((), (4,), (6,), (7, 8), (), (), (), (), (3,), (0,), (1,), (2,))


def by_block(row, count):
    found, done = [], 0
    while done < count:
        b, first = divmod(row + done, GROUP)
        rows = min(count - done, GROUP - first)
        found.append((b, first, rows, done))
        done += rows
    return found


def backward_kernel(total, batch, piece, per, buckets, owned, pm, dg, *refs):
    wq, wo, wi, wd, h1_i, q_i, qb_i, kv_i, att_i, a_i, x1_i, h2_i, gp_i, u_i, y_i, cot_i, spread_i, tok_i = refs[:18]
    blk, grad_o, act_o = refs[18:21]
    big1, big2, big3, wa, wb, f1, f2, s1, s2, s3, s4, kv_got, dmv, dmf, kmask, ring = refs[21:37]
    got, half_sum, strip_sum, zgot = refs[37:41], refs[41:45], refs[45:49], refs[49]
    ordered, picked, dmf_got, dmod = refs[50:54]
    psend, precv, zsend, zrecv, msend, mrecv, vsend, vrecv, xsend, xrecv, lsem, asem, bsem = refs[54:67]
    gsend, grecv, hsend, hrecv = refs[67:]
    y, x, c, z, at_x, at_y, at_c = plane()
    f = 4 * y + 2 * x + c
    me = f * batch + z

    def load(src, dst, n):
        return local(src, dst, lsem.at[n])

    cot_l = load(cot_i, s3, 0)
    u_l = [load(u_i.at[:, pl.ds(1024 * n, 1024)], big1.at[:, pl.ds(1024 * n, 1024)], 1 + n) for n in range(4)]
    h2_l = load(h2_i, s2, 5)
    gp_l = load(gp_i, big2, 6)
    x1_l = load(x1_i, f2, 7)
    a_l = load(a_i, s4, 8)
    down_tiles = [wd.at[pl.ds(512 * t, 512)] for t in range(8)] + [wo.at[pl.ds(512 * t, 512)] for t in range(2)]
    in_tiles = [wi.at[:, pl.ds(512 * t, 512)] for t in range(8)] + [wq.at[:, pl.ds(512 * t, 512)] for t in range(6)]
    fetched = {}

    def fetch(tiles, buf, sem, t):
        if t < len(tiles):
            fetched[id(tiles), t] = local(tiles[t], buf.at[t % 2], sem.at[t % 2])

    for t in range(2):
        fetch(down_tiles, wb, bsem, t)
        fetch(in_tiles, wa, asem, t)

    def tile(tiles, buf, t):
        fetched[id(tiles), t].wait()
        return buf[t % 2]

    greet_all(total, batch)
    mine, g = f // per, f % per
    sel, _ = frames_of(buckets, mine, g, piece, per)
    videos = []

    def send_video(s, part, dst, n):
        for k in range(1, 4):
            v = (mine + k) % 4
            videos.append(remote(part(v), dst.at[mine], vsend.at[s, k], vrecv.at[s, k], (v * per + g, z)))
        videos.append(local(part(mine), dst.at[mine], lsem.at[n]))

    slots = {}
    counter = [0]

    def push(key, src, dst, device):
        s = counter[0]
        counter[0] += 1
        slots.setdefault(key, []).append(remote(src, dst, psend.at[s], precv.at[s], device))

    def arrive(key):
        for copy in slots[key]:
            copy.wait_recv()

    def emit(n, left, right):
        m, row, j = LEAVES[n]
        for w in range(2):
            ring[n % 2, :, 512 * w : 512 * w + 512] = dot_tn(left, right[:, 512 * w : 512 * w + 512]).astype(BF16)
        push(
            (n, 0),
            ring.at[n % 2, :, lanes(512 * (1 - c), 512)],
            got[m].at[pl.ds(row, 1024), pl.ds(512 * j, 512)],
            at_c,
        )

    def add_block(dst, dst_row, dst_col, src, src_row, src_col, width, count):
        def body(i, carry):
            to = pl.ds(pl.multiple_of(dst_row + i * 128, 128), 128)
            at = pl.ds(pl.multiple_of(src_row + i * 128, 128), 128)
            dst[to, lanes(dst_col, width)] = dst[to, lanes(dst_col, width)] + src[at, lanes(src_col, width)]
            return carry

        lax.fori_loop(0, count // 128, body, 0)

    def absorb(n):
        m, row, j = LEAVES[n]
        arrive((n, 0))
        add_block(got[m], row, 512 * j, ring.at[n % 2], 0, 512 * c, 512, 1024)
        for copy in slots[(n, 0)]:
            copy.wait_send()

    def step1(n):
        m, row, j = LEAVES[n]
        for yy in range(2):
            push(
                (n, 1),
                got[m].at[pl.ds(row, 512), lanes(512 * j + 256 * yy + 128 * (1 - x), 128)],
                half_sum[m].at[pl.ds(row, 512), lanes(256 * j + 128 * yy, 128)],
                at_x,
            )
        push(
            (n, 1),
            got[m].at[pl.ds(row + 512, 512), lanes(512 * j + 256 * (1 - y), 256)],
            half_sum[m].at[pl.ds(row + 512, 512), lanes(256 * j, 256)],
            at_y,
        )

    def step2(n):
        m, row, j = LEAVES[n]
        arrive((n, 1))
        for yy in range(2):
            add_block(half_sum[m], row, 256 * j + 128 * yy, got[m], row, 512 * j + 256 * yy + 128 * x, 128, 512)
        add_block(half_sum[m], row + 512, 256 * j, got[m], row + 512, 512 * j + 256 * y, 256, 512)
        push(
            (n, 2),
            half_sum[m].at[pl.ds(row, 512), lanes(256 * j + 128 * (1 - y), 128)],
            strip_sum[m].at[pl.ds(row, 512), lanes(128 * j, 128)],
            at_y,
        )
        push(
            (n, 2),
            half_sum[m].at[pl.ds(row + 512, 512), lanes(256 * j + 128 * (1 - x), 128)],
            strip_sum[m].at[pl.ds(row + 512, 512), lanes(128 * j, 128)],
            at_x,
        )

    def step3(n):
        m, row, j = LEAVES[n]
        arrive((n, 2))
        add_block(strip_sum[m], row, 128 * j, half_sum[m], row, 256 * j + 128 * y, 128, 512)
        add_block(strip_sum[m], row + 512, 128 * j, half_sum[m], row + 512, 256 * j + 128 * x, 128, 512)
        if m == 2:

            @pl.when(z != j)
            def _():
                k = (j - z + batch) % batch
                remote(
                    strip_sum[m].at[:, pl.ds(128 * j, 128)],
                    zgot.at[k - 1, pl.ds(1120, 1024)],
                    zsend.at[IN_DEAL, k],
                    zrecv.at[IN_DEAL, k],
                    (f, j),
                )

        for d in DEALS_AFTER[n]:
            for k in range(1, batch):
                to = (z + k) % batch
                for held_row, count, at, col in deal_pieces(BACK_DEALS, d, to):
                    remote(
                        strip_sum[m].at[pl.ds(pl.multiple_of(at, 16), count), lanes(128 * col, 128)],
                        zgot.at[k - 1, pl.ds(held_row, count)],
                        zsend.at[d, k],
                        zrecv.at[d, k],
                        (f, to),
                    )

    pumped = [0]

    def pump_to(r):
        while pumped[0] <= r:
            n = pumped[0]
            pumped[0] += 1
            if 0 <= n - 2 < 12:
                step2(n - 2)
            if n < 12:
                step1(n)
            if 0 <= n - 3 < 12:
                step3(n - 3)

    def whole(d, k):
        return zgot.at[k - 1, pl.ds(0, BACK_DEALS[d][4])]

    def last(d):
        m = [kind for kind, _, _ in KINDS].index(BACK_DEALS[d][0])
        for k in range(1, batch):
            pltpu.make_async_copy(whole(d, k), whole(d, k), zrecv.at[d, k]).wait()
        for row, count, at, j in deal_pieces(BACK_DEALS, d, z):
            for b, first, rows, skip in by_block(row, count):
                value = strip_sum[m][pl.ds(pl.multiple_of(at + skip, 16), rows), lanes(128 * j, 128)].astype(F32)
                for k in range(batch - 1):
                    value = value + zgot[k, row + skip : row + skip + rows, :].astype(F32)
                ordered[FIRST + b, first : first + rows, :] = value.astype(BF16)

    def mod_row(j, p):
        return pm[pl.ds(4 * j + p, 1), :]

    def by_rows(p, body, sums):
        def one(i, carry):
            return body(pl.ds(pl.multiple_of(p * piece + i * 16, 16), 16), *carry)

        start = tuple(jnp.zeros((8, 1024), F32) for _ in range(sums))
        return [jnp.sum(s, axis=0, keepdims=True) for s in lax.fori_loop(0, piece // 16, one, start)]

    cot_l.wait()
    for p in range(4):
        gate = mod_row(5, p)

        def d_mlp(rows, gate=gate):
            s1[rows, :] = (gate * s3[rows, :].astype(F32)).astype(BF16)
            return ()

        by_rows(p, d_mlp, 0)
        dmv[pl.ds(20 + p, 1), :] = dg[pl.ds(p, 1), :]
    for n in range(4):
        u_l[n].wait()
        emit(n, big1[:, 1024 * n : 1024 * n + 1024], s1)
        if n >= 1:
            absorb(n - 1)
        if n % 2 == 1:
            pump_to(n // 2)
    kv_l = [load(kv_i.at[d], big1.at[:, pl.ds(2048 * d, 2048)], 10 + d) for d in range(2)]
    gp_l.wait()
    for t in range(8):
        cols = slice(512 * t, 512 * t + 512)
        d_act = dot_nt(s1[...], tile(down_tiles, wb, t))
        big3[:, cols] = (d_act * big2[:, cols].astype(F32)).astype(BF16)
        fetch(down_tiles, wb, bsem, t + 2)
        if t == 0:
            absorb(3)
        if t == 5:
            pump_to(2)
    h2_l.wait()
    for j in range(4):
        emit(4 + j, s2[...], big3.at[:, 1024 * j : 1024 * j + 1024])
        if j >= 1:
            absorb(3 + j)
        if j == 2:
            pump_to(3)
    att_l = load(att_i, s2, 5)
    for t in range(8):
        part = dot_nt(big3[:, 512 * t : 512 * t + 512], tile(in_tiles, wa, t))
        f1[...] = part if t == 0 else f1[...] + part
        fetch(in_tiles, wa, asem, t + 2)
        if t == 0:
            absorb(7)
        if t == 4:
            pump_to(4)
    qb_l = load(qb_i, big3.at[:, pl.ds(3072, 1024)], 6)

    x1_l.wait()
    a_l.wait()
    for p in range(4):
        gate, scale = mod_row(2, p), mod_row(4, p)

        def back_two(rows, d_scale, d_shift, d_gate, gate=gate, scale=scale):
            normed, inv_std = norm_rows(f2[rows, :])
            d_h = f1[rows, :]
            d_mid = s3[rows, :].astype(F32) + norm_back(d_h * (1.0 + scale), normed, inv_std)
            f2[rows, :] = d_mid
            s1[rows, :] = (gate * d_mid).astype(BF16)
            return (
                d_scale + fold_rows(d_h * normed),
                d_shift + fold_rows(d_h),
                d_gate + fold_rows(d_mid * s4[rows, :].astype(F32)),
            )

        d_scale, d_shift, d_gate = by_rows(p, back_two, 3)
        dmv[pl.ds(16 + p, 1), :] = d_scale
        dmv[pl.ds(12 + p, 1), :] = d_shift
        dmv[pl.ds(8 + p, 1), :] = d_gate
    q_l = load(q_i, s4, 8)
    pump_to(5)

    att_l.wait()
    emit(8, s2[...], s1)
    for t in range(2):
        s3[:, 512 * t : 512 * t + 512] = dot_nt(s1[...], tile(down_tiles, wb, 8 + t)).astype(BF16)
    h1_l = load(h1_i, wb.at[0], 7)
    tok_l = load(tok_i, wb.at[1], 12)
    absorb(8)

    keys = 2 * 4 * piece
    kmask[...] = key_mask(keys, piece, per).astype(BF16)
    for copy in kv_l:
        copy.wait()
    qb_l.wait()
    q_l.wait()

    def heads(h):
        pair = lanes(128 * h, 128)
        k_pair = jnp.concatenate([big1[:, lanes(2048 * d + 128 * h, 128)] for d in range(2)], axis=0)
        v_pair = jnp.concatenate([big1[:, lanes(2048 * d + 1024 + 128 * h, 128)] for d in range(2)], axis=0)
        dks, dvs, dqs = [], [], []
        first = lane_half(0)
        ones = in_lanes([1.0, 1.0, 1.0], 0)
        for e in range(2):
            mask = lane_half(e)
            k_e = choose(mask, k_pair, kmask[...])
            v_e = choose(mask, v_pair, ones)
            dk = dv = 0.0
            dq = []
            for w in range(2):
                rows = slice(256 * w, 256 * w + 256)
                q_w, d_w, o_w = s4[rows, pair], s3[rows, pair], s2[rows, pair]
                q_e = choose(mask, q_w, big3[rows, lanes(3072 + 128 * h, 128)])
                dot_rows = jnp.sum(
                    jnp.where(mask, d_w.astype(F32) * o_w.astype(F32), 0.0), axis=1, keepdims=True
                )
                d_e = choose(mask, d_w, in_lanes(three_parts(-dot_rows), 0))
                prob = jnp.exp(dot_nt(k_e, q_e))
                d_s = (prob * dot_nt(v_e, d_e)).astype(BF16)
                dv = dv + dot_nn(prob.astype(BF16), d_w)
                dk = dk + dot_nn(d_s, q_w)
                dq.append(dot_tn(d_s, k_pair))
            dks.append(dk)
            dvs.append(dv)
            dqs.append(jnp.concatenate(dq, axis=0))
        dk = choose(first, dks[0], dks[1])
        dv = choose(first, dvs[0], dvs[1])
        big3[:, pair] = (choose(first, dqs[0], dqs[1]).astype(F32) * HD ** (-0.5)).astype(BF16)
        for d in range(2):
            big2[:, lanes(2048 * d + 128 * h, 128)] = dk[512 * d : 512 * d + 512]
            big2[:, lanes(2048 * d + 1024 + 128 * h, 128)] = dv[512 * d : 512 * d + 512]

    exchanges = []
    for h in range(8):
        lax.fori_loop(h, h + 1, lambda n, t: (heads(n), t)[1], 0)
        if h % 4 == 3:
            for part in range(2):
                at = 1024 * part + 512 * (h // 4)
                s = len(exchanges)
                exchanges.append(
                    remote(
                        big2.at[:, lanes(2048 * (1 - c) + at, 512)],
                        kv_got.at[:, pl.ds(at, 512)],
                        xsend.at[s],
                        xrecv.at[s],
                        at_c,
                    )
                )
        if h % 2 == 0:
            pump_to(min(6 + h // 2, 8))

    spread_l = load(spread_i, big1.at[pl.ds(0, 384), pl.ds(0, ADA)], 10)
    h1_l.wait()
    emit(9, wb[0], big3.at[:, 0:1024])
    for copy in exchanges:
        copy.wait_recv()
    for part in range(2):

        def join(i, carry, part=part):
            rows = pl.ds(pl.multiple_of(i * 64, 64), 64)
            value = big2[rows, lanes(2048 * c + 1024 * part, 1024)].astype(F32) + kv_got[
                rows, 1024 * part : 1024 * part + 1024
            ].astype(F32)
            big3[rows, 1024 + 1024 * part : 2048 + 1024 * part] = value.astype(BF16)
            return carry

        lax.fori_loop(0, 8, join, 0)
        emit(10 + part, wb[0], big3.at[:, 1024 + 1024 * part : 2048 + 1024 * part])
        absorb(9 + part)
        pump_to(9 + part)
    for t in range(6):
        part = dot_nt(big3[:, 512 * t : 512 * t + 512], tile(in_tiles, wa, 8 + t))
        f1[...] = part if t == 0 else f1[...] + part
        fetch(in_tiles, wa, asem, 8 + t + 2)
        if t == 0:
            absorb(11)
        if t == 2:
            pump_to(11)

    tok_l.wait()
    for p in range(4):
        scale = mod_row(1, p)

        def back_one(rows, d_scale, d_shift, scale=scale):
            normed, inv_std = norm_rows(wb[1, rows, :].astype(F32))
            d_h = f1[rows, :]
            s1[rows, :] = (f2[rows, :] + norm_back(d_h * (1.0 + scale), normed, inv_std)).astype(BF16)
            return d_scale + fold_rows(d_h * normed), d_shift + fold_rows(d_h)

        d_scale, d_shift = by_rows(p, back_one, 2)
        dmv[pl.ds(4 + p, 1), :] = d_scale
        dmv[pl.ds(p, 1), :] = d_shift
    send_video(0, lambda v: s1.at[pl.ds(pl.multiple_of(v * piece, piece), piece)], grad_o, 0)
    for j in range(6):
        for fr in range(4):
            value = sel[0][fr] * dmv[pl.ds(4 * j, 1), :]
            for p in range(1, 4):
                value = value + sel[p][fr] * dmv[pl.ds(4 * j + p, 1), :]
            dmf[pl.ds(4 * j + fr, 1), :] = value
    half_copy = remote(dmf, dmf_got, hsend, hrecv, at_c)

    def mod_group(k, start):
        other = (f // 2 * batch + z + k) % (4 * batch)
        chip, oz = other // batch, other % batch
        copy = pltpu.make_async_remote_copy(
            src_ref=dmf_got.at[:, lanes(512 * c + 128 * chip, 128)],
            dst_ref=dmod.at[4 * z + f // 2],
            send_sem=msend.at[k],
            recv_sem=mrecv.at[k],
            device_id=(2 * chip + c, oz),
            device_id_type=MESH,
        )
        if start:
            copy.start()
        else:
            copy.wait()

    pump_to(12)
    half_copy.wait()
    dmf_got[...] = dmf_got[...] + dmf[...]
    lax.fori_loop(1, 4 * batch, lambda k, u: (mod_group(k, True), u)[1], 0)
    dmod[4 * z + f // 2] = dmf_got[:, lanes(512 * c + 128 * (f // 2), 128)]
    for d in (4, 6, 7, 8):
        last(d)
    pump_to(13)
    send_video(1, lambda v: y_i.at[v], act_o, 1)
    last(IN_DEAL)
    last(3)
    last(0)
    pump_to(14)

    spread_l.wait()
    lax.fori_loop(1, 4 * batch, lambda k, u: (mod_group(k, False), u)[1], 0)
    parts = [part.astype(BF16) for part in three_parts(dmod[...].reshape(384, 128))]
    for n in range(ADA // 128):
        wide = big1[0:384, 128 * n : 128 * n + 128]
        value = (dot_tn(wide, parts[0]) + dot_tn(wide, parts[1]) + dot_tn(wide, parts[2])).astype(BF16)
        spans = [(0, FIRST * GROUP)]
        spans += [(FIRST * GROUP + THIRD * q + 16, FIRST * GROUP + THIRD * q + THIRD) for q in range(3)]
        for lo, hi in spans:
            lo, hi = max(lo, 128 * n), min(hi, 128 * n + 128)
            for b, first, rows, skip in by_block(lo, max(hi - lo, 0)):
                ordered[b, first : first + rows, :] = value[lo - 128 * n + skip : lo - 128 * n + skip + rows]
    for d in (1, 2):
        last(d)

    def spot(of, oz):
        return blk.at[pl.ds(pl.multiple_of(GROUP * oz, 16), GROUP), lanes(128 * strip_of(of), 128)]

    def to_owner(k, start):
        other = (me + k) % total
        copy = pltpu.make_async_remote_copy(
            src_ref=picked.at[other],
            dst_ref=spot(f, z),
            send_sem=gsend.at[k],
            recv_sem=grecv.at[k],
            device_id=(other // batch, other % batch),
            device_id_type=MESH,
        )
        if start:
            copy.start()
        else:
            copy.wait()

    def pick(d, carry):
        picked[d] = ordered[owned[d]]
        return carry

    lax.fori_loop(0, total, pick, 0)
    lax.fori_loop(1, total, lambda k, u: (to_owner(k, True), u)[1], 0)
    blk_own = local(picked.at[me], spot(f, z), lsem.at[2])
    for n, copies in slots.items():
        if n[1] > 0:
            for copy in copies:
                copy.wait_send()
    for d in range(len(BACK_DEALS)):
        for k in range(1, batch):
            pltpu.make_async_copy(whole(d, k), whole(d, k), zsend.at[d, k]).wait()
    for copy in exchanges:
        copy.wait_send()
    for copy in videos:
        copy.wait()
    blk_own.wait()
    lax.fori_loop(1, total, lambda k, u: (to_owner(k, False), u)[1], 0)


def backward(buckets, owned, pm, dg, arrays, total, batch, piece, per):
    def sums(width):
        return [pltpu.VMEM((depth, blocks * width), BF16) for _, depth, blocks in KINDS]

    def buf(*shape, dtype=BF16):
        return pltpu.VMEM(shape, dtype)

    whole = pl.BlockSpec(memory_space=pltpu.VMEM)
    dma = pltpu.SemaphoreType.DMA
    return pl.pallas_call(
        partial(backward_kernel, total, batch, piece, per),
        out_shape=[
            jax.ShapeDtypeStruct((ROWS, 1024), BF16),
            jax.ShapeDtypeStruct((4, piece, 1024), BF16),
            jax.ShapeDtypeStruct((4, piece, 1024), BF16),
        ],
        in_specs=[pl.BlockSpec(memory_space=pltpu.SMEM)] * 2 + [whole, whole] + [ANY] * len(arrays),
        out_specs=[ANY, ANY, ANY],
        scratch_shapes=[buf(512, 4096) for _ in range(3)]
        + [buf(2, 1024, 512), buf(2, 512, 1024)]
        + [buf(512, 1024, dtype=F32) for _ in range(2)]
        + [buf(512, 1024) for _ in range(4)]
        + [buf(512, 2048), buf(24, 1024, dtype=F32), buf(24, 1024, dtype=F32), buf(1024, 128), buf(2, 1024, 1024)]
        + sums(512)
        + sums(256)
        + sums(128)
        + [buf(batch - 1, HELD, 128), buf(total, GROUP, 128), buf(total, GROUP, 128)]
        + [buf(24, 1024, dtype=F32), buf(16, 24, 128, dtype=F32)]
        + [
            dma((72,)),
            dma((72,)),
            dma((len(BACK_DEALS), batch)),
            dma((len(BACK_DEALS), batch)),
            dma((4 * batch,)),
            dma((4 * batch,)),
            dma((2, 4)),
            dma((2, 4)),
            dma((4,)),
            dma((4,)),
            dma((13,)),
            dma((2,)),
            dma((2,)),
            dma((total,)),
            dma((total,)),
            dma,
            dma,
        ],
        compiler_params=pltpu.CompilerParams(
            collective_id=2, has_side_effects=True, vmem_limit_bytes=VMEM_LIMIT
        ),
        name="backward",
    )(buckets, owned, pm, dg, *arrays)


def own_rows_of(owned, table, me):
    return table[pl.ds(owned[me], 1), :]


def cut_kernel(batch, owned, table, master, out):
    f, z = frame_index()
    rows = own_rows_of(owned, table, f * batch + z)
    swap = (rows == lax.broadcasted_iota(jnp.int32, (ROWS, ROWS), 0)).astype(F32).astype(BF16)
    for s in range(8):
        strip = master[pl.ds(s, ROWS, stride=8), :].astype(BF16)
        out[:, 128 * s : 128 * s + 128] = dot_tn(swap, strip).astype(BF16)


def cut_owned(owned, table, master, batch):
    whole = pl.BlockSpec(memory_space=pltpu.VMEM)
    return pl.pallas_call(
        partial(cut_kernel, batch),
        out_shape=jax.ShapeDtypeStruct((ROWS, 1024), BF16),
        in_specs=[pl.BlockSpec(memory_space=pltpu.SMEM), whole, whole],
        out_specs=whole,
        compiler_params=pltpu.CompilerParams(vmem_limit_bytes=VMEM_LIMIT),
        name="cut_owned",
    )(owned, table, master)


def adam(grad, master, first, second):
    new_first = BETA_ONE * first + (1.0 - BETA_ONE) * grad
    new_second = BETA_TWO * second + (1.0 - BETA_TWO) * grad * grad
    fix_one = 1.0 - BETA_ONE**STEP
    fix_two = 1.0 - BETA_TWO**STEP
    update = new_first / fix_one / (jnp.sqrt(new_second / fix_two) + ADAM_EPS)
    return master - LEARN_RATE * (update + WEIGHT_DECAY * master), new_first, new_second


UPDATE_ROWS = 144


def update_kernel(batch, owned, table, grad, master, first, second, act, inp, *refs):
    new_master, new_first, new_second, act_o, inp_o = refs
    act_o[...] = act[...]
    inp_o[...] = inp[...]
    f, z = frame_index()
    rows = own_rows_of(owned, table, f * batch + z)
    base = pl.program_id(0) * UPDATE_ROWS
    swap = (rows == base + lax.broadcasted_iota(jnp.int32, (UPDATE_ROWS, ROWS), 0)).astype(F32).astype(BF16)
    for s in range(8):
        at = pl.ds(s, UPDATE_ROWS, stride=8)
        value = dot_nn(swap, grad[:, 128 * s : 128 * s + 128])
        new_master[at, :], new_first[at, :], new_second[at, :] = adam(
            value, master[at, :], first[at, :], second[at, :]
        )


def update_owned(owned, table, grad, master, first, second, act, inp, batch):
    part = pl.BlockSpec((8 * UPDATE_ROWS, 128), lambda i: (i, 0))
    slot = pl.BlockSpec((1,) + act.shape[1:], lambda i: (i, 0, 0))
    return pl.pallas_call(
        partial(update_kernel, batch),
        grid=(ROWS // UPDATE_ROWS,),
        out_shape=[jax.ShapeDtypeStruct(master.shape, F32)] * 3
        + [jax.ShapeDtypeStruct(a.shape, a.dtype) for a in (act, inp)],
        in_specs=[
            pl.BlockSpec(memory_space=pltpu.SMEM),
            pl.BlockSpec(table.shape, lambda i: (0, 0)),
            pl.BlockSpec((ROWS, 1024), lambda i: (0, 0)),
            part,
            part,
            part,
            slot,
            slot,
        ],
        out_specs=[part] * 3 + [slot, slot],
        compiler_params=pltpu.CompilerParams(vmem_limit_bytes=VMEM_LIMIT),
        name="update_owned",
    )(owned, table, grad, master, first, second, act, inp)


def key_positions(rows, piece, per):
    i = lax.broadcasted_iota(jnp.int32, (rows, 1), 0)
    local_rows = rows // per
    return ((i % local_rows) // piece * per + i // local_rows) * piece + i % piece


def scores_t(k, q, ends, piece, per):
    s = lax.dot_general(k, q, (((1,), (1,)), ((), ())), preferred_element_type=F32)
    pos = key_positions(k.shape[0], piece, per)
    cols = []
    for t in range(q.shape[0] // piece):
        part = s[:, t * piece : (t + 1) * piece]
        cols.append(jnp.where(pos < ends[t], part, NEG_FILL))
    return jnp.concatenate(cols, axis=1)


def attend_kernel(piece, per, ends, q, k, v, o):
    outs = []
    for a in range(2):
        cut = slice(64 * a, 64 * a + 64)
        s = scores_t(k[:, cut], q[:, cut], ends, piece, per)
        peak = jnp.max(s, axis=0, keepdims=True)
        e = jnp.exp(s - peak)
        p = (e * (1.0 / jnp.sum(e, axis=0, keepdims=True))).astype(BF16)
        outs.append(lax.dot_general(p, v[:, cut], (((0,), (0,)), ((), ())), preferred_element_type=F32))
    o[...] = jnp.concatenate(outs, axis=1).astype(BF16)


def attend(ends, q, kv, piece, per):
    rows, width = q.shape
    keys = kv.shape[0]
    pairs = width // 128
    return pl.pallas_call(
        partial(attend_kernel, piece, per),
        grid_spec=pltpu.PrefetchScalarGridSpec(
            num_scalar_prefetch=1,
            grid=(pairs,),
            in_specs=[
                pl.BlockSpec((rows, 128), lambda h, e: (0, h)),
                pl.BlockSpec((keys, 128), lambda h, e: (0, h)),
                pl.BlockSpec((keys, 128), lambda h, e: (0, h + pairs)),
            ],
            out_specs=pl.BlockSpec((rows, 128), lambda h, e: (0, h)),
        ),
        out_shape=jax.ShapeDtypeStruct((rows, width), BF16),
        compiler_params=pltpu.CompilerParams(vmem_limit_bytes=VMEM_LIMIT),
        cost_estimate=pl.CostEstimate(
            flops=4 * rows * keys * width, bytes_accessed=4 * (rows + keys) * width, transcendentals=rows * keys * H
        ),
        name="attend",
    )(ends, q, kv, kv)


def attend_back_kernel(piece, per, ends, q, k, v, do, dq, dk, dv):
    dqs, dks, dvs = [], [], []
    for a in range(2):
        cut = slice(64 * a, 64 * a + 64)
        qa, ka, va, da = q[:, cut], k[:, cut], v[:, cut], do[:, cut]
        s = scores_t(ka, qa, ends, piece, per)
        peak = jnp.max(s, axis=0, keepdims=True)
        e = jnp.exp(s - peak)
        p = e * (1.0 / jnp.sum(e, axis=0, keepdims=True))
        dvs.append(jnp.dot(p.astype(BF16), da, preferred_element_type=F32))
        dp = lax.dot_general(va, da, (((1,), (1,)), ((), ())), preferred_element_type=F32)
        pdp = p * dp
        row = jnp.sum(pdp, axis=0, keepdims=True)
        ds = (pdp - p * row).astype(BF16)
        dks.append(jnp.dot(ds, qa, preferred_element_type=F32))
        dqs.append(lax.dot_general(ds, ka, (((0,), (0,)), ((), ())), preferred_element_type=F32))
    dq[...] = jnp.concatenate(dqs, axis=1).astype(BF16)
    dk[...] = jnp.concatenate(dks, axis=1).astype(BF16)
    dv[...] = jnp.concatenate(dvs, axis=1).astype(BF16)


def attend_back(ends, q, kv, do, piece, per):
    rows, width = q.shape
    keys = kv.shape[0]
    pairs = width // 128
    mine = pl.BlockSpec((rows, 128), lambda h, e: (0, h))
    allk = pl.BlockSpec((keys, 128), lambda h, e: (0, h))
    return pl.pallas_call(
        partial(attend_back_kernel, piece, per),
        grid_spec=pltpu.PrefetchScalarGridSpec(
            num_scalar_prefetch=1,
            grid=(pairs,),
            in_specs=[mine, allk, pl.BlockSpec((keys, 128), lambda h, e: (0, h + pairs)), mine],
            out_specs=[mine, allk, allk],
        ),
        out_shape=[
            jax.ShapeDtypeStruct((rows, width), BF16),
            jax.ShapeDtypeStruct((keys, width), BF16),
            jax.ShapeDtypeStruct((keys, width), BF16),
        ],
        compiler_params=pltpu.CompilerParams(vmem_limit_bytes=VMEM_LIMIT),
        cost_estimate=pl.CostEstimate(
            flops=10 * rows * keys * width, bytes_accessed=6 * (rows + keys) * width, transcendentals=rows * keys * H
        ),
        name="attend_back",
    )(ends, q, kv, kv, do)


def layer_stats(values):
    centre = values - jnp.mean(values, axis=-1, keepdims=True)
    inv_std = lax.rsqrt(jnp.mean(centre * centre, axis=-1, keepdims=True) + 1e-06)
    return (centre * inv_std, inv_std)


def norm_back(upstream, normed, inv_std):
    mean_grad = jnp.mean(upstream, axis=-1, keepdims=True)
    mean_cross = jnp.mean(upstream * normed, axis=-1, keepdims=True)
    return inv_std * (upstream - mean_grad - normed * mean_cross)


def noise_embedding(levels, feature_width):
    half_width = feature_width // 2
    frequencies = jnp.exp(
        -math.log(10000.0) * jnp.arange(half_width, dtype=jnp.float32) / half_width
    )
    angles = levels.astype(jnp.float32)[:, None] * frequencies[None, :]
    return jnp.concatenate([jnp.cos(angles), jnp.sin(angles)], axis=1)


def silu_embedding(levels, width):
    return jax.nn.silu(noise_embedding(levels, width)).astype(BF16)


def split_flat(flat_values, model_width, hidden_width):
    matrix_shapes = (
        (model_width, 6 * model_width),
        (model_width, 3 * model_width),
        (model_width, model_width),
        (model_width, hidden_width),
        (hidden_width, model_width),
    )
    matrices = []
    offset_now = 0
    for matrix_shape in matrix_shapes:
        entry_count = matrix_shape[0] * matrix_shape[1]
        matrices.append(flat_values[offset_now : offset_now + entry_count].reshape(matrix_shape))
        offset_now = offset_now + entry_count
    return matrices


def shards(
    frame_size,
    batch_size,
    tokens,
    out_cotangent,
    buckets,
    noise_levels,
    owned_block,
    master,
    first_moment,
    second_moment,
):
    micro_count, piece, width = tokens.shape
    block_size = master.shape[1]
    frame_count = noise_levels.shape[1]
    total = frame_size * batch_size
    videos = micro_count
    per = frame_size // videos
    rows = videos * piece
    keys = rows * per
    q_scale = HD ** (-0.5)
    f, z = frame_index()
    me = f * batch_size + z
    mine, g = f // per, f % per
    direct = frame_size == 8 and batch_size == 4 and block_size == ROWS * 1024 and videos == 4 and frame_count == 4

    if direct:
        order = jnp.arange(total, dtype=jnp.int32)
        inverse = jnp.sum(jnp.where(owned_block[None, :] == order[:, None], order[None, :], 0), axis=1)
        table = jnp.asarray(np.stack([block_rows(b) for b in range(total)]).astype(np.int32))
        blk = cut_owned(owned_block, table, master.reshape(-1, 128), batch_size)
        cond = silu_embedding(noise_levels.reshape(16), width)
    else:
        tok, cot = swap_videos([tokens, out_cotangent], videos, per, 0)
        gathered = lax.all_gather(master.astype(BF16), ("frame", "batch"), axis=0, tiled=True)
        placed = jnp.take(gathered, jnp.argsort(owned_block), axis=0).reshape(-1)
        w_ada, w_qkv, w_out, w_in, w_down = split_flat(placed, width, FF)
        cond = silu_embedding(lax.dynamic_index_in_dim(noise_levels, mine, 0, keepdims=False), width)
        modulation = jnp.dot(cond, w_ada, preferred_element_type=F32).reshape(frame_count, 6, width)

    def flat(a):
        return a.reshape(rows, a.shape[-1])

    def cube(a):
        return a.reshape(videos, piece, a.shape[-1])

    def partners(k):
        return [(i, i // per * per + (i + k) % per) for i in range(frame_size)]

    def split_mod(piece_mod):
        return [piece_mod[j][:, None, :] for j in range(6)]

    if direct:
        saved = forward(inverse, buckets, blk, cond, tokens, out_cotangent, total, batch_size, piece, per)
        *saved, block_output, piece_mod, d_gate, cot, cond_all, tokens_own = saved
        grad_block, input_grads, outputs = backward(
            buckets,
            owned_block,
            piece_mod,
            d_gate,
            [*saved, cube(block_output), cot, cond_all, tokens_own],
            total,
            batch_size,
            piece,
            per,
        )
    else:
        frame_len = FRAME_LO * (1 + 3 * buckets[mine])
        piece_at = (jnp.arange(videos, dtype=jnp.int32) * per + g) * piece
        piece_frame = piece_at // frame_len
        ends = (piece_frame + 1) * frame_len
        selector = (piece_frame[:, None] == jnp.arange(frame_count, dtype=jnp.int32)[None, :]).astype(F32)
        x_float = tok.astype(F32)
        normed_one, inv_one = layer_stats(x_float)
        piece_mod = jnp.einsum("pf,fjd->jpd", selector, modulation, precision=HIGHEST)
        shift_one, scale_one, gate_one, shift_two, scale_two, gate_two = split_mod(piece_mod)

        h_one = flat((normed_one * (1.0 + scale_one) + shift_one).astype(BF16))
        projected = jnp.dot(h_one, w_qkv, preferred_element_type=F32)
        queries = (projected[:, :width] * q_scale).astype(BF16)
        kv_own = projected[:, width:].astype(BF16)

        kv_all = jnp.zeros((per, rows, 2 * width), BF16)
        kv_all = lax.dynamic_update_index_in_dim(kv_all, kv_own, g, 0)
        for k in range(1, per):
            kv_all = lax.dynamic_update_index_in_dim(
                kv_all, lax.ppermute(kv_own, "frame", partners(k)), (g + per - k) % per, 0
            )
        kv_all = kv_all.reshape(keys, 2 * width)
        attended = attend(ends, queries, kv_all, piece, per)
        attn_out = jnp.dot(attended, w_out, preferred_element_type=F32)
        middle = x_float + gate_one * cube(attn_out)
        normed_two, inv_two = layer_stats(middle)
        h_two = flat((normed_two * (1.0 + scale_two) + shift_two).astype(BF16))
        pre_act = jnp.dot(h_two, w_in, preferred_element_type=F32)
        activated, gelu_back = jax.vjp(partial(jax.nn.gelu, approximate=True), pre_act)
        act_low = activated.astype(BF16)
        slope = gelu_back(jnp.ones_like(pre_act))[0]
        mlp_out = jnp.dot(act_low, w_down, preferred_element_type=F32)
        block_output = (middle + gate_two * cube(mlp_out)).astype(BF16)

        grad_out = cot.astype(F32)
        d_mlp = flat((gate_two * grad_out).astype(BF16))
        g_down = jnp.dot(act_low.T, d_mlp, preferred_element_type=F32).astype(BF16)
        d_act = jnp.dot(d_mlp, w_down.T, preferred_element_type=F32)
        d_pre = (d_act * slope.astype(F32)).astype(BF16)
        g_in = jnp.dot(h_two.T, d_pre, preferred_element_type=F32).astype(BF16)
        d_htwo = cube(jnp.dot(d_pre, w_in.T, preferred_element_type=F32))
        d_gate_two = jnp.sum(grad_out * cube(mlp_out), axis=1)
        d_scale_two = jnp.sum(d_htwo * normed_two, axis=1)
        d_shift_two = jnp.sum(d_htwo, axis=1)
        d_middle = grad_out + norm_back(d_htwo * (1.0 + scale_two), normed_two, inv_two)
        d_attn = flat((gate_one * d_middle).astype(BF16))
        d_gate_one = jnp.sum(d_middle * cube(attn_out), axis=1)
        g_out = jnp.dot(attended.T, d_attn, preferred_element_type=F32).astype(BF16)
        d_attended = jnp.dot(d_attn, w_out.T, preferred_element_type=F32).astype(BF16)
        dq, dk, dv = attend_back(ends, queries, kv_all, d_attended, piece, per)
        dkv = jnp.concatenate([dk, dv], axis=1).reshape(per, rows, 2 * width)
        dkv_own = lax.dynamic_index_in_dim(dkv, g, 0, keepdims=False).astype(F32)
        for k in range(1, per):
            sent = lax.dynamic_index_in_dim(dkv, (g + k) % per, 0, keepdims=False)
            dkv_own = dkv_own + lax.ppermute(sent, "frame", partners(k)).astype(F32)
        d_proj = jnp.concatenate([dq * jnp.asarray(q_scale, BF16), dkv_own.astype(BF16)], axis=1)
        g_qkv = jnp.dot(h_one.T, d_proj, preferred_element_type=F32).astype(BF16)
        d_hone = cube(jnp.dot(d_proj, w_qkv.T, preferred_element_type=F32))
        d_scale_one = jnp.sum(d_hone * normed_one, axis=1)
        d_shift_one = jnp.sum(d_hone, axis=1)
        d_input = d_middle + norm_back(d_hone * (1.0 + scale_one), normed_one, inv_one)
        input_grad = d_input.astype(BF16)
        piece_dmod = jnp.stack([d_shift_one, d_scale_one, d_gate_one, d_shift_two, d_scale_two, d_gate_two])
        frame_dmod = jnp.einsum("pf,jpd->jfd", selector, piece_dmod, precision=HIGHEST)

    if direct:
        updated = update_owned(
            owned_block,
            table,
            grad_block,
            master.reshape(-1, 128),
            first_moment.reshape(-1, 128),
            second_moment.reshape(-1, 128),
            outputs,
            input_grads,
            batch_size,
        )
        new_master, new_first, new_second = [a.reshape(1, block_size) for a in updated[:3]]
        outputs, input_grads = updated[3:]
    else:
        outputs, input_grads = swap_videos([block_output, input_grad], videos, per, 1)
        g_ada = lax.dot_general(
            cond.astype(F32),
            frame_dmod.transpose(1, 0, 2).reshape(frame_count, 6 * width),
            (((0,), (0,)), ((), ())),
            precision=HIGHEST,
        )
        flat_grads = jnp.concatenate(
            [piece_grad.astype(F32).reshape(-1) for piece_grad in (g_ada, g_qkv, g_out, g_in, g_down)]
        )
        arranged = jnp.take(flat_grads.reshape(-1, block_size), owned_block, axis=0).reshape(-1)
        shard_total = lax.psum_scatter(
            arranged, ("frame", "batch"), scatter_dimension=0, tiled=True
        ).reshape(1, block_size)
        new_master, new_first, new_second = adam(shard_total, master, first_moment, second_moment)
    return (outputs, input_grads, new_master, new_first, new_second)


def solution(mesh):
    placed = (
        P("batch", "frame", None),
        P("batch", "frame", None),
        P("batch"),
        P("batch", None),
        P(),
        P(("frame", "batch"), None),
        P(("frame", "batch"), None),
        P(("frame", "batch"), None),
    )
    return jax.shard_map(
        partial(shards, mesh.shape["frame"], mesh.shape["batch"]),
        mesh=mesh,
        in_specs=placed,
        out_specs=(
            P("batch", "frame", None),
            P("batch", "frame", None),
            P(("frame", "batch"), None),
            P(("frame", "batch"), None),
            P(("frame", "batch"), None),
        ),
        check_vma=False,
    )
```

```python
from functools import partial
import math

import jax
import jax.numpy as jnp
import numpy as np
from jax import lax
from jax.experimental import pallas as pl
from jax.experimental.pallas import tpu as pltpu
from jax.sharding import PartitionSpec as P

H = 16
HD = 64
FF = 4096
FRAME_LO = 256
STEP = 10

HIGHEST = lax.Precision.HIGHEST
NEG_FILL = -1e30
BETA_ONE = 0.5
BETA_TWO = 0.5
LEARN_RATE = 0.05
WEIGHT_DECAY = 0.1
ADAM_EPS = 1e-08
MESH = pl.DeviceIdType.MESH
F32 = jnp.float32
BF16 = jnp.bfloat16
ANY = pl.BlockSpec(memory_space=pl.ANY)
VMEM_LIMIT = 63 * 1024 * 1024

ROWS = 576
GROUP = 144
FIRST = 10
KINDS = (("qkv", 1024, 3), ("out", 1024, 1), ("in", 1024, 4), ("down", 4096, 1))
HELD = 3168
THIRD = 48
ADA = 1664


def pieces(kind, z):
    if kind == "qkv":
        found = [(48 * j, 16, 16 * z, j) for j in range(3)]
        for k in range(5):
            found += [(144 + 144 * k + 48 * j, 48, 64 + 192 * k + 48 * z, j) for j in range(3)]
        return found
    if kind == "out":
        return [(864, 144, 144 * z, 0), (1008, 112, 576 + 112 * z, 0)]
    if kind == "in":
        return [(1120, 1024, 0, z)]
    found = [(2144, 16, 16 * z, 0)]
    return found + [(2160 + 144 * k, 144, 64 + 576 * k + 144 * z, 0) for k in range(7)]


def block_rows(block):
    t = np.arange(GROUP)
    groups = []
    for z in range(4):
        if block == 10:
            i, j = t % THIRD, t // THIRD
            rows = np.where(i < 16, 384 + 3 * (16 * z + i) + j, 96 * z + 32 * j + i - 16)
        elif 11 <= block <= 15:
            rows = 3 * (48 * z + t % 48) + t // 48
        elif block == 17:
            rows = np.where(t < 112, 112 * z + t, 448 + 4 * (t - 112) + z)
        elif 18 <= block <= 23:
            rows = 4 * t + z
        elif block == 24:
            rows = np.where(t < 128, 4 * t + z, 512 + 16 * z + t - 128)
        else:
            rows = GROUP * z + t
        groups.append(rows)
    return np.concatenate(groups)


def ada_place(n, z):
    b, t = n // GROUP, n % GROUP
    i = t % THIRD - 16
    a = 32 * (t // THIRD) + i
    row = jnp.where(b < 10, 96 * b + 24 * z + t // 6, 960 + 16 * z + a // 6)
    col = jnp.where(b < 10, t % 6, a % 6)
    none = (b > 10) | ((b == 10) & (i < 0))
    return jnp.where(none, -1, row), col


def frame_index():
    return lax.axis_index("frame"), lax.axis_index("batch")


def strip_of(f):
    return 4 * (f % 2) + f // 2


def greet(devices):
    barrier = pltpu.get_barrier_semaphore()
    for device in devices:
        pl.semaphore_signal(barrier, inc=1, device_id=device, device_id_type=MESH)
    pl.semaphore_wait(barrier, len(devices))


def greet_all(total, batch):
    f, z = frame_index()
    me = f * batch + z
    barrier = pltpu.get_barrier_semaphore()

    def hail(k, carry):
        other = (me + k) % total
        pl.semaphore_signal(barrier, inc=1, device_id=(other // batch, other % batch), device_id_type=MESH)
        return carry

    lax.fori_loop(1, total, hail, 0)
    pl.semaphore_wait(barrier, total - 1)


def remote(src, dst, send, recv, device):
    copy = pltpu.make_async_remote_copy(
        src_ref=src, dst_ref=dst, send_sem=send, recv_sem=recv, device_id=device, device_id_type=MESH
    )
    copy.start()
    return copy


def local(src, dst, sem):
    copy = pltpu.make_async_copy(src, dst, sem)
    copy.start()
    return copy


def video_kernel(videos, per, arrays, *refs):
    ins, outs = refs[:arrays], refs[arrays : 2 * arrays]
    send, recv, own = refs[2 * arrays :]
    f, z = frame_index()
    mine, g = f // per, f % per
    others = [((mine + k) % videos, k) for k in range(1, videos)]
    greet([(v * per + g, z) for v, k in others])
    copies = []
    for a in range(arrays):
        for v, k in others:
            copies.append(
                remote(ins[a].at[v], outs[a].at[mine], send.at[a, k], recv.at[a, k], (v * per + g, z))
            )
        copies.append(local(ins[a].at[mine], outs[a].at[mine], own.at[a]))
    for copy in copies:
        copy.wait()


def swap_videos(arrays, videos, per, ident):
    count = len(arrays)
    return pl.pallas_call(
        partial(video_kernel, videos, per, count),
        out_shape=[jax.ShapeDtypeStruct(a.shape, a.dtype) for a in arrays],
        in_specs=[ANY] * count,
        out_specs=[ANY] * count,
        scratch_shapes=[
            pltpu.SemaphoreType.DMA((count, videos)),
            pltpu.SemaphoreType.DMA((count, videos)),
            pltpu.SemaphoreType.DMA((count,)),
        ],
        compiler_params=pltpu.CompilerParams(collective_id=ident, has_side_effects=True),
        name="swap_videos",
    )(*arrays)


def plane():
    f, z = frame_index()
    y, x, c = f // 4, (f // 2) % 2, f % 2
    at_x = (4 * y + 2 * (1 - x) + c, z)
    at_y = (4 * (1 - y) + 2 * x + c, z)
    at_c = (4 * y + 2 * x + 1 - c, z)
    return y, x, c, z, at_x, at_y, at_c


def lanes(first, count):
    return pl.ds(pl.multiple_of(first, 128), count)


UNITS = (
    [("qkv", 0, 1024, 1024 * j) for j in range(3)]
    + [("out", 0, 1024, 0)]
    + [("down", 1024 * n, 1024, 0) for n in range(4)]
    + [("in", 0, 1024, 1024 * j) for j in range(4)]
)
AHEAD = 2
PLACE = {"qkv": (0, 1, 2), "out": (3,), "down": (4, 5, 6, 7), "in": (8, 9, 10, 11)}
DOWN_DEALS = [("down", 0, 0, 1216, 304), ("down", 0, 1216, 1152, 288), ("down", 0, 2368, 1152, 288), ("down", 0, 3520, 576, 144)]
QKV_DEALS = [("qkv", j, 0, 1024, 256) for j in range(3)]
OUT_DEAL = ("out", 0, 0, 1024, 256)
DEALS = QKV_DEALS + [OUT_DEAL]
for n in range(4):
    DEALS += [DOWN_DEALS[n], ("in", None, 256 * n, 256, 256)]
DEALS_OF = ((0,), (1,), (2,), (3,), (4,), (6,), (8,), (10,)) + ((5, 7, 9, 11),) * 4
BACK_DEALS = QKV_DEALS + [OUT_DEAL, DOWN_DEALS[0], ("in", None, 0, 1024, 1024)] + DOWN_DEALS[1:]
IN_DEAL = 5


def deal_pieces(deals, d, z):
    kind, j, first, count, _ = deals[d]
    if kind == "in":
        return [(1120 + first, count, first, z)]
    found = zip(pieces(kind, z), pieces(kind, 0))
    if kind == "down":
        return [p for p, at_zero in found if first <= at_zero[2] < first + count]
    return [p for p, _ in found if p[3] == j]


GELU_A = math.sqrt(2.0 / math.pi)
GELU_B = 0.044715


def row_loop(count, step, body):
    def one(i, carry):
        body(pl.multiple_of(i * step, step))
        return carry

    lax.fori_loop(0, count // step, one, 0)


def norm_rows(values):
    centre = values - jnp.mean(values, axis=-1, keepdims=True)
    inv_std = lax.rsqrt(jnp.mean(centre * centre, axis=-1, keepdims=True) + 1e-06)
    return centre * inv_std, inv_std


def lane_half(e):
    return lax.broadcasted_iota(jnp.int32, (1, 128), 1) // 64 == e


def choose(mask, one, other):
    return jnp.where(mask, one.astype(F32), other.astype(F32)).astype(BF16)


def three_parts(value):
    high = value.astype(BF16).astype(F32)
    rest = value - high
    middle = rest.astype(BF16).astype(F32)
    return high, middle, rest - middle


def in_lanes(parts, first):
    lane = lax.broadcasted_iota(jnp.int32, (1, 128), 1) % 64
    total = 0.0
    for n, part in enumerate(parts):
        total = total + jnp.where(lane == first + n, part, 0.0)
    return total


def query_mask(ends, piece):
    lane = lax.broadcasted_iota(jnp.int32, (piece, 128), 1) % 64
    found = []
    for t in range(4):
        hidden = (lane < 4) & (lane * FRAME_LO >= ends[t])
        found.append(jnp.where(hidden, NEG_FILL, 0.0))
    return jnp.concatenate(found, axis=0)


def key_mask(keys, piece, per):
    lane = lax.broadcasted_iota(jnp.int32, (keys, 128), 1) % 64
    quarter = key_positions(keys, piece, per) // FRAME_LO
    return jnp.where((lane == quarter) | ((lane >= 4) & (lane < 7)), 1.0, 0.0)


def dot_nt(a, b):
    return lax.dot_general(a, b, (((1,), (1,)), ((), ())), preferred_element_type=F32)


def dot_tn(a, b):
    return lax.dot_general(a, b, (((0,), (0,)), ((), ())), preferred_element_type=F32)


def dot_nn(a, b):
    return jnp.dot(a, b, preferred_element_type=F32)


def fold_rows(values):
    return values[:8] + values[8:]


def frames_of(buckets, mine, g, piece, per):
    large = buckets[mine] > 0
    sel, ends = [], []
    for p in range(4):
        at = (p * per + g) * piece
        frame = jnp.where(large, at // (4 * FRAME_LO), at // FRAME_LO)
        sel.append([jnp.where(frame == fr, 1.0, 0.0) for fr in range(4)])
        ends.append((frame + 1) * jnp.where(large, 4 * FRAME_LO, FRAME_LO))
    return sel, ends


def forward_kernel(total, batch, piece, per, inverse, buckets, blk, cond_i, tok_i, cot_i, *refs):
    hbm, vm, sems = refs[:20], refs[20:49], refs[49:]
    wq_o, wo_o, wi_o, wd_o, h1_o, q_o, qb_o, kv_o, att_o, a_o, x1_o, h2_o, gp_o, u_o, y_o, pm_o, dg_o, cot_o, spread_o, tok_o = hbm
    wq, wo, wi, wd, h1, q, qb, kv, att, a, x1, h2, gp, u, acc, pm, mod_v, dg, kmask, cot = vm[:20]
    tok, held, cond, spread, mod, *cut, mod_half = vm[20:]
    zsend, zrecv, psend, precv, msend, mrecv, own, wsem, osem, kvsend, kvrecv, vsend, vrecv = sems[:13]
    csend, crecv, lsend, lrecv, hsend, hrecv = sems[13:]
    mats = {"qkv": wq, "out": wo, "in": wi, "down": wd}
    mats_o = {"qkv": wq_o, "out": wo_o, "in": wi_o, "down": wd_o}
    y, x, c, z, at_x, at_y, at_c = plane()
    f = 4 * y + 2 * x + c
    me = f * batch + z
    strip = 4 * c + 2 * y + x
    mine, g = f // per, f % per
    sel, ends = frames_of(buckets, mine, g, piece, per)
    greet_all(total, batch)

    def third_of(n, of, oz):
        return blk.at[
            pl.ds(pl.multiple_of(GROUP * oz + THIRD * n, 16), THIRD), lanes(128 * strip_of(of), 128)
        ]

    def send_third(n):
        def one(k, carry):
            other = (me + k) % total
            of, oz = other // batch, other % batch
            pltpu.make_async_remote_copy(
                src_ref=third_of(n, of, oz),
                dst_ref=cut[n].at[me],
                send_sem=csend.at[n],
                recv_sem=crecv.at[n],
                device_id=(of, oz),
                device_id_type=MESH,
            ).start()
            return carry

        lax.fori_loop(1, total, one, 0)

    def others(n):
        return cut[n].at[pl.ds(0, total - 1)]

    def take_third(n):
        pltpu.make_async_copy(others(n), others(n), crecv.at[n]).wait()
        own_thirds[n].wait()
        if n + 2 < 3:
            send_third(n + 2)

        def one(b, carry):
            held[pl.ds(pl.multiple_of(GROUP * b + THIRD * n, 16), THIRD), :] = cut[n][inverse[b]]
            return carry

        lax.fori_loop(0, total, one, 0)

    def send_video(src, dst, s, sem):
        for k in range(1, 4):
            v = (mine + k) % 4
            videos[s].append(
                remote(
                    src.at[v],
                    dst.at[pl.ds(pl.multiple_of(mine * piece, piece), piece)],
                    vsend.at[s, k],
                    vrecv.at[s, k],
                    (v * per + g, z),
                )
            )
        videos[s].append(local(src.at[mine], dst.at[pl.ds(pl.multiple_of(mine * piece, piece), piece)], sem))

    videos = ([], [])
    send_third(0)
    send_third(1)
    levels = [
        remote(cond_i, cond.at[pl.ds(pl.multiple_of(16 * z, 16), 16)], lsend.at[k], lrecv.at[k], (f, (z + k) % batch))
        for k in range(1, batch)
    ]
    levels.append(local(cond_i, cond.at[pl.ds(pl.multiple_of(16 * z, 16), 16)], own.at[len(DEALS)]))
    own_thirds = [local(third_of(n, f, z), cut[n].at[me], own.at[len(DEALS) + 1 + n]) for n in range(3)]
    send_video(tok_i, tok, 0, own.at[len(DEALS) + 4])

    def mod_group(k, start):
        other = (f // 2 * batch + z + k) % (4 * batch)
        chip, oz = other // batch, other % batch
        copy = pltpu.make_async_remote_copy(
            src_ref=mod.at[4 * oz + chip],
            dst_ref=mod_v.at[z, :, lanes(128 * (f // 2), 128)],
            send_sem=msend.at[k],
            recv_sem=mrecv.at[k],
            device_id=(2 * chip + c, oz),
            device_id_type=MESH,
        )
        if start:
            copy.start()
        else:
            copy.wait()

    def spot(kind, to, count, j):
        return mats[kind].at[pl.ds(pl.multiple_of(to, 16), count), lanes(1024 * j + 128 * strip, 128)]

    base = FIRST * GROUP

    def deal(d):
        kind = DEALS[d][0]
        for k in range(1, batch):
            for row, count, to, j in deal_pieces(DEALS, d, z):
                remote(
                    held.at[pl.ds(base + row, count)], spot(kind, to, count, j), zsend.at[d, k], zrecv.at[d, k],
                    (f, (z + k) % batch),
                )
        for row, count, to, j in deal_pieces(DEALS, d, z):
            local(held.at[pl.ds(base + row, count)], spot(kind, to, count, j), own.at[d])

    def whole(d):
        return held.at[pl.ds(0, DEALS[d][4])]

    dealt = set()
    following = [2]

    def deal_wait(d):
        if d in dealt:
            return
        dealt.add(d)
        for k in range(1, batch):
            pltpu.make_async_copy(whole(d), whole(d), zrecv.at[d, k]).wait()
        pltpu.make_async_copy(whole(d), whole(d), own.at[d]).wait()
        while following[0] <= min(d + AHEAD, len(DEALS) - 1):
            deal(following[0])
            following[0] += 1

    slots = {}
    counter = [0]

    def push(key, mat, row, count, col, width, device):
        s = counter[0]
        counter[0] += 1
        ref = mat.at[pl.ds(row, count), lanes(col, width)]
        slots.setdefault(key, []).append(remote(ref, ref, psend.at[s], precv.at[s], device))

    def stage_a(n):
        kind, row, rows, col = UNITS[n]
        half = rows // 2
        for d in DEALS_OF[n]:
            deal_wait(d)
        push((n, 1), mats[kind], row, half, col + 128 * strip, 128, at_x)
        push((n, 1), mats[kind], row + half, half, col + 128 * strip, 128, at_y)

    def stage_b(n):
        kind, row, rows, col = UNITS[n]
        half = rows // 2
        for copy in slots[(n, 1)]:
            copy.wait_recv()
        push((n, 2), mats[kind], row, half, col + 512 * c + 256 * y, 256, at_y)
        for yy in range(2):
            push((n, 2), mats[kind], row + half, half, col + 512 * c + 256 * yy + 128 * x, 128, at_x)

    def stage_c(n):
        kind, row, rows, col = UNITS[n]
        for copy in slots[(n, 2)]:
            copy.wait_recv()
        push((n, 3), mats[kind], row, rows, col + 512 * c, 512, at_c)

    saves = []

    def ready(n):
        kind, row, rows, col = UNITS[n]
        for copy in slots[(n, 3)]:
            copy.wait_recv()
        ref = (pl.ds(row, rows), pl.ds(col, 1024))
        saves.append(local(mats[kind].at[ref], mats_o[kind].at[ref], wsem.at[n]))

    pumped = [0]
    last_unit = len(UNITS)

    def pump():
        s = pumped[0]
        pumped[0] += 1
        if 0 <= s - 2 < last_unit:
            stage_b(s - 2)
        if s < last_unit:
            stage_a(s)
        if 0 <= s - 3 < last_unit:
            stage_c(s - 3)

    def pump_to(s):
        while pumped[0] <= s:
            pump()

    def save(src, dst, n):
        saves.append(local(src, dst, osem.at[n]))

    take_third(0)
    deal(0)
    send_video(cot_i, cot, 1, own.at[len(DEALS) + 5])
    take_third(1)
    deal(1)
    take_third(2)
    pump_to(0)
    for copy in levels:
        copy.wait()
    row_id = lax.broadcasted_iota(jnp.int32, (384, 1), 0)
    expand = (
        lax.broadcasted_iota(jnp.int32, (384, 64), 1) == 4 * (row_id // 24) + row_id % 4
    ).astype(F32).astype(BF16)

    def mod_tile(n, carry):
        index = 128 * n + lax.broadcasted_iota(jnp.int32, (1, 128), 1)
        row, col = ada_place(index, z)
        pick = (lax.broadcasted_iota(jnp.int32, (1024, 128), 0) == row).astype(F32).astype(BF16)
        wide = dot_nn(expand, dot_nn(cond[...], pick).astype(BF16))
        wide = jnp.where(col == (row_id % 24) // 4, wide, 0.0).astype(BF16)
        spread[:, lanes(128 * n, 128)] = wide
        part = dot_nn(wide, held[pl.ds(pl.multiple_of(128 * n, 128), 128), :])
        return carry + part

    part = jnp.zeros((384, 128), F32)
    part = lax.fori_loop(0, 7, mod_tile, part)
    pump_to(1)
    part = lax.fori_loop(7, 13, mod_tile, part)
    for v in range(16):
        mod[v] = part[24 * v : 24 * v + 24]
    lax.fori_loop(1, 4 * batch, lambda k, t: (mod_group(k, True), t)[1], 0)
    mod_own = local(mod.at[4 * z + f // 2], mod_v.at[z, :, lanes(128 * (f // 2), 128)], own.at[len(DEALS) + 6])
    pump_to(2)
    lax.fori_loop(1, 4 * batch, lambda k, t: (mod_group(k, False), t)[1], 0)
    mod_own.wait()
    half_row = mod_v[0]
    for s in range(1, batch):
        half_row = half_row + mod_v[s]
    mod_half[c] = half_row
    half_copy = remote(mod_half.at[c], mod_half.at[c], hsend, hrecv, at_c)
    save(spread, spread_o, 14)
    half_copy.wait()
    for copy in videos[0]:
        copy.wait()
    save(tok, tok_o, 15)
    for j in range(6):
        for p in range(4):
            value = jnp.zeros((1, 1024), F32)
            for fr in range(4):
                row = [mod_half[e, pl.ds(4 * j + fr, 1), :] for e in range(2)]
                value = value + sel[p][fr] * jnp.concatenate(row, axis=1)
            pm[pl.ds(4 * j + p, 1), :] = value
    save(pm, pm_o, 0)

    def mod_row(j, p):
        return pm[pl.ds(4 * j + p, 1), :]

    step = 32
    for p in range(4):
        shift, scale = mod_row(0, p), mod_row(1, p)

        def one(i, p=p, shift=shift, scale=scale):
            rows = pl.ds(pl.multiple_of(p * piece + i, step), step)
            normed, _ = norm_rows(tok[rows, :].astype(F32))
            h1[rows, :] = (normed * (1.0 + scale) + shift).astype(BF16)

        row_loop(piece, step, one)
    save(h1, h1_o, 1)
    saves_h1 = saves[-1]

    pump_to(4)
    for j in range(3):
        pump_to(3 + j)
        ready(j)

        def cols(n, j=j):
            value = jnp.dot(h1[...], wq[:, lanes(1024 * j + n, 512)], preferred_element_type=F32)
            if j == 0:
                q[:, lanes(n, 512)] = (value * HD ** (-0.5)).astype(BF16)
            else:
                kv[c, :, lanes(1024 * (j - 1) + n, 512)] = value.astype(BF16)

        row_loop(1024, 512, cols)
    save(q, q_o, 2)
    kv_copy = remote(kv.at[c], kv.at[c], kvsend, kvrecv, at_c)
    pump_to(6)
    kv_copy.wait_recv()
    save(kv, kv_o, 3)

    keys = 2 * 4 * piece
    qb_mask = query_mask(ends, piece)
    acc[:, 0:128] = qb_mask
    kmask[...] = key_mask(keys, piece, per).astype(BF16)

    def heads(h):
        pair = lanes(128 * h, 128)
        k_pair = kv[:, :, pair].reshape(keys, 128)
        v_pair = kv[:, :, lanes(1024 + 128 * h, 128)].reshape(keys, 128)
        q_pair = q[:, pair]
        outs, parts = [], []
        for e in range(2):
            mine = lane_half(e)
            s = dot_nt(choose(mine, q_pair, acc[:, 0:128]), choose(mine, k_pair, kmask[...]))
            peak = jnp.max(s, axis=1, keepdims=True)
            w = jnp.exp(s - peak).astype(BF16)
            o = dot_nn(w, choose(mine, v_pair, jnp.ones_like(v_pair)))
            outs.append(o / pltpu.roll(o, 64, 1))
            parts.append(-(peak + jnp.log(jnp.where(mine, 1.0, o))))
        att[:, pair] = choose(lane_half(0), outs[0], outs[1])
        level = jnp.where(lane_half(1), parts[0], parts[1])
        qb[:, pair] = (acc[:, 0:128] + in_lanes(three_parts(level), 4)).astype(BF16)

    for n in range(4):
        lax.fori_loop(2 * n, 2 * n + 2, lambda h, t: (heads(h), t)[1], 0)
        pump_to(7 + n)
    save(att, att_o, 4)
    save(qb, qb_o, 12)

    ready(3)

    def out_cols(n):
        value = dot_nn(att[...], wo[:, lanes(n, 512)])
        acc[:, lanes(n, 512)] = value
        a[:, lanes(n, 512)] = value.astype(BF16)

    row_loop(1024, 512, out_cols)
    save(a, a_o, 5)
    for p in range(4):
        gate, shift, scale = mod_row(2, p), mod_row(3, p), mod_row(4, p)

        def two(i, p=p, gate=gate, shift=shift, scale=scale):
            rows = pl.ds(pl.multiple_of(p * piece + i, step), step)
            middle = tok[rows, :].astype(F32) + gate * acc[rows, :]
            x1[rows, :] = middle
            normed, _ = norm_rows(middle)
            h2[rows, :] = (normed * (1.0 + scale) + shift).astype(BF16)

        row_loop(piece, step, two)
    save(x1, x1_o, 6)
    save(h2, h2_o, 7)

    for j in range(4):
        pump_to(11 + j)
        ready(PLACE["in"][j])

        def in_cols(n, j=j):
            col = 1024 * j + n
            pre = jnp.dot(h2[...], wi[:, lanes(col, 512)], preferred_element_type=F32)
            square = pre * pre
            t = jnp.tanh(GELU_A * (pre + GELU_B * (square * pre)))
            lift = 0.5 * (1.0 + t)
            u[:, lanes(col, 512)] = (pre * lift).astype(BF16)
            slope = lift + (0.5 * GELU_A) * pre * (1.0 - t * t) * (1.0 + 3.0 * GELU_B * square)
            gp[:, lanes(col, 512)] = slope.astype(BF16)

        row_loop(1024, 512, in_cols)
        if j == 0:
            for n in PLACE["down"]:
                ready(n)

        def down_cols(col, j=j):
            part = dot_nn(u[:, 1024 * j : 1024 * j + 1024], wd[1024 * j : 1024 * j + 1024, lanes(col, 512)])
            if j == 0:
                acc[:, lanes(col, 512)] = part
            else:
                acc[:, lanes(col, 512)] = acc[:, lanes(col, 512)] + part

        row_loop(1024, 512, down_cols)
    save(u, u_o, 8)
    save(gp, gp_o, 9)
    saves_h1.wait()
    for copy in videos[1]:
        copy.wait()
    save(cot, cot_o, 13)
    for p in range(4):
        gate = mod_row(5, p)

        def three(i, total_grad, p=p, gate=gate):
            rows = pl.ds(pl.multiple_of(p * piece + i * 16, 16), 16)
            value = acc[rows, :]
            h1[rows, :] = (x1[rows, :] + gate * value).astype(BF16)
            return total_grad + fold_rows(cot[rows, :].astype(F32) * value)

        part = lax.fori_loop(0, piece // 16, three, jnp.zeros((8, 1024), F32))
        dg[pl.ds(p, 1), :] = jnp.sum(part, axis=0, keepdims=True)
    dg[pl.ds(4, 4), :] = jnp.zeros((4, 1024), F32)
    save(dg, dg_o, 10)
    save(h1, y_o, 11)
    for copy in saves:
        if copy is not saves_h1:
            copy.wait()
    kv_copy.wait_send()
    for copies in slots.values():
        for copy in copies:
            copy.wait_send()
    for n in range(3):
        pltpu.make_async_copy(others(n), others(n), csend.at[n]).wait()
    for d in range(len(DEALS)):
        for k in range(1, batch):
            pltpu.make_async_copy(whole(d), whole(d), zsend.at[d, k]).wait()


def forward(inverse, buckets, blk, cond, tok, cot, total, batch, piece, per):
    def out(*shape, dtype=BF16):
        return jax.ShapeDtypeStruct(shape, dtype)

    outs = [out(depth, 1024 * blocks) for _, depth, blocks in KINDS] + [
        out(512, 1024),
        out(512, 1024),
        out(512, 1024),
        out(2, 512, 2048),
        out(512, 1024),
        out(512, 1024),
        out(512, 1024, dtype=F32),
        out(512, 1024),
        out(512, 4096),
        out(512, 4096),
        out(512, 1024),
        out(24, 1024, dtype=F32),
        out(8, 1024, dtype=F32),
        out(512, 1024),
        out(384, ADA),
        out(512, 1024),
    ]
    bufs = [pltpu.VMEM(o.shape, o.dtype) for o in outs[:14]] + [
        pltpu.VMEM((512, 1024), F32),
        pltpu.VMEM((24, 1024), F32),
        pltpu.VMEM((batch, 24, 512), F32),
        pltpu.VMEM((8, 1024), F32),
        pltpu.VMEM((1024, 128), BF16),
        pltpu.VMEM((512, 1024), BF16),
        pltpu.VMEM((512, 1024), BF16),
        pltpu.VMEM((total * GROUP, 128), BF16),
        pltpu.VMEM((64, 1024), BF16),
        pltpu.VMEM((384, ADA), BF16),
        pltpu.VMEM((16, 24, 128), F32),
    ] + [pltpu.VMEM((total, THIRD, 128), BF16) for _ in range(3)]
    bufs.append(pltpu.VMEM((2, 24, 512), F32))
    smem = pl.BlockSpec(memory_space=pltpu.SMEM)
    dma = pltpu.SemaphoreType.DMA
    return pl.pallas_call(
        partial(forward_kernel, total, batch, piece, per),
        out_shape=outs,
        in_specs=[smem, smem] + [ANY] * 4,
        out_specs=[ANY] * len(outs),
        scratch_shapes=bufs
        + [
            dma((len(DEALS), batch)),
            dma((len(DEALS), batch)),
            dma((6 * len(UNITS),)),
            dma((6 * len(UNITS),)),
            dma((total,)),
            dma((total,)),
            dma((len(DEALS) + 7,)),
            dma((len(UNITS),)),
            dma((16,)),
            dma,
            dma,
            dma((2, 4)),
            dma((2, 4)),
            dma((3,)),
            dma((3,)),
            dma((batch,)),
            dma((batch,)),
            dma,
            dma,
        ],
        compiler_params=pltpu.CompilerParams(
            collective_id=1, has_side_effects=True, vmem_limit_bytes=VMEM_LIMIT
        ),
        name="forward",
    )(inverse, buckets, blk, cond, tok, cot)


LEAVES = (
    [(3, 1024 * n, 0) for n in range(4)] + [(2, 0, j) for j in range(4)] + [(1, 0, 0)] + [(0, 0, j) for j in range(3)]
)
DEALS_AFTER = ((), (4,), (6,), (7, 8), (), (), (), (), (3,), (0,), (1,), (2,))


def by_block(row, count):
    found, done = [], 0
    while done < count:
        b, first = divmod(row + done, GROUP)
        rows = min(count - done, GROUP - first)
        found.append((b, first, rows, done))
        done += rows
    return found


def backward_kernel(total, batch, piece, per, buckets, owned, pm, dg, *refs):
    wq, wo, wi, wd, h1_i, q_i, qb_i, kv_i, att_i, a_i, x1_i, h2_i, gp_i, u_i, y_i, cot_i, spread_i, tok_i = refs[:18]
    blk, grad_o, act_o = refs[18:21]
    big1, big2, big3, wa, wb, f1, f2, s1, s2, s3, s4, kv_got, dmv, dmf, kmask, ring = refs[21:37]
    got, half_sum, strip_sum, zgot = refs[37:41], refs[41:45], refs[45:49], refs[49]
    ordered, picked, dmf_got, dmod = refs[50:54]
    psend, precv, zsend, zrecv, msend, mrecv, vsend, vrecv, xsend, xrecv, lsem, asem, bsem = refs[54:67]
    gsend, grecv, hsend, hrecv = refs[67:]
    y, x, c, z, at_x, at_y, at_c = plane()
    f = 4 * y + 2 * x + c
    me = f * batch + z

    def load(src, dst, n):
        return local(src, dst, lsem.at[n])

    cot_l = load(cot_i, s3, 0)
    u_l = [load(u_i.at[:, pl.ds(1024 * n, 1024)], big1.at[:, pl.ds(1024 * n, 1024)], 1 + n) for n in range(4)]
    h2_l = load(h2_i, s2, 5)
    gp_l = load(gp_i, big2, 6)
    x1_l = load(x1_i, f2, 7)
    a_l = load(a_i, s4, 8)
    down_tiles = [wd.at[pl.ds(512 * t, 512)] for t in range(8)] + [wo.at[pl.ds(512 * t, 512)] for t in range(2)]
    in_tiles = [wi.at[:, pl.ds(512 * t, 512)] for t in range(8)] + [wq.at[:, pl.ds(512 * t, 512)] for t in range(6)]
    fetched = {}

    def fetch(tiles, buf, sem, t):
        if t < len(tiles):
            fetched[id(tiles), t] = local(tiles[t], buf.at[t % 2], sem.at[t % 2])

    for t in range(2):
        fetch(down_tiles, wb, bsem, t)
        fetch(in_tiles, wa, asem, t)

    def tile(tiles, buf, t):
        fetched[id(tiles), t].wait()
        return buf[t % 2]

    greet_all(total, batch)
    mine, g = f // per, f % per
    sel, _ = frames_of(buckets, mine, g, piece, per)
    videos = []

    def send_video(s, part, dst, n):
        for k in range(1, 4):
            v = (mine + k) % 4
            videos.append(remote(part(v), dst.at[mine], vsend.at[s, k], vrecv.at[s, k], (v * per + g, z)))
        videos.append(local(part(mine), dst.at[mine], lsem.at[n]))

    slots = {}
    counter = [0]

    def push(key, src, dst, device):
        s = counter[0]
        counter[0] += 1
        slots.setdefault(key, []).append(remote(src, dst, psend.at[s], precv.at[s], device))

    def arrive(key):
        for copy in slots[key]:
            copy.wait_recv()

    def emit(n, left, right):
        m, row, j = LEAVES[n]
        for w in range(2):
            ring[n % 2, :, 512 * w : 512 * w + 512] = dot_tn(left, right[:, 512 * w : 512 * w + 512]).astype(BF16)
        push(
            (n, 0),
            ring.at[n % 2, :, lanes(512 * (1 - c), 512)],
            got[m].at[pl.ds(row, 1024), pl.ds(512 * j, 512)],
            at_c,
        )

    def add_block(dst, dst_row, dst_col, src, src_row, src_col, width, count):
        def body(i, carry):
            to = pl.ds(pl.multiple_of(dst_row + i * 128, 128), 128)
            at = pl.ds(pl.multiple_of(src_row + i * 128, 128), 128)
            dst[to, lanes(dst_col, width)] = dst[to, lanes(dst_col, width)] + src[at, lanes(src_col, width)]
            return carry

        lax.fori_loop(0, count // 128, body, 0)

    def absorb(n):
        m, row, j = LEAVES[n]
        arrive((n, 0))
        add_block(got[m], row, 512 * j, ring.at[n % 2], 0, 512 * c, 512, 1024)
        for copy in slots[(n, 0)]:
            copy.wait_send()

    def step1(n):
        m, row, j = LEAVES[n]
        for yy in range(2):
            push(
                (n, 1),
                got[m].at[pl.ds(row, 512), lanes(512 * j + 256 * yy + 128 * (1 - x), 128)],
                half_sum[m].at[pl.ds(row, 512), lanes(256 * j + 128 * yy, 128)],
                at_x,
            )
        push(
            (n, 1),
            got[m].at[pl.ds(row + 512, 512), lanes(512 * j + 256 * (1 - y), 256)],
            half_sum[m].at[pl.ds(row + 512, 512), lanes(256 * j, 256)],
            at_y,
        )

    def step2(n):
        m, row, j = LEAVES[n]
        arrive((n, 1))
        for yy in range(2):
            add_block(half_sum[m], row, 256 * j + 128 * yy, got[m], row, 512 * j + 256 * yy + 128 * x, 128, 512)
        add_block(half_sum[m], row + 512, 256 * j, got[m], row + 512, 512 * j + 256 * y, 256, 512)
        push(
            (n, 2),
            half_sum[m].at[pl.ds(row, 512), lanes(256 * j + 128 * (1 - y), 128)],
            strip_sum[m].at[pl.ds(row, 512), lanes(128 * j, 128)],
            at_y,
        )
        push(
            (n, 2),
            half_sum[m].at[pl.ds(row + 512, 512), lanes(256 * j + 128 * (1 - x), 128)],
            strip_sum[m].at[pl.ds(row + 512, 512), lanes(128 * j, 128)],
            at_x,
        )

    def step3(n):
        m, row, j = LEAVES[n]
        arrive((n, 2))
        add_block(strip_sum[m], row, 128 * j, half_sum[m], row, 256 * j + 128 * y, 128, 512)
        add_block(strip_sum[m], row + 512, 128 * j, half_sum[m], row + 512, 256 * j + 128 * x, 128, 512)
        if m == 2:

            @pl.when(z != j)
            def _():
                k = (j - z + batch) % batch
                remote(
                    strip_sum[m].at[:, pl.ds(128 * j, 128)],
                    zgot.at[k - 1, pl.ds(1120, 1024)],
                    zsend.at[IN_DEAL, k],
                    zrecv.at[IN_DEAL, k],
                    (f, j),
                )

        for d in DEALS_AFTER[n]:
            for k in range(1, batch):
                to = (z + k) % batch
                for held_row, count, at, col in deal_pieces(BACK_DEALS, d, to):
                    remote(
                        strip_sum[m].at[pl.ds(pl.multiple_of(at, 16), count), lanes(128 * col, 128)],
                        zgot.at[k - 1, pl.ds(held_row, count)],
                        zsend.at[d, k],
                        zrecv.at[d, k],
                        (f, to),
                    )

    pumped = [0]

    def pump_to(r):
        while pumped[0] <= r:
            n = pumped[0]
            pumped[0] += 1
            if 0 <= n - 2 < 12:
                step2(n - 2)
            if n < 12:
                step1(n)
            if 0 <= n - 3 < 12:
                step3(n - 3)

    def whole(d, k):
        return zgot.at[k - 1, pl.ds(0, BACK_DEALS[d][4])]

    def last(d):
        m = [kind for kind, _, _ in KINDS].index(BACK_DEALS[d][0])
        for k in range(1, batch):
            pltpu.make_async_copy(whole(d, k), whole(d, k), zrecv.at[d, k]).wait()
        for row, count, at, j in deal_pieces(BACK_DEALS, d, z):
            for b, first, rows, skip in by_block(row, count):
                value = strip_sum[m][pl.ds(pl.multiple_of(at + skip, 16), rows), lanes(128 * j, 128)].astype(F32)
                for k in range(batch - 1):
                    value = value + zgot[k, row + skip : row + skip + rows, :].astype(F32)
                ordered[FIRST + b, first : first + rows, :] = value.astype(BF16)

    def mod_row(j, p):
        return pm[pl.ds(4 * j + p, 1), :]

    def by_rows(p, body, sums):
        def one(i, carry):
            return body(pl.ds(pl.multiple_of(p * piece + i * 16, 16), 16), *carry)

        start = tuple(jnp.zeros((8, 1024), F32) for _ in range(sums))
        return [jnp.sum(s, axis=0, keepdims=True) for s in lax.fori_loop(0, piece // 16, one, start)]

    cot_l.wait()
    for p in range(4):
        gate = mod_row(5, p)

        def d_mlp(rows, gate=gate):
            s1[rows, :] = (gate * s3[rows, :].astype(F32)).astype(BF16)
            return ()

        by_rows(p, d_mlp, 0)
        dmv[pl.ds(20 + p, 1), :] = dg[pl.ds(p, 1), :]
    for n in range(4):
        u_l[n].wait()
        emit(n, big1[:, 1024 * n : 1024 * n + 1024], s1)
        if n >= 1:
            absorb(n - 1)
        if n % 2 == 1:
            pump_to(n // 2)
    kv_l = [load(kv_i.at[d], big1.at[:, pl.ds(2048 * d, 2048)], 10 + d) for d in range(2)]
    gp_l.wait()
    for t in range(8):
        cols = slice(512 * t, 512 * t + 512)
        d_act = dot_nt(s1[...], tile(down_tiles, wb, t))
        big3[:, cols] = (d_act * big2[:, cols].astype(F32)).astype(BF16)
        fetch(down_tiles, wb, bsem, t + 2)
        if t == 0:
            absorb(3)
        if t == 5:
            pump_to(2)
    h2_l.wait()
    for j in range(4):
        emit(4 + j, s2[...], big3.at[:, 1024 * j : 1024 * j + 1024])
        if j >= 1:
            absorb(3 + j)
        if j == 2:
            pump_to(3)
    att_l = load(att_i, s2, 5)
    for t in range(8):
        part = dot_nt(big3[:, 512 * t : 512 * t + 512], tile(in_tiles, wa, t))
        f1[...] = part if t == 0 else f1[...] + part
        fetch(in_tiles, wa, asem, t + 2)
        if t == 0:
            absorb(7)
        if t == 4:
            pump_to(4)
    qb_l = load(qb_i, big3.at[:, pl.ds(3072, 1024)], 6)

    x1_l.wait()
    a_l.wait()
    for p in range(4):
        gate, scale = mod_row(2, p), mod_row(4, p)

        def back_two(rows, d_scale, d_shift, d_gate, gate=gate, scale=scale):
            normed, inv_std = norm_rows(f2[rows, :])
            d_h = f1[rows, :]
            d_mid = s3[rows, :].astype(F32) + norm_back(d_h * (1.0 + scale), normed, inv_std)
            f2[rows, :] = d_mid
            s1[rows, :] = (gate * d_mid).astype(BF16)
            return (
                d_scale + fold_rows(d_h * normed),
                d_shift + fold_rows(d_h),
                d_gate + fold_rows(d_mid * s4[rows, :].astype(F32)),
            )

        d_scale, d_shift, d_gate = by_rows(p, back_two, 3)
        dmv[pl.ds(16 + p, 1), :] = d_scale
        dmv[pl.ds(12 + p, 1), :] = d_shift
        dmv[pl.ds(8 + p, 1), :] = d_gate
    q_l = load(q_i, s4, 8)
    pump_to(5)

    att_l.wait()
    emit(8, s2[...], s1)
    for t in range(2):
        s3[:, 512 * t : 512 * t + 512] = dot_nt(s1[...], tile(down_tiles, wb, 8 + t)).astype(BF16)
    h1_l = load(h1_i, wb.at[0], 7)
    tok_l = load(tok_i, wb.at[1], 12)
    absorb(8)

    keys = 2 * 4 * piece
    kmask[...] = key_mask(keys, piece, per).astype(BF16)
    for copy in kv_l:
        copy.wait()
    qb_l.wait()
    q_l.wait()

    def heads(h):
        pair = lanes(128 * h, 128)
        k_pair = jnp.concatenate([big1[:, lanes(2048 * d + 128 * h, 128)] for d in range(2)], axis=0)
        v_pair = jnp.concatenate([big1[:, lanes(2048 * d + 1024 + 128 * h, 128)] for d in range(2)], axis=0)
        dks, dvs, dqs = [], [], []
        first = lane_half(0)
        ones = in_lanes([1.0, 1.0, 1.0], 0)
        for e in range(2):
            mask = lane_half(e)
            k_e = choose(mask, k_pair, kmask[...])
            v_e = choose(mask, v_pair, ones)
            dk = dv = 0.0
            dq = []
            for w in range(2):
                rows = slice(256 * w, 256 * w + 256)
                q_w, d_w, o_w = s4[rows, pair], s3[rows, pair], s2[rows, pair]
                q_e = choose(mask, q_w, big3[rows, lanes(3072 + 128 * h, 128)])
                dot_rows = jnp.sum(
                    jnp.where(mask, d_w.astype(F32) * o_w.astype(F32), 0.0), axis=1, keepdims=True
                )
                d_e = choose(mask, d_w, in_lanes(three_parts(-dot_rows), 0))
                prob = jnp.exp(dot_nt(k_e, q_e))
                d_s = (prob * dot_nt(v_e, d_e)).astype(BF16)
                dv = dv + dot_nn(prob.astype(BF16), d_w)
                dk = dk + dot_nn(d_s, q_w)
                dq.append(dot_tn(d_s, k_pair))
            dks.append(dk)
            dvs.append(dv)
            dqs.append(jnp.concatenate(dq, axis=0))
        dk = choose(first, dks[0], dks[1])
        dv = choose(first, dvs[0], dvs[1])
        big3[:, pair] = (choose(first, dqs[0], dqs[1]).astype(F32) * HD ** (-0.5)).astype(BF16)
        for d in range(2):
            big2[:, lanes(2048 * d + 128 * h, 128)] = dk[512 * d : 512 * d + 512]
            big2[:, lanes(2048 * d + 1024 + 128 * h, 128)] = dv[512 * d : 512 * d + 512]

    exchanges = []
    for h in range(8):
        lax.fori_loop(h, h + 1, lambda n, t: (heads(n), t)[1], 0)
        if h % 4 == 3:
            for part in range(2):
                at = 1024 * part + 512 * (h // 4)
                s = len(exchanges)
                exchanges.append(
                    remote(
                        big2.at[:, lanes(2048 * (1 - c) + at, 512)],
                        kv_got.at[:, pl.ds(at, 512)],
                        xsend.at[s],
                        xrecv.at[s],
                        at_c,
                    )
                )
        if h % 2 == 0:
            pump_to(min(6 + h // 2, 8))

    spread_l = load(spread_i, big1.at[pl.ds(0, 384), pl.ds(0, ADA)], 10)
    h1_l.wait()
    emit(9, wb[0], big3.at[:, 0:1024])
    for copy in exchanges:
        copy.wait_recv()
    for part in range(2):

        def join(i, carry, part=part):
            rows = pl.ds(pl.multiple_of(i * 64, 64), 64)
            value = big2[rows, lanes(2048 * c + 1024 * part, 1024)].astype(F32) + kv_got[
                rows, 1024 * part : 1024 * part + 1024
            ].astype(F32)
            big3[rows, 1024 + 1024 * part : 2048 + 1024 * part] = value.astype(BF16)
            return carry

        lax.fori_loop(0, 8, join, 0)
        emit(10 + part, wb[0], big3.at[:, 1024 + 1024 * part : 2048 + 1024 * part])
        absorb(9 + part)
        pump_to(9 + part)
    for t in range(6):
        part = dot_nt(big3[:, 512 * t : 512 * t + 512], tile(in_tiles, wa, 8 + t))
        f1[...] = part if t == 0 else f1[...] + part
        fetch(in_tiles, wa, asem, 8 + t + 2)
        if t == 0:
            absorb(11)
        if t == 2:
            pump_to(11)

    tok_l.wait()
    for p in range(4):
        scale = mod_row(1, p)

        def back_one(rows, d_scale, d_shift, scale=scale):
            normed, inv_std = norm_rows(wb[1, rows, :].astype(F32))
            d_h = f1[rows, :]
            s1[rows, :] = (f2[rows, :] + norm_back(d_h * (1.0 + scale), normed, inv_std)).astype(BF16)
            return d_scale + fold_rows(d_h * normed), d_shift + fold_rows(d_h)

        d_scale, d_shift = by_rows(p, back_one, 2)
        dmv[pl.ds(4 + p, 1), :] = d_scale
        dmv[pl.ds(p, 1), :] = d_shift
    send_video(0, lambda v: s1.at[pl.ds(pl.multiple_of(v * piece, piece), piece)], grad_o, 0)
    for j in range(6):
        for fr in range(4):
            value = sel[0][fr] * dmv[pl.ds(4 * j, 1), :]
            for p in range(1, 4):
                value = value + sel[p][fr] * dmv[pl.ds(4 * j + p, 1), :]
            dmf[pl.ds(4 * j + fr, 1), :] = value
    half_copy = remote(dmf, dmf_got, hsend, hrecv, at_c)

    def mod_group(k, start):
        other = (f // 2 * batch + z + k) % (4 * batch)
        chip, oz = other // batch, other % batch
        copy = pltpu.make_async_remote_copy(
            src_ref=dmf_got.at[:, lanes(512 * c + 128 * chip, 128)],
            dst_ref=dmod.at[4 * z + f // 2],
            send_sem=msend.at[k],
            recv_sem=mrecv.at[k],
            device_id=(2 * chip + c, oz),
            device_id_type=MESH,
        )
        if start:
            copy.start()
        else:
            copy.wait()

    pump_to(12)
    half_copy.wait()
    dmf_got[...] = dmf_got[...] + dmf[...]
    lax.fori_loop(1, 4 * batch, lambda k, u: (mod_group(k, True), u)[1], 0)
    dmod[4 * z + f // 2] = dmf_got[:, lanes(512 * c + 128 * (f // 2), 128)]
    for d in (4, 6, 7, 8):
        last(d)
    pump_to(13)
    send_video(1, lambda v: y_i.at[v], act_o, 1)
    last(IN_DEAL)
    last(3)
    last(0)
    pump_to(14)

    spread_l.wait()
    lax.fori_loop(1, 4 * batch, lambda k, u: (mod_group(k, False), u)[1], 0)
    parts = [part.astype(BF16) for part in three_parts(dmod[...].reshape(384, 128))]
    for n in range(ADA // 128):
        wide = big1[0:384, 128 * n : 128 * n + 128]
        value = (dot_tn(wide, parts[0]) + dot_tn(wide, parts[1]) + dot_tn(wide, parts[2])).astype(BF16)
        spans = [(0, FIRST * GROUP)]
        spans += [(FIRST * GROUP + THIRD * q + 16, FIRST * GROUP + THIRD * q + THIRD) for q in range(3)]
        for lo, hi in spans:
            lo, hi = max(lo, 128 * n), min(hi, 128 * n + 128)
            for b, first, rows, skip in by_block(lo, max(hi - lo, 0)):
                ordered[b, first : first + rows, :] = value[lo - 128 * n + skip : lo - 128 * n + skip + rows]
    for d in (1, 2):
        last(d)

    def spot(of, oz):
        return blk.at[pl.ds(pl.multiple_of(GROUP * oz, 16), GROUP), lanes(128 * strip_of(of), 128)]

    def to_owner(k, start):
        other = (me + k) % total
        copy = pltpu.make_async_remote_copy(
            src_ref=picked.at[other],
            dst_ref=spot(f, z),
            send_sem=gsend.at[k],
            recv_sem=grecv.at[k],
            device_id=(other // batch, other % batch),
            device_id_type=MESH,
        )
        if start:
            copy.start()
        else:
            copy.wait()

    def pick(d, carry):
        picked[d] = ordered[owned[d]]
        return carry

    lax.fori_loop(0, total, pick, 0)
    lax.fori_loop(1, total, lambda k, u: (to_owner(k, True), u)[1], 0)
    blk_own = local(picked.at[me], spot(f, z), lsem.at[2])
    for n, copies in slots.items():
        if n[1] > 0:
            for copy in copies:
                copy.wait_send()
    for d in range(len(BACK_DEALS)):
        for k in range(1, batch):
            pltpu.make_async_copy(whole(d, k), whole(d, k), zsend.at[d, k]).wait()
    for copy in exchanges:
        copy.wait_send()
    for copy in videos:
        copy.wait()
    blk_own.wait()
    lax.fori_loop(1, total, lambda k, u: (to_owner(k, False), u)[1], 0)


def backward(buckets, owned, pm, dg, arrays, total, batch, piece, per):
    def sums(width):
        return [pltpu.VMEM((depth, blocks * width), BF16) for _, depth, blocks in KINDS]

    def buf(*shape, dtype=BF16):
        return pltpu.VMEM(shape, dtype)

    whole = pl.BlockSpec(memory_space=pltpu.VMEM)
    dma = pltpu.SemaphoreType.DMA
    return pl.pallas_call(
        partial(backward_kernel, total, batch, piece, per),
        out_shape=[
            jax.ShapeDtypeStruct((ROWS, 1024), BF16),
            jax.ShapeDtypeStruct((4, piece, 1024), BF16),
            jax.ShapeDtypeStruct((4, piece, 1024), BF16),
        ],
        in_specs=[pl.BlockSpec(memory_space=pltpu.SMEM)] * 2 + [whole, whole] + [ANY] * len(arrays),
        out_specs=[ANY, ANY, ANY],
        scratch_shapes=[buf(512, 4096) for _ in range(3)]
        + [buf(2, 1024, 512), buf(2, 512, 1024)]
        + [buf(512, 1024, dtype=F32) for _ in range(2)]
        + [buf(512, 1024) for _ in range(4)]
        + [buf(512, 2048), buf(24, 1024, dtype=F32), buf(24, 1024, dtype=F32), buf(1024, 128), buf(2, 1024, 1024)]
        + sums(512)
        + sums(256)
        + sums(128)
        + [buf(batch - 1, HELD, 128), buf(total, GROUP, 128), buf(total, GROUP, 128)]
        + [buf(24, 1024, dtype=F32), buf(16, 24, 128, dtype=F32)]
        + [
            dma((72,)),
            dma((72,)),
            dma((len(BACK_DEALS), batch)),
            dma((len(BACK_DEALS), batch)),
            dma((4 * batch,)),
            dma((4 * batch,)),
            dma((2, 4)),
            dma((2, 4)),
            dma((4,)),
            dma((4,)),
            dma((13,)),
            dma((2,)),
            dma((2,)),
            dma((total,)),
            dma((total,)),
            dma,
            dma,
        ],
        compiler_params=pltpu.CompilerParams(
            collective_id=2, has_side_effects=True, vmem_limit_bytes=VMEM_LIMIT
        ),
        name="backward",
    )(buckets, owned, pm, dg, *arrays)


def own_rows_of(owned, table, me):
    return table[pl.ds(owned[me], 1), :]


def cut_kernel(batch, owned, table, master, out):
    f, z = frame_index()
    rows = own_rows_of(owned, table, f * batch + z)
    swap = (rows == lax.broadcasted_iota(jnp.int32, (ROWS, ROWS), 0)).astype(F32).astype(BF16)
    strips = [master[pl.ds(s, ROWS, stride=8), :].astype(BF16) for s in range(8)]
    out[...] = dot_tn(swap, jnp.concatenate(strips, axis=1)).astype(BF16)


def cut_owned(owned, table, master, batch):
    whole = pl.BlockSpec(memory_space=pltpu.VMEM)
    return pl.pallas_call(
        partial(cut_kernel, batch),
        out_shape=jax.ShapeDtypeStruct((ROWS, 1024), BF16),
        in_specs=[pl.BlockSpec(memory_space=pltpu.SMEM), whole, whole],
        out_specs=whole,
        compiler_params=pltpu.CompilerParams(vmem_limit_bytes=VMEM_LIMIT),
        name="cut_owned",
    )(owned, table, master)


def adam(grad, master, first, second):
    new_first = BETA_ONE * first + (1.0 - BETA_ONE) * grad
    new_second = BETA_TWO * second + (1.0 - BETA_TWO) * grad * grad
    fix_one = 1.0 - BETA_ONE**STEP
    fix_two = 1.0 - BETA_TWO**STEP
    update = new_first / fix_one / (jnp.sqrt(new_second / fix_two) + ADAM_EPS)
    return master - LEARN_RATE * (update + WEIGHT_DECAY * master), new_first, new_second


UPDATE_ROWS = 144


def update_kernel(batch, owned, table, grad, master, first, second, act, inp, *refs):
    new_master, new_first, new_second, act_o, inp_o = refs
    act_o[...] = act[...]
    inp_o[...] = inp[...]
    f, z = frame_index()
    rows = own_rows_of(owned, table, f * batch + z)
    base = pl.program_id(0) * UPDATE_ROWS
    swap = (rows == base + lax.broadcasted_iota(jnp.int32, (UPDATE_ROWS, ROWS), 0)).astype(F32).astype(BF16)
    for s in range(8):
        at = pl.ds(s, UPDATE_ROWS, stride=8)
        value = dot_nn(swap, grad[:, 128 * s : 128 * s + 128])
        new_master[at, :], new_first[at, :], new_second[at, :] = adam(
            value, master[at, :], first[at, :], second[at, :]
        )


def update_owned(owned, table, grad, master, first, second, act, inp, batch):
    part = pl.BlockSpec((8 * UPDATE_ROWS, 128), lambda i: (i, 0))
    slot = pl.BlockSpec((1,) + act.shape[1:], lambda i: (i, 0, 0))
    return pl.pallas_call(
        partial(update_kernel, batch),
        grid=(ROWS // UPDATE_ROWS,),
        out_shape=[jax.ShapeDtypeStruct(master.shape, F32)] * 3
        + [jax.ShapeDtypeStruct(a.shape, a.dtype) for a in (act, inp)],
        in_specs=[
            pl.BlockSpec(memory_space=pltpu.SMEM),
            pl.BlockSpec(table.shape, lambda i: (0, 0)),
            pl.BlockSpec((ROWS, 1024), lambda i: (0, 0)),
            part,
            part,
            part,
            slot,
            slot,
        ],
        out_specs=[part] * 3 + [slot, slot],
        compiler_params=pltpu.CompilerParams(vmem_limit_bytes=VMEM_LIMIT),
        name="update_owned",
    )(owned, table, grad, master, first, second, act, inp)


def key_positions(rows, piece, per):
    i = lax.broadcasted_iota(jnp.int32, (rows, 1), 0)
    local_rows = rows // per
    return ((i % local_rows) // piece * per + i // local_rows) * piece + i % piece


def scores_t(k, q, ends, piece, per):
    s = lax.dot_general(k, q, (((1,), (1,)), ((), ())), preferred_element_type=F32)
    pos = key_positions(k.shape[0], piece, per)
    cols = []
    for t in range(q.shape[0] // piece):
        part = s[:, t * piece : (t + 1) * piece]
        cols.append(jnp.where(pos < ends[t], part, NEG_FILL))
    return jnp.concatenate(cols, axis=1)


def attend_kernel(piece, per, ends, q, k, v, o):
    outs = []
    for a in range(2):
        cut = slice(64 * a, 64 * a + 64)
        s = scores_t(k[:, cut], q[:, cut], ends, piece, per)
        peak = jnp.max(s, axis=0, keepdims=True)
        e = jnp.exp(s - peak)
        p = (e * (1.0 / jnp.sum(e, axis=0, keepdims=True))).astype(BF16)
        outs.append(lax.dot_general(p, v[:, cut], (((0,), (0,)), ((), ())), preferred_element_type=F32))
    o[...] = jnp.concatenate(outs, axis=1).astype(BF16)


def attend(ends, q, kv, piece, per):
    rows, width = q.shape
    keys = kv.shape[0]
    pairs = width // 128
    return pl.pallas_call(
        partial(attend_kernel, piece, per),
        grid_spec=pltpu.PrefetchScalarGridSpec(
            num_scalar_prefetch=1,
            grid=(pairs,),
            in_specs=[
                pl.BlockSpec((rows, 128), lambda h, e: (0, h)),
                pl.BlockSpec((keys, 128), lambda h, e: (0, h)),
                pl.BlockSpec((keys, 128), lambda h, e: (0, h + pairs)),
            ],
            out_specs=pl.BlockSpec((rows, 128), lambda h, e: (0, h)),
        ),
        out_shape=jax.ShapeDtypeStruct((rows, width), BF16),
        compiler_params=pltpu.CompilerParams(vmem_limit_bytes=VMEM_LIMIT),
        cost_estimate=pl.CostEstimate(
            flops=4 * rows * keys * width, bytes_accessed=4 * (rows + keys) * width, transcendentals=rows * keys * H
        ),
        name="attend",
    )(ends, q, kv, kv)


def attend_back_kernel(piece, per, ends, q, k, v, do, dq, dk, dv):
    dqs, dks, dvs = [], [], []
    for a in range(2):
        cut = slice(64 * a, 64 * a + 64)
        qa, ka, va, da = q[:, cut], k[:, cut], v[:, cut], do[:, cut]
        s = scores_t(ka, qa, ends, piece, per)
        peak = jnp.max(s, axis=0, keepdims=True)
        e = jnp.exp(s - peak)
        p = e * (1.0 / jnp.sum(e, axis=0, keepdims=True))
        dvs.append(jnp.dot(p.astype(BF16), da, preferred_element_type=F32))
        dp = lax.dot_general(va, da, (((1,), (1,)), ((), ())), preferred_element_type=F32)
        pdp = p * dp
        row = jnp.sum(pdp, axis=0, keepdims=True)
        ds = (pdp - p * row).astype(BF16)
        dks.append(jnp.dot(ds, qa, preferred_element_type=F32))
        dqs.append(lax.dot_general(ds, ka, (((0,), (0,)), ((), ())), preferred_element_type=F32))
    dq[...] = jnp.concatenate(dqs, axis=1).astype(BF16)
    dk[...] = jnp.concatenate(dks, axis=1).astype(BF16)
    dv[...] = jnp.concatenate(dvs, axis=1).astype(BF16)


def attend_back(ends, q, kv, do, piece, per):
    rows, width = q.shape
    keys = kv.shape[0]
    pairs = width // 128
    mine = pl.BlockSpec((rows, 128), lambda h, e: (0, h))
    allk = pl.BlockSpec((keys, 128), lambda h, e: (0, h))
    return pl.pallas_call(
        partial(attend_back_kernel, piece, per),
        grid_spec=pltpu.PrefetchScalarGridSpec(
            num_scalar_prefetch=1,
            grid=(pairs,),
            in_specs=[mine, allk, pl.BlockSpec((keys, 128), lambda h, e: (0, h + pairs)), mine],
            out_specs=[mine, allk, allk],
        ),
        out_shape=[
            jax.ShapeDtypeStruct((rows, width), BF16),
            jax.ShapeDtypeStruct((keys, width), BF16),
            jax.ShapeDtypeStruct((keys, width), BF16),
        ],
        compiler_params=pltpu.CompilerParams(vmem_limit_bytes=VMEM_LIMIT),
        cost_estimate=pl.CostEstimate(
            flops=10 * rows * keys * width, bytes_accessed=6 * (rows + keys) * width, transcendentals=rows * keys * H
        ),
        name="attend_back",
    )(ends, q, kv, kv, do)


def layer_stats(values):
    centre = values - jnp.mean(values, axis=-1, keepdims=True)
    inv_std = lax.rsqrt(jnp.mean(centre * centre, axis=-1, keepdims=True) + 1e-06)
    return (centre * inv_std, inv_std)


def norm_back(upstream, normed, inv_std):
    mean_grad = jnp.mean(upstream, axis=-1, keepdims=True)
    mean_cross = jnp.mean(upstream * normed, axis=-1, keepdims=True)
    return inv_std * (upstream - mean_grad - normed * mean_cross)


def noise_embedding(levels, feature_width):
    half_width = feature_width // 2
    frequencies = jnp.exp(
        -math.log(10000.0) * jnp.arange(half_width, dtype=jnp.float32) / half_width
    )
    angles = levels.astype(jnp.float32)[:, None] * frequencies[None, :]
    return jnp.concatenate([jnp.cos(angles), jnp.sin(angles)], axis=1)


def silu_embedding(levels, width):
    return jax.nn.silu(noise_embedding(levels, width)).astype(BF16)


def split_flat(flat_values, model_width, hidden_width):
    matrix_shapes = (
        (model_width, 6 * model_width),
        (model_width, 3 * model_width),
        (model_width, model_width),
        (model_width, hidden_width),
        (hidden_width, model_width),
    )
    matrices = []
    offset_now = 0
    for matrix_shape in matrix_shapes:
        entry_count = matrix_shape[0] * matrix_shape[1]
        matrices.append(flat_values[offset_now : offset_now + entry_count].reshape(matrix_shape))
        offset_now = offset_now + entry_count
    return matrices


def shards(
    frame_size,
    batch_size,
    tokens,
    out_cotangent,
    buckets,
    noise_levels,
    owned_block,
    master,
    first_moment,
    second_moment,
):
    micro_count, piece, width = tokens.shape
    block_size = master.shape[1]
    frame_count = noise_levels.shape[1]
    total = frame_size * batch_size
    videos = micro_count
    per = frame_size // videos
    rows = videos * piece
    keys = rows * per
    q_scale = HD ** (-0.5)
    f, z = frame_index()
    me = f * batch_size + z
    mine, g = f // per, f % per
    direct = frame_size == 8 and batch_size == 4 and block_size == ROWS * 1024 and videos == 4 and frame_count == 4

    if direct:
        order = jnp.arange(total, dtype=jnp.int32)
        inverse = jnp.sum(jnp.where(owned_block[None, :] == order[:, None], order[None, :], 0), axis=1)
        table = jnp.asarray(np.stack([block_rows(b) for b in range(total)]).astype(np.int32))
        blk = cut_owned(owned_block, table, master.reshape(-1, 128), batch_size)
        cond = silu_embedding(noise_levels.reshape(16), width)
    else:
        tok, cot = swap_videos([tokens, out_cotangent], videos, per, 0)
        gathered = lax.all_gather(master.astype(BF16), ("frame", "batch"), axis=0, tiled=True)
        placed = jnp.take(gathered, jnp.argsort(owned_block), axis=0).reshape(-1)
        w_ada, w_qkv, w_out, w_in, w_down = split_flat(placed, width, FF)
        cond = silu_embedding(lax.dynamic_index_in_dim(noise_levels, mine, 0, keepdims=False), width)
        modulation = jnp.dot(cond, w_ada, preferred_element_type=F32).reshape(frame_count, 6, width)

    def flat(a):
        return a.reshape(rows, a.shape[-1])

    def cube(a):
        return a.reshape(videos, piece, a.shape[-1])

    def partners(k):
        return [(i, i // per * per + (i + k) % per) for i in range(frame_size)]

    def split_mod(piece_mod):
        return [piece_mod[j][:, None, :] for j in range(6)]

    if direct:
        saved = forward(inverse, buckets, blk, cond, tokens, out_cotangent, total, batch_size, piece, per)
        *saved, block_output, piece_mod, d_gate, cot, cond_all, tokens_own = saved
        grad_block, input_grads, outputs = backward(
            buckets,
            owned_block,
            piece_mod,
            d_gate,
            [*saved, cube(block_output), cot, cond_all, tokens_own],
            total,
            batch_size,
            piece,
            per,
        )
    else:
        frame_len = FRAME_LO * (1 + 3 * buckets[mine])
        piece_at = (jnp.arange(videos, dtype=jnp.int32) * per + g) * piece
        piece_frame = piece_at // frame_len
        ends = (piece_frame + 1) * frame_len
        selector = (piece_frame[:, None] == jnp.arange(frame_count, dtype=jnp.int32)[None, :]).astype(F32)
        x_float = tok.astype(F32)
        normed_one, inv_one = layer_stats(x_float)
        piece_mod = jnp.einsum("pf,fjd->jpd", selector, modulation, precision=HIGHEST)
        shift_one, scale_one, gate_one, shift_two, scale_two, gate_two = split_mod(piece_mod)

        h_one = flat((normed_one * (1.0 + scale_one) + shift_one).astype(BF16))
        projected = jnp.dot(h_one, w_qkv, preferred_element_type=F32)
        queries = (projected[:, :width] * q_scale).astype(BF16)
        kv_own = projected[:, width:].astype(BF16)

        kv_all = jnp.zeros((per, rows, 2 * width), BF16)
        kv_all = lax.dynamic_update_index_in_dim(kv_all, kv_own, g, 0)
        for k in range(1, per):
            kv_all = lax.dynamic_update_index_in_dim(
                kv_all, lax.ppermute(kv_own, "frame", partners(k)), (g + per - k) % per, 0
            )
        kv_all = kv_all.reshape(keys, 2 * width)
        attended = attend(ends, queries, kv_all, piece, per)
        attn_out = jnp.dot(attended, w_out, preferred_element_type=F32)
        middle = x_float + gate_one * cube(attn_out)
        normed_two, inv_two = layer_stats(middle)
        h_two = flat((normed_two * (1.0 + scale_two) + shift_two).astype(BF16))
        pre_act = jnp.dot(h_two, w_in, preferred_element_type=F32)
        activated, gelu_back = jax.vjp(partial(jax.nn.gelu, approximate=True), pre_act)
        act_low = activated.astype(BF16)
        slope = gelu_back(jnp.ones_like(pre_act))[0]
        mlp_out = jnp.dot(act_low, w_down, preferred_element_type=F32)
        block_output = (middle + gate_two * cube(mlp_out)).astype(BF16)

        grad_out = cot.astype(F32)
        d_mlp = flat((gate_two * grad_out).astype(BF16))
        g_down = jnp.dot(act_low.T, d_mlp, preferred_element_type=F32).astype(BF16)
        d_act = jnp.dot(d_mlp, w_down.T, preferred_element_type=F32)
        d_pre = (d_act * slope.astype(F32)).astype(BF16)
        g_in = jnp.dot(h_two.T, d_pre, preferred_element_type=F32).astype(BF16)
        d_htwo = cube(jnp.dot(d_pre, w_in.T, preferred_element_type=F32))
        d_gate_two = jnp.sum(grad_out * cube(mlp_out), axis=1)
        d_scale_two = jnp.sum(d_htwo * normed_two, axis=1)
        d_shift_two = jnp.sum(d_htwo, axis=1)
        d_middle = grad_out + norm_back(d_htwo * (1.0 + scale_two), normed_two, inv_two)
        d_attn = flat((gate_one * d_middle).astype(BF16))
        d_gate_one = jnp.sum(d_middle * cube(attn_out), axis=1)
        g_out = jnp.dot(attended.T, d_attn, preferred_element_type=F32).astype(BF16)
        d_attended = jnp.dot(d_attn, w_out.T, preferred_element_type=F32).astype(BF16)
        dq, dk, dv = attend_back(ends, queries, kv_all, d_attended, piece, per)
        dkv = jnp.concatenate([dk, dv], axis=1).reshape(per, rows, 2 * width)
        dkv_own = lax.dynamic_index_in_dim(dkv, g, 0, keepdims=False).astype(F32)
        for k in range(1, per):
            sent = lax.dynamic_index_in_dim(dkv, (g + k) % per, 0, keepdims=False)
            dkv_own = dkv_own + lax.ppermute(sent, "frame", partners(k)).astype(F32)
        d_proj = jnp.concatenate([dq * jnp.asarray(q_scale, BF16), dkv_own.astype(BF16)], axis=1)
        g_qkv = jnp.dot(h_one.T, d_proj, preferred_element_type=F32).astype(BF16)
        d_hone = cube(jnp.dot(d_proj, w_qkv.T, preferred_element_type=F32))
        d_scale_one = jnp.sum(d_hone * normed_one, axis=1)
        d_shift_one = jnp.sum(d_hone, axis=1)
        d_input = d_middle + norm_back(d_hone * (1.0 + scale_one), normed_one, inv_one)
        input_grad = d_input.astype(BF16)
        piece_dmod = jnp.stack([d_shift_one, d_scale_one, d_gate_one, d_shift_two, d_scale_two, d_gate_two])
        frame_dmod = jnp.einsum("pf,jpd->jfd", selector, piece_dmod, precision=HIGHEST)

    if direct:
        updated = update_owned(
            owned_block,
            table,
            grad_block,
            master.reshape(-1, 128),
            first_moment.reshape(-1, 128),
            second_moment.reshape(-1, 128),
            outputs,
            input_grads,
            batch_size,
        )
        new_master, new_first, new_second = [a.reshape(1, block_size) for a in updated[:3]]
        outputs, input_grads = updated[3:]
    else:
        outputs, input_grads = swap_videos([block_output, input_grad], videos, per, 1)
        g_ada = lax.dot_general(
            cond.astype(F32),
            frame_dmod.transpose(1, 0, 2).reshape(frame_count, 6 * width),
            (((0,), (0,)), ((), ())),
            precision=HIGHEST,
        )
        flat_grads = jnp.concatenate(
            [piece_grad.astype(F32).reshape(-1) for piece_grad in (g_ada, g_qkv, g_out, g_in, g_down)]
        )
        arranged = jnp.take(flat_grads.reshape(-1, block_size), owned_block, axis=0).reshape(-1)
        shard_total = lax.psum_scatter(
            arranged, ("frame", "batch"), scatter_dimension=0, tiled=True
        ).reshape(1, block_size)
        new_master, new_first, new_second = adam(shard_total, master, first_moment, second_moment)
    return (outputs, input_grads, new_master, new_first, new_second)


def solution(mesh):
    placed = (
        P("batch", "frame", None),
        P("batch", "frame", None),
        P("batch"),
        P("batch", None),
        P(),
        P(("frame", "batch"), None),
        P(("frame", "batch"), None),
        P(("frame", "batch"), None),
    )
    return jax.shard_map(
        partial(shards, mesh.shape["frame"], mesh.shape["batch"]),
        mesh=mesh,
        in_specs=placed,
        out_specs=(
            P("batch", "frame", None),
            P("batch", "frame", None),
            P(("frame", "batch"), None),
            P(("frame", "batch"), None),
            P(("frame", "batch"), None),
        ),
        check_vma=False,
    )
```
